32 devices in a mesh: node: 16 (over z, y, x), board: 2 (over core).
Axes of the slice: x: 2, y: 2, z: 4, core: 2. Of those that a mesh axis runs over, the one named last changes fastest.
Arguments:
- logits: float32 [2, 4, 512, 1326], P('board', None, 'node'), may hold values from -310 to 310
- pot_size: float32 [4, 512], P(None, 'node'), may hold values from 1 to 20
- node_type: int32 [4, 512], P(None, 'node'), may hold values from 0 to 2, as said below
- parent_slot: int32 [4, 512], P(None, 'node'), may hold values from 0 to 511, as said below
- range_one: float32 [2, 1326], P('board'), may hold values from 0.05 to 1
- range_two: float32 [2, 1326], P('board'), may hold values from 0.05 to 1
- hand_rank: int32 [2, 1326], P('board'), may hold values from 0 to 7461
- live_mask: int32 [2, 1326], P('board'), may hold values 0 or 1
Outputs:
- new_logits: float32 [2, 4, 512, 1326], P('board', None, 'node')
- values_half: float32 [2, 4, 512, 1326], P('board', None, 'node')
The draws below stay inside these ranges and needn't reach their ends.
Inputs may be any that keep to these rules, and one draw needn't show every extreme that they name: `node_type`: 0 marks an inner node. At each level but the last, each aligned group of four slots holds exactly one node of type 0; the last level holds none. `parent_slot`: at level 0 every entry is 0. At a level above 0 the four nodes of an aligned group of four share one parent, a node of type 0 at the level before, and every such node is the parent of exactly one group; the parent's group index is the group's own index minus an offset of 0 to 7, one offset a level, modulo 512 / 4.
All inputs are finite; a program needn't handle non-finite values. No bound on the sum of `live_mask` on one device may be relied on, other than what follows from the above.
Results may differ from the reference program's by a relative error of at most 0.0003.
Values sent between devices are 32-bit elements; how exact they have to be, the bound alone decides.
No kernel may reach another device: no remote copies, remote signals or barrier semaphores. Data moves between devices by JAX's collectives and lax.ppermute only.
A program may use at most 64 MiB of HBM per device.

```python
import math
import jax
import jax.numpy as jnp
import numpy as np

HANDS = 1326
RANKS = 7462
LEVELS = 4
STEPS = 1
SLOT_DEV = 32
SLOTS = 512
BOARDS = 2


def draw_logits(key, part):
    full_shape = (BOARDS, LEVELS, SLOTS, HANDS)
    return 1.5 * jax.random.normal(key, full_shape, jnp.float32)


def tree_tables(key):
    groups = SLOTS // 4
    key_off, key_pick, key_kind = jax.random.split(jax.random.fold_in(key, 7), 3)
    offset = jax.random.randint(key_off, (LEVELS,), 0, SLOT_DEV // 4)
    branch = jax.random.randint(key_pick, (LEVELS, groups), 0, 4)
    end_kind = jax.random.randint(key_kind, (LEVELS, SLOTS), 1, 3)
    slot_ids = jnp.arange(SLOTS)
    group_ids = slot_ids // 4
    level_ids = jnp.arange(LEVELS)[:, None]
    owner_group = (group_ids[None, :] - offset[:, None]) % groups
    prev_branch = jnp.concatenate([branch[:1], branch[:-1]], axis=0)
    above_slot = 4 * owner_group + jnp.take_along_axis(prev_branch, owner_group, axis=1)
    parent_table = jnp.where(level_ids == 0, 0, above_slot)
    inner_mask = (slot_ids[None, :] % 4 == branch[:, group_ids]) & (level_ids < LEVELS - 1)
    type_table = jnp.where(inner_mask, 0, end_kind)
    return (parent_table.astype(jnp.int32), type_table.astype(jnp.int32))


def draw_node_type(key, part):
    return tree_tables(key)[1]


def draw_parent_slot(key, part):
    return tree_tables(key)[0]


def touch_ends(drawn, own_key, smallest, top_value):
    shape = drawn.shape
    place = [jax.random.randint(jax.random.fold_in(own_key, axis), (), 0, shape[axis]) for axis in range(len(shape))]
    drawn = drawn.at[tuple(place)].set(smallest)
    longest = shape.index(max(shape))
    place[longest] = (place[longest] + 1) % shape[longest]
    return drawn.at[tuple(place)].set(top_value)


def level_of(key, dims, pieces, low, top_value):
    level = 1.0
    for dim, parts in pieces:
        draws = jax.random.uniform(jax.random.fold_in(jax.random.fold_in(key, 6), dim), (parts,), jnp.float32, low / len(pieces), top_value / len(pieces))
        level = level * jnp.repeat(jnp.exp(draws), dims[dim] // parts).reshape((-1,) + (1,) * (len(dims) - 1 - dim))
    return level


def setup_inputs(seed: int = 0) -> dict:
    keys = jax.random.split(jax.random.key(seed), 9)
    logits = draw_logits(jax.random.fold_in(keys[8], 71), 0)
    pot_size = jnp.clip(jnp.exp(math.log(20.0) - 2.9957323 * jax.random.uniform(keys[1], (LEVELS, SLOTS), jnp.float32) ** level_of(keys[1], (LEVELS, SLOTS), ((1, 16),), -0.2, 0.2)), 1.0, 20.0)
    node_type = draw_node_type(jax.random.fold_in(keys[8], 71), 0)
    parent_slot = draw_parent_slot(jax.random.fold_in(keys[8], 71), 0)
    range_one = jnp.clip(0.05 + 0.95 * jax.random.uniform(keys[4], (BOARDS, HANDS), jnp.float32) ** level_of(keys[4], (BOARDS, HANDS), ((0, 2),), -0.2, 0.2), 0.05, 1.0)
    range_two = jnp.clip(0.05 + 0.95 * jax.random.uniform(keys[5], (BOARDS, HANDS), jnp.float32) ** level_of(keys[5], (BOARDS, HANDS), ((0, 2),), -0.2, 0.2), 0.05, 1.0)
    hand_rank = touch_ends(jax.random.randint(keys[6], (BOARDS, HANDS), 0, RANKS), jax.random.fold_in(keys[6], 1), 0, RANKS - 1).astype(jnp.int32)
    live_mask = touch_ends((jax.random.randint(keys[7], (BOARDS, HANDS), 0, 5) < 4).astype(jnp.int32), jax.random.fold_in(keys[7], 1), 0, 1)
    return dict(logits=logits, pot_size=pot_size, node_type=node_type, parent_slot=parent_slot, range_one=range_one, range_two=range_two, hand_rank=hand_rank, live_mask=live_mask)


step_scale = 0.5
eps_value = 1e-06

def card_pairs(hand_count):
    low_list = []
    high_list = []
    for low_card in range(52):
        for high_card in range(low_card + 1, 52):
            low_list.append(low_card)
            high_list.append(high_card)
    return (np.array(low_list[:hand_count], np.int32), np.array(high_list[:hand_count], np.int32))

def payoff_blocks(hand_rank, live_mask):
    low_np, high_np = card_pairs(hand_rank.shape[-1])
    low_card = jnp.asarray(low_np)
    high_card = jnp.asarray(high_np)
    clash_mask = (low_card[:, None] == low_card[None, :]) | (low_card[:, None] == high_card[None, :]) | (high_card[:, None] == low_card[None, :]) | (high_card[:, None] == high_card[None, :])
    alive_flag = live_mask > 0
    keep_pair = jnp.logical_not(clash_mask)[None] & alive_flag[:, :, None] & alive_flag[:, None, :]
    higher = hand_rank[:, :, None] > hand_rank[:, None, :]
    lower = hand_rank[:, :, None] < hand_rank[:, None, :]
    order_value = jnp.where(higher, 1.0, jnp.where(lower, -1.0, 0.0))
    show_block = jnp.where(keep_pair, order_value, 0.0).astype(jnp.bfloat16)
    compat_block = jnp.where(keep_pair, 1.0, 0.0).astype(jnp.bfloat16)
    return (show_block, compat_block)

def policy(logits):
    full_shape = logits.shape
    grouped = logits.reshape(full_shape[0], full_shape[1], full_shape[2] // 4, 4, full_shape[3])
    return jax.nn.softmax(grouped, axis=3).reshape(full_shape)

def reach_all(strategy, parent_slot, range_one, range_two):
    reach_one = range_one[:, None, :] * strategy[:, 0]
    reach_two = jnp.broadcast_to(range_two[:, None, :], reach_one.shape)
    list_one = [reach_one]
    list_two = [reach_two]
    for depth_idx in range(1, LEVELS):
        above_one = jnp.take(reach_one, parent_slot[depth_idx], axis=1)
        above_two = jnp.take(reach_two, parent_slot[depth_idx], axis=1)
        if depth_idx % 2 == 0:
            reach_one = above_one * strategy[:, depth_idx]
            reach_two = above_two
        else:
            reach_one = above_one
            reach_two = above_two * strategy[:, depth_idx]
        list_one.append(reach_one)
        list_two.append(reach_two)
    return (jnp.stack(list_one, axis=1), jnp.stack(list_two, axis=1))

def terminal_pay(reach_one, reach_two, pot_size, node_type, show_block, compat_block):
    boards = reach_one.shape[0]
    column_count = LEVELS * SLOTS
    level_sign = jnp.where(jnp.arange(LEVELS) % 2 == 0, -1.0, 1.0).astype(jnp.float32)
    show_scale = jnp.where(node_type == 2, pot_size, 0.0).astype(jnp.float32)
    fold_scale = jnp.where(node_type == 1, pot_size, 0.0).astype(jnp.float32) * level_sign[:, None]

    def columns(reach_value, scale_value):
        return (reach_value * scale_value[None, :, :, None]).astype(jnp.bfloat16).reshape(boards, column_count, HANDS)
    show_cols = jnp.concatenate([columns(reach_two, show_scale), columns(reach_one, show_scale)], axis=1)
    fold_cols = jnp.concatenate([columns(reach_two, fold_scale), -columns(reach_one, fold_scale)], axis=1)
    product = jnp.einsum('bij,bnj->bni', show_block.astype(jnp.float32), show_cols.astype(jnp.float32)) + jnp.einsum('bij,bnj->bni', compat_block.astype(jnp.float32), fold_cols.astype(jnp.float32))
    pay_one = product[:, :column_count].reshape(boards, LEVELS, SLOTS, HANDS)
    pay_two = product[:, column_count:].reshape(boards, LEVELS, SLOTS, HANDS)
    return (pay_one, pay_two)

def values_all(strategy, parent_slot, pay_one, pay_two):
    value_one = pay_one[:, LEVELS - 1]
    value_two = pay_two[:, LEVELS - 1]
    found_list = [None] * LEVELS
    found_list[LEVELS - 1] = value_one if (LEVELS - 1) % 2 == 0 else value_two

    def sum_up(term_value, child_level):
        moved = jnp.swapaxes(term_value, 0, 1)
        summed = jax.ops.segment_sum(moved, parent_slot[child_level], num_segments=SLOTS)
        return jnp.swapaxes(summed, 0, 1)
    for depth_idx in range(LEVELS - 2, -1, -1):
        child_level = depth_idx + 1
        weight = strategy[:, child_level]
        if child_level % 2 == 0:
            term_one = weight * value_one
            term_two = value_two
        else:
            term_one = value_one
            term_two = weight * value_two
        value_one = pay_one[:, depth_idx] + sum_up(term_one, child_level)
        value_two = pay_two[:, depth_idx] + sum_up(term_two, child_level)
        found_list[depth_idx] = value_one if depth_idx % 2 == 0 else value_two
    return jnp.stack(found_list, axis=1)

def operate(point, pot_size, node_type, parent_slot, range_one, range_two, show_block, compat_block):
    strategy = policy(point)
    reach_one, reach_two = reach_all(strategy, parent_slot, range_one, range_two)
    pay_one, pay_two = terminal_pay(reach_one, reach_two, pot_size, node_type, show_block, compat_block)
    return values_all(strategy, parent_slot, pay_one, pay_two)

def rate_for(values_found):
    square_sum = jnp.sum(values_found * values_found)
    return step_scale / jnp.sqrt(square_sum / values_found.size + eps_value)

def reference(logits, pot_size, node_type, parent_slot, range_one, range_two, hand_rank, live_mask):
    show_block, compat_block = payoff_blocks(hand_rank, live_mask)
    current = logits
    values_half = logits
    for turn_idx in range(STEPS):
        anchor_mix = 1.0 / (turn_idx + 2)
        base_point = current + anchor_mix * (logits - current)
        values_now = operate(current, pot_size, node_type, parent_slot, range_one, range_two, show_block, compat_block)
        half_point = base_point + rate_for(values_now) * values_now
        values_half = operate(half_point, pot_size, node_type, parent_slot, range_one, range_two, show_block, compat_block)
        current = base_point + rate_for(values_half) * values_half
    return (current, values_half)
```

```python
import functools

import jax
import jax.numpy as jnp
import numpy as np
from jax import lax
from jax.experimental import pallas as pl
from jax.experimental.pallas import tpu as pltpu
from jax.sharding import PartitionSpec as P

LANES = 128
CARDS = 52
step_scale = 0.5
eps_value = 1e-06
MEBI = 1 << 20


def padded(count):
    return -(-count // LANES) * LANES


def passed_along(value, axis, steps):
    count = lax.axis_size(axis)
    pairs = [(source, (source + steps) % count) for source in range(count)]
    return lax.ppermute(value, axis, pairs)


def card_rows(hand_count, wide):
    pairs = [(low, high) for low in range(CARDS) for high in range(low + 1, CARDS)]
    rows = np.full((2, wide), -1, np.int32)
    rows[:, :hand_count] = np.array(pairs[:hand_count], np.int32).T
    return rows


def payoff_kernel(hands, cards_ref, rank_ref, live_ref, out_ref, flat, left, right):
    wide = out_ref.shape[1]
    flat[...] = jnp.zeros(flat.shape, jnp.float32)
    flat[0:1, 0:hands] = rank_ref[...].astype(jnp.float32)
    flat[1:2, 0:hands] = (live_ref[...] > 0).astype(jnp.float32)
    dead = 1.0 - flat[1:2, :]
    feature = lax.broadcasted_iota(jnp.int32, (LANES, wide), 0)
    hit = (feature == cards_ref[0:1, :]) | (feature == cards_ref[1:2, :])
    base = jnp.where(hit, 1.0, 0.0)
    left[...] = jnp.where(feature == CARDS, dead, jnp.where(feature == CARDS + 1, 1.0, base))
    right[...] = jnp.where(
        feature == CARDS, 1.0, jnp.where(feature == CARDS + 1, dead, base)
    ).astype(jnp.bfloat16)
    rank_row = flat[0:1, :]
    for block in range(wide // LANES):
        part = slice(block * LANES, (block + 1) * LANES)
        left_block = left[:, part].T.astype(jnp.bfloat16)
        rank_col = jnp.broadcast_to(flat[0:1, part], (LANES, LANES)).T[:, 0:1]
        hits = jnp.dot(left_block, right[...], preferred_element_type=jnp.float32)
        compat = jnp.where(hits == 0.0, 1.0, 0.0)
        order = jnp.clip(rank_row - rank_col, -1.0, 1.0)
        out_ref[part, :] = (order * compat).astype(jnp.bfloat16)
        out_ref[wide + block * LANES : wide + (block + 1) * LANES, :] = compat.astype(jnp.bfloat16)


def payoff_blocks(hand_rank, live_mask):
    hands = hand_rank.shape[-1]
    wide = padded(hands)
    return pl.pallas_call(
        functools.partial(payoff_kernel, hands),
        out_shape=jax.ShapeDtypeStruct((2 * wide, wide), jnp.bfloat16),
        scratch_shapes=[
            pltpu.VMEM((8, wide), jnp.float32),
            pltpu.VMEM((LANES, wide), jnp.float32),
            pltpu.VMEM((LANES, wide), jnp.bfloat16),
        ],
        compiler_params=pltpu.CompilerParams(vmem_limit_bytes=20 * MEBI),
        cost_estimate=pl.CostEstimate(
            flops=2 * wide * wide * LANES, bytes_accessed=4 * wide * wide, transcendentals=0
        ),
        name="payoff",
    )(jnp.asarray(card_rows(hands, wide)), hand_rank, live_mask)


def pack_kernel(logits_ref, pot_ref, kind_ref, home_ref, right_ref, left_ref, far_ref, flat):
    levels, tiles, slots, _ = home_ref.shape
    hands = logits_ref.shape[-1]
    pot = pot_ref[...]
    kind = kind_ref[...]
    level = lax.broadcasted_iota(jnp.int32, pot.shape, 0)
    sign = jnp.where(level % 2 == 0, -1.0, 1.0)
    flat[...] = jnp.zeros(flat.shape, jnp.float32)
    flat[0:levels, 0:slots] = jnp.where(kind == 2, pot, 0.0)
    flat[levels : 2 * levels, 0:slots] = jnp.where(kind == 1, pot, 0.0) * sign
    turned = flat[...].T
    lane = lax.broadcasted_iota(jnp.int32, (slots, LANES), 1)
    for idx in range(levels):
        show = turned[0:slots, idx : idx + 1]
        fold = turned[0:slots, levels + idx : levels + idx + 1]
        home_ref[idx, tiles - 1] = jnp.where(
            lane == LANES - 2, show, jnp.where(lane == LANES - 1, fold, 0.0)
        )
        for tile in range(tiles):
            start = tile * LANES
            stop = min(start + LANES, hands)
            home_ref[idx, tile, :, 0 : stop - start] = logits_ref[0, idx, :, start:stop]
    right_ref[...] = home_ref[0]
    left_ref[...] = home_ref[2:4]
    far_ref[...] = home_ref[3, :, 0 : slots - 8, :]


def message_shapes(levels, slots, wide):
    tiles = wide // LANES
    return (
        jax.ShapeDtypeStruct((levels, tiles, slots, LANES), jnp.float32),
        jax.ShapeDtypeStruct((tiles, slots, LANES), jnp.float32),
        jax.ShapeDtypeStruct((2, tiles, slots, LANES), jnp.float32),
        jax.ShapeDtypeStruct((tiles, slots - 8, LANES), jnp.float32),
    )


def packed_rows(logits, pot_size, node_type):
    _, levels, slots, hands = logits.shape
    return pl.pallas_call(
        pack_kernel,
        out_shape=message_shapes(levels, slots, padded(hands)),
        scratch_shapes=[pltpu.VMEM((LANES, LANES), jnp.float32)],
        compiler_params=pltpu.CompilerParams(vmem_limit_bytes=10 * MEBI),
        name="pack",
    )(logits, pot_size, node_type)


def level_offsets(parent_ref, node_count, slots):
    groups = slots // 4
    total = groups * node_count
    first = lax.axis_index("node") * groups
    return [lax.rem(first - parent_ref[idx, 0] // 4 + total, total) for idx in (1, 2, 3)]


def inner_sum(inner, rows):
    total = jnp.where(inner[0], rows[0], 0.0)
    for idx in range(1, 4):
        total = total + jnp.where(inner[idx], rows[idx], 0.0)
    return total


def softmax_four(rows):
    top = jnp.maximum(jnp.maximum(rows[0], rows[1]), jnp.maximum(rows[2], rows[3]))
    lifted = [jnp.exp(row - top) for row in rows]
    total = (lifted[0] + lifted[1]) + (lifted[2] + lifted[3])
    return [row / total for row in lifted]


def operator_q(point, show, fold, range_one, range_two, block_ref, cols, pay):
    wide = block_ref.shape[1]
    inner = [
        [(show[idx][slot] == 0.0) & (fold[idx][slot] == 0.0) for slot in range(4)]
        for idx in range(4)
    ]
    strategy = [softmax_four(point[idx]) for idx in range(4)]
    top_one = [range_one * row for row in strategy[0]]
    above_one = inner_sum(inner[0], top_one)
    mid_two = [range_two * row for row in strategy[1]]
    above_two = inner_sum(inner[1], mid_two)
    low_one = [above_one * row for row in strategy[2]]
    last_one = inner_sum(inner[2], low_one)
    end_two = [above_two * row for row in strategy[3]]
    wide_two = jnp.broadcast_to(range_two, above_two.shape)
    reach_rows = [
        (0, [wide_two] * 4, 1.0),
        (1, mid_two, 1.0),
        (2, [above_two] * 4, 1.0),
        (3, end_two, 1.0),
        (1, [above_one] * 4, -1.0),
        (2, low_one, -1.0),
        (3, [last_one] * 4, -1.0),
    ]
    for unit, (idx, rows, fold_sign) in enumerate(reach_rows):
        for half in range(2):
            place = slice(unit * 32 + half * 16, unit * 32 + half * 16 + 16)
            pair = (2 * half, 2 * half + 1)
            cols[place, 0:wide] = jnp.concatenate(
                [rows[slot] * show[idx][slot] for slot in pair], axis=0
            ).astype(jnp.bfloat16)
            cols[place, wide : 2 * wide] = jnp.concatenate(
                [rows[slot] * (fold[idx][slot] * fold_sign) for slot in pair], axis=0
            ).astype(jnp.bfloat16)
    for start in range(0, wide, 2 * LANES):
        stop = min(start + 2 * LANES, wide)
        pay[:, start:stop] = jnp.dot(
            cols[...], block_ref[:, start:stop], preferred_element_type=jnp.float32
        )

    def paid(unit):
        return [pay[unit * 32 + slot * 8 : unit * 32 + slot * 8 + 8, :] for slot in range(4)]

    def added(rows):
        return (rows[0] + rows[1]) + (rows[2] + rows[3])

    def landed(rows, kept, term):
        return [rows[slot] + jnp.where(kept[slot], term, 0.0) for slot in range(4)]

    value_two_end = paid(6)
    term_two = added([strategy[3][slot] * value_two_end[slot] for slot in range(4)])
    term_two = added(landed(paid(5), inner[2], term_two))
    value_two_mid = landed(paid(4), inner[1], term_two)
    value_one_low = landed(paid(2), inner[2], added(paid(3)))
    term_one = added([strategy[2][slot] * value_one_low[slot] for slot in range(4)])
    term_one = added(landed(paid(1), inner[1], term_one))
    value_one_top = landed(paid(0), inner[0], term_one)
    return [value_one_top, value_two_mid, value_one_low, value_two_end]


def squares(found):
    total = None
    for rows in found:
        for row in rows:
            total = row * row if total is None else total + row * row
    return jnp.broadcast_to(jnp.sum(total), (1, LANES))


def scale_columns(rows):
    wide = rows[0][0].shape[1]
    show = [[row[:, wide - 2 : wide - 1] for row in level] for level in rows]
    fold = [[row[:, wide - 1 : wide] for row in level] for level in rows]
    return show, fold


def wide_row(store, place, row_ref):
    hands = row_ref.shape[1]
    store[place : place + 1, 0:hands] = row_ref[...]
    return store[place : place + 1, :]


def first_kernel(
    node_count,
    parent_ref,
    home_ref,
    from_left_ref,
    from_right_ref,
    from_far_ref,
    one_ref,
    two_ref,
    block_ref,
    chain_ref,
    value_ref,
    square_ref,
    window,
    ranges,
    cols,
    pay,
):
    _, tiles, slots, _ = home_ref.shape
    off_one, off_two, off_three = level_offsets(parent_ref, node_count, slots)
    window[0, :, 0:slots] = from_left_ref[...]
    window[0, :, slots : 2 * slots] = home_ref[0]
    window[1, :, 0:slots] = home_ref[1]
    window[2, :, 0:slots] = home_ref[2]
    window[2, :, slots : 2 * slots] = from_right_ref[0]
    window[3, :, 0:slots] = home_ref[3]
    window[3, :, slots : 2 * slots] = from_right_ref[1]
    window[3, :, 2 * slots : 3 * slots - 8] = from_far_ref[...]
    starts = [slots - 4 * off_one, 0, 4 * off_two, 4 * (off_two + off_three)]
    point = []
    for idx in range(4):
        rows = []
        for slot in range(4):
            place = pl.ds(starts[idx] + slot, slots // 4, stride=4)
            row = jnp.concatenate([window[idx, tile, place, :] for tile in range(tiles)], axis=1)
            chain_ref[idx, slot] = row
            rows.append(row)
        point.append(rows)
    show, fold = scale_columns(point)
    ranges[...] = jnp.zeros(ranges.shape, jnp.float32)
    range_one = wide_row(ranges, 0, one_ref)
    range_two = wide_row(ranges, 1, two_ref)
    found = operator_q(point, show, fold, range_one, range_two, block_ref, cols, pay)
    for idx in range(4):
        for slot in range(4):
            value_ref[idx, slot] = found[idx][slot]
    square_ref[...] = squares(found)


def rate_of(parts_ref, entry_count):
    square_sum = jnp.sum(parts_ref[...], axis=0, keepdims=True)[:, 0:1]
    return step_scale / jnp.sqrt(square_sum / entry_count + eps_value)


def second_kernel(
    entry_count,
    chain_ref,
    value_ref,
    parts_ref,
    one_ref,
    two_ref,
    block_ref,
    own_ref,
    left_ref,
    right_ref,
    far_ref,
    square_ref,
    ranges,
    cols,
    pay,
):
    _, tiles, slots, _ = own_ref.shape
    rate = rate_of(parts_ref, entry_count)
    raw = [[chain_ref[idx, slot] for slot in range(4)] for idx in range(4)]
    show, fold = scale_columns(raw)
    point = [
        [raw[idx][slot] + rate * value_ref[idx, slot] for slot in range(4)] for idx in range(4)
    ]
    ranges[...] = jnp.zeros(ranges.shape, jnp.float32)
    range_one = wide_row(ranges, 0, one_ref)
    range_two = wide_row(ranges, 1, two_ref)
    found = operator_q(point, show, fold, range_one, range_two, block_ref, cols, pay)
    square_ref[...] = squares(found)
    for idx in range(4):
        for slot in range(4):
            for tile in range(tiles):
                part = found[idx][slot][:, tile * LANES : (tile + 1) * LANES]
                own_ref[idx, tile, pl.ds(slot, slots // 4, stride=4), :] = part
    left_ref[...] = own_ref[0]
    right_ref[...] = own_ref[2:4]
    far_ref[...] = own_ref[3, :, 8:slots, :]


def last_kernel(
    node_count,
    entry_count,
    hands,
    parent_ref,
    own_ref,
    from_right_ref,
    from_left_ref,
    from_far_ref,
    parts_ref,
    logits_ref,
    new_ref,
    half_ref,
    window,
):
    _, tiles, slots, _ = own_ref.shape
    off_one, off_two, off_three = level_offsets(parent_ref, node_count, slots)
    rate = rate_of(parts_ref, entry_count)
    window[0, :, 0:slots] = own_ref[0]
    window[0, :, slots : 2 * slots] = from_right_ref[...]
    window[1, :, 0:slots] = own_ref[1]
    window[2, :, 0:slots] = from_left_ref[0]
    window[2, :, slots : 2 * slots] = own_ref[2]
    window[3, :, 8:slots] = from_far_ref[...]
    window[3, :, slots : 2 * slots] = from_left_ref[1]
    window[3, :, 2 * slots : 3 * slots] = own_ref[3]
    starts = [4 * off_one, 0, slots - 4 * off_two, 2 * slots - 4 * (off_two + off_three)]
    for idx in range(4):
        for tile in range(tiles):
            start = tile * LANES
            stop = min(start + LANES, hands)
            value = window[idx, tile, pl.ds(starts[idx], slots), :][:, 0 : stop - start]
            half_ref[0, idx, :, start:stop] = value
            new_ref[0, idx, :, start:stop] = logits_ref[0, idx, :, start:stop] + rate * value


def shared_parts(part):
    count = lax.axis_size("node") * lax.axis_size("board")
    spread = jnp.broadcast_to(part, (count, LANES))
    return lax.all_to_all(spread, ("node", "board"), 0, 0, tiled=True)


def per_device(
    logits, pot_size, node_type, parent_slot, range_one, range_two, hand_rank, live_mask
):
    _, levels, slots, hands = logits.shape
    wide = padded(hands)
    groups = slots // 4
    node_count = lax.axis_size("node")
    entry_count = float(logits.size * node_count * lax.axis_size("board"))
    vmem = pl.BlockSpec(memory_space=pltpu.VMEM)
    smem = pl.BlockSpec(memory_space=pltpu.SMEM)
    f32 = jnp.float32
    home, to_right, to_left, to_far = packed_rows(logits, pot_size, node_type)
    from_left = passed_along(to_right, "node", 1)
    from_right = passed_along(to_left, "node", -1)
    from_far = passed_along(to_far, "node", -2)
    blocks = payoff_blocks(hand_rank, live_mask)
    rows = 7 * slots
    work = [
        pltpu.VMEM((8, wide), f32),
        pltpu.VMEM((rows, 2 * wide), jnp.bfloat16),
        pltpu.VMEM((rows, wide), f32),
    ]
    chain_shape = jax.ShapeDtypeStruct((levels, 4, groups, wide), f32)
    square_shape = jax.ShapeDtypeStruct((1, LANES), f32)
    limit = pltpu.CompilerParams(vmem_limit_bytes=32 * MEBI)
    cost = pl.CostEstimate(
        flops=4 * rows * wide * wide, bytes_accessed=6 * wide * wide, transcendentals=0
    )
    chain, value, part = pl.pallas_call(
        functools.partial(first_kernel, node_count),
        out_shape=(chain_shape, chain_shape, square_shape),
        in_specs=[smem] + [vmem] * 7,
        scratch_shapes=[pltpu.VMEM((levels, wide // LANES, 3 * slots, LANES), f32)] + work,
        compiler_params=limit,
        cost_estimate=cost,
        name="first",
    )(parent_slot, home, from_left, from_right, from_far, range_one, range_two, blocks)
    parts = shared_parts(part)
    own, to_left, to_right, to_far, part = pl.pallas_call(
        functools.partial(second_kernel, entry_count),
        out_shape=message_shapes(levels, slots, wide) + (square_shape,),
        in_specs=[vmem] * 6,
        scratch_shapes=work,
        compiler_params=limit,
        cost_estimate=cost,
        name="second",
    )(chain, value, parts, range_one, range_two, blocks)
    from_right = passed_along(to_left, "node", -1)
    from_left = passed_along(to_right, "node", 1)
    from_far = passed_along(to_far, "node", 2)
    parts = shared_parts(part)
    out_shape = jax.ShapeDtypeStruct(logits.shape, f32)
    return pl.pallas_call(
        functools.partial(last_kernel, node_count, entry_count, hands),
        out_shape=(out_shape, out_shape),
        in_specs=[smem] + [vmem] * 6,
        scratch_shapes=[pltpu.VMEM((levels, wide // LANES, 3 * slots, LANES), f32)],
        compiler_params=pltpu.CompilerParams(vmem_limit_bytes=20 * MEBI),
        name="last",
    )(parent_slot, own, from_right, from_left, from_far, parts, logits)


def solution(mesh):
    return jax.shard_map(
        per_device,
        mesh=mesh,
        in_specs=(
            P("board", None, "node", None),
            P(None, "node"),
            P(None, "node"),
            P(None, "node"),
            P("board", None),
            P("board", None),
            P("board", None),
            P("board", None),
        ),
        out_specs=(P("board", None, "node", None), P("board", None, "node", None)),
        check_vma=False,
    )
```

```python
import functools

import jax
import jax.numpy as jnp
import numpy as np
from jax import lax
from jax.experimental import pallas as pl
from jax.experimental.pallas import tpu as pltpu
from jax.sharding import PartitionSpec as P

LANES = 128
CARDS = 52
step_scale = 0.5
eps_value = 1e-06
MEBI = 1 << 20


def padded(count):
    return -(-count // LANES) * LANES


def passed_along(value, axis, steps):
    count = lax.axis_size(axis)
    pairs = [(source, (source + steps) % count) for source in range(count)]
    return lax.ppermute(value, axis, pairs)


def card_rows(hand_count, wide):
    pairs = [(low, high) for low in range(CARDS) for high in range(low + 1, CARDS)]
    rows = np.full((2, wide), -1, np.int32)
    rows[:, :hand_count] = np.array(pairs[:hand_count], np.int32).T
    return rows


def payoff_kernel(hands, cards_ref, rank_ref, live_ref, out_ref, flat, left, right):
    wide = out_ref.shape[1]
    flat[...] = jnp.zeros(flat.shape, jnp.float32)
    flat[0:1, 0:hands] = rank_ref[...].astype(jnp.float32)
    flat[1:2, 0:hands] = (live_ref[...] > 0).astype(jnp.float32)
    dead = 1.0 - flat[1:2, :]
    feature = lax.broadcasted_iota(jnp.int32, (LANES, wide), 0)
    hit = (feature == cards_ref[0:1, :]) | (feature == cards_ref[1:2, :])
    base = jnp.where(hit, 1.0, 0.0)
    left[...] = jnp.where(feature == CARDS, dead, jnp.where(feature == CARDS + 1, 1.0, base))
    right[...] = jnp.where(
        feature == CARDS, 1.0, jnp.where(feature == CARDS + 1, dead, base)
    ).astype(jnp.bfloat16)
    rank_row = flat[0:1, :]
    for block in range(wide // LANES):
        part = slice(block * LANES, (block + 1) * LANES)
        left_block = left[:, part].T.astype(jnp.bfloat16)
        rank_col = jnp.broadcast_to(flat[0:1, part], (LANES, LANES)).T[:, 0:1]
        hits = jnp.dot(left_block, right[...], preferred_element_type=jnp.float32)
        compat = jnp.where(hits == 0.0, 1.0, 0.0)
        order = jnp.clip(rank_row - rank_col, -1.0, 1.0)
        out_ref[part, :] = (order * compat).astype(jnp.bfloat16)
        out_ref[wide + block * LANES : wide + (block + 1) * LANES, :] = compat.astype(jnp.bfloat16)


def payoff_blocks(hand_rank, live_mask):
    hands = hand_rank.shape[-1]
    wide = padded(hands)
    return pl.pallas_call(
        functools.partial(payoff_kernel, hands),
        out_shape=jax.ShapeDtypeStruct((2 * wide, wide), jnp.bfloat16),
        scratch_shapes=[
            pltpu.VMEM((8, wide), jnp.float32),
            pltpu.VMEM((LANES, wide), jnp.float32),
            pltpu.VMEM((LANES, wide), jnp.bfloat16),
        ],
        compiler_params=pltpu.CompilerParams(vmem_limit_bytes=20 * MEBI),
        cost_estimate=pl.CostEstimate(
            flops=2 * wide * wide * LANES, bytes_accessed=4 * wide * wide, transcendentals=0
        ),
        name="payoff",
    )(jnp.asarray(card_rows(hands, wide)), hand_rank, live_mask)


def pack_kernel(logits_ref, pot_ref, kind_ref, home_ref, right_ref, left_ref, far_ref, flat):
    levels, tiles, slots, _ = home_ref.shape
    hands = logits_ref.shape[-1]
    pot = pot_ref[...]
    kind = kind_ref[...]
    level = lax.broadcasted_iota(jnp.int32, pot.shape, 0)
    sign = jnp.where(level % 2 == 0, -1.0, 1.0)
    flat[...] = jnp.zeros(flat.shape, jnp.float32)
    flat[0:levels, 0:slots] = jnp.where(kind == 2, pot, 0.0)
    flat[levels : 2 * levels, 0:slots] = jnp.where(kind == 1, pot, 0.0) * sign
    turned = flat[...].T
    lane = lax.broadcasted_iota(jnp.int32, (slots, LANES), 1)
    for idx in range(levels):
        show = turned[0:slots, idx : idx + 1]
        fold = turned[0:slots, levels + idx : levels + idx + 1]
        home_ref[idx, tiles - 1] = jnp.where(
            lane == LANES - 2, show, jnp.where(lane == LANES - 1, fold, 0.0)
        )
        for tile in range(tiles):
            start = tile * LANES
            stop = min(start + LANES, hands)
            home_ref[idx, tile, :, 0 : stop - start] = logits_ref[0, idx, :, start:stop]
    right_ref[...] = home_ref[0]
    left_ref[...] = home_ref[2:4]
    far_ref[...] = home_ref[3, :, 0 : slots - 8, :]


def message_shapes(levels, slots, wide):
    tiles = wide // LANES
    return (
        jax.ShapeDtypeStruct((levels, tiles, slots, LANES), jnp.float32),
        jax.ShapeDtypeStruct((tiles, slots, LANES), jnp.float32),
        jax.ShapeDtypeStruct((2, tiles, slots, LANES), jnp.float32),
        jax.ShapeDtypeStruct((tiles, slots - 8, LANES), jnp.float32),
    )


def packed_rows(logits, pot_size, node_type):
    _, levels, slots, hands = logits.shape
    return pl.pallas_call(
        pack_kernel,
        out_shape=message_shapes(levels, slots, padded(hands)),
        scratch_shapes=[pltpu.VMEM((LANES, LANES), jnp.float32)],
        compiler_params=pltpu.CompilerParams(vmem_limit_bytes=10 * MEBI),
        name="pack",
    )(logits, pot_size, node_type)


def level_offsets(parent_ref, node_count, slots):
    groups = slots // 4
    total = groups * node_count
    first = lax.axis_index("node") * groups
    return [lax.rem(first - parent_ref[idx, 0] // 4 + total, total) for idx in (1, 2, 3)]


def inner_sum(inner, rows):
    total = jnp.where(inner[0], rows[0], 0.0)
    for idx in range(1, 4):
        total = total + jnp.where(inner[idx], rows[idx], 0.0)
    return total


def softmax_four(rows):
    top = jnp.maximum(jnp.maximum(rows[0], rows[1]), jnp.maximum(rows[2], rows[3]))
    lifted = [jnp.exp(row - top) for row in rows]
    total = (lifted[0] + lifted[1]) + (lifted[2] + lifted[3])
    return [row / total for row in lifted]


def operator_q(point, show, fold, range_one, range_two, block_ref, cols, pay):
    wide = block_ref.shape[1]
    inner = [
        [(show[idx][slot] == 0.0) & (fold[idx][slot] == 0.0) for slot in range(4)]
        for idx in range(4)
    ]
    strategy = [softmax_four(point[idx]) for idx in range(4)]
    top_one = [range_one * row for row in strategy[0]]
    above_one = inner_sum(inner[0], top_one)
    mid_two = [range_two * row for row in strategy[1]]
    above_two = inner_sum(inner[1], mid_two)
    low_one = [above_one * row for row in strategy[2]]
    last_one = inner_sum(inner[2], low_one)
    end_two = [above_two * row for row in strategy[3]]
    wide_two = jnp.broadcast_to(range_two, above_two.shape)
    reach_rows = [
        (0, [wide_two] * 4, 1.0),
        (1, mid_two, 1.0),
        (2, [above_two] * 4, 1.0),
        (3, end_two, 1.0),
        (1, [above_one] * 4, -1.0),
        (2, low_one, -1.0),
        (3, [last_one] * 4, -1.0),
    ]
    for unit, (idx, rows, fold_sign) in enumerate(reach_rows):
        for half in range(2):
            place = slice(unit * 32 + half * 16, unit * 32 + half * 16 + 16)
            pair = (2 * half, 2 * half + 1)
            cols[place, 0:wide] = jnp.concatenate(
                [rows[slot] * show[idx][slot] for slot in pair], axis=0
            ).astype(jnp.bfloat16)
            cols[place, wide : 2 * wide] = jnp.concatenate(
                [rows[slot] * (fold[idx][slot] * fold_sign) for slot in pair], axis=0
            ).astype(jnp.bfloat16)
    for start in range(0, wide, 2 * LANES):
        stop = min(start + 2 * LANES, wide)
        pay[:, start:stop] = jnp.dot(
            cols[...], block_ref[:, start:stop], preferred_element_type=jnp.float32
        )

    def paid(unit):
        return [pay[unit * 32 + slot * 8 : unit * 32 + slot * 8 + 8, :] for slot in range(4)]

    def added(rows):
        return (rows[0] + rows[1]) + (rows[2] + rows[3])

    def landed(rows, kept, term):
        return [rows[slot] + jnp.where(kept[slot], term, 0.0) for slot in range(4)]

    value_two_end = paid(6)
    term_two = added([strategy[3][slot] * value_two_end[slot] for slot in range(4)])
    term_two = added(landed(paid(5), inner[2], term_two))
    value_two_mid = landed(paid(4), inner[1], term_two)
    value_one_low = landed(paid(2), inner[2], added(paid(3)))
    term_one = added([strategy[2][slot] * value_one_low[slot] for slot in range(4)])
    term_one = added(landed(paid(1), inner[1], term_one))
    value_one_top = landed(paid(0), inner[0], term_one)
    return [value_one_top, value_two_mid, value_one_low, value_two_end]


def squares(found):
    total = None
    for rows in found:
        for row in rows:
            total = row * row if total is None else total + row * row
    return jnp.broadcast_to(jnp.sum(total), (1, LANES))


def scale_columns(rows):
    wide = rows[0][0].shape[1]
    show = [[row[:, wide - 2 : wide - 1] for row in level] for level in rows]
    fold = [[row[:, wide - 1 : wide] for row in level] for level in rows]
    return show, fold


def wide_row(store, place, row_ref):
    hands = row_ref.shape[1]
    store[place : place + 1, 0:hands] = row_ref[...]
    return store[place : place + 1, :]


def first_kernel(
    node_count,
    parent_ref,
    home_ref,
    from_left_ref,
    from_right_ref,
    from_far_ref,
    one_ref,
    two_ref,
    block_ref,
    chain_ref,
    value_ref,
    square_ref,
    window,
    ranges,
    cols,
    pay,
):
    _, tiles, slots, _ = home_ref.shape
    off_one, off_two, off_three = level_offsets(parent_ref, node_count, slots)
    window[0, :, 0:slots] = from_left_ref[...]
    window[0, :, slots : 2 * slots] = home_ref[0]
    window[1, :, 0:slots] = home_ref[1]
    window[2, :, 0:slots] = home_ref[2]
    window[2, :, slots : 2 * slots] = from_right_ref[0]
    window[3, :, 0:slots] = home_ref[3]
    window[3, :, slots : 2 * slots] = from_right_ref[1]
    window[3, :, 2 * slots : 3 * slots - 8] = from_far_ref[...]
    starts = [slots - 4 * off_one, 0, 4 * off_two, 4 * (off_two + off_three)]
    point = []
    for idx in range(4):
        rows = []
        for slot in range(4):
            place = pl.ds(starts[idx] + slot, slots // 4, stride=4)
            row = jnp.concatenate([window[idx, tile, place, :] for tile in range(tiles)], axis=1)
            chain_ref[idx, slot] = row
            rows.append(row)
        point.append(rows)
    show, fold = scale_columns(point)
    ranges[...] = jnp.zeros(ranges.shape, jnp.float32)
    range_one = wide_row(ranges, 0, one_ref)
    range_two = wide_row(ranges, 1, two_ref)
    found = operator_q(point, show, fold, range_one, range_two, block_ref, cols, pay)
    for idx in range(4):
        for slot in range(4):
            value_ref[idx, slot] = found[idx][slot]
    square_ref[...] = squares(found)


def rate_of(parts_ref, entry_count):
    square_sum = jnp.sum(parts_ref[...], axis=0, keepdims=True)[:, 0:1]
    return step_scale / jnp.sqrt(square_sum / entry_count + eps_value)


def second_kernel(
    entry_count,
    chain_ref,
    value_ref,
    parts_ref,
    one_ref,
    two_ref,
    block_ref,
    own_ref,
    left_ref,
    right_ref,
    far_ref,
    square_ref,
    ranges,
    cols,
    pay,
):
    _, tiles, slots, _ = own_ref.shape
    rate = rate_of(parts_ref, entry_count)
    raw = [[chain_ref[idx, slot] for slot in range(4)] for idx in range(4)]
    show, fold = scale_columns(raw)
    point = [
        [raw[idx][slot] + rate * value_ref[idx, slot] for slot in range(4)] for idx in range(4)
    ]
    ranges[...] = jnp.zeros(ranges.shape, jnp.float32)
    range_one = wide_row(ranges, 0, one_ref)
    range_two = wide_row(ranges, 1, two_ref)
    found = operator_q(point, show, fold, range_one, range_two, block_ref, cols, pay)
    square_ref[...] = squares(found)
    for idx in range(4):
        for slot in range(4):
            for tile in range(tiles):
                part = found[idx][slot][:, tile * LANES : (tile + 1) * LANES]
                own_ref[idx, tile, pl.ds(slot, slots // 4, stride=4), :] = part
    left_ref[...] = own_ref[0]
    right_ref[...] = own_ref[2:4]
    far_ref[...] = own_ref[3, :, 8:slots, :]


def last_kernel(
    node_count,
    entry_count,
    hands,
    parent_ref,
    own_ref,
    from_right_ref,
    from_left_ref,
    from_far_ref,
    parts_ref,
    logits_ref,
    new_ref,
    half_ref,
    window,
):
    _, tiles, slots, _ = own_ref.shape
    off_one, off_two, off_three = level_offsets(parent_ref, node_count, slots)
    rate = rate_of(parts_ref, entry_count)
    window[0, :, 0:slots] = own_ref[0]
    window[0, :, slots : 2 * slots] = from_right_ref[...]
    window[1, :, 0:slots] = own_ref[1]
    window[2, :, 0:slots] = from_left_ref[0]
    window[2, :, slots : 2 * slots] = own_ref[2]
    window[3, :, 8:slots] = from_far_ref[...]
    window[3, :, slots : 2 * slots] = from_left_ref[1]
    window[3, :, 2 * slots : 3 * slots] = own_ref[3]
    starts = [4 * off_one, 0, slots - 4 * off_two, 2 * slots - 4 * (off_two + off_three)]
    for idx in range(4):
        for tile in range(tiles):
            start = tile * LANES
            stop = min(start + LANES, hands)
            value = window[idx, tile, pl.ds(starts[idx], slots), :][:, 0 : stop - start]
            half_ref[0, idx, :, start:stop] = value
            new_ref[0, idx, :, start:stop] = logits_ref[0, idx, :, start:stop] + rate * value


def swapped_sum(part, axis, groups=None):
    count = len(groups[0]) if groups else lax.axis_size(axis)
    spread = jnp.broadcast_to(part, (count, LANES))
    got = lax.all_to_all(spread, axis, 0, 0, axis_index_groups=groups, tiled=True)
    return jnp.sum(got, axis=0, keepdims=True)


def staged_parts(part):
    count = lax.axis_size("node")
    inner = 1
    while inner * inner < count:
        inner *= 2
    near = [list(range(start, start + inner)) for start in range(0, count, inner)]
    across = [list(range(start, count, inner)) for start in range(inner)]
    part = swapped_sum(part, "board")
    part = swapped_sum(part, "node", near)
    return swapped_sum(part, "node", across)


def gathered_parts(part):
    return lax.all_gather(part, ("node", "board"), axis=0, tiled=True)


def per_device(
    logits, pot_size, node_type, parent_slot, range_one, range_two, hand_rank, live_mask
):
    _, levels, slots, hands = logits.shape
    wide = padded(hands)
    groups = slots // 4
    node_count = lax.axis_size("node")
    entry_count = float(logits.size * node_count * lax.axis_size("board"))
    vmem = pl.BlockSpec(memory_space=pltpu.VMEM)
    smem = pl.BlockSpec(memory_space=pltpu.SMEM)
    f32 = jnp.float32
    home, to_right, to_left, to_far = packed_rows(logits, pot_size, node_type)
    from_left = passed_along(to_right, "node", 1)
    from_right = passed_along(to_left, "node", -1)
    from_far = passed_along(to_far, "node", -2)
    blocks = payoff_blocks(hand_rank, live_mask)
    rows = 7 * slots
    work = [
        pltpu.VMEM((8, wide), f32),
        pltpu.VMEM((rows, 2 * wide), jnp.bfloat16),
        pltpu.VMEM((rows, wide), f32),
    ]
    chain_shape = jax.ShapeDtypeStruct((levels, 4, groups, wide), f32)
    square_shape = jax.ShapeDtypeStruct((1, LANES), f32)
    limit = pltpu.CompilerParams(vmem_limit_bytes=32 * MEBI)
    cost = pl.CostEstimate(
        flops=4 * rows * wide * wide, bytes_accessed=6 * wide * wide, transcendentals=0
    )
    chain, value, part = pl.pallas_call(
        functools.partial(first_kernel, node_count),
        out_shape=(chain_shape, chain_shape, square_shape),
        in_specs=[smem] + [vmem] * 7,
        scratch_shapes=[pltpu.VMEM((levels, wide // LANES, 3 * slots, LANES), f32)] + work,
        compiler_params=limit,
        cost_estimate=cost,
        name="first",
    )(parent_slot, home, from_left, from_right, from_far, range_one, range_two, blocks)
    parts = gathered_parts(part)
    own, to_left, to_right, to_far, part = pl.pallas_call(
        functools.partial(second_kernel, entry_count),
        out_shape=message_shapes(levels, slots, wide) + (square_shape,),
        in_specs=[vmem] * 6,
        scratch_shapes=work,
        compiler_params=limit,
        cost_estimate=cost,
        name="second",
    )(chain, value, parts, range_one, range_two, blocks)
    from_right = passed_along(to_left, "node", -1)
    from_left = passed_along(to_right, "node", 1)
    from_far = passed_along(to_far, "node", 2)
    parts = staged_parts(part)
    out_shape = jax.ShapeDtypeStruct(logits.shape, f32)
    return pl.pallas_call(
        functools.partial(last_kernel, node_count, entry_count, hands),
        out_shape=(out_shape, out_shape),
        in_specs=[smem] + [vmem] * 6,
        scratch_shapes=[pltpu.VMEM((levels, wide // LANES, 3 * slots, LANES), f32)],
        compiler_params=pltpu.CompilerParams(vmem_limit_bytes=20 * MEBI),
        name="last",
    )(parent_slot, own, from_right, from_left, from_far, parts, logits)


def solution(mesh):
    return jax.shard_map(
        per_device,
        mesh=mesh,
        in_specs=(
            P("board", None, "node", None),
            P(None, "node"),
            P(None, "node"),
            P(None, "node"),
            P("board", None),
            P("board", None),
            P("board", None),
            P("board", None),
        ),
        out_specs=(P("board", None, "node", None), P("board", None, "node", None)),
        check_vma=False,
    )
```

```python
import functools

import jax
import jax.numpy as jnp
import numpy as np
from jax import lax
from jax.experimental import pallas as pl
from jax.experimental.pallas import tpu as pltpu
from jax.sharding import PartitionSpec as P

LANES = 128
CARDS = 52
step_scale = 0.5
eps_value = 1e-06
MEBI = 1 << 20


def padded(count):
    return -(-count // LANES) * LANES


def passed_along(value, axis, steps):
    count = lax.axis_size(axis)
    pairs = [(source, (source + steps) % count) for source in range(count)]
    return lax.ppermute(value, axis, pairs)


def card_rows(hand_count, wide):
    pairs = [(low, high) for low in range(CARDS) for high in range(low + 1, CARDS)]
    rows = np.full((2, wide), -1, np.int32)
    rows[:, :hand_count] = np.array(pairs[:hand_count], np.int32).T
    return rows


def payoff_kernel(hands, cards_ref, rank_ref, live_ref, out_ref, flat, left, right):
    wide = out_ref.shape[1]
    flat[...] = jnp.zeros(flat.shape, jnp.float32)
    flat[0:1, 0:hands] = rank_ref[...].astype(jnp.float32)
    flat[1:2, 0:hands] = (live_ref[...] > 0).astype(jnp.float32)
    dead = 1.0 - flat[1:2, :]
    feature = lax.broadcasted_iota(jnp.int32, (LANES, wide), 0)
    hit = (feature == cards_ref[0:1, :]) | (feature == cards_ref[1:2, :])
    base = jnp.where(hit, 1.0, 0.0)
    left[...] = jnp.where(feature == CARDS, dead, jnp.where(feature == CARDS + 1, 1.0, base))
    right[...] = jnp.where(
        feature == CARDS, 1.0, jnp.where(feature == CARDS + 1, dead, base)
    ).astype(jnp.bfloat16)
    rank_row = flat[0:1, :]
    for block in range(wide // LANES):
        part = slice(block * LANES, (block + 1) * LANES)
        left_block = left[:, part].T.astype(jnp.bfloat16)
        rank_col = jnp.broadcast_to(flat[0:1, part], (LANES, LANES)).T[:, 0:1]
        hits = jnp.dot(left_block, right[...], preferred_element_type=jnp.float32)
        compat = jnp.where(hits == 0.0, 1.0, 0.0)
        order = jnp.clip(rank_row - rank_col, -1.0, 1.0)
        out_ref[part, :] = (order * compat).astype(jnp.bfloat16)
        out_ref[wide + block * LANES : wide + (block + 1) * LANES, :] = compat.astype(jnp.bfloat16)


def payoff_blocks(hand_rank, live_mask):
    hands = hand_rank.shape[-1]
    wide = padded(hands)
    return pl.pallas_call(
        functools.partial(payoff_kernel, hands),
        out_shape=jax.ShapeDtypeStruct((2 * wide, wide), jnp.bfloat16),
        scratch_shapes=[
            pltpu.VMEM((8, wide), jnp.float32),
            pltpu.VMEM((LANES, wide), jnp.float32),
            pltpu.VMEM((LANES, wide), jnp.bfloat16),
        ],
        compiler_params=pltpu.CompilerParams(vmem_limit_bytes=20 * MEBI),
        cost_estimate=pl.CostEstimate(
            flops=2 * wide * wide * LANES, bytes_accessed=4 * wide * wide, transcendentals=0
        ),
        name="payoff",
    )(jnp.asarray(card_rows(hands, wide)), hand_rank, live_mask)


def pack_kernel(logits_ref, pot_ref, kind_ref, home_ref, right_ref, left_ref, far_ref, flat):
    levels, tiles, slots, _ = home_ref.shape
    hands = logits_ref.shape[-1]
    pot = pot_ref[...]
    kind = kind_ref[...]
    level = lax.broadcasted_iota(jnp.int32, pot.shape, 0)
    sign = jnp.where(level % 2 == 0, -1.0, 1.0)
    flat[...] = jnp.zeros(flat.shape, jnp.float32)
    flat[0:levels, 0:slots] = jnp.where(kind == 2, pot, 0.0)
    flat[levels : 2 * levels, 0:slots] = jnp.where(kind == 1, pot, 0.0) * sign
    turned = flat[...].T
    lane = lax.broadcasted_iota(jnp.int32, (slots, LANES), 1)
    for idx in range(levels):
        show = turned[0:slots, idx : idx + 1]
        fold = turned[0:slots, levels + idx : levels + idx + 1]
        home_ref[idx, tiles - 1] = jnp.where(
            lane == LANES - 2, show, jnp.where(lane == LANES - 1, fold, 0.0)
        )
        for tile in range(tiles):
            start = tile * LANES
            stop = min(start + LANES, hands)
            home_ref[idx, tile, :, 0 : stop - start] = logits_ref[0, idx, :, start:stop]
    right_ref[...] = home_ref[0]
    left_ref[...] = home_ref[2:4]
    far_ref[...] = home_ref[3, :, 0 : slots - 8, :]


def message_shapes(levels, slots, wide):
    tiles = wide // LANES
    return (
        jax.ShapeDtypeStruct((levels, tiles, slots, LANES), jnp.float32),
        jax.ShapeDtypeStruct((tiles, slots, LANES), jnp.float32),
        jax.ShapeDtypeStruct((2, tiles, slots, LANES), jnp.float32),
        jax.ShapeDtypeStruct((tiles, slots - 8, LANES), jnp.float32),
    )


def packed_rows(logits, pot_size, node_type):
    _, levels, slots, hands = logits.shape
    return pl.pallas_call(
        pack_kernel,
        out_shape=message_shapes(levels, slots, padded(hands)),
        scratch_shapes=[pltpu.VMEM((LANES, LANES), jnp.float32)],
        compiler_params=pltpu.CompilerParams(vmem_limit_bytes=10 * MEBI),
        name="pack",
    )(logits, pot_size, node_type)


def level_offsets(parent_ref, node_count, slots):
    groups = slots // 4
    total = groups * node_count
    first = lax.axis_index("node") * groups
    return [lax.rem(first - parent_ref[idx, 0] // 4 + total, total) for idx in (1, 2, 3)]


def inner_sum(inner, rows):
    total = jnp.where(inner[0], rows[0], 0.0)
    for idx in range(1, 4):
        total = total + jnp.where(inner[idx], rows[idx], 0.0)
    return total


def softmax_four(rows):
    top = jnp.maximum(jnp.maximum(rows[0], rows[1]), jnp.maximum(rows[2], rows[3]))
    lifted = [jnp.exp(row - top) for row in rows]
    total = (lifted[0] + lifted[1]) + (lifted[2] + lifted[3])
    return [row / total for row in lifted]


def operator_q(point, show, fold, range_one, range_two, block_ref, cols, pay):
    wide = block_ref.shape[1]
    inner = [
        [(show[idx][slot] == 0.0) & (fold[idx][slot] == 0.0) for slot in range(4)]
        for idx in range(4)
    ]
    strategy = [softmax_four(point[idx]) for idx in range(4)]
    top_one = [range_one * row for row in strategy[0]]
    above_one = inner_sum(inner[0], top_one)
    mid_two = [range_two * row for row in strategy[1]]
    above_two = inner_sum(inner[1], mid_two)
    low_one = [above_one * row for row in strategy[2]]
    last_one = inner_sum(inner[2], low_one)
    end_two = [above_two * row for row in strategy[3]]
    wide_two = jnp.broadcast_to(range_two, above_two.shape)
    reach_rows = [
        (0, [wide_two] * 4, 1.0),
        (1, mid_two, 1.0),
        (2, [above_two] * 4, 1.0),
        (3, end_two, 1.0),
        (1, [above_one] * 4, -1.0),
        (2, low_one, -1.0),
        (3, [last_one] * 4, -1.0),
    ]
    for unit, (idx, rows, fold_sign) in enumerate(reach_rows):
        for half in range(2):
            place = slice(unit * 32 + half * 16, unit * 32 + half * 16 + 16)
            pair = (2 * half, 2 * half + 1)
            cols[place, 0:wide] = jnp.concatenate(
                [rows[slot] * show[idx][slot] for slot in pair], axis=0
            ).astype(jnp.bfloat16)
            cols[place, wide : 2 * wide] = jnp.concatenate(
                [rows[slot] * (fold[idx][slot] * fold_sign) for slot in pair], axis=0
            ).astype(jnp.bfloat16)
    for start in range(0, wide, 2 * LANES):
        stop = min(start + 2 * LANES, wide)
        pay[:, start:stop] = jnp.dot(
            cols[...], block_ref[:, start:stop], preferred_element_type=jnp.float32
        )

    def paid(unit):
        return [pay[unit * 32 + slot * 8 : unit * 32 + slot * 8 + 8, :] for slot in range(4)]

    def added(rows):
        return (rows[0] + rows[1]) + (rows[2] + rows[3])

    def landed(rows, kept, term):
        return [rows[slot] + jnp.where(kept[slot], term, 0.0) for slot in range(4)]

    value_two_end = paid(6)
    term_two = added([strategy[3][slot] * value_two_end[slot] for slot in range(4)])
    term_two = added(landed(paid(5), inner[2], term_two))
    value_two_mid = landed(paid(4), inner[1], term_two)
    value_one_low = landed(paid(2), inner[2], added(paid(3)))
    term_one = added([strategy[2][slot] * value_one_low[slot] for slot in range(4)])
    term_one = added(landed(paid(1), inner[1], term_one))
    value_one_top = landed(paid(0), inner[0], term_one)
    return [value_one_top, value_two_mid, value_one_low, value_two_end]


def squares(found):
    total = None
    for rows in found:
        for row in rows:
            total = row * row if total is None else total + row * row
    return jnp.broadcast_to(jnp.sum(total), (1, LANES))


def scale_columns(rows):
    wide = rows[0][0].shape[1]
    show = [[row[:, wide - 2 : wide - 1] for row in level] for level in rows]
    fold = [[row[:, wide - 1 : wide] for row in level] for level in rows]
    return show, fold


def wide_row(store, place, row_ref):
    hands = row_ref.shape[1]
    store[place : place + 1, 0:hands] = row_ref[...]
    return store[place : place + 1, :]


def first_kernel(
    node_count,
    parent_ref,
    home_ref,
    from_left_ref,
    from_right_ref,
    from_far_ref,
    one_ref,
    two_ref,
    block_ref,
    chain_ref,
    value_ref,
    square_ref,
    window,
    ranges,
    cols,
    pay,
):
    _, tiles, slots, _ = home_ref.shape
    off_one, off_two, off_three = level_offsets(parent_ref, node_count, slots)
    window[0, :, 0:slots] = from_left_ref[...]
    window[0, :, slots : 2 * slots] = home_ref[0]
    window[1, :, 0:slots] = home_ref[1]
    window[2, :, 0:slots] = home_ref[2]
    window[2, :, slots : 2 * slots] = from_right_ref[0]
    window[3, :, 0:slots] = home_ref[3]
    window[3, :, slots : 2 * slots] = from_right_ref[1]
    window[3, :, 2 * slots : 3 * slots - 8] = from_far_ref[...]
    starts = [slots - 4 * off_one, 0, 4 * off_two, 4 * (off_two + off_three)]
    point = []
    for idx in range(4):
        rows = []
        for slot in range(4):
            place = pl.ds(starts[idx] + slot, slots // 4, stride=4)
            row = jnp.concatenate([window[idx, tile, place, :] for tile in range(tiles)], axis=1)
            chain_ref[idx, slot] = row
            rows.append(row)
        point.append(rows)
    show, fold = scale_columns(point)
    ranges[...] = jnp.zeros(ranges.shape, jnp.float32)
    range_one = wide_row(ranges, 0, one_ref)
    range_two = wide_row(ranges, 1, two_ref)
    found = operator_q(point, show, fold, range_one, range_two, block_ref, cols, pay)
    for idx in range(4):
        for slot in range(4):
            value_ref[idx, slot] = found[idx][slot]
    square_ref[...] = squares(found)


def rate_of(parts_ref, entry_count):
    square_sum = jnp.sum(parts_ref[...], axis=0, keepdims=True)[:, 0:1]
    return step_scale / jnp.sqrt(square_sum / entry_count + eps_value)


def second_kernel(
    entry_count,
    chain_ref,
    value_ref,
    parts_ref,
    one_ref,
    two_ref,
    block_ref,
    own_ref,
    left_ref,
    right_ref,
    far_ref,
    square_ref,
    ranges,
    cols,
    pay,
):
    _, tiles, slots, _ = own_ref.shape
    rate = rate_of(parts_ref, entry_count)
    raw = [[chain_ref[idx, slot] for slot in range(4)] for idx in range(4)]
    show, fold = scale_columns(raw)
    point = [
        [raw[idx][slot] + rate * value_ref[idx, slot] for slot in range(4)] for idx in range(4)
    ]
    ranges[...] = jnp.zeros(ranges.shape, jnp.float32)
    range_one = wide_row(ranges, 0, one_ref)
    range_two = wide_row(ranges, 1, two_ref)
    found = operator_q(point, show, fold, range_one, range_two, block_ref, cols, pay)
    square_ref[...] = squares(found)
    for idx in range(4):
        for slot in range(4):
            for tile in range(tiles):
                part = found[idx][slot][:, tile * LANES : (tile + 1) * LANES]
                own_ref[idx, tile, pl.ds(slot, slots // 4, stride=4), :] = part
    left_ref[...] = own_ref[0]
    right_ref[...] = own_ref[2:4]
    far_ref[...] = own_ref[3, :, 8:slots, :]


def last_kernel(
    node_count,
    entry_count,
    hands,
    parent_ref,
    own_ref,
    from_right_ref,
    from_left_ref,
    from_far_ref,
    parts_ref,
    logits_ref,
    new_ref,
    half_ref,
    window,
):
    _, tiles, slots, _ = own_ref.shape
    off_one, off_two, off_three = level_offsets(parent_ref, node_count, slots)
    rate = rate_of(parts_ref, entry_count)
    window[0, :, 0:slots] = own_ref[0]
    window[0, :, slots : 2 * slots] = from_right_ref[...]
    window[1, :, 0:slots] = own_ref[1]
    window[2, :, 0:slots] = from_left_ref[0]
    window[2, :, slots : 2 * slots] = own_ref[2]
    window[3, :, 8:slots] = from_far_ref[...]
    window[3, :, slots : 2 * slots] = from_left_ref[1]
    window[3, :, 2 * slots : 3 * slots] = own_ref[3]
    starts = [4 * off_one, 0, slots - 4 * off_two, 2 * slots - 4 * (off_two + off_three)]
    for idx in range(4):
        for tile in range(tiles):
            start = tile * LANES
            stop = min(start + LANES, hands)
            value = window[idx, tile, pl.ds(starts[idx], slots), :][:, 0 : stop - start]
            half_ref[0, idx, :, start:stop] = value
            new_ref[0, idx, :, start:stop] = logits_ref[0, idx, :, start:stop] + rate * value


def shared_parts(part):
    nodes = lax.axis_size("node")
    boards = lax.axis_size("board")
    near = part
    for flip in range(2):
        for turn in range(boards):
            if flip == 0 and turn == 0:
                continue
            pairs = [
                (node * boards + board, (node ^ flip) * boards + (board + turn) % boards)
                for node in range(nodes)
                for board in range(boards)
            ]
            near = near + lax.ppermute(part, ("node", "board"), pairs)
    groups = [list(range(start, nodes, 2)) for start in range(2)]
    spread = jnp.broadcast_to(near, (nodes // 2, LANES))
    return lax.all_to_all(spread, "node", 0, 0, axis_index_groups=groups, tiled=True)


def per_device(
    logits, pot_size, node_type, parent_slot, range_one, range_two, hand_rank, live_mask
):
    _, levels, slots, hands = logits.shape
    wide = padded(hands)
    groups = slots // 4
    node_count = lax.axis_size("node")
    entry_count = float(logits.size * node_count * lax.axis_size("board"))
    vmem = pl.BlockSpec(memory_space=pltpu.VMEM)
    smem = pl.BlockSpec(memory_space=pltpu.SMEM)
    f32 = jnp.float32
    home, to_right, to_left, to_far = packed_rows(logits, pot_size, node_type)
    from_left = passed_along(to_right, "node", 1)
    from_right = passed_along(to_left, "node", -1)
    from_far = passed_along(to_far, "node", -2)
    blocks = payoff_blocks(hand_rank, live_mask)
    rows = 7 * slots
    work = [
        pltpu.VMEM((8, wide), f32),
        pltpu.VMEM((rows, 2 * wide), jnp.bfloat16),
        pltpu.VMEM((rows, wide), f32),
    ]
    chain_shape = jax.ShapeDtypeStruct((levels, 4, groups, wide), f32)
    square_shape = jax.ShapeDtypeStruct((1, LANES), f32)
    limit = pltpu.CompilerParams(vmem_limit_bytes=32 * MEBI)
    cost = pl.CostEstimate(
        flops=4 * rows * wide * wide, bytes_accessed=6 * wide * wide, transcendentals=0
    )
    chain, value, part = pl.pallas_call(
        functools.partial(first_kernel, node_count),
        out_shape=(chain_shape, chain_shape, square_shape),
        in_specs=[smem] + [vmem] * 7,
        scratch_shapes=[pltpu.VMEM((levels, wide // LANES, 3 * slots, LANES), f32)] + work,
        compiler_params=limit,
        cost_estimate=cost,
        name="first",
    )(parent_slot, home, from_left, from_right, from_far, range_one, range_two, blocks)
    parts = shared_parts(part)
    own, to_left, to_right, to_far, part = pl.pallas_call(
        functools.partial(second_kernel, entry_count),
        out_shape=message_shapes(levels, slots, wide) + (square_shape,),
        in_specs=[vmem] * 6,
        scratch_shapes=work,
        compiler_params=limit,
        cost_estimate=cost,
        name="second",
    )(chain, value, parts, range_one, range_two, blocks)
    from_right = passed_along(to_left, "node", -1)
    from_left = passed_along(to_right, "node", 1)
    from_far = passed_along(to_far, "node", 2)
    parts = shared_parts(part)
    out_shape = jax.ShapeDtypeStruct(logits.shape, f32)
    return pl.pallas_call(
        functools.partial(last_kernel, node_count, entry_count, hands),
        out_shape=(out_shape, out_shape),
        in_specs=[smem] + [vmem] * 6,
        scratch_shapes=[pltpu.VMEM((levels, wide // LANES, 3 * slots, LANES), f32)],
        compiler_params=pltpu.CompilerParams(vmem_limit_bytes=20 * MEBI),
        name="last",
    )(parent_slot, own, from_right, from_left, from_far, parts, logits)


def solution(mesh):
    return jax.shard_map(
        per_device,
        mesh=mesh,
        in_specs=(
            P("board", None, "node", None),
            P(None, "node"),
            P(None, "node"),
            P(None, "node"),
            P("board", None),
            P("board", None),
            P("board", None),
            P("board", None),
        ),
        out_specs=(P("board", None, "node", None), P("board", None, "node", None)),
        check_vma=False,
    )
```

```python
import functools

import jax
import jax.numpy as jnp
import numpy as np
from jax import lax
from jax.experimental import pallas as pl
from jax.experimental.pallas import tpu as pltpu
from jax.sharding import PartitionSpec as P

LANES = 128
CARDS = 52
step_scale = 0.5
eps_value = 1e-06
MEBI = 1 << 20
CLASSES = (5, 8, 10, 16)
FAR = 5


def padded(count):
    return -(-count // LANES) * LANES


def card_rows(hand_count, wide):
    pairs = [(low, high) for low in range(CARDS) for high in range(low + 1, CARDS)]
    rows = np.full((2, wide), -1, np.int32)
    rows[:, :hand_count] = np.array(pairs[:hand_count], np.int32).T
    return rows


def payoff_kernel(hands, cards_ref, rank_ref, live_ref, out_ref, flat, left, right):
    wide = out_ref.shape[1]
    flat[...] = jnp.zeros(flat.shape, jnp.float32)
    flat[0:1, 0:hands] = rank_ref[...].astype(jnp.float32)
    flat[1:2, 0:hands] = (live_ref[...] > 0).astype(jnp.float32)
    dead = 1.0 - flat[1:2, :]
    feature = lax.broadcasted_iota(jnp.int32, (LANES, wide), 0)
    hit = (feature == cards_ref[0:1, :]) | (feature == cards_ref[1:2, :])
    base = jnp.where(hit, 1.0, 0.0)
    left[...] = jnp.where(feature == CARDS, dead, jnp.where(feature == CARDS + 1, 1.0, base))
    right[...] = jnp.where(
        feature == CARDS, 1.0, jnp.where(feature == CARDS + 1, dead, base)
    ).astype(jnp.bfloat16)
    rank_row = flat[0:1, :]
    for block in range(wide // LANES):
        part = slice(block * LANES, (block + 1) * LANES)
        left_block = left[:, part].T.astype(jnp.bfloat16)
        rank_col = jnp.broadcast_to(flat[0:1, part], (LANES, LANES)).T[:, 0:1]
        hits = jnp.dot(left_block, right[...], preferred_element_type=jnp.float32)
        compat = jnp.where(hits == 0.0, 1.0, 0.0)
        order = jnp.clip(rank_row - rank_col, -1.0, 1.0)
        out_ref[part, :] = (order * compat).astype(jnp.bfloat16)
        out_ref[wide + block * LANES : wide + (block + 1) * LANES, :] = compat.astype(jnp.bfloat16)


def payoff_blocks(hand_rank, live_mask):
    hands = hand_rank.shape[-1]
    wide = padded(hands)
    return pl.pallas_call(
        functools.partial(payoff_kernel, hands),
        out_shape=jax.ShapeDtypeStruct((2 * wide, wide), jnp.bfloat16),
        scratch_shapes=[
            pltpu.VMEM((8, wide), jnp.float32),
            pltpu.VMEM((LANES, wide), jnp.float32),
            pltpu.VMEM((LANES, wide), jnp.bfloat16),
        ],
        compiler_params=pltpu.CompilerParams(vmem_limit_bytes=20 * MEBI),
        cost_estimate=pl.CostEstimate(
            flops=2 * wide * wide * LANES, bytes_accessed=4 * wide * wide, transcendentals=0
        ),
        name="payoff",
    )(jnp.asarray(card_rows(hands, wide)), hand_rank, live_mask)


def row_count(planes, groups):
    return -(-planes * groups // 8) * 8


def plan_of(parent_ref, node_count, groups):
    total = groups * node_count
    first = lax.axis_index("node") * groups
    off = [lax.rem(first - (parent_ref[idx, 0] >> 2) + total, total) for idx in (1, 2, 3)]
    one = off[0]
    two = one + off[1]
    three = two + off[2]
    low = jnp.maximum(one, three - groups)
    high = jnp.minimum(two, groups)
    middle = jnp.minimum(jnp.maximum((one + two + three + 2) >> 2, low), high)
    return middle, middle - one, two - middle, three - middle


def class_kernel(node_count, groups, parent_ref, class_ref):
    shift = plan_of(parent_ref, node_count, groups)
    need = jnp.maximum(shift[0] + shift[1], shift[2] + shift[3])
    found = jnp.int32(0)
    for size in CLASSES[:-1]:
        found = found + (need > size).astype(jnp.int32)
    class_ref[0] = jnp.where(shift[3] > groups, len(CLASSES) - 1, found)


def size_class(parent_slot, groups):
    smem = pl.BlockSpec(memory_space=pltpu.SMEM)
    return pl.pallas_call(
        functools.partial(class_kernel, lax.axis_size("node"), groups),
        out_shape=jax.ShapeDtypeStruct((1,), jnp.int32),
        in_specs=[smem],
        out_specs=smem,
        name="size_class",
    )(parent_slot)[0]


def fill_message(stage, message_ref, size, blocks, keep_from=8):
    tiles, planes = stage.shape[:2]
    for tile in range(tiles):
        for plane in range(planes):
            for block_ref, level, start in blocks:
                stage[tile, plane, pl.ds(start, 8), :] = block_ref[level, tile, plane]
            message_ref[tile, plane * size : plane * size + size, :] = stage[
                tile, plane, keep_from : keep_from + size, :
            ]


def wrap_message(node, wrap_ref, left_ref, right_ref):
    wrap_ref[...] = jnp.where(node == 0, left_ref[...], right_ref[...])


def pack_kernel(node_count, size, far, parent_ref, logits_ref, pot_ref, kind_ref, *rest):
    if far:
        home_ref, right_ref, left_ref, wrap_ref, far_ref, raw, flat, turned, stage = rest
    else:
        home_ref, right_ref, left_ref, wrap_ref, raw, flat, turned, stage = rest
    levels, tiles, planes, groups, _ = home_ref.shape
    slots = 4 * groups
    hands = logits_ref.shape[-1]
    pot = pot_ref[...]
    kind = kind_ref[...]
    level = lax.broadcasted_iota(jnp.int32, pot.shape, 0)
    sign = jnp.where(level % 2 == 0, -1.0, 1.0)
    flat[...] = jnp.zeros(flat.shape, jnp.float32)
    flat[0:levels, 0:slots] = jnp.where(kind == 2, pot, 0.0)
    flat[levels : 2 * levels, 0:slots] = jnp.where(kind == 1, pot, 0.0) * sign
    turned[...] = flat[...].T
    lane = lax.broadcasted_iota(jnp.int32, (groups, LANES), 1)
    for idx in range(levels):
        raw[idx, tiles - 1] = jnp.zeros((slots, LANES), jnp.float32)
        for tile in range(tiles):
            start = tile * LANES
            stop = min(start + LANES, hands)
            raw[idx, tile, :, 0 : stop - start] = logits_ref[0, idx, :, start:stop]
            first = raw[idx, tile, pl.ds(0, groups, stride=4), :]
            for plane in range(planes):
                row = raw[idx, tile, pl.ds(plane + 1, groups, stride=4), :] - first
                if tile == tiles - 1 and plane == 0:
                    for slot in range(4):
                        scale = turned[pl.ds(slot, groups, stride=4), :]
                        row = jnp.where(lane == LANES - 8 + slot, scale[:, idx : idx + 1], row)
                        fold = scale[:, levels + idx : levels + idx + 1]
                        row = jnp.where(lane == LANES - 4 + slot, fold, row)
                home_ref[idx, tile, plane] = row
    shift = plan_of(parent_ref, node_count, groups)
    fill_message(
        stage, right_ref, size, [(home_ref, 1, shift[0] + shift[1]), (home_ref, 0, shift[0])]
    )
    fill_message(stage, left_ref, size, [(home_ref, 2, 8), (home_ref, 3, 8 + shift[2])])
    wrap_message(lax.axis_index("node"), wrap_ref, left_ref, right_ref)
    if far:
        for tile in range(tiles):
            for plane in range(planes):
                far_ref[tile, plane * FAR : plane * FAR + FAR, :] = home_ref[3, tile, plane, 0:FAR, :]


def message_shapes(levels, planes, groups, wide, size, far):
    tiles = wide // LANES
    message = jax.ShapeDtypeStruct((tiles, row_count(planes, size), LANES), jnp.float32)
    shapes = [jax.ShapeDtypeStruct((levels, tiles, planes, groups, LANES), jnp.float32)]
    shapes += [message] * 3
    if far:
        shapes.append(jax.ShapeDtypeStruct((tiles, row_count(planes, FAR), LANES), jnp.float32))
    return shapes


def sent_on(right, left, wrap, far, far_steps):
    count = lax.axis_size("node")
    from_left = lax.ppermute(right, "node", [(src, src + 1) for src in range(count - 1)])
    from_right = lax.ppermute(left, "node", [(src + 1, src) for src in range(count - 1)])
    around = lax.ppermute(wrap, "node", [(0, count - 1), (count - 1, 0)])
    got = [from_left, from_right, around]
    for message in far:
        pairs = [(src, (src + far_steps) % count) for src in range(count)]
        got.append(lax.ppermute(message, "node", pairs))
    return got


def spread_message(stage, message_ref, around_ref, use_around, size):
    tiles, planes = stage.shape[:2]
    for tile in range(tiles):
        for plane in range(planes):
            place = slice(plane * size, plane * size + size)
            stage[tile, plane, 8 : 8 + size, :] = jnp.where(
                use_around, around_ref[tile, place, :], message_ref[tile, place, :]
            )


def inner_sum(inner, rows):
    total = jnp.where(inner[0], rows[0], 0.0)
    for idx in range(1, 4):
        total = total + jnp.where(inner[idx], rows[idx], 0.0)
    return total


def softmax_four(rows):
    top = jnp.maximum(jnp.maximum(rows[0], rows[1]), jnp.maximum(rows[2], 0.0))
    lifted = [jnp.exp(-top)] + [jnp.exp(row - top) for row in rows]
    total = (lifted[0] + lifted[1]) + (lifted[2] + lifted[3])
    return [row / total for row in lifted]


def operator_q(point, show, fold, range_one, range_two, block_ref, cols, pay, top_value=None):
    wide = block_ref.shape[1]
    inner = [
        [(show[idx][slot] == 0.0) & (fold[idx][slot] == 0.0) for slot in range(4)]
        for idx in range(4)
    ]
    strategy = [softmax_four(point[idx]) for idx in range(4)]
    top_one = [range_one * row for row in strategy[0]]
    above_one = inner_sum(inner[0], top_one)
    mid_two = [range_two * row for row in strategy[1]]
    above_two = inner_sum(inner[1], mid_two)
    low_one = [above_one * row for row in strategy[2]]
    last_one = inner_sum(inner[2], low_one)
    end_two = [above_two * row for row in strategy[3]]
    wide_two = jnp.broadcast_to(range_two, above_two.shape)
    reach_rows = [
        (0, [wide_two] * 4, 1.0),
        (1, mid_two, 1.0),
        (2, [above_two] * 4, 1.0),
        (3, end_two, 1.0),
        (1, [above_one] * 4, -1.0),
        (2, low_one, -1.0),
        (3, [last_one] * 4, -1.0),
    ]
    if top_value is not None:
        reach_rows = reach_rows[1:]
    skipped = 7 - len(reach_rows)
    for unit, (idx, rows, fold_sign) in enumerate(reach_rows):
        for half in range(2):
            place = slice(unit * 32 + half * 16, unit * 32 + half * 16 + 16)
            pair = (2 * half, 2 * half + 1)
            cols[place, 0:wide] = jnp.concatenate(
                [rows[slot] * show[idx][slot] for slot in pair], axis=0
            ).astype(jnp.bfloat16)
            cols[place, wide : 2 * wide] = jnp.concatenate(
                [rows[slot] * (fold[idx][slot] * fold_sign) for slot in pair], axis=0
            ).astype(jnp.bfloat16)
    for start in range(0, wide, 2 * LANES):
        stop = min(start + 2 * LANES, wide)
        pay[:, start:stop] = jnp.dot(
            cols[...], block_ref[:, start:stop], preferred_element_type=jnp.float32
        )

    def paid(unit):
        start = (unit - skipped) * 32
        return [pay[start + slot * 8 : start + slot * 8 + 8, :] for slot in range(4)]

    def added(rows):
        return (rows[0] + rows[1]) + (rows[2] + rows[3])

    def landed(rows, kept, term):
        return [rows[slot] + jnp.where(kept[slot], term, 0.0) for slot in range(4)]

    value_two_end = paid(6)
    term_two = added([strategy[3][slot] * value_two_end[slot] for slot in range(4)])
    term_two = added(landed(paid(5), inner[2], term_two))
    value_two_mid = landed(paid(4), inner[1], term_two)
    value_one_low = landed(paid(2), inner[2], added(paid(3)))
    term_one = added([strategy[2][slot] * value_one_low[slot] for slot in range(4)])
    term_one = added(landed(paid(1), inner[1], term_one))
    if top_value is None:
        value_one_top = landed(paid(0), inner[0], term_one)
    else:
        value_one_top = [
            jnp.where(inner[0][slot], term_one, top_value[slot]) for slot in range(4)
        ]
    return [value_one_top, value_two_mid, value_one_low, value_two_end]


def squares(found):
    total = None
    for rows in found:
        for row in rows:
            total = row * row if total is None else total + row * row
    return jnp.broadcast_to(jnp.sum(total), (1, LANES))


def scale_columns(rows):
    wide = rows[0][0].shape[1]
    show = [
        [level[0][:, wide - 8 + slot : wide - 7 + slot] for slot in range(4)] for level in rows
    ]
    fold = [
        [level[0][:, wide - 4 + slot : wide - 4 + slot + 1] for slot in range(4)] for level in rows
    ]
    return show, fold


def wide_row(store, place, row_ref):
    hands = row_ref.shape[1]
    store[place : place + 1, 0:hands] = row_ref[...]
    return store[place : place + 1, :]


def first_kernel(node_count, size, far, parent_ref, home_ref, left_ref, right_ref, wrap_ref, *rest):
    if far:
        far_ref, rest = rest[0], rest[1:]
    one_ref, two_ref, block_ref, chain_ref, value_ref, square_ref = rest[:6]
    from_left, from_right, window, ranges, cols, pay = rest[6:]
    _, tiles, planes, groups, _ = home_ref.shape
    node = lax.axis_index("node")
    shift = plan_of(parent_ref, node_count, groups)
    spread_message(from_left, left_ref, wrap_ref, node == 0, size)
    spread_message(from_right, right_ref, wrap_ref, node == node_count - 1, size)
    chain = lax.broadcasted_iota(jnp.int32, (groups, LANES), 0)
    point = [[[] for _ in range(planes)] for _ in range(4)]
    for tile in range(tiles):
        for plane in range(planes):
            part = window.at[tile, plane]
            part[8:16, :] = home_ref[0, tile, plane]
            part[24:32, :] = home_ref[1, tile, plane]
            part[32:40, :] = home_ref[3, tile, plane]
            from_right[tile, plane, 0:8, :] = home_ref[2, tile, plane]
            top = jnp.where(
                chain < shift[0],
                from_left[tile, plane, 8:16, :],
                part[pl.ds(8 - shift[0], 8), :],
            )
            mid = jnp.where(
                chain < shift[1],
                from_left[tile, plane, pl.ds(8 + shift[0], 8), :],
                part[pl.ds(24 - shift[1], 8), :],
            )
            low = from_right[tile, plane, pl.ds(shift[2], 8), :]
            end = jnp.where(
                chain + shift[3] < 8,
                part[pl.ds(32 + shift[3], 8), :],
                from_right[tile, plane, pl.ds(shift[2] + shift[3], 8), :],
            )
            if far:
                part[56 : 56 + FAR, :] = far_ref[tile, plane * FAR : plane * FAR + FAR, :]
                end = jnp.where(chain + shift[3] < 16, end, part[pl.ds(40 + shift[3], 8), :])
            for idx, row in enumerate((top, mid, low, end)):
                point[idx][plane].append(row)
    point = [[jnp.concatenate(rows, axis=1) for rows in level] for level in point]
    for idx in range(4):
        for plane in range(planes):
            chain_ref[idx, plane] = point[idx][plane]
    show, fold = scale_columns(point)
    ranges[...] = jnp.zeros(ranges.shape, jnp.float32)
    range_one = wide_row(ranges, 0, one_ref)
    range_two = wide_row(ranges, 1, two_ref)
    found = operator_q(point, show, fold, range_one, range_two, block_ref, cols, pay)
    for idx in range(4):
        for slot in range(4):
            value_ref[idx, slot] = found[idx][slot]
    square_ref[...] = squares(found)


def rate_of(parts_ref, entry_count):
    square_sum = jnp.sum(parts_ref[...], axis=0, keepdims=True)[:, 0:1]
    return step_scale / jnp.sqrt(square_sum / entry_count + eps_value)


def second_kernel(node_count, entry_count, size, far, parent_ref, chain_ref, value_ref, *rest):
    parts_ref, one_ref, two_ref, block_ref, own_ref, right_ref, left_ref, wrap_ref = rest[:8]
    rest = rest[8:]
    if far:
        far_ref, rest = rest[0], rest[1:]
    square_ref, stage, ranges, cols, pay = rest
    _, tiles, planes, groups, _ = own_ref.shape
    rate = rate_of(parts_ref, entry_count)
    raw = [[chain_ref[idx, plane] for plane in range(3)] for idx in range(4)]
    show, fold = scale_columns(raw)
    point = [
        [
            raw[idx][plane] + rate * (value_ref[idx, plane + 1] - value_ref[idx, 0])
            for plane in range(3)
        ]
        for idx in range(4)
    ]
    ranges[...] = jnp.zeros(ranges.shape, jnp.float32)
    range_one = wide_row(ranges, 0, one_ref)
    range_two = wide_row(ranges, 1, two_ref)
    top_value = [value_ref[0, slot] for slot in range(4)]
    found = operator_q(point, show, fold, range_one, range_two, block_ref, cols, pay, top_value)
    square_ref[...] = squares(found)
    for idx in range(4):
        for slot in range(4):
            for tile in range(tiles):
                own_ref[idx, tile, slot] = found[idx][slot][:, tile * LANES : (tile + 1) * LANES]
    shift = plan_of(parent_ref, node_count, groups)
    fill_message(stage, left_ref, size, [(own_ref, 0, 8), (own_ref, 1, 8 + shift[0])])
    fill_message(
        stage, right_ref, size, [(own_ref, 3, shift[2] + shift[3]), (own_ref, 2, shift[2])]
    )
    wrap_message(lax.axis_index("node"), wrap_ref, left_ref, right_ref)
    if far:
        for tile in range(tiles):
            for plane in range(planes):
                stage[tile, plane, pl.ds(jnp.maximum(shift[3] - 8, 0), 8), :] = own_ref[
                    3, tile, plane
                ]
                far_ref[tile, plane * FAR : plane * FAR + FAR, :] = stage[tile, plane, 8 : 8 + FAR, :]


def last_kernel(node_count, entry_count, size, far, parent_ref, own_ref, left_ref, right_ref, *rest):
    wrap_ref, rest = rest[0], rest[1:]
    if far:
        far_ref, rest = rest[0], rest[1:]
    parts_ref, logits_ref, new_ref, half_ref, from_left, from_right, window, lined = rest
    _, tiles, planes, groups, _ = own_ref.shape
    hands = logits_ref.shape[-1]
    node = lax.axis_index("node")
    shift = plan_of(parent_ref, node_count, groups)
    rate = rate_of(parts_ref, entry_count)
    spread_message(from_left, left_ref, wrap_ref, node == 0, size)
    spread_message(from_right, right_ref, wrap_ref, node == node_count - 1, size)
    group = lax.broadcasted_iota(jnp.int32, (groups, LANES), 0)
    for tile in range(tiles):
        start = tile * LANES
        stop = min(start + LANES, hands)
        for plane in range(planes):
            part = window.at[tile, plane]
            part[0:8, :] = own_ref[1, tile, plane]
            part[24:32, :] = own_ref[2, tile, plane]
            part[40:48, :] = own_ref[3, tile, plane]
            from_right[tile, plane, 0:8, :] = own_ref[0, tile, plane]
            top = from_right[tile, plane, pl.ds(shift[0], 8), :]
            mid = jnp.where(
                group + shift[1] < 8,
                part[pl.ds(shift[1], 8), :],
                from_right[tile, plane, pl.ds(shift[0] + shift[1], 8), :],
            )
            low = jnp.where(
                group < shift[2],
                from_left[tile, plane, 8:16, :],
                part[pl.ds(24 - shift[2], 8), :],
            )
            end = jnp.where(
                group < shift[3],
                from_left[tile, plane, pl.ds(8 + shift[2], 8), :],
                part[pl.ds(40 - jnp.minimum(shift[3], 8), 8), :],
            )
            if far:
                part[56 : 56 + FAR, :] = far_ref[tile, plane * FAR : plane * FAR + FAR, :]
                end = jnp.where(group < shift[3] - 8, part[56:64, :], end)
            for idx, row in enumerate((top, mid, low, end)):
                lined[idx, tile, pl.ds(plane, groups, stride=4), :] = row
        for idx in range(4):
            value = lined[idx, tile][:, 0 : stop - start]
            half_ref[0, idx, :, start:stop] = value
            new_ref[0, idx, :, start:stop] = logits_ref[0, idx, :, start:stop] + rate * value


def shared_parts(part):
    count = lax.axis_size("node") * lax.axis_size("board")
    spread = jnp.broadcast_to(part, (count, LANES))
    return lax.all_to_all(spread, ("node", "board"), 0, 0, tiled=True)


def step_of_class(
    size,
    far,
    logits,
    pot_size,
    node_type,
    parent_slot,
    range_one,
    range_two,
    hand_rank,
    live_mask,
):
    _, levels, slots, hands = logits.shape
    wide = padded(hands)
    tiles = wide // LANES
    groups = slots // 4
    node_count = lax.axis_size("node")
    entry_count = float(logits.size * node_count * lax.axis_size("board"))
    vmem = pl.BlockSpec(memory_space=pltpu.VMEM)
    smem = pl.BlockSpec(memory_space=pltpu.SMEM)
    f32 = jnp.float32

    def limit(mebi):
        return pltpu.CompilerParams(vmem_limit_bytes=mebi * MEBI)

    def stage(planes, rows=32):
        return pltpu.VMEM((tiles, planes, rows, LANES), f32)

    home, *sent = pl.pallas_call(
        functools.partial(pack_kernel, node_count, size, far),
        out_shape=message_shapes(levels, 3, groups, wide, size, far),
        in_specs=[smem] + [vmem] * 3,
        scratch_shapes=[
            pltpu.VMEM((levels, tiles, slots, LANES), f32),
            pltpu.VMEM((LANES, LANES), f32),
            pltpu.VMEM((LANES, LANES), f32),
            stage(3),
        ],
        compiler_params=limit(12),
        name="pack",
    )(parent_slot, logits, pot_size, node_type)
    got = sent_on(sent[0], sent[1], sent[2], sent[3:], -2)
    blocks = payoff_blocks(hand_rank, live_mask)
    rows = 7 * slots

    def work(count):
        return [
            pltpu.VMEM((8, wide), f32),
            pltpu.VMEM((count, 2 * wide), jnp.bfloat16),
            pltpu.VMEM((count, wide), f32),
        ]

    def cost(count):
        return pl.CostEstimate(
            flops=4 * count * wide * wide, bytes_accessed=6 * wide * wide, transcendentals=0
        )

    square_shape = jax.ShapeDtypeStruct((1, LANES), f32)
    chain, value, part = pl.pallas_call(
        functools.partial(first_kernel, node_count, size, far),
        out_shape=(
            jax.ShapeDtypeStruct((levels, 3, groups, wide), f32),
            jax.ShapeDtypeStruct((levels, 4, groups, wide), f32),
            square_shape,
        ),
        in_specs=[smem] + [vmem] * (4 + len(got)),
        scratch_shapes=[stage(3), stage(3), stage(3, 64)] + work(rows),
        compiler_params=limit(32),
        cost_estimate=cost(rows),
        name="first",
    )(parent_slot, home, *got, range_one, range_two, blocks)
    parts = shared_parts(part)
    own, *sent, part = pl.pallas_call(
        functools.partial(second_kernel, node_count, entry_count, size, far),
        out_shape=message_shapes(levels, 4, groups, wide, size, far) + [square_shape],
        in_specs=[smem] + [vmem] * 6,
        scratch_shapes=[stage(4)] + work(rows - slots),
        compiler_params=limit(32),
        cost_estimate=cost(rows - slots),
        name="second",
    )(parent_slot, chain, value, parts, range_one, range_two, blocks)
    got = sent_on(sent[0], sent[1], sent[2], sent[3:], 2)
    parts = shared_parts(part)
    out_shape = jax.ShapeDtypeStruct(logits.shape, f32)
    return pl.pallas_call(
        functools.partial(last_kernel, node_count, entry_count, size, far),
        out_shape=(out_shape, out_shape),
        in_specs=[smem] + [vmem] * (3 + len(got)),
        scratch_shapes=[
            stage(4),
            stage(4),
            stage(4, 64),
            pltpu.VMEM((levels, tiles, slots, LANES), f32),
        ],
        compiler_params=limit(24),
        name="last",
    )(parent_slot, own, *got, parts, logits)


def per_device(
    logits, pot_size, node_type, parent_slot, range_one, range_two, hand_rank, live_mask
):
    branches = [
        functools.partial(step_of_class, size, size == CLASSES[-1]) for size in CLASSES
    ]
    return lax.switch(
        size_class(parent_slot, logits.shape[2] // 4),
        branches,
        logits,
        pot_size,
        node_type,
        parent_slot,
        range_one,
        range_two,
        hand_rank,
        live_mask,
    )


def solution(mesh):
    return jax.shard_map(
        per_device,
        mesh=mesh,
        in_specs=(
            P("board", None, "node", None),
            P(None, "node"),
            P(None, "node"),
            P(None, "node"),
            P("board", None),
            P("board", None),
            P("board", None),
            P("board", None),
        ),
        out_specs=(P("board", None, "node", None), P("board", None, "node", None)),
        check_vma=False,
    )
```

```python
import functools

import jax
import jax.numpy as jnp
import numpy as np
from jax import lax
from jax.experimental import pallas as pl
from jax.experimental.pallas import tpu as pltpu
from jax.sharding import PartitionSpec as P

LANES = 128
CARDS = 52
step_scale = 0.5
eps_value = 1e-06
MEBI = 1 << 20
CLASSES = (5, 8, 10, 16)
FAR = 5


def padded(count):
    return -(-count // LANES) * LANES


def card_rows(hand_count, wide):
    pairs = [(low, high) for low in range(CARDS) for high in range(low + 1, CARDS)]
    rows = np.full((2, wide), -1, np.int32)
    rows[:, :hand_count] = np.array(pairs[:hand_count], np.int32).T
    return rows


def payoff_kernel(hands, cards_ref, rank_ref, live_ref, out_ref, flat, left, right):
    wide = out_ref.shape[1]
    flat[...] = jnp.zeros(flat.shape, jnp.float32)
    flat[0:1, 0:hands] = rank_ref[...].astype(jnp.float32)
    flat[1:2, 0:hands] = (live_ref[...] > 0).astype(jnp.float32)
    dead = 1.0 - flat[1:2, :]
    feature = lax.broadcasted_iota(jnp.int32, (LANES, wide), 0)
    hit = (feature == cards_ref[0:1, :]) | (feature == cards_ref[1:2, :])
    base = jnp.where(hit, 1.0, 0.0)
    left[...] = jnp.where(feature == CARDS, dead, jnp.where(feature == CARDS + 1, 1.0, base))
    right[...] = jnp.where(
        feature == CARDS, 1.0, jnp.where(feature == CARDS + 1, dead, base)
    ).astype(jnp.bfloat16)
    rank_row = flat[0:1, :]
    for block in range(wide // LANES):
        part = slice(block * LANES, (block + 1) * LANES)
        left_block = left[:, part].T.astype(jnp.bfloat16)
        rank_col = jnp.broadcast_to(flat[0:1, part], (LANES, LANES)).T[:, 0:1]
        hits = jnp.dot(left_block, right[...], preferred_element_type=jnp.float32)
        compat = jnp.where(hits == 0.0, 1.0, 0.0)
        order = jnp.clip(rank_row - rank_col, -1.0, 1.0)
        out_ref[part, :] = (order * compat).astype(jnp.bfloat16)
        out_ref[wide + block * LANES : wide + (block + 1) * LANES, :] = compat.astype(jnp.bfloat16)


def payoff_blocks(hand_rank, live_mask):
    hands = hand_rank.shape[-1]
    wide = padded(hands)
    return pl.pallas_call(
        functools.partial(payoff_kernel, hands),
        out_shape=jax.ShapeDtypeStruct((2 * wide, wide), jnp.bfloat16),
        scratch_shapes=[
            pltpu.VMEM((8, wide), jnp.float32),
            pltpu.VMEM((LANES, wide), jnp.float32),
            pltpu.VMEM((LANES, wide), jnp.bfloat16),
        ],
        compiler_params=pltpu.CompilerParams(vmem_limit_bytes=20 * MEBI),
        cost_estimate=pl.CostEstimate(
            flops=2 * wide * wide * LANES, bytes_accessed=4 * wide * wide, transcendentals=0
        ),
        name="payoff",
    )(jnp.asarray(card_rows(hands, wide)), hand_rank, live_mask)


def row_count(planes, groups):
    return -(-planes * groups // 8) * 8


def plan_of(parent_ref, node_count, groups):
    total = groups * node_count
    first = lax.axis_index("node") * groups
    off = [lax.rem(first - (parent_ref[idx, 0] >> 2) + total, total) for idx in (1, 2, 3)]
    one = off[0]
    two = one + off[1]
    three = two + off[2]
    low = jnp.maximum(one, three - groups)
    high = jnp.minimum(two, groups)
    middle = jnp.minimum(jnp.maximum((one + two + three + 2) >> 2, low), high)
    return middle, middle - one, two - middle, three - middle


def class_kernel(node_count, groups, parent_ref, class_ref):
    shift = plan_of(parent_ref, node_count, groups)
    need = jnp.maximum(shift[0] + shift[1], shift[2] + shift[3])
    found = jnp.int32(0)
    for size in CLASSES[:-1]:
        found = found + (need > size).astype(jnp.int32)
    class_ref[0] = jnp.where(shift[3] > groups, len(CLASSES) - 1, found)


def size_class(parent_slot, groups):
    smem = pl.BlockSpec(memory_space=pltpu.SMEM)
    return pl.pallas_call(
        functools.partial(class_kernel, lax.axis_size("node"), groups),
        out_shape=jax.ShapeDtypeStruct((1,), jnp.int32),
        in_specs=[smem],
        out_specs=smem,
        name="size_class",
    )(parent_slot)[0]


def fill_message(stage, message_ref, size, blocks, keep_from=8):
    tiles, planes = stage.shape[:2]
    for tile in range(tiles):
        for plane in range(planes):
            for block_ref, level, start in blocks:
                stage[tile, plane, pl.ds(start, 8), :] = block_ref[level, tile, plane]
            message_ref[tile, plane * size : plane * size + size, :] = stage[
                tile, plane, keep_from : keep_from + size, :
            ]


def fill_messages(node, stage, message_refs, size, block_ref, to_left, to_right):
    even = lax.rem(node, 2) == 0
    for message_ref, on_left in zip(message_refs, (even, jnp.logical_not(even))):
        blocks = [
            (block_ref, jnp.where(on_left, near[0], far[0]), jnp.where(on_left, near[1], far[1]))
            for near, far in zip(to_left, to_right)
        ]
        fill_message(stage, message_ref, size, blocks)


def pack_kernel(node_count, size, far, parent_ref, logits_ref, pot_ref, kind_ref, *rest):
    if far:
        home_ref, odd_ref, even_ref, far_ref, raw, flat, turned, stage = rest
    else:
        home_ref, odd_ref, even_ref, raw, flat, turned, stage = rest
    levels, tiles, planes, groups, _ = home_ref.shape
    slots = 4 * groups
    hands = logits_ref.shape[-1]
    pot = pot_ref[...]
    kind = kind_ref[...]
    level = lax.broadcasted_iota(jnp.int32, pot.shape, 0)
    sign = jnp.where(level % 2 == 0, -1.0, 1.0)
    flat[...] = jnp.zeros(flat.shape, jnp.float32)
    flat[0:levels, 0:slots] = jnp.where(kind == 2, pot, 0.0)
    flat[levels : 2 * levels, 0:slots] = jnp.where(kind == 1, pot, 0.0) * sign
    turned[...] = flat[...].T
    lane = lax.broadcasted_iota(jnp.int32, (groups, LANES), 1)
    for idx in range(levels):
        raw[idx, tiles - 1] = jnp.zeros((slots, LANES), jnp.float32)
        for tile in range(tiles):
            start = tile * LANES
            stop = min(start + LANES, hands)
            raw[idx, tile, :, 0 : stop - start] = logits_ref[0, idx, :, start:stop]
            first = raw[idx, tile, pl.ds(0, groups, stride=4), :]
            for plane in range(planes):
                row = raw[idx, tile, pl.ds(plane + 1, groups, stride=4), :] - first
                if tile == tiles - 1 and plane == 0:
                    for slot in range(4):
                        scale = turned[pl.ds(slot, groups, stride=4), :]
                        row = jnp.where(lane == LANES - 8 + slot, scale[:, idx : idx + 1], row)
                        fold = scale[:, levels + idx : levels + idx + 1]
                        row = jnp.where(lane == LANES - 4 + slot, fold, row)
                home_ref[idx, tile, plane] = row
    shift = plan_of(parent_ref, node_count, groups)
    fill_messages(
        lax.axis_index("node"),
        stage,
        (odd_ref, even_ref),
        size,
        home_ref,
        [(2, 8), (3, 8 + shift[2])],
        [(1, shift[0] + shift[1]), (0, shift[0])],
    )
    if far:
        for tile in range(tiles):
            for plane in range(planes):
                far_ref[tile, plane * FAR : plane * FAR + FAR, :] = home_ref[3, tile, plane, 0:FAR, :]


def message_shapes(levels, planes, groups, wide, size, far):
    tiles = wide // LANES
    message = jax.ShapeDtypeStruct((tiles, row_count(planes, size), LANES), jnp.float32)
    shapes = [jax.ShapeDtypeStruct((levels, tiles, planes, groups, LANES), jnp.float32)]
    shapes += [message] * 2
    if far:
        shapes.append(jax.ShapeDtypeStruct((tiles, row_count(planes, FAR), LANES), jnp.float32))
    return shapes


def sent_on(odd, even, far, far_steps):
    count = lax.axis_size("node")
    edges = [(src, (src + 1) % count) for src in range(count)]
    got = []
    for message, first in ((odd, 1), (even, 0)):
        pairs = [pair for edge in edges[first::2] for pair in (edge, edge[::-1])]
        got.append(lax.ppermute(message, "node", pairs))
    for message in far:
        pairs = [(src, (src + far_steps) % count) for src in range(count)]
        got.append(lax.ppermute(message, "node", pairs))
    return got


def spread_messages(node, from_left, from_right, odd_ref, even_ref, size):
    tiles, planes = from_left.shape[:2]
    even = lax.rem(node, 2) == 0
    for tile in range(tiles):
        for plane in range(planes):
            place = slice(plane * size, plane * size + size)
            odd_part = odd_ref[tile, place, :]
            even_part = even_ref[tile, place, :]
            from_left[tile, plane, 8 : 8 + size, :] = jnp.where(even, odd_part, even_part)
            from_right[tile, plane, 8 : 8 + size, :] = jnp.where(even, even_part, odd_part)


def inner_sum(inner, rows):
    total = jnp.where(inner[0], rows[0], 0.0)
    for idx in range(1, 4):
        total = total + jnp.where(inner[idx], rows[idx], 0.0)
    return total


def softmax_four(rows):
    top = jnp.maximum(jnp.maximum(rows[0], rows[1]), jnp.maximum(rows[2], 0.0))
    lifted = [jnp.exp(-top)] + [jnp.exp(row - top) for row in rows]
    total = (lifted[0] + lifted[1]) + (lifted[2] + lifted[3])
    return [row / total for row in lifted]


def operator_q(point, show, fold, range_one, range_two, block_ref, cols, pay, top_value=None):
    wide = block_ref.shape[1]
    inner = [
        [(show[idx][slot] == 0.0) & (fold[idx][slot] == 0.0) for slot in range(4)]
        for idx in range(4)
    ]
    strategy = [softmax_four(point[idx]) for idx in range(4)]
    top_one = [range_one * row for row in strategy[0]]
    above_one = inner_sum(inner[0], top_one)
    mid_two = [range_two * row for row in strategy[1]]
    above_two = inner_sum(inner[1], mid_two)
    low_one = [above_one * row for row in strategy[2]]
    last_one = inner_sum(inner[2], low_one)
    end_two = [above_two * row for row in strategy[3]]
    wide_two = jnp.broadcast_to(range_two, above_two.shape)
    reach_rows = [
        (0, [wide_two] * 4, 1.0),
        (1, mid_two, 1.0),
        (2, [above_two] * 4, 1.0),
        (3, end_two, 1.0),
        (1, [above_one] * 4, -1.0),
        (2, low_one, -1.0),
        (3, [last_one] * 4, -1.0),
    ]
    if top_value is not None:
        reach_rows = reach_rows[1:]
    skipped = 7 - len(reach_rows)
    for unit, (idx, rows, fold_sign) in enumerate(reach_rows):
        for half in range(2):
            place = slice(unit * 32 + half * 16, unit * 32 + half * 16 + 16)
            pair = (2 * half, 2 * half + 1)
            cols[place, 0:wide] = jnp.concatenate(
                [rows[slot] * show[idx][slot] for slot in pair], axis=0
            ).astype(jnp.bfloat16)
            cols[place, wide : 2 * wide] = jnp.concatenate(
                [rows[slot] * (fold[idx][slot] * fold_sign) for slot in pair], axis=0
            ).astype(jnp.bfloat16)
    for start in range(0, wide, 2 * LANES):
        stop = min(start + 2 * LANES, wide)
        pay[:, start:stop] = jnp.dot(
            cols[...], block_ref[:, start:stop], preferred_element_type=jnp.float32
        )

    def paid(unit):
        start = (unit - skipped) * 32
        return [pay[start + slot * 8 : start + slot * 8 + 8, :] for slot in range(4)]

    def added(rows):
        return (rows[0] + rows[1]) + (rows[2] + rows[3])

    def landed(rows, kept, term):
        return [rows[slot] + jnp.where(kept[slot], term, 0.0) for slot in range(4)]

    value_two_end = paid(6)
    term_two = added([strategy[3][slot] * value_two_end[slot] for slot in range(4)])
    term_two = added(landed(paid(5), inner[2], term_two))
    value_two_mid = landed(paid(4), inner[1], term_two)
    value_one_low = landed(paid(2), inner[2], added(paid(3)))
    term_one = added([strategy[2][slot] * value_one_low[slot] for slot in range(4)])
    term_one = added(landed(paid(1), inner[1], term_one))
    if top_value is None:
        value_one_top = landed(paid(0), inner[0], term_one)
    else:
        value_one_top = [
            jnp.where(inner[0][slot], term_one, top_value[slot]) for slot in range(4)
        ]
    return [value_one_top, value_two_mid, value_one_low, value_two_end]


def squares(found):
    total = None
    for rows in found:
        for row in rows:
            total = row * row if total is None else total + row * row
    return jnp.broadcast_to(jnp.sum(total), (1, LANES))


def scale_columns(rows):
    wide = rows[0][0].shape[1]
    show = [
        [level[0][:, wide - 8 + slot : wide - 7 + slot] for slot in range(4)] for level in rows
    ]
    fold = [
        [level[0][:, wide - 4 + slot : wide - 4 + slot + 1] for slot in range(4)] for level in rows
    ]
    return show, fold


def wide_row(store, place, row_ref):
    hands = row_ref.shape[1]
    store[place : place + 1, 0:hands] = row_ref[...]
    return store[place : place + 1, :]


def first_kernel(node_count, size, far, parent_ref, home_ref, odd_ref, even_ref, *rest):
    if far:
        far_ref, rest = rest[0], rest[1:]
    one_ref, two_ref, block_ref, chain_ref, value_ref, square_ref = rest[:6]
    from_left, from_right, window, ranges, cols, pay = rest[6:]
    _, tiles, planes, groups, _ = home_ref.shape
    shift = plan_of(parent_ref, node_count, groups)
    spread_messages(lax.axis_index("node"), from_left, from_right, odd_ref, even_ref, size)
    chain = lax.broadcasted_iota(jnp.int32, (groups, LANES), 0)
    point = [[[] for _ in range(planes)] for _ in range(4)]
    for tile in range(tiles):
        for plane in range(planes):
            part = window.at[tile, plane]
            part[8:16, :] = home_ref[0, tile, plane]
            part[24:32, :] = home_ref[1, tile, plane]
            part[32:40, :] = home_ref[3, tile, plane]
            from_right[tile, plane, 0:8, :] = home_ref[2, tile, plane]
            top = jnp.where(
                chain < shift[0],
                from_left[tile, plane, 8:16, :],
                part[pl.ds(8 - shift[0], 8), :],
            )
            mid = jnp.where(
                chain < shift[1],
                from_left[tile, plane, pl.ds(8 + shift[0], 8), :],
                part[pl.ds(24 - shift[1], 8), :],
            )
            low = from_right[tile, plane, pl.ds(shift[2], 8), :]
            end = jnp.where(
                chain + shift[3] < 8,
                part[pl.ds(32 + shift[3], 8), :],
                from_right[tile, plane, pl.ds(shift[2] + shift[3], 8), :],
            )
            if far:
                part[56 : 56 + FAR, :] = far_ref[tile, plane * FAR : plane * FAR + FAR, :]
                end = jnp.where(chain + shift[3] < 16, end, part[pl.ds(40 + shift[3], 8), :])
            for idx, row in enumerate((top, mid, low, end)):
                point[idx][plane].append(row)
    point = [[jnp.concatenate(rows, axis=1) for rows in level] for level in point]
    for idx in range(4):
        for plane in range(planes):
            chain_ref[idx, plane] = point[idx][plane]
    show, fold = scale_columns(point)
    ranges[...] = jnp.zeros(ranges.shape, jnp.float32)
    range_one = wide_row(ranges, 0, one_ref)
    range_two = wide_row(ranges, 1, two_ref)
    found = operator_q(point, show, fold, range_one, range_two, block_ref, cols, pay)
    for idx in range(4):
        for slot in range(4):
            value_ref[idx, slot] = found[idx][slot]
    square_ref[...] = squares(found)


def rate_of(parts_ref, entry_count):
    square_sum = jnp.sum(parts_ref[...], axis=0, keepdims=True)[:, 0:1]
    return step_scale / jnp.sqrt(square_sum / entry_count + eps_value)


def second_kernel(node_count, entry_count, size, far, parent_ref, chain_ref, value_ref, *rest):
    parts_ref, one_ref, two_ref, block_ref, own_ref, odd_ref, even_ref = rest[:7]
    rest = rest[7:]
    if far:
        far_ref, rest = rest[0], rest[1:]
    square_ref, stage, ranges, cols, pay = rest
    _, tiles, planes, groups, _ = own_ref.shape
    rate = rate_of(parts_ref, entry_count)
    raw = [[chain_ref[idx, plane] for plane in range(3)] for idx in range(4)]
    show, fold = scale_columns(raw)
    point = [
        [
            raw[idx][plane] + rate * (value_ref[idx, plane + 1] - value_ref[idx, 0])
            for plane in range(3)
        ]
        for idx in range(4)
    ]
    ranges[...] = jnp.zeros(ranges.shape, jnp.float32)
    range_one = wide_row(ranges, 0, one_ref)
    range_two = wide_row(ranges, 1, two_ref)
    top_value = [value_ref[0, slot] for slot in range(4)]
    found = operator_q(point, show, fold, range_one, range_two, block_ref, cols, pay, top_value)
    square_ref[...] = squares(found)
    for idx in range(4):
        for slot in range(4):
            for tile in range(tiles):
                own_ref[idx, tile, slot] = found[idx][slot][:, tile * LANES : (tile + 1) * LANES]
    shift = plan_of(parent_ref, node_count, groups)
    fill_messages(
        lax.axis_index("node"),
        stage,
        (odd_ref, even_ref),
        size,
        own_ref,
        [(0, 8), (1, 8 + shift[0])],
        [(3, shift[2] + shift[3]), (2, shift[2])],
    )
    if far:
        for tile in range(tiles):
            for plane in range(planes):
                stage[tile, plane, pl.ds(jnp.maximum(shift[3] - 8, 0), 8), :] = own_ref[
                    3, tile, plane
                ]
                far_ref[tile, plane * FAR : plane * FAR + FAR, :] = stage[tile, plane, 8 : 8 + FAR, :]


def last_kernel(node_count, entry_count, size, far, parent_ref, own_ref, odd_ref, even_ref, *rest):
    if far:
        far_ref, rest = rest[0], rest[1:]
    parts_ref, logits_ref, new_ref, half_ref, from_left, from_right, window, lined = rest
    _, tiles, planes, groups, _ = own_ref.shape
    hands = logits_ref.shape[-1]
    shift = plan_of(parent_ref, node_count, groups)
    rate = rate_of(parts_ref, entry_count)
    spread_messages(lax.axis_index("node"), from_left, from_right, odd_ref, even_ref, size)
    group = lax.broadcasted_iota(jnp.int32, (groups, LANES), 0)
    for tile in range(tiles):
        start = tile * LANES
        stop = min(start + LANES, hands)
        for plane in range(planes):
            part = window.at[tile, plane]
            part[0:8, :] = own_ref[1, tile, plane]
            part[24:32, :] = own_ref[2, tile, plane]
            part[40:48, :] = own_ref[3, tile, plane]
            from_right[tile, plane, 0:8, :] = own_ref[0, tile, plane]
            top = from_right[tile, plane, pl.ds(shift[0], 8), :]
            mid = jnp.where(
                group + shift[1] < 8,
                part[pl.ds(shift[1], 8), :],
                from_right[tile, plane, pl.ds(shift[0] + shift[1], 8), :],
            )
            low = jnp.where(
                group < shift[2],
                from_left[tile, plane, 8:16, :],
                part[pl.ds(24 - shift[2], 8), :],
            )
            end = jnp.where(
                group < shift[3],
                from_left[tile, plane, pl.ds(8 + shift[2], 8), :],
                part[pl.ds(40 - jnp.minimum(shift[3], 8), 8), :],
            )
            if far:
                part[56 : 56 + FAR, :] = far_ref[tile, plane * FAR : plane * FAR + FAR, :]
                end = jnp.where(group < shift[3] - 8, part[56:64, :], end)
            for idx, row in enumerate((top, mid, low, end)):
                lined[idx, tile, pl.ds(plane, groups, stride=4), :] = row
        for idx in range(4):
            value = lined[idx, tile][:, 0 : stop - start]
            half_ref[0, idx, :, start:stop] = value
            new_ref[0, idx, :, start:stop] = logits_ref[0, idx, :, start:stop] + rate * value


def shared_parts(part):
    count = lax.axis_size("node") * lax.axis_size("board")
    spread = jnp.broadcast_to(part, (count, LANES))
    return lax.all_to_all(spread, ("node", "board"), 0, 0, tiled=True)


def step_of_class(
    size,
    far,
    logits,
    pot_size,
    node_type,
    parent_slot,
    range_one,
    range_two,
    hand_rank,
    live_mask,
):
    _, levels, slots, hands = logits.shape
    wide = padded(hands)
    tiles = wide // LANES
    groups = slots // 4
    node_count = lax.axis_size("node")
    entry_count = float(logits.size * node_count * lax.axis_size("board"))
    vmem = pl.BlockSpec(memory_space=pltpu.VMEM)
    smem = pl.BlockSpec(memory_space=pltpu.SMEM)
    f32 = jnp.float32

    def limit(mebi):
        return pltpu.CompilerParams(vmem_limit_bytes=mebi * MEBI)

    def stage(planes, rows=32):
        return pltpu.VMEM((tiles, planes, rows, LANES), f32)

    home, *sent = pl.pallas_call(
        functools.partial(pack_kernel, node_count, size, far),
        out_shape=message_shapes(levels, 3, groups, wide, size, far),
        in_specs=[smem] + [vmem] * 3,
        scratch_shapes=[
            pltpu.VMEM((levels, tiles, slots, LANES), f32),
            pltpu.VMEM((LANES, LANES), f32),
            pltpu.VMEM((LANES, LANES), f32),
            stage(3),
        ],
        compiler_params=limit(12),
        name="pack",
    )(parent_slot, logits, pot_size, node_type)
    got = sent_on(sent[0], sent[1], sent[2:], -2)
    blocks = payoff_blocks(hand_rank, live_mask)
    rows = 7 * slots

    def work(count):
        return [
            pltpu.VMEM((8, wide), f32),
            pltpu.VMEM((count, 2 * wide), jnp.bfloat16),
            pltpu.VMEM((count, wide), f32),
        ]

    def cost(count):
        return pl.CostEstimate(
            flops=4 * count * wide * wide, bytes_accessed=6 * wide * wide, transcendentals=0
        )

    square_shape = jax.ShapeDtypeStruct((1, LANES), f32)
    chain, value, part = pl.pallas_call(
        functools.partial(first_kernel, node_count, size, far),
        out_shape=(
            jax.ShapeDtypeStruct((levels, 3, groups, wide), f32),
            jax.ShapeDtypeStruct((levels, 4, groups, wide), f32),
            square_shape,
        ),
        in_specs=[smem] + [vmem] * (4 + len(got)),
        scratch_shapes=[stage(3), stage(3), stage(3, 64)] + work(rows),
        compiler_params=limit(32),
        cost_estimate=cost(rows),
        name="first",
    )(parent_slot, home, *got, range_one, range_two, blocks)
    parts = shared_parts(part)
    own, *sent, part = pl.pallas_call(
        functools.partial(second_kernel, node_count, entry_count, size, far),
        out_shape=message_shapes(levels, 4, groups, wide, size, far) + [square_shape],
        in_specs=[smem] + [vmem] * 6,
        scratch_shapes=[stage(4)] + work(rows - slots),
        compiler_params=limit(32),
        cost_estimate=cost(rows - slots),
        name="second",
    )(parent_slot, chain, value, parts, range_one, range_two, blocks)
    got = sent_on(sent[0], sent[1], sent[2:], 2)
    parts = shared_parts(part)
    out_shape = jax.ShapeDtypeStruct(logits.shape, f32)
    return pl.pallas_call(
        functools.partial(last_kernel, node_count, entry_count, size, far),
        out_shape=(out_shape, out_shape),
        in_specs=[smem] + [vmem] * (3 + len(got)),
        scratch_shapes=[
            stage(4),
            stage(4),
            stage(4, 64),
            pltpu.VMEM((levels, tiles, slots, LANES), f32),
        ],
        compiler_params=limit(24),
        name="last",
    )(parent_slot, own, *got, parts, logits)


def per_device(
    logits, pot_size, node_type, parent_slot, range_one, range_two, hand_rank, live_mask
):
    branches = [
        functools.partial(step_of_class, size, size == CLASSES[-1]) for size in CLASSES
    ]
    return lax.switch(
        size_class(parent_slot, logits.shape[2] // 4),
        branches,
        logits,
        pot_size,
        node_type,
        parent_slot,
        range_one,
        range_two,
        hand_rank,
        live_mask,
    )


def solution(mesh):
    return jax.shard_map(
        per_device,
        mesh=mesh,
        in_specs=(
            P("board", None, "node", None),
            P(None, "node"),
            P(None, "node"),
            P(None, "node"),
            P("board", None),
            P("board", None),
            P("board", None),
            P("board", None),
        ),
        out_specs=(P("board", None, "node", None), P("board", None, "node", None)),
        check_vma=False,
    )
```

```python
import functools

import jax
import jax.numpy as jnp
import numpy as np
from jax import lax
from jax.experimental import pallas as pl
from jax.experimental.pallas import tpu as pltpu
from jax.sharding import PartitionSpec as P

LANES = 128
CARDS = 52
step_scale = 0.5
eps_value = 1e-06
MEBI = 1 << 20
CLASSES = (5, 8, 10, 16)
FAR = 5


def padded(count):
    return -(-count // LANES) * LANES


def card_rows(hand_count, wide):
    pairs = [(low, high) for low in range(CARDS) for high in range(low + 1, CARDS)]
    rows = np.full((2, wide), -1, np.int32)
    rows[:, :hand_count] = np.array(pairs[:hand_count], np.int32).T
    return rows


def payoff_kernel(hands, cards_ref, rank_ref, live_ref, out_ref, flat, left, right):
    wide = out_ref.shape[1]
    flat[...] = jnp.zeros(flat.shape, jnp.float32)
    flat[0:1, 0:hands] = rank_ref[...].astype(jnp.float32)
    flat[1:2, 0:hands] = (live_ref[...] > 0).astype(jnp.float32)
    dead = 1.0 - flat[1:2, :]
    feature = lax.broadcasted_iota(jnp.int32, (LANES, wide), 0)
    hit = (feature == cards_ref[0:1, :]) | (feature == cards_ref[1:2, :])
    base = jnp.where(hit, 1.0, 0.0)
    left[...] = jnp.where(feature == CARDS, dead, jnp.where(feature == CARDS + 1, 1.0, base))
    right[...] = jnp.where(
        feature == CARDS, 1.0, jnp.where(feature == CARDS + 1, dead, base)
    ).astype(jnp.bfloat16)
    rank_row = flat[0:1, :]
    for block in range(wide // LANES):
        part = slice(block * LANES, (block + 1) * LANES)
        left_block = left[:, part].T.astype(jnp.bfloat16)
        rank_col = jnp.broadcast_to(flat[0:1, part], (LANES, LANES)).T[:, 0:1]
        hits = jnp.dot(left_block, right[...], preferred_element_type=jnp.float32)
        compat = jnp.where(hits == 0.0, 1.0, 0.0)
        order = jnp.clip(rank_row - rank_col, -1.0, 1.0)
        out_ref[part, :] = (order * compat).astype(jnp.bfloat16)
        out_ref[wide + block * LANES : wide + (block + 1) * LANES, :] = compat.astype(jnp.bfloat16)


def payoff_blocks(hand_rank, live_mask):
    hands = hand_rank.shape[-1]
    wide = padded(hands)
    return pl.pallas_call(
        functools.partial(payoff_kernel, hands),
        out_shape=jax.ShapeDtypeStruct((2 * wide, wide), jnp.bfloat16),
        scratch_shapes=[
            pltpu.VMEM((8, wide), jnp.float32),
            pltpu.VMEM((LANES, wide), jnp.float32),
            pltpu.VMEM((LANES, wide), jnp.bfloat16),
        ],
        compiler_params=pltpu.CompilerParams(vmem_limit_bytes=20 * MEBI),
        cost_estimate=pl.CostEstimate(
            flops=2 * wide * wide * LANES, bytes_accessed=4 * wide * wide, transcendentals=0
        ),
        name="payoff",
    )(jnp.asarray(card_rows(hands, wide)), hand_rank, live_mask)


def row_count(planes, groups):
    return -(-planes * groups // 8) * 8


def plan_of(parent_ref, node_count, groups):
    total = groups * node_count
    first = lax.axis_index("node") * groups
    off = [lax.rem(first - (parent_ref[idx, 0] >> 2) + total, total) for idx in (1, 2, 3)]
    one = off[0]
    two = one + off[1]
    three = two + off[2]
    low = jnp.maximum(one, three - groups)
    high = jnp.minimum(two, groups)
    middle = jnp.minimum(jnp.maximum((one + two + three + 2) >> 2, low), high)
    return middle, middle - one, two - middle, three - middle


def class_of(shift, groups):
    need = jnp.maximum(shift[0] + shift[1], shift[2] + shift[3])
    found = jnp.int32(0)
    for size in CLASSES[:-1]:
        found = found + (need > size).astype(jnp.int32)
    return jnp.where(shift[3] > groups, len(CLASSES) - 1, found)


def fill_message(stage, message_ref, size, blocks, tail_ref):
    tiles, planes = stage.shape[:2]
    for tile in range(tiles):
        for plane in range(planes):
            for block_ref, level, start in blocks:
                if tail_ref is not None and tile == tiles - 1 and plane == 0:
                    block = tail_ref[level]
                else:
                    block = block_ref[level, tile, plane]
                stage[tile, plane, pl.ds(start, 8), :] = block
            message_ref[tile, plane * size : plane * size + size, :] = stage[
                tile, plane, 8 : 8 + size, :
            ]


def fill_messages(
    node, stage, message_refs, size, block_ref, to_left, to_right, tail_ref=None
):
    even = lax.rem(node, 2) == 0
    for message_ref, on_left in zip(message_refs, (even, jnp.logical_not(even))):
        blocks = [
            (block_ref, jnp.where(on_left, near[0], far[0]), jnp.where(on_left, near[1], far[1]))
            for near, far in zip(to_left, to_right)
        ]
        fill_message(stage, message_ref, size, blocks, tail_ref)


def prepare_kernel(node_count, parent_ref, logits_ref, home_ref, class_ref, raw):
    levels, tiles, planes, groups, _ = home_ref.shape
    slots = 4 * groups
    hands = logits_ref.shape[-1]
    class_ref[0] = class_of(plan_of(parent_ref, node_count, groups), groups)
    for idx in range(levels):
        raw[idx, tiles - 1] = jnp.zeros((slots, LANES), jnp.float32)
        for tile in range(tiles):
            start = tile * LANES
            stop = min(start + LANES, hands)
            raw[idx, tile, :, 0 : stop - start] = logits_ref[0, idx, :, start:stop]
            first = raw[idx, tile, pl.ds(0, groups, stride=4), :]
            for plane in range(planes):
                row = raw[idx, tile, pl.ds(plane + 1, groups, stride=4), :] - first
                home_ref[idx, tile, plane] = row


def prepared(logits, parent_slot):
    _, levels, slots, hands = logits.shape
    groups = slots // 4
    tiles = padded(hands) // LANES
    vmem = pl.BlockSpec(memory_space=pltpu.VMEM)
    smem = pl.BlockSpec(memory_space=pltpu.SMEM)
    return pl.pallas_call(
        functools.partial(prepare_kernel, lax.axis_size("node")),
        out_shape=(
            jax.ShapeDtypeStruct((levels, tiles, 3, groups, LANES), jnp.float32),
            jax.ShapeDtypeStruct((1,), jnp.int32),
        ),
        in_specs=[smem, vmem],
        out_specs=(vmem, smem),
        scratch_shapes=[pltpu.VMEM((levels, tiles, slots, LANES), jnp.float32)],
        compiler_params=pltpu.CompilerParams(vmem_limit_bytes=10 * MEBI),
        name="prepare",
    )(parent_slot, logits)


def pack_kernel(
    node_count,
    size,
    far,
    parent_ref,
    pot_ref,
    kind_ref,
    home_ref,
    odd_ref,
    even_ref,
    *rest,
):
    far_ref = rest[0] if far else None
    tail_ref, stage = rest[-2:]
    levels, tiles, planes, groups, _ = home_ref.shape
    group = lax.broadcasted_iota(jnp.int32, (groups, LANES), 0)
    lane = lax.broadcasted_iota(jnp.int32, (groups, LANES), 1)
    spot = [
        [(group == row) & (lane == LANES - 8 + column) for column in range(8)]
        for row in range(groups)
    ]
    for idx in range(levels):
        sign = -1.0 if idx % 2 == 0 else 1.0
        row = home_ref[idx, tiles - 1, 0]
        for place in range(4 * groups):
            pot = pot_ref[idx, place]
            kind = kind_ref[idx, place]
            show = jnp.where(kind == 2, pot, 0.0)
            fold = jnp.where(kind == 1, pot, 0.0) * sign
            row = jnp.where(spot[place // 4][place % 4], show, row)
            row = jnp.where(spot[place // 4][place % 4 + 4], fold, row)
        tail_ref[idx] = row
    shift = plan_of(parent_ref, node_count, groups)
    fill_messages(
        lax.axis_index("node"),
        stage,
        (odd_ref, even_ref),
        size,
        home_ref,
        [(2, 8), (3, 8 + shift[2])],
        [(1, shift[0] + shift[1]), (0, shift[0])],
        tail_ref,
    )
    if far:
        for tile in range(tiles):
            for plane in range(planes):
                block = home_ref[3, tile, plane]
                if tile == tiles - 1 and plane == 0:
                    block = tail_ref[3]
                far_ref[tile, plane * FAR : plane * FAR + FAR, :] = block[0:FAR, :]


def message_shapes(planes, wide, size, far):
    tiles = wide // LANES
    message = jax.ShapeDtypeStruct((tiles, row_count(planes, size), LANES), jnp.float32)
    shapes = [message] * 2
    if far:
        shapes.append(jax.ShapeDtypeStruct((tiles, row_count(planes, FAR), LANES), jnp.float32))
    return shapes


def sent_on(odd, even, far, far_steps):
    count = lax.axis_size("node")
    edges = [(src, (src + 1) % count) for src in range(count)]
    got = []
    for message, first in ((odd, 1), (even, 0)):
        pairs = [pair for edge in edges[first::2] for pair in (edge, edge[::-1])]
        got.append(lax.ppermute(message, "node", pairs))
    for message in far:
        pairs = [(src, (src + far_steps) % count) for src in range(count)]
        got.append(lax.ppermute(message, "node", pairs))
    return got


def spread_messages(node, from_left, from_right, odd_ref, even_ref, size):
    tiles, planes = from_left.shape[:2]
    even = lax.rem(node, 2) == 0
    for tile in range(tiles):
        for plane in range(planes):
            place = slice(plane * size, plane * size + size)
            odd_part = odd_ref[tile, place, :]
            even_part = even_ref[tile, place, :]
            from_left[tile, plane, 8 : 8 + size, :] = jnp.where(even, odd_part, even_part)
            from_right[tile, plane, 8 : 8 + size, :] = jnp.where(even, even_part, odd_part)


def inner_sum(inner, rows):
    total = jnp.where(inner[0], rows[0], 0.0)
    for idx in range(1, 4):
        total = total + jnp.where(inner[idx], rows[idx], 0.0)
    return total


def softmax_four(rows):
    top = jnp.maximum(jnp.maximum(rows[0], rows[1]), jnp.maximum(rows[2], 0.0))
    lifted = [jnp.exp(-top)] + [jnp.exp(row - top) for row in rows]
    total = (lifted[0] + lifted[1]) + (lifted[2] + lifted[3])
    return [row / total for row in lifted]


def operator_q(point, show, fold, range_one, range_two, block_ref, cols, put, top_ref=None):
    wide = block_ref.shape[1]
    inner = [
        [(show[idx][slot] == 0.0) & (fold[idx][slot] == 0.0) for slot in range(4)]
        for idx in range(4)
    ]
    strategy = [softmax_four(point[idx]) for idx in range(4)]
    top_one = [range_one * row for row in strategy[0]]
    above_one = inner_sum(inner[0], top_one)
    mid_two = [range_two * row for row in strategy[1]]
    above_two = inner_sum(inner[1], mid_two)
    low_one = [above_one * row for row in strategy[2]]
    last_one = inner_sum(inner[2], low_one)
    end_two = [above_two * row for row in strategy[3]]
    wide_two = jnp.broadcast_to(range_two, above_two.shape)
    reach_rows = [
        (0, [wide_two] * 4, 1.0),
        (1, mid_two, 1.0),
        (2, [above_two] * 4, 1.0),
        (3, end_two, 1.0),
        (1, [above_one] * 4, -1.0),
        (2, low_one, -1.0),
        (3, [last_one] * 4, -1.0),
    ]
    if top_ref is not None:
        reach_rows = reach_rows[1:]
    skipped = 7 - len(reach_rows)
    for unit, (idx, rows, fold_sign) in enumerate(reach_rows):
        for half in range(2):
            place = slice(unit * 32 + half * 16, unit * 32 + half * 16 + 16)
            pair = (2 * half, 2 * half + 1)
            cols[place, 0:wide] = jnp.concatenate(
                [rows[slot] * show[idx][slot] for slot in pair], axis=0
            ).astype(jnp.bfloat16)
            cols[place, wide : 2 * wide] = jnp.concatenate(
                [rows[slot] * (fold[idx][slot] * fold_sign) for slot in pair], axis=0
            ).astype(jnp.bfloat16)
    def added(rows):
        return (rows[0] + rows[1]) + (rows[2] + rows[3])

    def landed(rows, kept, term):
        return [rows[slot] + jnp.where(kept[slot], term, 0.0) for slot in range(4)]

    total = None
    for start in range(0, wide, 2 * LANES):
        stop = min(start + 2 * LANES, wide)
        pay = jnp.dot(cols[...], block_ref[:, start:stop], preferred_element_type=jnp.float32)

        def paid(unit):
            first = (unit - skipped) * 32
            return [pay[first + slot * 8 : first + slot * 8 + 8, :] for slot in range(4)]

        def weighed(idx, rows):
            return added([strategy[idx][slot][:, start:stop] * rows[slot] for slot in range(4)])

        value_two_end = paid(6)
        term_two = added(landed(paid(5), inner[2], weighed(3, value_two_end)))
        value_two_mid = landed(paid(4), inner[1], term_two)
        value_one_low = landed(paid(2), inner[2], added(paid(3)))
        term_one = added(landed(paid(1), inner[1], weighed(2, value_one_low)))
        if top_ref is None:
            value_one_top = landed(paid(0), inner[0], term_one)
        else:
            value_one_top = [
                jnp.where(inner[0][slot], term_one, top_ref[0, slot, :, start:stop])
                for slot in range(4)
            ]
        found = [value_one_top, value_two_mid, value_one_low, value_two_end]
        put(start, stop, found)
        part = squares(found)
        total = part if total is None else total + part
    return total


def squares(found):
    total = None
    for rows in found:
        for row in rows:
            total = row * row if total is None else total + row * row
    return jnp.broadcast_to(jnp.sum(total), (1, LANES))


def scale_columns(rows):
    wide = rows[0][0].shape[1]
    show = [
        [level[0][:, wide - 8 + slot : wide - 7 + slot] for slot in range(4)] for level in rows
    ]
    fold = [
        [level[0][:, wide - 4 + slot : wide - 4 + slot + 1] for slot in range(4)] for level in rows
    ]
    return show, fold


def wide_row(store, place, row_ref):
    hands = row_ref.shape[1]
    store[place : place + 1, 0:hands] = row_ref[...]
    return store[place : place + 1, :]


def first_kernel(node_count, size, far, parent_ref, home_ref, tail_ref, odd_ref, even_ref, *rest):
    if far:
        far_ref, rest = rest[0], rest[1:]
    one_ref, two_ref, block_ref, chain_ref, value_ref, square_ref = rest[:6]
    from_left, from_right, window, ranges, cols = rest[6:]
    _, tiles, planes, groups, _ = home_ref.shape
    shift = plan_of(parent_ref, node_count, groups)
    spread_messages(lax.axis_index("node"), from_left, from_right, odd_ref, even_ref, size)
    chain = lax.broadcasted_iota(jnp.int32, (groups, LANES), 0)
    point = [[[] for _ in range(planes)] for _ in range(4)]
    for tile in range(tiles):
        for plane in range(planes):
            part = window.at[tile, plane]
            home = [home_ref[idx, tile, plane] for idx in range(4)]
            if tile == tiles - 1 and plane == 0:
                home = [tail_ref[idx] for idx in range(4)]
            part[8:16, :] = home[0]
            part[24:32, :] = home[1]
            part[32:40, :] = home[3]
            from_right[tile, plane, 0:8, :] = home[2]
            top = jnp.where(
                chain < shift[0],
                from_left[tile, plane, 8:16, :],
                part[pl.ds(8 - shift[0], 8), :],
            )
            mid = jnp.where(
                chain < shift[1],
                from_left[tile, plane, pl.ds(8 + shift[0], 8), :],
                part[pl.ds(24 - shift[1], 8), :],
            )
            low = from_right[tile, plane, pl.ds(shift[2], 8), :]
            end = jnp.where(
                chain + shift[3] < 8,
                part[pl.ds(32 + shift[3], 8), :],
                from_right[tile, plane, pl.ds(shift[2] + shift[3], 8), :],
            )
            if far:
                part[56 : 56 + FAR, :] = far_ref[tile, plane * FAR : plane * FAR + FAR, :]
                end = jnp.where(chain + shift[3] < 16, end, part[pl.ds(40 + shift[3], 8), :])
            for idx, row in enumerate((top, mid, low, end)):
                point[idx][plane].append(row)
    point = [[jnp.concatenate(rows, axis=1) for rows in level] for level in point]
    for idx in range(4):
        for plane in range(planes):
            chain_ref[idx, plane] = point[idx][plane]
    show, fold = scale_columns(point)
    ranges[...] = jnp.zeros(ranges.shape, jnp.float32)
    range_one = wide_row(ranges, 0, one_ref)
    range_two = wide_row(ranges, 1, two_ref)

    def put(start, stop, found):
        for idx in range(4):
            for slot in range(4):
                value_ref[idx, slot, :, start:stop] = found[idx][slot]

    square_ref[...] = operator_q(
        point, show, fold, range_one, range_two, block_ref, cols, put
    )


def rate_of(parts_ref, entry_count):
    square_sum = jnp.sum(parts_ref[...], axis=0, keepdims=True)[:, 0:1]
    return step_scale / jnp.sqrt(square_sum / entry_count + eps_value)


def second_kernel(node_count, entry_count, size, far, parent_ref, chain_ref, value_ref, *rest):
    parts_ref, one_ref, two_ref, block_ref, own_ref, odd_ref, even_ref = rest[:7]
    rest = rest[7:]
    if far:
        far_ref, rest = rest[0], rest[1:]
    square_ref, stage, ranges, cols = rest
    _, tiles, planes, groups, _ = own_ref.shape
    rate = rate_of(parts_ref, entry_count)
    raw = [[chain_ref[idx, plane] for plane in range(3)] for idx in range(4)]
    show, fold = scale_columns(raw)
    point = [
        [
            raw[idx][plane] + rate * (value_ref[idx, plane + 1] - value_ref[idx, 0])
            for plane in range(3)
        ]
        for idx in range(4)
    ]
    ranges[...] = jnp.zeros(ranges.shape, jnp.float32)
    range_one = wide_row(ranges, 0, one_ref)
    range_two = wide_row(ranges, 1, two_ref)

    def put(start, stop, found):
        for idx in range(4):
            for slot in range(4):
                for lane in range(start, stop, LANES):
                    row = found[idx][slot][:, lane - start : lane - start + LANES]
                    own_ref[idx, lane // LANES, slot] = row

    square_ref[...] = operator_q(
        point, show, fold, range_one, range_two, block_ref, cols, put, value_ref
    )
    shift = plan_of(parent_ref, node_count, groups)
    fill_messages(
        lax.axis_index("node"),
        stage,
        (odd_ref, even_ref),
        size,
        own_ref,
        [(0, 8), (1, 8 + shift[0])],
        [(3, shift[2] + shift[3]), (2, shift[2])],
    )
    if far:
        for tile in range(tiles):
            for plane in range(planes):
                stage[tile, plane, pl.ds(jnp.maximum(shift[3] - 8, 0), 8), :] = own_ref[
                    3, tile, plane
                ]
                far_ref[tile, plane * FAR : plane * FAR + FAR, :] = stage[tile, plane, 8 : 8 + FAR, :]


def last_kernel(node_count, entry_count, size, far, parent_ref, own_ref, odd_ref, even_ref, *rest):
    far_ref, rest = (rest[0], rest[1:]) if far else (None, rest)
    parts_ref, logits_ref, new_ref, half_ref, from_left, from_right, window, lined = rest
    _, tiles, planes, groups, _ = own_ref.shape
    hands = logits_ref.shape[-1]
    shift = plan_of(parent_ref, node_count, groups)
    rate = rate_of(parts_ref, entry_count)
    level = pl.program_id(0)
    group = lax.broadcasted_iota(jnp.int32, (groups, LANES), 0)

    @pl.when(level == 0)
    def _():
        spread_messages(lax.axis_index("node"), from_left, from_right, odd_ref, even_ref, size)

    def place_level(idx, found):
        for tile in range(tiles):
            start = tile * LANES
            stop = min(start + LANES, hands)
            for plane in range(planes):
                row = found(window.at[tile, plane], tile, plane, own_ref[idx, tile, plane])
                lined[tile, pl.ds(plane, groups, stride=4), :] = row
            value = lined[tile][:, 0 : stop - start]
            half_ref[0, 0, :, start:stop] = value
            new_ref[0, 0, :, start:stop] = logits_ref[0, 0, :, start:stop] + rate * value

    def top(part, tile, plane, own):
        from_right[tile, plane, 0:8, :] = own
        return from_right[tile, plane, pl.ds(shift[0], 8), :]

    def mid(part, tile, plane, own):
        part[0:8, :] = own
        return jnp.where(
            group + shift[1] < 8,
            part[pl.ds(shift[1], 8), :],
            from_right[tile, plane, pl.ds(shift[0] + shift[1], 8), :],
        )

    def low(part, tile, plane, own):
        part[8:16, :] = own
        return jnp.where(
            group < shift[2], from_left[tile, plane, 8:16, :], part[pl.ds(8 - shift[2], 8), :]
        )

    def end(part, tile, plane, own):
        part[8:16, :] = own
        row = jnp.where(
            group < shift[3],
            from_left[tile, plane, pl.ds(8 + shift[2], 8), :],
            part[pl.ds(8 - jnp.minimum(shift[3], 8), 8), :],
        )
        if far:
            part[24 : 24 + FAR, :] = far_ref[tile, plane * FAR : plane * FAR + FAR, :]
            row = jnp.where(group < shift[3] - 8, part[24:32, :], row)
        return row

    for idx, found in enumerate((top, mid, low, end)):
        pl.when(level == idx)(functools.partial(place_level, idx, found))


def shared_parts(part):
    count = lax.axis_size("node") * lax.axis_size("board")
    spread = jnp.broadcast_to(part, (count, LANES))
    return lax.all_to_all(spread, ("node", "board"), 0, 0, tiled=True)


def step_of_class(
    size,
    far,
    home,
    logits,
    pot_size,
    node_type,
    parent_slot,
    range_one,
    range_two,
    hand_rank,
    live_mask,
):
    _, levels, slots, hands = logits.shape
    wide = padded(hands)
    tiles = wide // LANES
    groups = slots // 4
    node_count = lax.axis_size("node")
    entry_count = float(logits.size * node_count * lax.axis_size("board"))
    vmem = pl.BlockSpec(memory_space=pltpu.VMEM)
    smem = pl.BlockSpec(memory_space=pltpu.SMEM)
    f32 = jnp.float32

    def limit(mebi):
        return pltpu.CompilerParams(vmem_limit_bytes=mebi * MEBI)

    def stage(planes, rows=32):
        return pltpu.VMEM((tiles, planes, rows, LANES), f32)

    *sent, tail = pl.pallas_call(
        functools.partial(pack_kernel, node_count, size, far),
        out_shape=message_shapes(3, wide, size, far)
        + [jax.ShapeDtypeStruct((levels, groups, LANES), f32)],
        in_specs=[smem, smem, smem, vmem],
        scratch_shapes=[stage(3)],
        compiler_params=limit(8),
        name="pack",
    )(parent_slot, pot_size, node_type, home)
    got = sent_on(sent[0], sent[1], sent[2:], -2)
    blocks = payoff_blocks(hand_rank, live_mask)
    rows = 7 * slots

    def work(count):
        return [
            pltpu.VMEM((8, wide), f32),
            pltpu.VMEM((count, 2 * wide), jnp.bfloat16),
        ]

    def cost(count):
        return pl.CostEstimate(
            flops=4 * count * wide * wide, bytes_accessed=6 * wide * wide, transcendentals=0
        )

    square_shape = jax.ShapeDtypeStruct((1, LANES), f32)
    chain, value, part = pl.pallas_call(
        functools.partial(first_kernel, node_count, size, far),
        out_shape=(
            jax.ShapeDtypeStruct((levels, 3, groups, wide), f32),
            jax.ShapeDtypeStruct((levels, 4, groups, wide), f32),
            square_shape,
        ),
        in_specs=[smem] + [vmem] * (5 + len(got)),
        scratch_shapes=[stage(3), stage(3), stage(3, 64)] + work(rows),
        compiler_params=limit(32),
        cost_estimate=cost(rows),
        name="first",
    )(parent_slot, home, tail, *got, range_one, range_two, blocks)
    parts = shared_parts(part)
    own, *sent, part = pl.pallas_call(
        functools.partial(second_kernel, node_count, entry_count, size, far),
        out_shape=[jax.ShapeDtypeStruct((levels, tiles, 4, groups, LANES), f32)]
        + message_shapes(4, wide, size, far)
        + [square_shape],
        in_specs=[smem] + [vmem] * 6,
        scratch_shapes=[stage(4)] + work(rows - slots),
        compiler_params=limit(32),
        cost_estimate=cost(rows - slots),
        name="second",
    )(parent_slot, chain, value, parts, range_one, range_two, blocks)
    got = sent_on(sent[0], sent[1], sent[2:], 2)
    parts = shared_parts(part)
    out_shape = jax.ShapeDtypeStruct(logits.shape, f32)
    by_level = pl.BlockSpec((1, 1, slots, hands), lambda level: (0, level, 0, 0))
    return pl.pallas_call(
        functools.partial(last_kernel, node_count, entry_count, size, far),
        out_shape=(out_shape, out_shape),
        grid=(levels,),
        in_specs=[smem] + [vmem] * (2 + len(got)) + [by_level],
        out_specs=(by_level, by_level),
        scratch_shapes=[stage(4), stage(4), stage(4), pltpu.VMEM((tiles, slots, LANES), f32)],
        compiler_params=limit(24),
        name="last",
    )(parent_slot, own, *got, parts, logits)


def per_device(
    logits, pot_size, node_type, parent_slot, range_one, range_two, hand_rank, live_mask
):
    branches = [
        functools.partial(step_of_class, size, size == CLASSES[-1]) for size in CLASSES
    ]
    home, found = prepared(logits, parent_slot)
    return lax.switch(
        found[0],
        branches,
        home,
        logits,
        pot_size,
        node_type,
        parent_slot,
        range_one,
        range_two,
        hand_rank,
        live_mask,
    )


def solution(mesh):
    return jax.shard_map(
        per_device,
        mesh=mesh,
        in_specs=(
            P("board", None, "node", None),
            P(None, "node"),
            P(None, "node"),
            P(None, "node"),
            P("board", None),
            P("board", None),
            P("board", None),
            P("board", None),
        ),
        out_specs=(P("board", None, "node", None), P("board", None, "node", None)),
        check_vma=False,
    )
```

```python
import functools

import jax
import jax.numpy as jnp
import numpy as np
from jax import lax
from jax.experimental import pallas as pl
from jax.experimental.pallas import tpu as pltpu
from jax.sharding import PartitionSpec as P

LANES = 128
CARDS = 52
step_scale = 0.5
eps_value = 1e-06
MEBI = 1 << 20
CLASSES = (5, 8, 10, 16)
FAR = 5


def padded(count):
    return -(-count // LANES) * LANES


def card_rows(hand_count, wide):
    pairs = [(low, high) for low in range(CARDS) for high in range(low + 1, CARDS)]
    rows = np.full((2, wide), -1, np.int32)
    rows[:, :hand_count] = np.array(pairs[:hand_count], np.int32).T
    return rows


def payoff_kernel(hands, cards_ref, rank_ref, live_ref, out_ref, flat, left, right):
    wide = out_ref.shape[1]
    flat[...] = jnp.zeros(flat.shape, jnp.float32)
    flat[0:1, 0:hands] = rank_ref[...].astype(jnp.float32)
    flat[1:2, 0:hands] = (live_ref[...] > 0).astype(jnp.float32)
    dead = 1.0 - flat[1:2, :]
    feature = lax.broadcasted_iota(jnp.int32, (LANES, wide), 0)
    hit = (feature == cards_ref[0:1, :]) | (feature == cards_ref[1:2, :])
    base = jnp.where(hit, 1.0, 0.0)
    left[...] = jnp.where(feature == CARDS, dead, jnp.where(feature == CARDS + 1, 1.0, base))
    right[...] = jnp.where(
        feature == CARDS, 1.0, jnp.where(feature == CARDS + 1, dead, base)
    ).astype(jnp.bfloat16)
    rank_row = flat[0:1, :]
    for block in range(wide // LANES):
        part = slice(block * LANES, (block + 1) * LANES)
        left_block = left[:, part].T.astype(jnp.bfloat16)
        rank_col = jnp.broadcast_to(flat[0:1, part], (LANES, LANES)).T[:, 0:1]
        hits = jnp.dot(left_block, right[...], preferred_element_type=jnp.float32)
        compat = jnp.where(hits == 0.0, 1.0, 0.0)
        order = jnp.clip(rank_row - rank_col, -1.0, 1.0)
        out_ref[part, :] = (order * compat).astype(jnp.bfloat16)
        out_ref[wide + block * LANES : wide + (block + 1) * LANES, :] = compat.astype(jnp.bfloat16)


def payoff_blocks(hand_rank, live_mask):
    hands = hand_rank.shape[-1]
    wide = padded(hands)
    return pl.pallas_call(
        functools.partial(payoff_kernel, hands),
        out_shape=jax.ShapeDtypeStruct((2 * wide, wide), jnp.bfloat16),
        scratch_shapes=[
            pltpu.VMEM((8, wide), jnp.float32),
            pltpu.VMEM((LANES, wide), jnp.float32),
            pltpu.VMEM((LANES, wide), jnp.bfloat16),
        ],
        compiler_params=pltpu.CompilerParams(vmem_limit_bytes=20 * MEBI),
        cost_estimate=pl.CostEstimate(
            flops=2 * wide * wide * LANES, bytes_accessed=4 * wide * wide, transcendentals=0
        ),
        name="payoff",
    )(jnp.asarray(card_rows(hands, wide)), hand_rank, live_mask)


def row_count(planes, groups):
    return -(-planes * groups // 8) * 8


def plan_of(parent_ref, node_count, groups):
    total = groups * node_count
    first = lax.axis_index("node") * groups
    off = [lax.rem(first - (parent_ref[idx, 0] >> 2) + total, total) for idx in (1, 2, 3)]
    one = off[0]
    two = one + off[1]
    three = two + off[2]
    low = jnp.maximum(one, three - groups)
    high = jnp.minimum(two, groups)
    middle = jnp.minimum(jnp.maximum((one + two + three + 2) >> 2, low), high)
    return middle, middle - one, two - middle, three - middle


def class_of(shift, groups):
    need = jnp.maximum(shift[0] + shift[1], shift[2] + shift[3])
    found = jnp.int32(0)
    for size in CLASSES[:-1]:
        found = found + (need > size).astype(jnp.int32)
    return jnp.where(shift[3] > groups, len(CLASSES) - 1, found)


def fill_message(stage, message_ref, size, blocks):
    tiles, planes = stage.shape[:2]
    for tile in range(tiles):
        for plane in range(planes):
            for block_ref, level, start in blocks:
                stage[tile, plane, pl.ds(start, 8), :] = block_ref[level, tile, plane]
            message_ref[tile, plane * size : plane * size + size, :] = stage[
                tile, plane, 8 : 8 + size, :
            ]


def fill_messages(node, stage, message_refs, size, block_ref, to_left, to_right):
    even = lax.rem(node, 2) == 0
    for message_ref, on_left in zip(message_refs, (even, jnp.logical_not(even))):
        blocks = [
            (block_ref, jnp.where(on_left, near[0], far[0]), jnp.where(on_left, near[1], far[1]))
            for near, far in zip(to_left, to_right)
        ]
        fill_message(stage, message_ref, size, blocks)


def prepare_kernel(
    node_count,
    parent_ref,
    logits_ref,
    pot_ref,
    kind_ref,
    home_ref,
    shift_ref,
    class_ref,
    raw,
    flat,
    turned,
):
    levels, tiles, planes, groups, _ = home_ref.shape
    slots = 4 * groups
    hands = logits_ref.shape[-1]
    shift = plan_of(parent_ref, node_count, groups)
    class_ref[0] = class_of(shift, groups)
    row_id = lax.broadcasted_iota(jnp.int32, shift_ref.shape, 0)
    spread = jnp.zeros(shift_ref.shape, jnp.int32)
    for idx in range(4):
        spread = jnp.where(row_id == idx, shift[idx], spread)
    shift_ref[...] = spread
    pot = pot_ref[...]
    kind = kind_ref[...]
    level = lax.broadcasted_iota(jnp.int32, pot.shape, 0)
    sign = jnp.where(level % 2 == 0, -1.0, 1.0)
    flat[...] = jnp.zeros(flat.shape, jnp.float32)
    flat[0:levels, 0:slots] = jnp.where(kind == 2, pot, 0.0)
    flat[levels : 2 * levels, 0:slots] = jnp.where(kind == 1, pot, 0.0) * sign
    turned[...] = flat[...].T
    lane = lax.broadcasted_iota(jnp.int32, (groups, LANES), 1)
    for idx in range(levels):
        raw[idx, tiles - 1] = jnp.zeros((slots, LANES), jnp.float32)
        for tile in range(tiles):
            start = tile * LANES
            stop = min(start + LANES, hands)
            raw[idx, tile, :, 0 : stop - start] = logits_ref[0, idx, :, start:stop]
            first = raw[idx, tile, pl.ds(0, groups, stride=4), :]
            for plane in range(planes):
                row = raw[idx, tile, pl.ds(plane + 1, groups, stride=4), :] - first
                if tile == tiles - 1 and plane == 0:
                    for slot in range(4):
                        scale = turned[pl.ds(slot, groups, stride=4), :]
                        row = jnp.where(lane == LANES - 8 + slot, scale[:, idx : idx + 1], row)
                        fold = scale[:, levels + idx : levels + idx + 1]
                        row = jnp.where(lane == LANES - 4 + slot, fold, row)
                home_ref[idx, tile, plane] = row


def prepared(logits, pot_size, node_type, parent_slot):
    _, levels, slots, hands = logits.shape
    groups = slots // 4
    tiles = padded(hands) // LANES
    vmem = pl.BlockSpec(memory_space=pltpu.VMEM)
    smem = pl.BlockSpec(memory_space=pltpu.SMEM)
    return pl.pallas_call(
        functools.partial(prepare_kernel, lax.axis_size("node")),
        out_shape=(
            jax.ShapeDtypeStruct((levels, tiles, 3, groups, LANES), jnp.float32),
            jax.ShapeDtypeStruct((8, LANES), jnp.int32),
            jax.ShapeDtypeStruct((1,), jnp.int32),
        ),
        in_specs=[smem] + [vmem] * 3,
        out_specs=(vmem, vmem, smem),
        scratch_shapes=[
            pltpu.VMEM((levels, tiles, slots, LANES), jnp.float32),
            pltpu.VMEM((LANES, LANES), jnp.float32),
            pltpu.VMEM((LANES, LANES), jnp.float32),
        ],
        compiler_params=pltpu.CompilerParams(vmem_limit_bytes=10 * MEBI),
        name="prepare",
    )(parent_slot, logits, pot_size, node_type)


def shifts_in(shift_ref):
    return [jnp.max(shift_ref[idx : idx + 1, :]) for idx in range(4)]


def pack_kernel(size, far, shift_ref, home_ref, _pot, _kind, _parent, odd_ref, even_ref, *rest):
    far_ref = rest[0] if far else None
    stage = rest[-1]
    _, tiles, planes, groups, _ = home_ref.shape
    shift = shifts_in(shift_ref)
    fill_messages(
        lax.axis_index("node"),
        stage,
        (odd_ref, even_ref),
        size,
        home_ref,
        [(2, 8), (3, 8 + shift[2])],
        [(1, shift[0] + shift[1]), (0, shift[0])],
    )
    if far:
        for tile in range(tiles):
            for plane in range(planes):
                far_ref[tile, plane * FAR : plane * FAR + FAR, :] = home_ref[3, tile, plane, 0:FAR, :]


def message_shapes(planes, wide, size, far):
    tiles = wide // LANES
    message = jax.ShapeDtypeStruct((tiles, row_count(planes, size), LANES), jnp.float32)
    shapes = [message] * 2
    if far:
        shapes.append(jax.ShapeDtypeStruct((tiles, row_count(planes, FAR), LANES), jnp.float32))
    return shapes


def sent_on(odd, even, far, far_steps):
    count = lax.axis_size("node")
    edges = [(src, (src + 1) % count) for src in range(count)]
    got = []
    for message, first in ((odd, 1), (even, 0)):
        pairs = [pair for edge in edges[first::2] for pair in (edge, edge[::-1])]
        got.append(lax.ppermute(message, "node", pairs))
    for message in far:
        pairs = [(src, (src + far_steps) % count) for src in range(count)]
        got.append(lax.ppermute(message, "node", pairs))
    return got


def spread_messages(node, from_left, from_right, odd_ref, even_ref, size):
    tiles, planes = from_left.shape[:2]
    even = lax.rem(node, 2) == 0
    for tile in range(tiles):
        for plane in range(planes):
            place = slice(plane * size, plane * size + size)
            odd_part = odd_ref[tile, place, :]
            even_part = even_ref[tile, place, :]
            from_left[tile, plane, 8 : 8 + size, :] = jnp.where(even, odd_part, even_part)
            from_right[tile, plane, 8 : 8 + size, :] = jnp.where(even, even_part, odd_part)


def inner_sum(inner, rows):
    total = jnp.where(inner[0], rows[0], 0.0)
    for idx in range(1, 4):
        total = total + jnp.where(inner[idx], rows[idx], 0.0)
    return total


def softmax_four(rows):
    top = jnp.maximum(jnp.maximum(rows[0], rows[1]), jnp.maximum(rows[2], 0.0))
    lifted = [jnp.exp(-top)] + [jnp.exp(row - top) for row in rows]
    total = (lifted[0] + lifted[1]) + (lifted[2] + lifted[3])
    return [row / total for row in lifted]


def operator_q(point, show, fold, range_one, range_two, block_ref, cols, put, top_ref=None):
    wide = block_ref.shape[1]
    inner = [
        [(show[idx][slot] == 0.0) & (fold[idx][slot] == 0.0) for slot in range(4)]
        for idx in range(4)
    ]
    strategy = [softmax_four(point[idx]) for idx in range(4)]
    top_one = [range_one * row for row in strategy[0]]
    above_one = inner_sum(inner[0], top_one)
    mid_two = [range_two * row for row in strategy[1]]
    above_two = inner_sum(inner[1], mid_two)
    low_one = [above_one * row for row in strategy[2]]
    last_one = inner_sum(inner[2], low_one)
    end_two = [above_two * row for row in strategy[3]]
    wide_two = jnp.broadcast_to(range_two, above_two.shape)
    reach_rows = [
        (0, [wide_two] * 4, 1.0),
        (1, mid_two, 1.0),
        (2, [above_two] * 4, 1.0),
        (3, end_two, 1.0),
        (1, [above_one] * 4, -1.0),
        (2, low_one, -1.0),
        (3, [last_one] * 4, -1.0),
    ]
    if top_ref is not None:
        reach_rows = reach_rows[1:]
    skipped = 7 - len(reach_rows)
    for unit, (idx, rows, fold_sign) in enumerate(reach_rows):
        for half in range(2):
            place = slice(unit * 32 + half * 16, unit * 32 + half * 16 + 16)
            pair = (2 * half, 2 * half + 1)
            cols[place, 0:wide] = jnp.concatenate(
                [rows[slot] * show[idx][slot] for slot in pair], axis=0
            ).astype(jnp.bfloat16)
            cols[place, wide : 2 * wide] = jnp.concatenate(
                [rows[slot] * (fold[idx][slot] * fold_sign) for slot in pair], axis=0
            ).astype(jnp.bfloat16)
    def added(rows):
        return (rows[0] + rows[1]) + (rows[2] + rows[3])

    def landed(rows, kept, term):
        return [rows[slot] + jnp.where(kept[slot], term, 0.0) for slot in range(4)]

    total = None
    for start in range(0, wide, 2 * LANES):
        stop = min(start + 2 * LANES, wide)
        pay = jnp.dot(cols[...], block_ref[:, start:stop], preferred_element_type=jnp.float32)

        def paid(unit):
            first = (unit - skipped) * 32
            return [pay[first + slot * 8 : first + slot * 8 + 8, :] for slot in range(4)]

        def weighed(idx, rows):
            return added([strategy[idx][slot][:, start:stop] * rows[slot] for slot in range(4)])

        value_two_end = paid(6)
        term_two = added(landed(paid(5), inner[2], weighed(3, value_two_end)))
        value_two_mid = landed(paid(4), inner[1], term_two)
        value_one_low = landed(paid(2), inner[2], added(paid(3)))
        term_one = added(landed(paid(1), inner[1], weighed(2, value_one_low)))
        if top_ref is None:
            value_one_top = landed(paid(0), inner[0], term_one)
        else:
            value_one_top = [
                jnp.where(inner[0][slot], term_one, top_ref[0, slot, :, start:stop])
                for slot in range(4)
            ]
        found = [value_one_top, value_two_mid, value_one_low, value_two_end]
        put(start, stop, found)
        part = squares(found)
        total = part if total is None else total + part
    return total


def squares(found):
    total = None
    for rows in found:
        for row in rows:
            total = row * row if total is None else total + row * row
    return jnp.broadcast_to(jnp.sum(total), (1, LANES))


def scale_columns(rows):
    wide = rows[0][0].shape[1]
    show = [
        [level[0][:, wide - 8 + slot : wide - 7 + slot] for slot in range(4)] for level in rows
    ]
    fold = [
        [level[0][:, wide - 4 + slot : wide - 4 + slot + 1] for slot in range(4)] for level in rows
    ]
    return show, fold


def wide_row(store, place, row_ref):
    hands = row_ref.shape[1]
    store[place : place + 1, 0:hands] = row_ref[...]
    return store[place : place + 1, :]


def first_kernel(size, far, shift_ref, home_ref, odd_ref, even_ref, *rest):
    if far:
        far_ref, rest = rest[0], rest[1:]
    one_ref, two_ref, block_ref, chain_ref, value_ref, square_ref = rest[:6]
    from_left, from_right, window, ranges, cols = rest[6:]
    _, tiles, planes, groups, _ = home_ref.shape
    shift = shifts_in(shift_ref)
    spread_messages(lax.axis_index("node"), from_left, from_right, odd_ref, even_ref, size)
    chain = lax.broadcasted_iota(jnp.int32, (groups, LANES), 0)
    point = [[[] for _ in range(planes)] for _ in range(4)]
    for tile in range(tiles):
        for plane in range(planes):
            part = window.at[tile, plane]
            home = [home_ref[idx, tile, plane] for idx in range(4)]
            part[8:16, :] = home[0]
            part[24:32, :] = home[1]
            part[32:40, :] = home[3]
            from_right[tile, plane, 0:8, :] = home[2]
            top = jnp.where(
                chain < shift[0],
                from_left[tile, plane, 8:16, :],
                part[pl.ds(8 - shift[0], 8), :],
            )
            mid = jnp.where(
                chain < shift[1],
                from_left[tile, plane, pl.ds(8 + shift[0], 8), :],
                part[pl.ds(24 - shift[1], 8), :],
            )
            low = from_right[tile, plane, pl.ds(shift[2], 8), :]
            end = jnp.where(
                chain + shift[3] < 8,
                part[pl.ds(32 + shift[3], 8), :],
                from_right[tile, plane, pl.ds(shift[2] + shift[3], 8), :],
            )
            if far:
                part[56 : 56 + FAR, :] = far_ref[tile, plane * FAR : plane * FAR + FAR, :]
                end = jnp.where(chain + shift[3] < 16, end, part[pl.ds(40 + shift[3], 8), :])
            for idx, row in enumerate((top, mid, low, end)):
                point[idx][plane].append(row)
    point = [[jnp.concatenate(rows, axis=1) for rows in level] for level in point]
    for idx in range(4):
        for plane in range(planes):
            chain_ref[idx, plane] = point[idx][plane]
    show, fold = scale_columns(point)
    ranges[...] = jnp.zeros(ranges.shape, jnp.float32)
    range_one = wide_row(ranges, 0, one_ref)
    range_two = wide_row(ranges, 1, two_ref)

    def put(start, stop, found):
        for idx in range(4):
            for slot in range(4):
                value_ref[idx, slot, :, start:stop] = found[idx][slot]

    square_ref[...] = operator_q(
        point, show, fold, range_one, range_two, block_ref, cols, put
    )


def rate_of(parts_ref, entry_count):
    square_sum = jnp.sum(parts_ref[...], axis=0, keepdims=True)[:, 0:1]
    return step_scale / jnp.sqrt(square_sum / entry_count + eps_value)


def second_kernel(entry_count, size, far, shift_ref, chain_ref, value_ref, *rest):
    parts_ref, one_ref, two_ref, block_ref, own_ref, odd_ref, even_ref = rest[:7]
    rest = rest[7:]
    if far:
        far_ref, rest = rest[0], rest[1:]
    square_ref, stage, ranges, cols = rest
    _, tiles, planes, groups, _ = own_ref.shape
    rate = rate_of(parts_ref, entry_count)
    raw = [[chain_ref[idx, plane] for plane in range(3)] for idx in range(4)]
    show, fold = scale_columns(raw)
    point = [
        [
            raw[idx][plane] + rate * (value_ref[idx, plane + 1] - value_ref[idx, 0])
            for plane in range(3)
        ]
        for idx in range(4)
    ]
    ranges[...] = jnp.zeros(ranges.shape, jnp.float32)
    range_one = wide_row(ranges, 0, one_ref)
    range_two = wide_row(ranges, 1, two_ref)

    def put(start, stop, found):
        for idx in range(4):
            for slot in range(4):
                for lane in range(start, stop, LANES):
                    row = found[idx][slot][:, lane - start : lane - start + LANES]
                    own_ref[idx, lane // LANES, slot] = row

    square_ref[...] = operator_q(
        point, show, fold, range_one, range_two, block_ref, cols, put, value_ref
    )
    shift = shifts_in(shift_ref)
    fill_messages(
        lax.axis_index("node"),
        stage,
        (odd_ref, even_ref),
        size,
        own_ref,
        [(0, 8), (1, 8 + shift[0])],
        [(3, shift[2] + shift[3]), (2, shift[2])],
    )
    if far:
        for tile in range(tiles):
            for plane in range(planes):
                stage[tile, plane, pl.ds(jnp.maximum(shift[3] - 8, 0), 8), :] = own_ref[
                    3, tile, plane
                ]
                far_ref[tile, plane * FAR : plane * FAR + FAR, :] = stage[tile, plane, 8 : 8 + FAR, :]


def last_kernel(entry_count, size, far, shift_ref, own_ref, odd_ref, even_ref, *rest):
    far_ref, rest = (rest[0], rest[1:]) if far else (None, rest)
    parts_ref, logits_hbm, new_hbm, half_hbm, from_left, from_right, window, lined = rest[:8]
    logits_ref, new_ref, half_ref, sems = rest[8:]
    levels, tiles, planes, groups, _ = own_ref.shape
    hands = logits_ref.shape[-1]
    fetches = [
        pltpu.make_async_copy(logits_hbm.at[0, idx], logits_ref.at[idx], sems.at[0, idx])
        for idx in range(levels)
    ]
    for fetch in fetches:
        fetch.start()
    shift = shifts_in(shift_ref)
    rate = rate_of(parts_ref, entry_count)
    group = lax.broadcasted_iota(jnp.int32, (groups, LANES), 0)
    spread_messages(lax.axis_index("node"), from_left, from_right, odd_ref, even_ref, size)
    leaving = []

    def place_level(idx, found):
        for tile in range(tiles):
            for plane in range(planes):
                row = found(window.at[tile, plane], tile, plane, own_ref[idx, tile, plane])
                lined[idx, tile, pl.ds(plane, groups, stride=4), :] = row
            start = tile * LANES
            stop = min(start + LANES, hands)
            half_ref[idx, :, start:stop] = lined[idx, tile][:, 0 : stop - start]
        leaving.append(
            pltpu.make_async_copy(half_ref.at[idx], half_hbm.at[0, idx], sems.at[1, idx])
        )
        leaving[-1].start()
        fetches[idx].wait()
        new_ref[idx] = logits_ref[idx] + rate * half_ref[idx]
        leaving.append(
            pltpu.make_async_copy(new_ref.at[idx], new_hbm.at[0, idx], sems.at[2, idx])
        )
        leaving[-1].start()

    def top(part, tile, plane, own):
        from_right[tile, plane, 0:8, :] = own
        return from_right[tile, plane, pl.ds(shift[0], 8), :]

    def mid(part, tile, plane, own):
        part[0:8, :] = own
        return jnp.where(
            group + shift[1] < 8,
            part[pl.ds(shift[1], 8), :],
            from_right[tile, plane, pl.ds(shift[0] + shift[1], 8), :],
        )

    def low(part, tile, plane, own):
        part[8:16, :] = own
        return jnp.where(
            group < shift[2], from_left[tile, plane, 8:16, :], part[pl.ds(8 - shift[2], 8), :]
        )

    def end(part, tile, plane, own):
        part[8:16, :] = own
        row = jnp.where(
            group < shift[3],
            from_left[tile, plane, pl.ds(8 + shift[2], 8), :],
            part[pl.ds(8 - jnp.minimum(shift[3], 8), 8), :],
        )
        if far:
            part[24 : 24 + FAR, :] = far_ref[tile, plane * FAR : plane * FAR + FAR, :]
            row = jnp.where(group < shift[3] - 8, part[24:32, :], row)
        return row

    for idx, found in enumerate((top, mid, low, end)):
        place_level(idx, found)
    for copy in leaving:
        copy.wait()


def shared_parts(part):
    count = lax.axis_size("node") * lax.axis_size("board")
    spread = jnp.broadcast_to(part, (count, LANES))
    return lax.all_to_all(spread, ("node", "board"), 0, 0, tiled=True)


def step_of_class(
    size,
    far,
    home,
    shift,
    logits,
    pot_size,
    node_type,
    parent_slot,
    range_one,
    range_two,
    hand_rank,
    live_mask,
):
    _, levels, slots, hands = logits.shape
    wide = padded(hands)
    tiles = wide // LANES
    groups = slots // 4
    entry_count = float(logits.size * lax.axis_size("node") * lax.axis_size("board"))
    vmem = pl.BlockSpec(memory_space=pltpu.VMEM)
    f32 = jnp.float32

    def limit(mebi):
        return pltpu.CompilerParams(vmem_limit_bytes=mebi * MEBI)

    def stage(planes, rows=32):
        return pltpu.VMEM((tiles, planes, rows, LANES), f32)

    anywhere = pl.BlockSpec(memory_space=pl.ANY)
    sent = pl.pallas_call(
        functools.partial(pack_kernel, size, far),
        out_shape=message_shapes(3, wide, size, far),
        in_specs=[vmem, vmem] + [anywhere] * 3,
        scratch_shapes=[stage(3)],
        compiler_params=limit(8),
        name="pack",
    )(shift, home, pot_size, node_type, parent_slot)
    got = sent_on(sent[0], sent[1], sent[2:], -2)
    blocks = payoff_blocks(hand_rank, live_mask)
    rows = 7 * slots

    def work(count):
        return [
            pltpu.VMEM((8, wide), f32),
            pltpu.VMEM((count, 2 * wide), jnp.bfloat16),
        ]

    def cost(count):
        return pl.CostEstimate(
            flops=4 * count * wide * wide, bytes_accessed=6 * wide * wide, transcendentals=0
        )

    square_shape = jax.ShapeDtypeStruct((1, LANES), f32)
    chain, value, part = pl.pallas_call(
        functools.partial(first_kernel, size, far),
        out_shape=(
            jax.ShapeDtypeStruct((levels, 3, groups, wide), f32),
            jax.ShapeDtypeStruct((levels, 4, groups, wide), f32),
            square_shape,
        ),
        in_specs=[vmem] * (5 + len(got)),
        scratch_shapes=[stage(3), stage(3), stage(3, 64)] + work(rows),
        compiler_params=limit(32),
        cost_estimate=cost(rows),
        name="first",
    )(shift, home, *got, range_one, range_two, blocks)
    parts = shared_parts(part)
    own, *sent, part = pl.pallas_call(
        functools.partial(second_kernel, entry_count, size, far),
        out_shape=[jax.ShapeDtypeStruct((levels, tiles, 4, groups, LANES), f32)]
        + message_shapes(4, wide, size, far)
        + [square_shape],
        in_specs=[vmem] * 7,
        scratch_shapes=[stage(4)] + work(rows - slots),
        compiler_params=limit(32),
        cost_estimate=cost(rows - slots),
        name="second",
    )(shift, chain, value, parts, range_one, range_two, blocks)
    got = sent_on(sent[0], sent[1], sent[2:], 2)
    parts = shared_parts(part)
    out_shape = jax.ShapeDtypeStruct(logits.shape, f32)
    level_shape = (levels, slots, hands)
    return pl.pallas_call(
        functools.partial(last_kernel, entry_count, size, far),
        out_shape=(out_shape, out_shape),
        in_specs=[vmem] * (3 + len(got)) + [anywhere],
        out_specs=(anywhere, anywhere),
        scratch_shapes=[
            stage(4),
            stage(4),
            stage(4),
            pltpu.VMEM((levels, tiles, slots, LANES), f32),
            pltpu.VMEM(level_shape, f32),
            pltpu.VMEM(level_shape, f32),
            pltpu.VMEM(level_shape, f32),
            pltpu.SemaphoreType.DMA((3, levels)),
        ],
        compiler_params=limit(24),
        name="last",
    )(shift, own, *got, parts, logits)


def per_device(
    logits, pot_size, node_type, parent_slot, range_one, range_two, hand_rank, live_mask
):
    branches = [
        functools.partial(step_of_class, size, size == CLASSES[-1]) for size in CLASSES
    ]
    home, shift, found = prepared(logits, pot_size, node_type, parent_slot)
    return lax.switch(
        found[0],
        branches,
        home,
        shift,
        logits,
        pot_size,
        node_type,
        parent_slot,
        range_one,
        range_two,
        hand_rank,
        live_mask,
    )


def solution(mesh):
    return jax.shard_map(
        per_device,
        mesh=mesh,
        in_specs=(
            P("board", None, "node", None),
            P(None, "node"),
            P(None, "node"),
            P(None, "node"),
            P("board", None),
            P("board", None),
            P("board", None),
            P("board", None),
        ),
        out_specs=(P("board", None, "node", None), P("board", None, "node", None)),
        check_vma=False,
    )
```

```python
import functools

import jax
import jax.numpy as jnp
import numpy as np
from jax import lax
from jax.experimental import pallas as pl
from jax.experimental.pallas import tpu as pltpu
from jax.sharding import PartitionSpec as P

LANES = 128
CARDS = 52
step_scale = 0.5
eps_value = 1e-06
MEBI = 1 << 20
CLASSES = (5, 8, 10, 13, 16)
FAR = 5


def padded(count):
    return -(-count // LANES) * LANES


def card_rows(hand_count, wide):
    pairs = [(low, high) for low in range(CARDS) for high in range(low + 1, CARDS)]
    rows = np.full((2, wide), -1, np.int32)
    rows[:, :hand_count] = np.array(pairs[:hand_count], np.int32).T
    return rows


def payoff_kernel(hands, cards_ref, rank_ref, live_ref, out_ref, flat, left, right):
    wide = out_ref.shape[1]
    flat[...] = jnp.zeros(flat.shape, jnp.float32)
    flat[0:1, 0:hands] = rank_ref[...].astype(jnp.float32)
    flat[1:2, 0:hands] = (live_ref[...] > 0).astype(jnp.float32)
    dead = 1.0 - flat[1:2, :]
    feature = lax.broadcasted_iota(jnp.int32, (LANES, wide), 0)
    hit = (feature == cards_ref[0:1, :]) | (feature == cards_ref[1:2, :])
    base = jnp.where(hit, 1.0, 0.0)
    left[...] = jnp.where(feature == CARDS, dead, jnp.where(feature == CARDS + 1, 1.0, base))
    right[...] = jnp.where(
        feature == CARDS, 1.0, jnp.where(feature == CARDS + 1, dead, base)
    ).astype(jnp.bfloat16)
    rank_row = flat[0:1, :]
    for block in range(wide // LANES):
        part = slice(block * LANES, (block + 1) * LANES)
        left_block = left[:, part].T.astype(jnp.bfloat16)
        rank_col = jnp.broadcast_to(flat[0:1, part], (LANES, LANES)).T[:, 0:1]
        hits = jnp.dot(left_block, right[...], preferred_element_type=jnp.float32)
        compat = jnp.where(hits == 0.0, 1.0, 0.0)
        order = jnp.clip(rank_row - rank_col, -1.0, 1.0)
        out_ref[part, :] = (order * compat).astype(jnp.bfloat16)
        out_ref[wide + block * LANES : wide + (block + 1) * LANES, :] = compat.astype(jnp.bfloat16)


def payoff_blocks(hand_rank, live_mask):
    hands = hand_rank.shape[-1]
    wide = padded(hands)
    return pl.pallas_call(
        functools.partial(payoff_kernel, hands),
        out_shape=jax.ShapeDtypeStruct((2 * wide, wide), jnp.bfloat16),
        scratch_shapes=[
            pltpu.VMEM((8, wide), jnp.float32),
            pltpu.VMEM((LANES, wide), jnp.float32),
            pltpu.VMEM((LANES, wide), jnp.bfloat16),
        ],
        compiler_params=pltpu.CompilerParams(vmem_limit_bytes=20 * MEBI),
        cost_estimate=pl.CostEstimate(
            flops=2 * wide * wide * LANES, bytes_accessed=4 * wide * wide, transcendentals=0
        ),
        name="payoff",
    )(jnp.asarray(card_rows(hands, wide)), hand_rank, live_mask)


def row_count(planes, groups):
    return -(-planes * groups // 8) * 8


def plan_of(parent_ref, node_count, groups):
    total = groups * node_count
    first = lax.axis_index("node") * groups
    off = [lax.rem(first - (parent_ref[idx, 0] >> 2) + total, total) for idx in (1, 2, 3)]
    one = off[0]
    two = one + off[1]
    three = two + off[2]
    low = jnp.maximum(one, three - groups)
    high = jnp.minimum(two, groups)
    middle = jnp.minimum(jnp.maximum((one + two + three + 2) >> 2, low), high)
    return middle, middle - one, two - middle, three - middle


def class_of(shift, groups):
    need = jnp.maximum(shift[0] + shift[1], shift[2] + shift[3])
    found = jnp.int32(0)
    for size in CLASSES[:-1]:
        found = found + (need > size).astype(jnp.int32)
    return jnp.where(shift[3] > groups, len(CLASSES) - 1, found)


def fill_messages(node, stage, message_refs, size, block_ref, to_left, to_right):
    _, tiles, planes = stage.shape[:3]
    even = lax.rem(node, 2) == 0
    places = [(tile, plane) for tile in range(tiles) for plane in range(planes)]
    for side, on_left in enumerate((even, jnp.logical_not(even))):
        for near, far in zip(to_left, to_right):
            level = jnp.where(on_left, near[0], far[0])
            start = jnp.where(on_left, near[1], far[1])
            for tile, plane in places:
                stage[side, tile, plane, pl.ds(start, 8), :] = block_ref[level, tile, plane]
    for side, message_ref in enumerate(message_refs):
        for tile, plane in places:
            message_ref[tile, plane * size : plane * size + size, :] = stage[
                side, tile, plane, 8 : 8 + size, :
            ]


def prepare_kernel(
    node_count,
    parent_ref,
    logits_ref,
    pot_ref,
    kind_ref,
    home_ref,
    shift_ref,
    class_ref,
    raw,
    flat,
    turned,
):
    levels, tiles, planes, groups, _ = home_ref.shape
    slots = 4 * groups
    hands = logits_ref.shape[-1]
    shift = plan_of(parent_ref, node_count, groups)
    class_ref[0] = class_of(shift, groups)
    row_id = lax.broadcasted_iota(jnp.int32, shift_ref.shape, 0)
    spread = jnp.zeros(shift_ref.shape, jnp.int32)
    for idx in range(4):
        spread = jnp.where(row_id == idx, shift[idx], spread)
    shift_ref[...] = spread
    pot = pot_ref[...]
    kind = kind_ref[...]
    level = lax.broadcasted_iota(jnp.int32, pot.shape, 0)
    sign = jnp.where(level % 2 == 0, -1.0, 1.0)
    flat[...] = jnp.zeros(flat.shape, jnp.float32)
    flat[0:levels, 0:slots] = jnp.where(kind == 2, pot, 0.0)
    flat[levels : 2 * levels, 0:slots] = jnp.where(kind == 1, pot, 0.0) * sign
    turned[...] = flat[...].T
    lane = lax.broadcasted_iota(jnp.int32, (groups, LANES), 1)
    for idx in range(levels):
        raw[idx, tiles - 1] = jnp.zeros((slots, LANES), jnp.float32)
    for idx in range(levels):
        for tile in range(tiles):
            start = tile * LANES
            stop = min(start + LANES, hands)
            raw[idx, tile, :, 0 : stop - start] = logits_ref[0, idx, :, start:stop]
    for idx in range(levels):
        for tile in range(tiles):
            first = raw[idx, tile, pl.ds(0, groups, stride=4), :]
            for plane in range(planes):
                row = raw[idx, tile, pl.ds(plane + 1, groups, stride=4), :] - first
                if tile == tiles - 1 and plane == 0:
                    for slot in range(4):
                        scale = turned[pl.ds(slot, groups, stride=4), :]
                        row = jnp.where(lane == LANES - 8 + slot, scale[:, idx : idx + 1], row)
                        fold = scale[:, levels + idx : levels + idx + 1]
                        row = jnp.where(lane == LANES - 4 + slot, fold, row)
                home_ref[idx, tile, plane] = row


def prepared(logits, pot_size, node_type, parent_slot):
    _, levels, slots, hands = logits.shape
    groups = slots // 4
    tiles = padded(hands) // LANES
    vmem = pl.BlockSpec(memory_space=pltpu.VMEM)
    smem = pl.BlockSpec(memory_space=pltpu.SMEM)
    return pl.pallas_call(
        functools.partial(prepare_kernel, lax.axis_size("node")),
        out_shape=(
            jax.ShapeDtypeStruct((levels, tiles, 3, groups, LANES), jnp.float32),
            jax.ShapeDtypeStruct((8, LANES), jnp.int32),
            jax.ShapeDtypeStruct((1,), jnp.int32),
        ),
        in_specs=[smem] + [vmem] * 3,
        out_specs=(vmem, vmem, smem),
        scratch_shapes=[
            pltpu.VMEM((levels, tiles, slots, LANES), jnp.float32),
            pltpu.VMEM((LANES, LANES), jnp.float32),
            pltpu.VMEM((LANES, LANES), jnp.float32),
        ],
        compiler_params=pltpu.CompilerParams(vmem_limit_bytes=10 * MEBI),
        name="prepare",
    )(parent_slot, logits, pot_size, node_type)


def shifts_in(shift_ref):
    return [jnp.max(shift_ref[idx : idx + 1, :]) for idx in range(4)]


def pack_kernel(size, far, shift_ref, home_ref, _pot, _kind, _parent, odd_ref, even_ref, *rest):
    far_ref = rest[0] if far else None
    stage = rest[-1]
    _, tiles, planes, groups, _ = home_ref.shape
    shift = shifts_in(shift_ref)
    fill_messages(
        lax.axis_index("node"),
        stage,
        (odd_ref, even_ref),
        size,
        home_ref,
        [(2, 8), (3, 8 + shift[2])],
        [(1, shift[0] + shift[1]), (0, shift[0])],
    )
    if far:
        for tile in range(tiles):
            for plane in range(planes):
                far_ref[tile, plane * FAR : plane * FAR + FAR, :] = home_ref[3, tile, plane, 0:FAR, :]


def message_shapes(planes, wide, size, far):
    tiles = wide // LANES
    message = jax.ShapeDtypeStruct((tiles, row_count(planes, size), LANES), jnp.float32)
    shapes = [message] * 2
    if far:
        shapes.append(jax.ShapeDtypeStruct((tiles, row_count(planes, FAR), LANES), jnp.float32))
    return shapes


def sent_on(odd, even, far, far_steps, order):
    count = lax.axis_size("node")
    edges = [(src, (src + 1) % count) for src in range(count)]
    got = [None, None]
    for side in order:
        pairs = [pair for edge in edges[1 - side :: 2] for pair in (edge, edge[::-1])]
        got[side] = lax.ppermute((odd, even)[side], "node", pairs)
    for message in far:
        pairs = [(src, (src + far_steps) % count) for src in range(count)]
        got.append(lax.ppermute(message, "node", pairs))
    return got


def spread_messages(node, from_left, from_right, odd_ref, even_ref, size):
    tiles, planes = from_left.shape[:2]
    even = lax.rem(node, 2) == 0
    for tile in range(tiles):
        for plane in range(planes):
            place = slice(plane * size, plane * size + size)
            odd_part = odd_ref[tile, place, :]
            even_part = even_ref[tile, place, :]
            from_left[tile, plane, 8 : 8 + size, :] = jnp.where(even, odd_part, even_part)
            from_right[tile, plane, 8 : 8 + size, :] = jnp.where(even, even_part, odd_part)


def inner_sum(inner, rows):
    total = jnp.where(inner[0], rows[0], 0.0)
    for idx in range(1, 4):
        total = total + jnp.where(inner[idx], rows[idx], 0.0)
    return total


def softmax_four(rows):
    top = jnp.maximum(jnp.maximum(rows[0], rows[1]), jnp.maximum(rows[2], 0.0))
    lifted = [jnp.exp(-top)] + [jnp.exp(row - top) for row in rows]
    total = (lifted[0] + lifted[1]) + (lifted[2] + lifted[3])
    return [row / total for row in lifted]


def operator_q(point, show, fold, range_one, range_two, block_ref, cols, put, top_ref=None):
    wide = block_ref.shape[1]
    inner = [
        [(show[idx][slot] == 0.0) & (fold[idx][slot] == 0.0) for slot in range(4)]
        for idx in range(4)
    ]
    strategy = [softmax_four(point[idx]) for idx in range(4)]
    top_one = [range_one * row for row in strategy[0]]
    above_one = inner_sum(inner[0], top_one)
    mid_two = [range_two * row for row in strategy[1]]
    above_two = inner_sum(inner[1], mid_two)
    low_one = [above_one * row for row in strategy[2]]
    last_one = inner_sum(inner[2], low_one)
    end_two = [above_two * row for row in strategy[3]]
    wide_two = jnp.broadcast_to(range_two, above_two.shape)
    reach_rows = [
        (0, [wide_two] * 4, 1.0),
        (1, mid_two, 1.0),
        (2, [above_two] * 4, 1.0),
        (3, end_two, 1.0),
        (1, [above_one] * 4, -1.0),
        (2, low_one, -1.0),
        (3, [last_one] * 4, -1.0),
    ]
    if top_ref is not None:
        reach_rows = reach_rows[1:]
    skipped = 7 - len(reach_rows)
    for unit, (idx, rows, fold_sign) in enumerate(reach_rows):
        for half in range(2):
            place = slice(unit * 32 + half * 16, unit * 32 + half * 16 + 16)
            pair = (2 * half, 2 * half + 1)
            cols[place, 0:wide] = jnp.concatenate(
                [rows[slot] * show[idx][slot] for slot in pair], axis=0
            ).astype(jnp.bfloat16)
            cols[place, wide : 2 * wide] = jnp.concatenate(
                [rows[slot] * (fold[idx][slot] * fold_sign) for slot in pair], axis=0
            ).astype(jnp.bfloat16)
    def added(rows):
        return (rows[0] + rows[1]) + (rows[2] + rows[3])

    def landed(rows, kept, term):
        return [rows[slot] + jnp.where(kept[slot], term, 0.0) for slot in range(4)]

    total = None
    for start in range(0, wide, 2 * LANES):
        stop = min(start + 2 * LANES, wide)
        pay = jnp.dot(cols[...], block_ref[:, start:stop], preferred_element_type=jnp.float32)

        def paid(unit):
            first = (unit - skipped) * 32
            return [pay[first + slot * 8 : first + slot * 8 + 8, :] for slot in range(4)]

        def weighed(idx, rows):
            return added([strategy[idx][slot][:, start:stop] * rows[slot] for slot in range(4)])

        value_two_end = paid(6)
        term_two = added(landed(paid(5), inner[2], weighed(3, value_two_end)))
        value_two_mid = landed(paid(4), inner[1], term_two)
        value_one_low = landed(paid(2), inner[2], added(paid(3)))
        term_one = added(landed(paid(1), inner[1], weighed(2, value_one_low)))
        if top_ref is None:
            value_one_top = landed(paid(0), inner[0], term_one)
        else:
            value_one_top = [
                jnp.where(inner[0][slot], term_one, top_ref[0, slot, :, start:stop])
                for slot in range(4)
            ]
        found = [value_one_top, value_two_mid, value_one_low, value_two_end]
        put(start, stop, found)
        part = squares(found)
        total = part if total is None else total + part
    return total


def squares(found):
    total = None
    for rows in found:
        for row in rows:
            total = row * row if total is None else total + row * row
    return jnp.broadcast_to(jnp.sum(total), (1, LANES))


def scale_columns(rows):
    wide = rows[0][0].shape[1]
    show = [
        [level[0][:, wide - 8 + slot : wide - 7 + slot] for slot in range(4)] for level in rows
    ]
    fold = [
        [level[0][:, wide - 4 + slot : wide - 4 + slot + 1] for slot in range(4)] for level in rows
    ]
    return show, fold


def wide_row(store, place, row_ref):
    hands = row_ref.shape[1]
    store[place : place + 1, 0:hands] = row_ref[...]
    return store[place : place + 1, :]


def first_kernel(size, far, shift_ref, home_ref, odd_ref, even_ref, *rest):
    if far:
        far_ref, rest = rest[0], rest[1:]
    one_ref, two_ref, block_ref, chain_ref, value_ref, square_ref = rest[:6]
    from_left, from_right, window, ranges, cols = rest[6:]
    _, tiles, planes, groups, _ = home_ref.shape
    shift = shifts_in(shift_ref)
    spread_messages(lax.axis_index("node"), from_left, from_right, odd_ref, even_ref, size)
    chain = lax.broadcasted_iota(jnp.int32, (groups, LANES), 0)
    places = [(tile, plane) for tile in range(tiles) for plane in range(planes)]
    for tile, plane in places:
        part = window.at[tile, plane]
        part[8:16, :] = home_ref[0, tile, plane]
        part[24:32, :] = home_ref[1, tile, plane]
        part[32:40, :] = home_ref[3, tile, plane]
        from_right[tile, plane, 0:8, :] = home_ref[2, tile, plane]
        if far:
            part[56 : 56 + FAR, :] = far_ref[tile, plane * FAR : plane * FAR + FAR, :]
    point = [[[] for _ in range(planes)] for _ in range(4)]
    for tile, plane in places:
        part = window.at[tile, plane]
        top = jnp.where(
            chain < shift[0],
            from_left[tile, plane, 8:16, :],
            part[pl.ds(8 - shift[0], 8), :],
        )
        mid = jnp.where(
            chain < shift[1],
            from_left[tile, plane, pl.ds(8 + shift[0], 8), :],
            part[pl.ds(24 - shift[1], 8), :],
        )
        low = from_right[tile, plane, pl.ds(shift[2], 8), :]
        end = jnp.where(
            chain + shift[3] < 8,
            part[pl.ds(32 + shift[3], 8), :],
            from_right[tile, plane, pl.ds(shift[2] + shift[3], 8), :],
        )
        if far:
            end = jnp.where(chain + shift[3] < 16, end, part[pl.ds(40 + shift[3], 8), :])
        for idx, row in enumerate((top, mid, low, end)):
            point[idx][plane].append(row)
    point = [[jnp.concatenate(rows, axis=1) for rows in level] for level in point]
    for idx in range(4):
        for plane in range(planes):
            chain_ref[idx, plane] = point[idx][plane]
    show, fold = scale_columns(point)
    ranges[...] = jnp.zeros(ranges.shape, jnp.float32)
    range_one = wide_row(ranges, 0, one_ref)
    range_two = wide_row(ranges, 1, two_ref)

    def put(start, stop, found):
        for idx in range(4):
            for slot in range(4):
                value_ref[idx, slot, :, start:stop] = found[idx][slot]

    square_ref[...] = operator_q(
        point, show, fold, range_one, range_two, block_ref, cols, put
    )


def rate_of(parts_ref, entry_count):
    square_sum = jnp.sum(parts_ref[...], axis=0, keepdims=True)[:, 0:1]
    return step_scale / jnp.sqrt(square_sum / entry_count + eps_value)


def second_kernel(entry_count, size, far, shift_ref, chain_ref, value_ref, *rest):
    parts_ref, one_ref, two_ref, block_ref, own_ref, odd_ref, even_ref = rest[:7]
    rest = rest[7:]
    if far:
        far_ref, rest = rest[0], rest[1:]
    square_ref, stage, ranges, cols = rest
    _, tiles, planes, groups, _ = own_ref.shape
    rate = rate_of(parts_ref, entry_count)
    raw = [[chain_ref[idx, plane] for plane in range(3)] for idx in range(4)]
    show, fold = scale_columns(raw)
    point = [
        [
            raw[idx][plane] + rate * (value_ref[idx, plane + 1] - value_ref[idx, 0])
            for plane in range(3)
        ]
        for idx in range(4)
    ]
    ranges[...] = jnp.zeros(ranges.shape, jnp.float32)
    range_one = wide_row(ranges, 0, one_ref)
    range_two = wide_row(ranges, 1, two_ref)

    def put(start, stop, found):
        for idx in range(4):
            for slot in range(4):
                for lane in range(start, stop, LANES):
                    row = found[idx][slot][:, lane - start : lane - start + LANES]
                    own_ref[idx, lane // LANES, slot] = row

    square_ref[...] = operator_q(
        point, show, fold, range_one, range_two, block_ref, cols, put, value_ref
    )
    shift = shifts_in(shift_ref)
    fill_messages(
        lax.axis_index("node"),
        stage,
        (odd_ref, even_ref),
        size,
        own_ref,
        [(0, 8), (1, 8 + shift[0])],
        [(3, shift[2] + shift[3]), (2, shift[2])],
    )
    if far:
        for tile in range(tiles):
            for plane in range(planes):
                part = stage.at[0, tile, plane]
                part[pl.ds(jnp.maximum(shift[3] - 8, 0), 8), :] = own_ref[3, tile, plane]
                far_ref[tile, plane * FAR : plane * FAR + FAR, :] = part[8 : 8 + FAR, :]


def last_kernel(entry_count, size, far, shift_ref, own_ref, even_ref, odd_ref, *rest):
    far_ref, rest = (rest[0], rest[1:]) if far else (None, rest)
    parts_ref, logits_hbm, new_hbm, half_hbm, from_left, from_right, window, lined = rest[:8]
    logits_ref, new_ref, half_ref, sems = rest[8:]
    levels, tiles, planes, groups, _ = own_ref.shape
    hands = logits_ref.shape[-1]
    fetches = [
        pltpu.make_async_copy(logits_hbm.at[0, idx], logits_ref.at[idx], sems.at[0, idx])
        for idx in range(levels)
    ]
    for fetch in fetches:
        fetch.start()
    shift = shifts_in(shift_ref)
    rate = rate_of(parts_ref, entry_count)
    group = lax.broadcasted_iota(jnp.int32, (groups, LANES), 0)
    spread_messages(lax.axis_index("node"), from_left, from_right, odd_ref, even_ref, size)
    places = [(tile, plane) for tile in range(tiles) for plane in range(planes)]
    for tile, plane in places:
        part = window.at[tile, plane]
        part[0:8, :] = own_ref[1, tile, plane]
        part[24:32, :] = own_ref[2, tile, plane]
        part[40:48, :] = own_ref[3, tile, plane]
        from_right[tile, plane, 0:8, :] = own_ref[0, tile, plane]
        if far:
            part[56 : 56 + FAR, :] = far_ref[tile, plane * FAR : plane * FAR + FAR, :]

    def top(tile, plane):
        return from_right[tile, plane, pl.ds(shift[0], 8), :]

    def mid(tile, plane):
        return jnp.where(
            group + shift[1] < 8,
            window[tile, plane, pl.ds(shift[1], 8), :],
            from_right[tile, plane, pl.ds(shift[0] + shift[1], 8), :],
        )

    def low(tile, plane):
        return jnp.where(
            group < shift[2],
            from_left[tile, plane, 8:16, :],
            window[tile, plane, pl.ds(24 - shift[2], 8), :],
        )

    def end(tile, plane):
        row = jnp.where(
            group < shift[3],
            from_left[tile, plane, pl.ds(8 + shift[2], 8), :],
            window[tile, plane, pl.ds(40 - jnp.minimum(shift[3], 8), 8), :],
        )
        if far:
            row = jnp.where(group < shift[3] - 8, window[tile, plane, 56:64, :], row)
        return row

    leaving = []

    def leave(source, target, kind, idx):
        leaving.append(pltpu.make_async_copy(source.at[idx], target.at[0, idx], sems.at[kind, idx]))
        leaving[-1].start()

    for idx, found in enumerate((top, mid, low, end)):
        for tile, plane in places:
            lined[idx, tile, pl.ds(plane, groups, stride=4), :] = found(tile, plane)
        fetches[idx].wait()
        for tile in range(tiles):
            start = tile * LANES
            stop = min(start + LANES, hands)
            value = lined[idx, tile][:, 0 : stop - start]
            half_ref[idx, :, start:stop] = value
            new_ref[idx, :, start:stop] = logits_ref[idx, :, start:stop] + rate * value
        leave(half_ref, half_hbm, 1, idx)
        leave(new_ref, new_hbm, 2, idx)
    for copy in leaving:
        copy.wait()


def shared_parts(part):
    count = lax.axis_size("node") * lax.axis_size("board")
    spread = jnp.broadcast_to(part, (count, LANES))
    return lax.all_to_all(spread, ("node", "board"), 0, 0, tiled=True)


def step_of_class(
    size,
    far,
    home,
    shift,
    logits,
    pot_size,
    node_type,
    parent_slot,
    range_one,
    range_two,
    hand_rank,
    live_mask,
):
    _, levels, slots, hands = logits.shape
    wide = padded(hands)
    tiles = wide // LANES
    groups = slots // 4
    entry_count = float(logits.size * lax.axis_size("node") * lax.axis_size("board"))
    vmem = pl.BlockSpec(memory_space=pltpu.VMEM)
    f32 = jnp.float32

    def limit(mebi):
        return pltpu.CompilerParams(vmem_limit_bytes=mebi * MEBI)

    def stage(planes, rows=32):
        return pltpu.VMEM((tiles, planes, rows, LANES), f32)

    def two_stages(planes):
        return pltpu.VMEM((2, tiles, planes, 32, LANES), f32)

    anywhere = pl.BlockSpec(memory_space=pl.ANY)
    sent = pl.pallas_call(
        functools.partial(pack_kernel, size, far),
        out_shape=message_shapes(3, wide, size, far),
        in_specs=[vmem, vmem] + [anywhere] * 3,
        scratch_shapes=[two_stages(3)],
        compiler_params=limit(8),
        name="pack",
    )(shift, home, pot_size, node_type, parent_slot)
    got = sent_on(sent[0], sent[1], sent[2:], -2, (0, 1))
    blocks = payoff_blocks(hand_rank, live_mask)
    rows = 7 * slots

    def work(count):
        return [
            pltpu.VMEM((8, wide), f32),
            pltpu.VMEM((count, 2 * wide), jnp.bfloat16),
        ]

    def cost(count):
        return pl.CostEstimate(
            flops=4 * count * wide * wide, bytes_accessed=6 * wide * wide, transcendentals=0
        )

    square_shape = jax.ShapeDtypeStruct((1, LANES), f32)
    chain, value, part = pl.pallas_call(
        functools.partial(first_kernel, size, far),
        out_shape=(
            jax.ShapeDtypeStruct((levels, 3, groups, wide), f32),
            jax.ShapeDtypeStruct((levels, 4, groups, wide), f32),
            square_shape,
        ),
        in_specs=[vmem] * (5 + len(got)),
        scratch_shapes=[stage(3), stage(3), stage(3, 64)] + work(rows),
        compiler_params=limit(32),
        cost_estimate=cost(rows),
        name="first",
    )(shift, home, *got, range_one, range_two, blocks)
    parts = shared_parts(part)
    own, *sent, part = pl.pallas_call(
        functools.partial(second_kernel, entry_count, size, far),
        out_shape=[jax.ShapeDtypeStruct((levels, tiles, 4, groups, LANES), f32)]
        + message_shapes(4, wide, size, far)
        + [square_shape],
        in_specs=[vmem] * 7,
        scratch_shapes=[two_stages(4)] + work(rows - slots),
        compiler_params=limit(32),
        cost_estimate=cost(rows - slots),
        name="second",
    )(shift, chain, value, parts, range_one, range_two, blocks)
    got = sent_on(sent[0], sent[1], sent[2:], 2, (1, 0))
    parts = shared_parts(part)
    out_shape = jax.ShapeDtypeStruct(logits.shape, f32)
    level_shape = (levels, slots, hands)
    return pl.pallas_call(
        functools.partial(last_kernel, entry_count, size, far),
        out_shape=(out_shape, out_shape),
        in_specs=[vmem] * (3 + len(got)) + [anywhere],
        out_specs=(anywhere, anywhere),
        scratch_shapes=[
            stage(4),
            stage(4),
            stage(4, 64),
            pltpu.VMEM((levels, tiles, slots, LANES), f32),
            pltpu.VMEM(level_shape, f32),
            pltpu.VMEM(level_shape, f32),
            pltpu.VMEM(level_shape, f32),
            pltpu.SemaphoreType.DMA((3, levels)),
        ],
        compiler_params=limit(24),
        name="last",
    )(shift, own, got[1], got[0], *got[2:], parts, logits)


def per_device(
    logits, pot_size, node_type, parent_slot, range_one, range_two, hand_rank, live_mask
):
    branches = [
        functools.partial(step_of_class, size, size == CLASSES[-1]) for size in CLASSES
    ]
    home, shift, found = prepared(logits, pot_size, node_type, parent_slot)
    return lax.switch(
        found[0],
        branches,
        home,
        shift,
        logits,
        pot_size,
        node_type,
        parent_slot,
        range_one,
        range_two,
        hand_rank,
        live_mask,
    )


def solution(mesh):
    return jax.shard_map(
        per_device,
        mesh=mesh,
        in_specs=(
            P("board", None, "node", None),
            P(None, "node"),
            P(None, "node"),
            P(None, "node"),
            P("board", None),
            P("board", None),
            P("board", None),
            P("board", None),
        ),
        out_specs=(P("board", None, "node", None), P("board", None, "node", None)),
        check_vma=False,
    )
```

```python
import functools

import jax
import jax.numpy as jnp
import numpy as np
from jax import lax
from jax.experimental import pallas as pl
from jax.experimental.pallas import tpu as pltpu
from jax.sharding import PartitionSpec as P

LANES = 128
CARDS = 52
step_scale = 0.5
eps_value = 1e-06
MEBI = 1 << 20
CLASSES = (8, 10, 13, 16)
FAR = 5


def padded(count):
    return -(-count // LANES) * LANES


def card_rows(hand_count, wide):
    pairs = [(low, high) for low in range(CARDS) for high in range(low + 1, CARDS)]
    rows = np.full((2, wide), -1, np.int32)
    rows[:, :hand_count] = np.array(pairs[:hand_count], np.int32).T
    return rows


def payoff_kernel(hands, cards_ref, rank_ref, live_ref, out_ref, flat, left, right):
    wide = out_ref.shape[1]
    flat[...] = jnp.zeros(flat.shape, jnp.float32)
    flat[0:1, 0:hands] = rank_ref[...].astype(jnp.float32)
    flat[1:2, 0:hands] = (live_ref[...] > 0).astype(jnp.float32)
    dead = 1.0 - flat[1:2, :]
    feature = lax.broadcasted_iota(jnp.int32, (LANES, wide), 0)
    hit = (feature == cards_ref[0:1, :]) | (feature == cards_ref[1:2, :])
    base = jnp.where(hit, 1.0, 0.0)
    left[...] = jnp.where(feature == CARDS, dead, jnp.where(feature == CARDS + 1, 1.0, base))
    right[...] = jnp.where(
        feature == CARDS, 1.0, jnp.where(feature == CARDS + 1, dead, base)
    ).astype(jnp.bfloat16)
    rank_row = flat[0:1, :]
    for block in range(wide // LANES):
        part = slice(block * LANES, (block + 1) * LANES)
        left_block = left[:, part].T.astype(jnp.bfloat16)
        rank_col = jnp.broadcast_to(flat[0:1, part], (LANES, LANES)).T[:, 0:1]
        hits = jnp.dot(left_block, right[...], preferred_element_type=jnp.float32)
        compat = jnp.where(hits == 0.0, 1.0, 0.0)
        order = jnp.clip(rank_row - rank_col, -1.0, 1.0)
        out_ref[part, :] = (order * compat).astype(jnp.bfloat16)
        out_ref[wide + block * LANES : wide + (block + 1) * LANES, :] = compat.astype(jnp.bfloat16)


def payoff_blocks(hand_rank, live_mask):
    hands = hand_rank.shape[-1]
    wide = padded(hands)
    return pl.pallas_call(
        functools.partial(payoff_kernel, hands),
        out_shape=jax.ShapeDtypeStruct((2 * wide, wide), jnp.bfloat16),
        scratch_shapes=[
            pltpu.VMEM((8, wide), jnp.float32),
            pltpu.VMEM((LANES, wide), jnp.float32),
            pltpu.VMEM((LANES, wide), jnp.bfloat16),
        ],
        compiler_params=pltpu.CompilerParams(vmem_limit_bytes=20 * MEBI),
        cost_estimate=pl.CostEstimate(
            flops=2 * wide * wide * LANES, bytes_accessed=4 * wide * wide, transcendentals=0
        ),
        name="payoff",
    )(jnp.asarray(card_rows(hands, wide)), hand_rank, live_mask)


def row_count(planes, groups):
    return -(-planes * groups // 8) * 8


def plan_of(parent_ref, node_count, groups):
    total = groups * node_count
    first = lax.axis_index("node") * groups
    off = [lax.rem(first - (parent_ref[idx, 0] >> 2) + total, total) for idx in (1, 2, 3)]
    one = off[0]
    two = one + off[1]
    three = two + off[2]
    low = jnp.maximum(one, three - groups)
    high = jnp.minimum(two, groups)
    middle = jnp.minimum(jnp.maximum((one + two + three + 2) >> 2, low), high)
    return middle, middle - one, two - middle, three - middle


def class_of(shift, groups):
    need = jnp.maximum(shift[0] + shift[1], shift[2] + shift[3])
    found = jnp.int32(0)
    for size in CLASSES[:-1]:
        found = found + (need > size).astype(jnp.int32)
    return jnp.where(shift[3] > groups, len(CLASSES) - 1, found)


def fill_messages(node, stage, message_refs, size, block_ref, to_left, to_right):
    _, tiles, planes = stage.shape[:3]
    even = lax.rem(node, 2) == 0
    places = [(tile, plane) for tile in range(tiles) for plane in range(planes)]
    for side, on_left in enumerate((even, jnp.logical_not(even))):
        for near, far in zip(to_left, to_right):
            level = jnp.where(on_left, near[0], far[0])
            start = jnp.where(on_left, near[1], far[1])
            for tile, plane in places:
                stage[side, tile, plane, pl.ds(start, 8), :] = block_ref[level, tile, plane]
    for side, message_ref in enumerate(message_refs):
        for tile, plane in places:
            message_ref[tile, plane * size : plane * size + size, :] = stage[
                side, tile, plane, 8 : 8 + size, :
            ]


def prepare_kernel(
    node_count,
    parent_ref,
    logits_hbm,
    pot_ref,
    kind_ref,
    home_ref,
    shift_ref,
    class_ref,
    logits_ref,
    raw,
    flat,
    turned,
    sems,
):
    levels, tiles, planes, groups, _ = home_ref.shape
    slots = 4 * groups
    hands = logits_ref.shape[-1]
    fetches = [
        pltpu.make_async_copy(logits_hbm.at[0, idx], logits_ref.at[idx], sems.at[idx])
        for idx in range(levels)
    ]
    for fetch in fetches:
        fetch.start()
    shift = plan_of(parent_ref, node_count, groups)
    row_id = lax.broadcasted_iota(jnp.int32, shift_ref.shape, 0)
    spread = jnp.zeros(shift_ref.shape, jnp.int32)
    class_ref[...] = jnp.full((1, 1), class_of(shift, groups))
    for idx, value in enumerate(shift):
        spread = jnp.where(row_id == idx, value, spread)
    shift_ref[...] = spread
    pot = pot_ref[...]
    kind = kind_ref[...]
    level = lax.broadcasted_iota(jnp.int32, pot.shape, 0)
    sign = jnp.where(level % 2 == 0, -1.0, 1.0)
    flat[...] = jnp.zeros(flat.shape, jnp.float32)
    flat[0:levels, 0:slots] = jnp.where(kind == 2, pot, 0.0)
    flat[levels : 2 * levels, 0:slots] = jnp.where(kind == 1, pot, 0.0) * sign
    turned[...] = flat[...].T
    lane = lax.broadcasted_iota(jnp.int32, (groups, LANES), 1)
    for idx in range(levels):
        raw[idx, tiles - 1] = jnp.zeros((slots, LANES), jnp.float32)
    for idx in range(levels):
        fetches[idx].wait()
        for tile in range(tiles):
            start = tile * LANES
            stop = min(start + LANES, hands)
            raw[idx, tile, :, 0 : stop - start] = logits_ref[idx, :, start:stop]
            first = raw[idx, tile, pl.ds(0, groups, stride=4), :]
            for plane in range(planes):
                row = raw[idx, tile, pl.ds(plane + 1, groups, stride=4), :] - first
                if tile == tiles - 1 and plane == 0:
                    for slot in range(4):
                        scale = turned[pl.ds(slot, groups, stride=4), :]
                        row = jnp.where(lane == LANES - 8 + slot, scale[:, idx : idx + 1], row)
                        fold = scale[:, levels + idx : levels + idx + 1]
                        row = jnp.where(lane == LANES - 4 + slot, fold, row)
                home_ref[idx, tile, plane] = row


def prepared(logits, pot_size, node_type, parent_slot):
    _, levels, slots, hands = logits.shape
    groups = slots // 4
    tiles = padded(hands) // LANES
    vmem = pl.BlockSpec(memory_space=pltpu.VMEM)
    smem = pl.BlockSpec(memory_space=pltpu.SMEM)
    return pl.pallas_call(
        functools.partial(prepare_kernel, lax.axis_size("node")),
        out_shape=(
            jax.ShapeDtypeStruct((levels, tiles, 3, groups, LANES), jnp.float32),
            jax.ShapeDtypeStruct((8, LANES), jnp.int32),
            jax.ShapeDtypeStruct((1, 1), jnp.int32),
        ),
        in_specs=[smem, pl.BlockSpec(memory_space=pl.ANY), vmem, vmem],
        out_specs=(vmem, vmem, vmem),
        scratch_shapes=[
            pltpu.VMEM((levels, slots, hands), jnp.float32),
            pltpu.VMEM((levels, tiles, slots, LANES), jnp.float32),
            pltpu.VMEM((LANES, LANES), jnp.float32),
            pltpu.VMEM((LANES, LANES), jnp.float32),
            pltpu.SemaphoreType.DMA((levels,)),
        ],
        compiler_params=pltpu.CompilerParams(vmem_limit_bytes=10 * MEBI),
        name="prepare",
    )(parent_slot, logits, pot_size, node_type)


def ahead(rows, count):
    return pltpu.roll(rows, (8 - count) & 7, 0)


def behind(rows, count):
    return pltpu.roll(rows, count & 7, 0)


def shifts_in(shift_ref):
    return [jnp.max(shift_ref[idx : idx + 1, :]) for idx in range(4)]


def pack_kernel(size, far, shift_ref, home_ref, _pot, _kind, _parent, odd_ref, even_ref, *rest):
    far_ref = rest[0] if far else None
    stage = rest[-1]
    _, tiles, planes, groups, _ = home_ref.shape
    shift = shifts_in(shift_ref)
    fill_messages(
        lax.axis_index("node"),
        stage,
        (odd_ref, even_ref),
        size,
        home_ref,
        [(2, 8), (3, 8 + shift[2])],
        [(1, shift[0] + shift[1]), (0, shift[0])],
    )
    if far:
        for tile in range(tiles):
            for plane in range(planes):
                far_ref[tile, plane * FAR : plane * FAR + FAR, :] = home_ref[3, tile, plane, 0:FAR, :]


def message_shapes(planes, wide, size, far):
    tiles = wide // LANES
    message = jax.ShapeDtypeStruct((tiles, row_count(planes, size), LANES), jnp.float32)
    shapes = [message] * 2
    if far:
        shapes.append(jax.ShapeDtypeStruct((tiles, row_count(planes, FAR), LANES), jnp.float32))
    return shapes


def sent_on(odd, even, far, far_steps, order):
    count = lax.axis_size("node")
    edges = [(src, (src + 1) % count) for src in range(count)]
    got = [None, None]
    for side in order:
        pairs = [pair for edge in edges[1 - side :: 2] for pair in (edge, edge[::-1])]
        got[side] = lax.ppermute((odd, even)[side], "node", pairs)
    for message in far:
        pairs = [(src, (src + far_steps) % count) for src in range(count)]
        got.append(lax.ppermute(message, "node", pairs))
    return got


def spread_messages(node, from_left, from_right, odd_ref, even_ref, size):
    tiles, planes = from_left.shape[:2]
    even = lax.rem(node, 2) == 0
    for tile in range(tiles):
        for plane in range(planes):
            place = slice(plane * size, plane * size + size)
            odd_part = odd_ref[tile, place, :]
            even_part = even_ref[tile, place, :]
            from_left[tile, plane, 8 : 8 + size, :] = jnp.where(even, odd_part, even_part)
            from_right[tile, plane, 8 : 8 + size, :] = jnp.where(even, even_part, odd_part)


def inner_sum(inner, rows):
    total = jnp.where(inner[0], rows[0], 0.0)
    for idx in range(1, 4):
        total = total + jnp.where(inner[idx], rows[idx], 0.0)
    return total


def softmax_four(rows):
    top = jnp.maximum(jnp.maximum(rows[0], rows[1]), jnp.maximum(rows[2], 0.0))
    lifted = [jnp.exp(-top)] + [jnp.exp(row - top) for row in rows]
    total = (lifted[0] + lifted[1]) + (lifted[2] + lifted[3])
    return [row / total for row in lifted]


def operator_q(point, show, fold, range_one, range_two, block_ref, cols, put, top_ref=None):
    wide = block_ref.shape[1]
    inner = [
        [(show[idx][slot] == 0.0) & (fold[idx][slot] == 0.0) for slot in range(4)]
        for idx in range(4)
    ]
    strategy = [softmax_four(point[idx]) for idx in range(4)]
    top_one = [range_one * row for row in strategy[0]]
    above_one = inner_sum(inner[0], top_one)
    mid_two = [range_two * row for row in strategy[1]]
    above_two = inner_sum(inner[1], mid_two)
    low_one = [above_one * row for row in strategy[2]]
    last_one = inner_sum(inner[2], low_one)
    end_two = [above_two * row for row in strategy[3]]
    wide_two = jnp.broadcast_to(range_two, above_two.shape)
    units = [
        (0, [wide_two] * 4, 1.0, False),
        (1, mid_two, 1.0, True),
        (2, [above_two] * 4, 1.0, False),
        (3, end_two, 1.0, True),
        (1, [above_one] * 4, -1.0, False),
        (2, low_one, -1.0, True),
        (3, [last_one] * 4, -1.0, False),
    ]
    first_unit = 0 if top_ref is None else 1
    begin = [0] * len(units)
    place = 0
    for unit in range(first_unit, len(units)):
        idx, rows, fold_sign, as_sum = units[unit]
        begin[unit] = place
        for side in range(2):
            lanes = slice(side * wide, side * wide + wide)
            if side == 0:
                scaled = [rows[slot] * show[idx][slot] for slot in range(4)]
            else:
                scaled = [rows[slot] * (fold[idx][slot] * fold_sign) for slot in range(4)]
            if as_sum:
                rounded = [row.astype(jnp.bfloat16).astype(jnp.float32) for row in scaled]
                total = (rounded[0] + rounded[1]) + (rounded[2] + rounded[3])
                high = total.astype(jnp.bfloat16).astype(jnp.float32)
                scaled = [high, total - high]
            for pair in range(0, len(scaled), 2):
                cols[place + pair * 8 : place + pair * 8 + 16, lanes] = jnp.concatenate(
                    scaled[pair : pair + 2], axis=0
                ).astype(jnp.bfloat16)
        place += 16 if as_sum else 32

    def added(rows):
        return (rows[0] + rows[1]) + (rows[2] + rows[3])

    def landed(rows, kept, term):
        return [rows[slot] + jnp.where(kept[slot], term, 0.0) for slot in range(4)]

    total = None
    for start in range(0, wide, 2 * LANES):
        stop = min(start + 2 * LANES, wide)
        pay = jnp.dot(cols[...], block_ref[:, start:stop], preferred_element_type=jnp.float32)

        def paid(unit):
            at = begin[unit]
            return [pay[at + slot * 8 : at + slot * 8 + 8, :] for slot in range(4)]

        def paid_sum(unit):
            at = begin[unit]
            return pay[at : at + 8, :] + pay[at + 8 : at + 16, :]

        def weighed(idx, rows):
            return added([strategy[idx][slot][:, start:stop] * rows[slot] for slot in range(4)])

        value_two_end = paid(6)
        term_two = paid_sum(5) + weighed(3, value_two_end)
        value_two_mid = landed(paid(4), inner[1], term_two)
        value_one_low = landed(paid(2), inner[2], paid_sum(3))
        term_one = paid_sum(1) + weighed(2, value_one_low)
        if top_ref is None:
            value_one_top = landed(paid(0), inner[0], term_one)
        else:
            value_one_top = [
                jnp.where(inner[0][slot], term_one, top_ref[0, slot, :, start:stop])
                for slot in range(4)
            ]
        found = [value_one_top, value_two_mid, value_one_low, value_two_end]
        put(start, stop, found)
        part = squares(found)
        total = part if total is None else total + part
    return total


def squares(found):
    total = None
    for rows in found:
        for row in rows:
            total = row * row if total is None else total + row * row
    return jnp.broadcast_to(jnp.sum(total), (1, LANES))


def scale_columns(rows):
    wide = rows[0][0].shape[1]
    show = [
        [level[0][:, wide - 8 + slot : wide - 7 + slot] for slot in range(4)] for level in rows
    ]
    fold = [
        [level[0][:, wide - 4 + slot : wide - 4 + slot + 1] for slot in range(4)] for level in rows
    ]
    return show, fold


def wide_row(store, place, row_ref):
    hands = row_ref.shape[1]
    store[place : place + 1, 0:hands] = row_ref[...]
    return store[place : place + 1, :]


def first_kernel(size, far, shift_ref, home_ref, odd_ref, even_ref, *rest):
    if far:
        far_ref, rest = rest[0], rest[1:]
    one_ref, two_ref, block_ref, chain_ref, value_ref, square_ref = rest[:6]
    from_left, from_right, window, ranges, cols = rest[6:]
    _, tiles, planes, groups, _ = home_ref.shape
    shift = shifts_in(shift_ref)
    spread_messages(lax.axis_index("node"), from_left, from_right, odd_ref, even_ref, size)
    chain = lax.broadcasted_iota(jnp.int32, (groups, LANES), 0)
    places = [(tile, plane) for tile in range(tiles) for plane in range(planes)]
    if far:
        for tile, plane in places:
            window[tile, plane, 16 : 16 + FAR, :] = far_ref[
                tile, plane * FAR : plane * FAR + FAR, :
            ]
    point = [[[] for _ in range(planes)] for _ in range(4)]
    for tile, plane in places:
        top = jnp.where(
            chain < shift[0],
            from_left[tile, plane, 8:16, :],
            behind(home_ref[0, tile, plane], shift[0]),
        )
        mid = jnp.where(
            chain < shift[1],
            from_left[tile, plane, pl.ds(8 + shift[0], 8), :],
            behind(home_ref[1, tile, plane], shift[1]),
        )
        low = jnp.where(
            chain + shift[2] < 8,
            ahead(home_ref[2, tile, plane], shift[2]),
            from_right[tile, plane, pl.ds(shift[2], 8), :],
        )
        end = jnp.where(
            chain + shift[3] < 8,
            ahead(home_ref[3, tile, plane], shift[3]),
            from_right[tile, plane, pl.ds(shift[2] + shift[3], 8), :],
        )
        if far:
            far_part = window[tile, plane, pl.ds(shift[3], 8), :]
            end = jnp.where(chain + shift[3] < 16, end, far_part)
        for idx, row in enumerate((top, mid, low, end)):
            point[idx][plane].append(row)
    point = [[jnp.concatenate(rows, axis=1) for rows in level] for level in point]
    for idx in range(4):
        for plane in range(planes):
            chain_ref[idx, plane] = point[idx][plane]
    show, fold = scale_columns(point)
    ranges[...] = jnp.zeros(ranges.shape, jnp.float32)
    range_one = wide_row(ranges, 0, one_ref)
    range_two = wide_row(ranges, 1, two_ref)

    def put(start, stop, found):
        for idx in range(4):
            for slot in range(4):
                value_ref[idx, slot, :, start:stop] = found[idx][slot]

    square_ref[...] = operator_q(
        point, show, fold, range_one, range_two, block_ref, cols, put
    )


def rate_of(parts_ref, entry_count):
    square_sum = jnp.sum(parts_ref[...], axis=0, keepdims=True)[:, 0:1]
    return step_scale / jnp.sqrt(square_sum / entry_count + eps_value)


def second_kernel(entry_count, size, far, shift_ref, chain_ref, value_ref, *rest):
    parts_ref, one_ref, two_ref, block_ref, own_ref, odd_ref, even_ref = rest[:7]
    rest = rest[7:]
    if far:
        far_ref, rest = rest[0], rest[1:]
    square_ref, stage, ranges, cols = rest
    _, tiles, planes, groups, _ = own_ref.shape
    rate = rate_of(parts_ref, entry_count)
    raw = [[chain_ref[idx, plane] for plane in range(3)] for idx in range(4)]
    show, fold = scale_columns(raw)
    point = [
        [
            raw[idx][plane] + rate * (value_ref[idx, plane + 1] - value_ref[idx, 0])
            for plane in range(3)
        ]
        for idx in range(4)
    ]
    ranges[...] = jnp.zeros(ranges.shape, jnp.float32)
    range_one = wide_row(ranges, 0, one_ref)
    range_two = wide_row(ranges, 1, two_ref)

    def put(start, stop, found):
        for idx in range(4):
            for slot in range(4):
                for lane in range(start, stop, LANES):
                    row = found[idx][slot][:, lane - start : lane - start + LANES]
                    own_ref[idx, lane // LANES, slot] = row

    square_ref[...] = operator_q(
        point, show, fold, range_one, range_two, block_ref, cols, put, value_ref
    )
    shift = shifts_in(shift_ref)
    fill_messages(
        lax.axis_index("node"),
        stage,
        (odd_ref, even_ref),
        size,
        own_ref,
        [(0, 8), (1, 8 + shift[0])],
        [(3, shift[2] + shift[3]), (2, shift[2])],
    )
    if far:
        for tile in range(tiles):
            for plane in range(planes):
                part = stage.at[0, tile, plane]
                part[pl.ds(jnp.maximum(shift[3] - 8, 0), 8), :] = own_ref[3, tile, plane]
                far_ref[tile, plane * FAR : plane * FAR + FAR, :] = part[8 : 8 + FAR, :]


def last_kernel(entry_count, size, far, shift_ref, own_ref, even_ref, odd_ref, *rest):
    far_ref, rest = (rest[0], rest[1:]) if far else (None, rest)
    parts_ref, logits_hbm, new_hbm, half_hbm, from_left, from_right, lined = rest[:7]
    logits_ref, new_ref, half_ref, sems = rest[7:]
    levels, tiles, planes, groups, _ = own_ref.shape
    hands = logits_ref.shape[-1]
    fetches = [
        pltpu.make_async_copy(logits_hbm.at[0, idx], logits_ref.at[idx], sems.at[0, idx])
        for idx in range(levels)
    ]
    for fetch in fetches:
        fetch.start()
    shift = shifts_in(shift_ref)
    rate = rate_of(parts_ref, entry_count)
    group = lax.broadcasted_iota(jnp.int32, (groups, LANES), 0)
    spread_messages(lax.axis_index("node"), from_left, from_right, odd_ref, even_ref, size)
    places = [(tile, plane) for tile in range(tiles) for plane in range(planes)]

    def top(tile, plane, own):
        return jnp.where(
            group + shift[0] < 8,
            ahead(own, shift[0]),
            from_right[tile, plane, pl.ds(shift[0], 8), :],
        )

    def mid(tile, plane, own):
        return jnp.where(
            group + shift[1] < 8,
            ahead(own, shift[1]),
            from_right[tile, plane, pl.ds(shift[0] + shift[1], 8), :],
        )

    def low(tile, plane, own):
        return jnp.where(
            group < shift[2], from_left[tile, plane, 8:16, :], behind(own, shift[2])
        )

    def end(tile, plane, own):
        row = jnp.where(
            group < shift[3],
            from_left[tile, plane, pl.ds(8 + shift[2], 8), :],
            behind(own, shift[3]),
        )
        if far:
            far_part = far_ref[tile, plane * FAR : plane * FAR + 8, :]
            row = jnp.where(group < shift[3] - 8, far_part, row)
        return row

    leaving = []

    def leave(source, target, kind, idx):
        leaving.append(pltpu.make_async_copy(source.at[idx], target.at[0, idx], sems.at[kind, idx]))
        leaving[-1].start()

    for idx, found in enumerate((top, mid, low, end)):
        for tile, plane in places:
            row = found(tile, plane, own_ref[idx, tile, plane])
            lined[idx, tile, pl.ds(plane, groups, stride=4), :] = row
        fetches[idx].wait()
        for tile in range(tiles):
            start = tile * LANES
            stop = min(start + LANES, hands)
            value = lined[idx, tile][:, 0 : stop - start]
            half_ref[idx, :, start:stop] = value
            new_ref[idx, :, start:stop] = logits_ref[idx, :, start:stop] + rate * value
        leave(half_ref, half_hbm, 1, idx)
        leave(new_ref, new_hbm, 2, idx)
    for copy in leaving:
        copy.wait()


def shared_parts(part):
    count = lax.axis_size("node") * lax.axis_size("board")
    spread = jnp.broadcast_to(part, (count, LANES))
    return lax.all_to_all(spread, ("node", "board"), 0, 0, tiled=True)


def step_of_class(
    size,
    far,
    home,
    shift,
    logits,
    pot_size,
    node_type,
    parent_slot,
    range_one,
    range_two,
    hand_rank,
    live_mask,
):
    _, levels, slots, hands = logits.shape
    wide = padded(hands)
    tiles = wide // LANES
    groups = slots // 4
    entry_count = float(logits.size * lax.axis_size("node") * lax.axis_size("board"))
    vmem = pl.BlockSpec(memory_space=pltpu.VMEM)
    f32 = jnp.float32

    def limit(mebi):
        return pltpu.CompilerParams(vmem_limit_bytes=mebi * MEBI)

    def stage(planes, rows=32):
        return pltpu.VMEM((tiles, planes, rows, LANES), f32)

    def two_stages(planes):
        return pltpu.VMEM((2, tiles, planes, 32, LANES), f32)

    anywhere = pl.BlockSpec(memory_space=pl.ANY)
    sent = pl.pallas_call(
        functools.partial(pack_kernel, size, far),
        out_shape=message_shapes(3, wide, size, far),
        in_specs=[vmem, vmem] + [anywhere] * 3,
        scratch_shapes=[two_stages(3)],
        compiler_params=limit(8),
        name="pack",
    )(shift, home, pot_size, node_type, parent_slot)
    got = sent_on(sent[0], sent[1], sent[2:], -2, (0, 1))
    blocks = payoff_blocks(hand_rank, live_mask)
    rows = 4 * slots + 3 * 16

    def work(count):
        return [
            pltpu.VMEM((8, wide), f32),
            pltpu.VMEM((count, 2 * wide), jnp.bfloat16),
        ]

    def cost(count):
        return pl.CostEstimate(
            flops=4 * count * wide * wide, bytes_accessed=6 * wide * wide, transcendentals=0
        )

    square_shape = jax.ShapeDtypeStruct((1, LANES), f32)
    chain, value, part = pl.pallas_call(
        functools.partial(first_kernel, size, far),
        out_shape=(
            jax.ShapeDtypeStruct((levels, 3, groups, wide), f32),
            jax.ShapeDtypeStruct((levels, 4, groups, wide), f32),
            square_shape,
        ),
        in_specs=[vmem] * (5 + len(got)),
        scratch_shapes=[stage(3), stage(3), stage(3)] + work(rows),
        compiler_params=limit(32),
        cost_estimate=cost(rows),
        name="first",
    )(shift, home, *got, range_one, range_two, blocks)
    parts = shared_parts(part)
    own, *sent, part = pl.pallas_call(
        functools.partial(second_kernel, entry_count, size, far),
        out_shape=[jax.ShapeDtypeStruct((levels, tiles, 4, groups, LANES), f32)]
        + message_shapes(4, wide, size, far)
        + [square_shape],
        in_specs=[vmem] * 7,
        scratch_shapes=[two_stages(4)] + work(rows - slots),
        compiler_params=limit(32),
        cost_estimate=cost(rows - slots),
        name="second",
    )(shift, chain, value, parts, range_one, range_two, blocks)
    got = sent_on(sent[0], sent[1], sent[2:], 2, (1, 0))
    parts = shared_parts(part)
    out_shape = jax.ShapeDtypeStruct(logits.shape, f32)
    level_shape = (levels, slots, hands)
    return pl.pallas_call(
        functools.partial(last_kernel, entry_count, size, far),
        out_shape=(out_shape, out_shape),
        in_specs=[vmem] * (3 + len(got)) + [anywhere],
        out_specs=(anywhere, anywhere),
        scratch_shapes=[
            stage(4),
            stage(4),
            pltpu.VMEM((levels, tiles, slots, LANES), f32),
            pltpu.VMEM(level_shape, f32),
            pltpu.VMEM(level_shape, f32),
            pltpu.VMEM(level_shape, f32),
            pltpu.SemaphoreType.DMA((3, levels)),
        ],
        compiler_params=limit(24),
        name="last",
    )(shift, own, got[1], got[0], *got[2:], parts, logits)


def per_device(
    logits, pot_size, node_type, parent_slot, range_one, range_two, hand_rank, live_mask
):
    branches = [
        functools.partial(step_of_class, size, size == CLASSES[-1]) for size in CLASSES
    ]
    home, shift, found = prepared(logits, pot_size, node_type, parent_slot)
    return lax.switch(
        found[0, 0],
        branches,
        home,
        shift,
        logits,
        pot_size,
        node_type,
        parent_slot,
        range_one,
        range_two,
        hand_rank,
        live_mask,
    )


def solution(mesh):
    return jax.shard_map(
        per_device,
        mesh=mesh,
        in_specs=(
            P("board", None, "node", None),
            P(None, "node"),
            P(None, "node"),
            P(None, "node"),
            P("board", None),
            P("board", None),
            P("board", None),
            P("board", None),
        ),
        out_specs=(P("board", None, "node", None), P("board", None, "node", None)),
        check_vma=False,
    )
```

```python
import functools

import jax
import jax.numpy as jnp
import numpy as np
from jax import lax
from jax.experimental import pallas as pl
from jax.experimental.pallas import tpu as pltpu
from jax.sharding import PartitionSpec as P

LANES = 128
CARDS = 52
step_scale = 0.5
eps_value = 1e-06
MEBI = 1 << 20
CLASSES = (8, 10, 12, 14)
FAR = 5


def padded(count):
    return -(-count // LANES) * LANES


def card_rows(hand_count, wide):
    pairs = [(low, high) for low in range(CARDS) for high in range(low + 1, CARDS)]
    rows = np.full((2, wide), -1, np.int32)
    rows[:, :hand_count] = np.array(pairs[:hand_count], np.int32).T
    return rows


def payoff_kernel(hands, cards_ref, rank_ref, live_ref, out_ref, flat, left, right):
    wide = out_ref.shape[1]
    flat[...] = jnp.zeros(flat.shape, jnp.float32)
    flat[0:1, 0:hands] = rank_ref[...].astype(jnp.float32)
    flat[1:2, 0:hands] = (live_ref[...] > 0).astype(jnp.float32)
    dead = 1.0 - flat[1:2, :]
    feature = lax.broadcasted_iota(jnp.int32, (LANES, wide), 0)
    hit = (feature == cards_ref[0:1, :]) | (feature == cards_ref[1:2, :])
    base = jnp.where(hit, 1.0, 0.0)
    left[...] = jnp.where(feature == CARDS, dead, jnp.where(feature == CARDS + 1, 1.0, base))
    right[...] = jnp.where(
        feature == CARDS, 1.0, jnp.where(feature == CARDS + 1, dead, base)
    ).astype(jnp.bfloat16)
    rank_row = flat[0:1, :]
    for block in range(wide // LANES):
        part = slice(block * LANES, (block + 1) * LANES)
        left_block = left[:, part].T.astype(jnp.bfloat16)
        rank_col = jnp.broadcast_to(flat[0:1, part], (LANES, LANES)).T[:, 0:1]
        hits = jnp.dot(left_block, right[...], preferred_element_type=jnp.float32)
        compat = jnp.where(hits == 0.0, 1.0, 0.0)
        order = jnp.clip(rank_row - rank_col, -1.0, 1.0)
        out_ref[part, :] = (order * compat).astype(jnp.bfloat16)
        out_ref[wide + block * LANES : wide + (block + 1) * LANES, :] = compat.astype(jnp.bfloat16)


def payoff_blocks(hand_rank, live_mask):
    hands = hand_rank.shape[-1]
    wide = padded(hands)
    return pl.pallas_call(
        functools.partial(payoff_kernel, hands),
        out_shape=jax.ShapeDtypeStruct((2 * wide, wide), jnp.bfloat16),
        scratch_shapes=[
            pltpu.VMEM((8, wide), jnp.float32),
            pltpu.VMEM((LANES, wide), jnp.float32),
            pltpu.VMEM((LANES, wide), jnp.bfloat16),
        ],
        compiler_params=pltpu.CompilerParams(vmem_limit_bytes=20 * MEBI),
        cost_estimate=pl.CostEstimate(
            flops=2 * wide * wide * LANES, bytes_accessed=4 * wide * wide, transcendentals=0
        ),
        name="payoff",
    )(jnp.asarray(card_rows(hands, wide)), hand_rank, live_mask)


def row_count(planes, groups):
    return -(-planes * groups // 8) * 8


def plan_of(parent_ref, node_count, groups):
    total = groups * node_count
    first = lax.axis_index("node") * groups
    off = [lax.rem(first - (parent_ref[idx, 0] >> 2) + total, total) for idx in (1, 2, 3)]
    one = off[0]
    two = one + off[1]
    three = two + off[2]
    low = jnp.maximum(one, three - groups)
    high = jnp.minimum(two, groups)
    middle = jnp.minimum(jnp.maximum((one + two + three + 2) >> 2, low), high)
    return middle, middle - one, two - middle, three - middle


def class_of(shift, groups):
    near = jnp.where(shift[3] > groups, 2 * groups - shift[3], shift[3])
    need = jnp.maximum(shift[0] + shift[1], shift[2] + near)
    found = jnp.int32(0)
    for size in CLASSES[:-1]:
        found = found + (need > size).astype(jnp.int32)
    return jnp.where(shift[3] > groups, len(CLASSES) - 1, found)


def fill_messages(
    node, stage, message_refs, size, block_ref, to_left, to_right, skipped=None
):
    _, tiles, planes = stage.shape[:3]
    even = lax.rem(node, 2) == 0
    places = [(tile, plane) for tile in range(tiles) for plane in range(planes)]
    for side, on_left in enumerate((even, jnp.logical_not(even))):
        for near, far in zip(to_left, to_right):
            level = jnp.where(on_left, near[0], far[0])
            start = jnp.where(on_left, near[1], far[1])
            for tile, plane in places:
                block = block_ref[level, tile, plane]
                if skipped is not None:
                    block = ahead(block, jnp.where(level == 3, skipped, 0))
                stage[side, tile, plane, pl.ds(start, 8), :] = block
    for side, message_ref in enumerate(message_refs):
        for tile, plane in places:
            message_ref[tile, plane * size : plane * size + size, :] = stage[
                side, tile, plane, 8 : 8 + size, :
            ]


def prepare_kernel(
    node_count,
    parent_hbm,
    logits_hbm,
    pot_hbm,
    kind_hbm,
    home_ref,
    shift_ref,
    class_ref,
    parent_ref,
    logits_ref,
    pot_ref,
    kind_ref,
    raw,
    flat,
    turned,
    sems,
):
    levels, tiles, planes, groups, _ = home_ref.shape
    slots = 4 * groups
    hands = logits_ref.shape[-1]
    fetches = [
        pltpu.make_async_copy(logits_hbm.at[0, idx], logits_ref.at[idx], sems.at[idx])
        for idx in range(levels)
    ]
    tables = [
        pltpu.make_async_copy(source, target, sems.at[levels + idx])
        for idx, (source, target) in enumerate(
            ((parent_hbm, parent_ref), (pot_hbm, pot_ref), (kind_hbm, kind_ref))
        )
    ]
    for fetch in tables + fetches:
        fetch.start()
    for fetch in tables:
        fetch.wait()
    shift = plan_of(parent_ref, node_count, groups)
    row_id = lax.broadcasted_iota(jnp.int32, shift_ref.shape, 0)
    spread = jnp.zeros(shift_ref.shape, jnp.int32)
    class_ref[...] = jnp.full((1, 1), class_of(shift, groups))
    for idx, value in enumerate(shift):
        spread = jnp.where(row_id == idx, value, spread)
    shift_ref[...] = spread
    pot = pot_ref[...]
    kind = kind_ref[...]
    level = lax.broadcasted_iota(jnp.int32, pot.shape, 0)
    sign = jnp.where(level % 2 == 0, -1.0, 1.0)
    flat[...] = jnp.zeros(flat.shape, jnp.float32)
    flat[0:levels, 0:slots] = jnp.where(kind == 2, pot, 0.0)
    flat[levels : 2 * levels, 0:slots] = jnp.where(kind == 1, pot, 0.0) * sign
    turned[...] = flat[...].T
    lane = lax.broadcasted_iota(jnp.int32, (groups, LANES), 1)
    for idx in range(levels):
        raw[idx, tiles - 1] = jnp.zeros((slots, LANES), jnp.float32)
    for idx in range(levels):
        fetches[idx].wait()
        for tile in range(tiles):
            start = tile * LANES
            stop = min(start + LANES, hands)
            raw[idx, tile, :, 0 : stop - start] = logits_ref[idx, :, start:stop]
            first = raw[idx, tile, pl.ds(0, groups, stride=4), :]
            for plane in range(planes):
                row = raw[idx, tile, pl.ds(plane + 1, groups, stride=4), :] - first
                if tile == tiles - 1 and plane == 0:
                    for slot in range(4):
                        scale = turned[pl.ds(slot, groups, stride=4), :]
                        row = jnp.where(lane == LANES - 8 + slot, scale[:, idx : idx + 1], row)
                        fold = scale[:, levels + idx : levels + idx + 1]
                        row = jnp.where(lane == LANES - 4 + slot, fold, row)
                home_ref[idx, tile, plane] = row


def prepared(logits, pot_size, node_type, parent_slot):
    _, levels, slots, hands = logits.shape
    groups = slots // 4
    tiles = padded(hands) // LANES
    vmem = pl.BlockSpec(memory_space=pltpu.VMEM)
    return pl.pallas_call(
        functools.partial(prepare_kernel, lax.axis_size("node")),
        out_shape=(
            jax.ShapeDtypeStruct((levels, tiles, 3, groups, LANES), jnp.float32),
            jax.ShapeDtypeStruct((8, LANES), jnp.int32),
            jax.ShapeDtypeStruct((1, 1), jnp.int32),
        ),
        in_specs=[pl.BlockSpec(memory_space=pl.ANY)] * 4,
        out_specs=(vmem, vmem, vmem),
        scratch_shapes=[
            pltpu.SMEM(parent_slot.shape, jnp.int32),
            pltpu.VMEM((levels, slots, hands), jnp.float32),
            pltpu.VMEM(pot_size.shape, jnp.float32),
            pltpu.VMEM(node_type.shape, jnp.int32),
            pltpu.VMEM((levels, tiles, slots, LANES), jnp.float32),
            pltpu.VMEM((LANES, LANES), jnp.float32),
            pltpu.VMEM((LANES, LANES), jnp.float32),
            pltpu.SemaphoreType.DMA((levels + 3,)),
        ],
        compiler_params=pltpu.CompilerParams(vmem_limit_bytes=10 * MEBI),
        name="prepare",
    )(parent_slot, logits, pot_size, node_type)


def ahead(rows, count):
    return pltpu.roll(rows, (8 - count) & 7, 0)


def behind(rows, count):
    return pltpu.roll(rows, count & 7, 0)


def shifts_in(shift_ref):
    return [jnp.max(shift_ref[idx : idx + 1, :]) for idx in range(4)]


def pack_kernel(size, far, shift_ref, home_ref, _pot, _kind, _parent, odd_ref, even_ref, *rest):
    far_ref = rest[0] if far else None
    stage = rest[-1]
    _, tiles, planes, groups, _ = home_ref.shape
    shift = shifts_in(shift_ref)
    skipped = jnp.maximum(shift[3] - 8, 0) if far else None
    fill_messages(
        lax.axis_index("node"),
        stage,
        (odd_ref, even_ref),
        size,
        home_ref,
        [(2, 8), (3, 8 + shift[2])],
        [(1, shift[0] + shift[1]), (0, shift[0])],
        skipped,
    )
    if far:
        for tile in range(tiles):
            for plane in range(planes):
                far_ref[tile, plane * FAR : plane * FAR + FAR, :] = home_ref[3, tile, plane, 0:FAR, :]


def message_shapes(planes, wide, size, far):
    tiles = wide // LANES
    message = jax.ShapeDtypeStruct((tiles, row_count(planes, size), LANES), jnp.float32)
    shapes = [message] * 2
    if far:
        shapes.append(jax.ShapeDtypeStruct((tiles, row_count(planes, FAR), LANES), jnp.float32))
    return shapes


def sent_on(odd, even, far, far_steps, order):
    count = lax.axis_size("node")
    edges = [(src, (src + 1) % count) for src in range(count)]
    got = [None, None]
    for side in order:
        pairs = [pair for edge in edges[1 - side :: 2] for pair in (edge, edge[::-1])]
        got[side] = lax.ppermute((odd, even)[side], "node", pairs)
    for message in far:
        pairs = [(src, (src + far_steps) % count) for src in range(count)]
        got.append(lax.ppermute(message, "node", pairs))
    return got


def spread_messages(node, from_left, from_right, odd_ref, even_ref, size):
    tiles, planes = from_left.shape[:2]
    even = lax.rem(node, 2) == 0
    for tile in range(tiles):
        for plane in range(planes):
            place = slice(plane * size, plane * size + size)
            odd_part = odd_ref[tile, place, :]
            even_part = even_ref[tile, place, :]
            from_left[tile, plane, 8 : 8 + size, :] = jnp.where(even, odd_part, even_part)
            from_right[tile, plane, 8 : 8 + size, :] = jnp.where(even, even_part, odd_part)


def inner_sum(inner, rows):
    total = jnp.where(inner[0], rows[0], 0.0)
    for idx in range(1, 4):
        total = total + jnp.where(inner[idx], rows[idx], 0.0)
    return total


def softmax_four(rows):
    top = jnp.maximum(jnp.maximum(rows[0], rows[1]), jnp.maximum(rows[2], 0.0))
    lifted = [jnp.exp(-top)] + [jnp.exp(row - top) for row in rows]
    total = (lifted[0] + lifted[1]) + (lifted[2] + lifted[3])
    return [row / total for row in lifted]


def operator_q(point, show, fold, range_one, range_two, block_ref, cols, put, top_ref=None):
    wide = block_ref.shape[1]
    inner = [
        [(show[idx][slot] == 0.0) & (fold[idx][slot] == 0.0) for slot in range(4)]
        for idx in range(4)
    ]
    strategy = [softmax_four(point[idx]) for idx in range(4)]
    top_one = [range_one * row for row in strategy[0]]
    above_one = inner_sum(inner[0], top_one)
    mid_two = [range_two * row for row in strategy[1]]
    above_two = inner_sum(inner[1], mid_two)
    low_one = [above_one * row for row in strategy[2]]
    last_one = inner_sum(inner[2], low_one)
    end_two = [above_two * row for row in strategy[3]]
    wide_two = jnp.broadcast_to(range_two, above_two.shape)
    units = [
        (0, [wide_two] * 4, 1.0, False),
        (1, mid_two, 1.0, True),
        (2, [above_two] * 4, 1.0, False),
        (3, end_two, 1.0, True),
        (1, [above_one] * 4, -1.0, False),
        (2, low_one, -1.0, True),
        (3, [last_one] * 4, -1.0, False),
    ]
    first_unit = 0 if top_ref is None else 1
    begin = [0] * len(units)
    place = 0
    for unit in range(first_unit, len(units)):
        idx, rows, fold_sign, as_sum = units[unit]
        begin[unit] = place
        for side in range(2):
            lanes = slice(side * wide, side * wide + wide)
            if side == 0:
                scaled = [rows[slot] * show[idx][slot] for slot in range(4)]
            else:
                scaled = [rows[slot] * (fold[idx][slot] * fold_sign) for slot in range(4)]
            if as_sum:
                rounded = [row.astype(jnp.bfloat16).astype(jnp.float32) for row in scaled]
                total = (rounded[0] + rounded[1]) + (rounded[2] + rounded[3])
                high = total.astype(jnp.bfloat16).astype(jnp.float32)
                scaled = [high, total - high]
            for pair in range(0, len(scaled), 2):
                cols[place + pair * 8 : place + pair * 8 + 16, lanes] = jnp.concatenate(
                    scaled[pair : pair + 2], axis=0
                ).astype(jnp.bfloat16)
        place += 16 if as_sum else 32

    def added(rows):
        return (rows[0] + rows[1]) + (rows[2] + rows[3])

    def landed(rows, kept, term):
        return [rows[slot] + jnp.where(kept[slot], term, 0.0) for slot in range(4)]

    total = None
    for start in range(0, wide, 2 * LANES):
        stop = min(start + 2 * LANES, wide)
        pay = jnp.dot(cols[...], block_ref[:, start:stop], preferred_element_type=jnp.float32)

        def paid(unit):
            at = begin[unit]
            return [pay[at + slot * 8 : at + slot * 8 + 8, :] for slot in range(4)]

        def paid_sum(unit):
            at = begin[unit]
            return pay[at : at + 8, :] + pay[at + 8 : at + 16, :]

        def weighed(idx, rows):
            return added([strategy[idx][slot][:, start:stop] * rows[slot] for slot in range(4)])

        value_two_end = paid(6)
        term_two = paid_sum(5) + weighed(3, value_two_end)
        value_two_mid = landed(paid(4), inner[1], term_two)
        value_one_low = landed(paid(2), inner[2], paid_sum(3))
        term_one = paid_sum(1) + weighed(2, value_one_low)
        if top_ref is None:
            value_one_top = landed(paid(0), inner[0], term_one)
        else:
            value_one_top = [
                jnp.where(inner[0][slot], term_one, top_ref[0, slot, :, start:stop])
                for slot in range(4)
            ]
        found = [value_one_top, value_two_mid, value_one_low, value_two_end]
        put(start, stop, found)
        part = squares(found)
        total = part if total is None else total + part
    return total


def squares(found):
    total = None
    for rows in found:
        for row in rows:
            total = row * row if total is None else total + row * row
    return jnp.broadcast_to(jnp.sum(total), (1, LANES))


def scale_columns(rows):
    wide = rows[0][0].shape[1]
    show = [
        [level[0][:, wide - 8 + slot : wide - 7 + slot] for slot in range(4)] for level in rows
    ]
    fold = [
        [level[0][:, wide - 4 + slot : wide - 4 + slot + 1] for slot in range(4)] for level in rows
    ]
    return show, fold


def wide_row(store, place, row_ref):
    hands = row_ref.shape[1]
    store[place : place + 1, 0:hands] = row_ref[...]
    return store[place : place + 1, :]


def first_kernel(size, far, shift_ref, home_ref, odd_ref, even_ref, *rest):
    if far:
        far_ref, rest = rest[0], rest[1:]
    one_ref, two_ref, block_ref, chain_ref, value_ref, square_ref = rest[:6]
    from_left, from_right, window, ranges, cols = rest[6:]
    _, tiles, planes, groups, _ = home_ref.shape
    shift = shifts_in(shift_ref)
    spread_messages(lax.axis_index("node"), from_left, from_right, odd_ref, even_ref, size)
    chain = lax.broadcasted_iota(jnp.int32, (groups, LANES), 0)
    places = [(tile, plane) for tile in range(tiles) for plane in range(planes)]
    if far:
        for tile, plane in places:
            window[tile, plane, 16 : 16 + FAR, :] = far_ref[
                tile, plane * FAR : plane * FAR + FAR, :
            ]
    point = [[[] for _ in range(planes)] for _ in range(4)]
    for tile, plane in places:
        top = jnp.where(
            chain < shift[0],
            from_left[tile, plane, 8:16, :],
            behind(home_ref[0, tile, plane], shift[0]),
        )
        mid = jnp.where(
            chain < shift[1],
            from_left[tile, plane, pl.ds(8 + shift[0], 8), :],
            behind(home_ref[1, tile, plane], shift[1]),
        )
        low = jnp.where(
            chain + shift[2] < 8,
            ahead(home_ref[2, tile, plane], shift[2]),
            from_right[tile, plane, pl.ds(shift[2], 8), :],
        )
        end = jnp.where(
            chain + shift[3] < 8,
            ahead(home_ref[3, tile, plane], shift[3]),
            from_right[tile, plane, pl.ds(shift[2] + jnp.minimum(shift[3], 8), 8), :],
        )
        if far:
            far_part = window[tile, plane, pl.ds(shift[3], 8), :]
            end = jnp.where(chain + shift[3] < 16, end, far_part)
        for idx, row in enumerate((top, mid, low, end)):
            point[idx][plane].append(row)
    point = [[jnp.concatenate(rows, axis=1) for rows in level] for level in point]
    for idx in range(4):
        for plane in range(planes):
            chain_ref[idx, plane] = point[idx][plane]
    show, fold = scale_columns(point)
    ranges[...] = jnp.zeros(ranges.shape, jnp.float32)
    range_one = wide_row(ranges, 0, one_ref)
    range_two = wide_row(ranges, 1, two_ref)

    def put(start, stop, found):
        for idx in range(4):
            for slot in range(4):
                value_ref[idx, slot, :, start:stop] = found[idx][slot]

    square_ref[...] = operator_q(
        point, show, fold, range_one, range_two, block_ref, cols, put
    )


def rate_of(parts_ref, entry_count):
    square_sum = jnp.sum(parts_ref[...], axis=0, keepdims=True)[:, 0:1]
    return step_scale / jnp.sqrt(square_sum / entry_count + eps_value)


def second_kernel(entry_count, size, far, shift_ref, chain_ref, value_ref, *rest):
    parts_ref, one_ref, two_ref, block_ref, own_ref, odd_ref, even_ref = rest[:7]
    rest = rest[7:]
    if far:
        far_ref, rest = rest[0], rest[1:]
    square_ref, stage, ranges, cols = rest
    _, tiles, planes, groups, _ = own_ref.shape
    rate = rate_of(parts_ref, entry_count)
    raw = [[chain_ref[idx, plane] for plane in range(3)] for idx in range(4)]
    show, fold = scale_columns(raw)
    point = [
        [
            raw[idx][plane] + rate * (value_ref[idx, plane + 1] - value_ref[idx, 0])
            for plane in range(3)
        ]
        for idx in range(4)
    ]
    ranges[...] = jnp.zeros(ranges.shape, jnp.float32)
    range_one = wide_row(ranges, 0, one_ref)
    range_two = wide_row(ranges, 1, two_ref)

    def put(start, stop, found):
        for idx in range(4):
            for slot in range(4):
                for lane in range(start, stop, LANES):
                    row = found[idx][slot][:, lane - start : lane - start + LANES]
                    own_ref[idx, lane // LANES, slot] = row

    square_ref[...] = operator_q(
        point, show, fold, range_one, range_two, block_ref, cols, put, value_ref
    )
    shift = shifts_in(shift_ref)
    fill_messages(
        lax.axis_index("node"),
        stage,
        (odd_ref, even_ref),
        size,
        own_ref,
        [(0, 8), (1, 8 + shift[0])],
        [(3, shift[2] + jnp.minimum(shift[3], 8)), (2, shift[2])],
    )
    if far:
        for tile in range(tiles):
            for plane in range(planes):
                part = stage.at[0, tile, plane]
                part[pl.ds(jnp.maximum(shift[3] - 8, 0), 8), :] = own_ref[3, tile, plane]
                far_ref[tile, plane * FAR : plane * FAR + FAR, :] = part[8 : 8 + FAR, :]


def last_kernel(entry_count, size, far, shift_ref, own_ref, even_ref, odd_ref, *rest):
    far_ref, rest = (rest[0], rest[1:]) if far else (None, rest)
    parts_ref, logits_hbm, new_hbm, half_hbm, from_left, from_right, lined = rest[:7]
    logits_ref, new_ref, half_ref, sems = rest[7:]
    levels, tiles, planes, groups, _ = own_ref.shape
    hands = logits_ref.shape[-1]
    fetches = [
        pltpu.make_async_copy(logits_hbm.at[0, idx], logits_ref.at[idx], sems.at[0, idx])
        for idx in range(levels)
    ]
    for fetch in fetches:
        fetch.start()
    shift = shifts_in(shift_ref)
    rate = rate_of(parts_ref, entry_count)
    group = lax.broadcasted_iota(jnp.int32, (groups, LANES), 0)
    spread_messages(lax.axis_index("node"), from_left, from_right, odd_ref, even_ref, size)
    places = [(tile, plane) for tile in range(tiles) for plane in range(planes)]

    def top(tile, plane, own):
        return jnp.where(
            group + shift[0] < 8,
            ahead(own, shift[0]),
            from_right[tile, plane, pl.ds(shift[0], 8), :],
        )

    def mid(tile, plane, own):
        return jnp.where(
            group + shift[1] < 8,
            ahead(own, shift[1]),
            from_right[tile, plane, pl.ds(shift[0] + shift[1], 8), :],
        )

    def low(tile, plane, own):
        return jnp.where(
            group < shift[2], from_left[tile, plane, 8:16, :], behind(own, shift[2])
        )

    def end(tile, plane, own):
        row = jnp.where(
            group < shift[3],
            from_left[tile, plane, pl.ds(8 + shift[2] - jnp.maximum(shift[3] - 8, 0), 8), :],
            behind(own, shift[3]),
        )
        if far:
            far_part = far_ref[tile, plane * FAR : plane * FAR + 8, :]
            row = jnp.where(group < shift[3] - 8, far_part, row)
        return row

    leaving = []

    def leave(source, target, kind, idx):
        leaving.append(pltpu.make_async_copy(source.at[idx], target.at[0, idx], sems.at[kind, idx]))
        leaving[-1].start()

    for idx, found in enumerate((top, mid, low, end)):
        for tile, plane in places:
            row = found(tile, plane, own_ref[idx, tile, plane])
            lined[idx, tile, pl.ds(plane, groups, stride=4), :] = row
        fetches[idx].wait()
        for tile in range(tiles):
            start = tile * LANES
            stop = min(start + LANES, hands)
            value = lined[idx, tile][:, 0 : stop - start]
            half_ref[idx, :, start:stop] = value
            new_ref[idx, :, start:stop] = logits_ref[idx, :, start:stop] + rate * value
        leave(half_ref, half_hbm, 1, idx)
        leave(new_ref, new_hbm, 2, idx)
    for copy in leaving:
        copy.wait()


def shared_parts(part):
    count = lax.axis_size("node") * lax.axis_size("board")
    spread = jnp.broadcast_to(part, (count, LANES))
    return lax.all_to_all(spread, ("node", "board"), 0, 0, tiled=True)


def step_of_class(
    size,
    far,
    home,
    shift,
    logits,
    pot_size,
    node_type,
    parent_slot,
    range_one,
    range_two,
    hand_rank,
    live_mask,
):
    _, levels, slots, hands = logits.shape
    wide = padded(hands)
    tiles = wide // LANES
    groups = slots // 4
    entry_count = float(logits.size * lax.axis_size("node") * lax.axis_size("board"))
    vmem = pl.BlockSpec(memory_space=pltpu.VMEM)
    f32 = jnp.float32

    def limit(mebi):
        return pltpu.CompilerParams(vmem_limit_bytes=mebi * MEBI)

    def stage(planes, rows=32):
        return pltpu.VMEM((tiles, planes, rows, LANES), f32)

    def two_stages(planes):
        return pltpu.VMEM((2, tiles, planes, 32, LANES), f32)

    anywhere = pl.BlockSpec(memory_space=pl.ANY)
    sent = pl.pallas_call(
        functools.partial(pack_kernel, size, far),
        out_shape=message_shapes(3, wide, size, far),
        in_specs=[vmem, vmem] + [anywhere] * 3,
        scratch_shapes=[two_stages(3)],
        compiler_params=limit(8),
        name="pack",
    )(shift, home, pot_size, node_type, parent_slot)
    got = sent_on(sent[0], sent[1], sent[2:], -2, (0, 1))
    blocks = payoff_blocks(hand_rank, live_mask)
    rows = 4 * slots + 3 * 16

    def work(count):
        return [
            pltpu.VMEM((8, wide), f32),
            pltpu.VMEM((count, 2 * wide), jnp.bfloat16),
        ]

    def cost(count):
        return pl.CostEstimate(
            flops=4 * count * wide * wide, bytes_accessed=6 * wide * wide, transcendentals=0
        )

    square_shape = jax.ShapeDtypeStruct((1, LANES), f32)
    chain, value, part = pl.pallas_call(
        functools.partial(first_kernel, size, far),
        out_shape=(
            jax.ShapeDtypeStruct((levels, 3, groups, wide), f32),
            jax.ShapeDtypeStruct((levels, 4, groups, wide), f32),
            square_shape,
        ),
        in_specs=[vmem] * (5 + len(got)),
        scratch_shapes=[stage(3), stage(3), stage(3)] + work(rows),
        compiler_params=limit(32),
        cost_estimate=cost(rows),
        name="first",
    )(shift, home, *got, range_one, range_two, blocks)
    parts = shared_parts(part)
    own, *sent, part = pl.pallas_call(
        functools.partial(second_kernel, entry_count, size, far),
        out_shape=[jax.ShapeDtypeStruct((levels, tiles, 4, groups, LANES), f32)]
        + message_shapes(4, wide, size, far)
        + [square_shape],
        in_specs=[vmem] * 7,
        scratch_shapes=[two_stages(4)] + work(rows - slots),
        compiler_params=limit(32),
        cost_estimate=cost(rows - slots),
        name="second",
    )(shift, chain, value, parts, range_one, range_two, blocks)
    got = sent_on(sent[0], sent[1], sent[2:], 2, (1, 0))
    parts = shared_parts(part)
    out_shape = jax.ShapeDtypeStruct(logits.shape, f32)
    level_shape = (levels, slots, hands)
    return pl.pallas_call(
        functools.partial(last_kernel, entry_count, size, far),
        out_shape=(out_shape, out_shape),
        in_specs=[vmem] * (3 + len(got)) + [anywhere],
        out_specs=(anywhere, anywhere),
        scratch_shapes=[
            stage(4),
            stage(4),
            pltpu.VMEM((levels, tiles, slots, LANES), f32),
            pltpu.VMEM(level_shape, f32),
            pltpu.VMEM(level_shape, f32),
            pltpu.VMEM(level_shape, f32),
            pltpu.SemaphoreType.DMA((3, levels)),
        ],
        compiler_params=limit(24),
        name="last",
    )(shift, own, got[1], got[0], *got[2:], parts, logits)


def per_device(
    logits, pot_size, node_type, parent_slot, range_one, range_two, hand_rank, live_mask
):
    branches = [
        functools.partial(step_of_class, size, size == CLASSES[-1]) for size in CLASSES
    ]
    home, shift, found = prepared(logits, pot_size, node_type, parent_slot)
    return lax.switch(
        found[0, 0],
        branches,
        home,
        shift,
        logits,
        pot_size,
        node_type,
        parent_slot,
        range_one,
        range_two,
        hand_rank,
        live_mask,
    )


def solution(mesh):
    return jax.shard_map(
        per_device,
        mesh=mesh,
        in_specs=(
            P("board", None, "node", None),
            P(None, "node"),
            P(None, "node"),
            P(None, "node"),
            P("board", None),
            P("board", None),
            P("board", None),
            P("board", None),
        ),
        out_specs=(P("board", None, "node", None), P("board", None, "node", None)),
        check_vma=False,
    )
```

```python
import functools

import jax
import jax.numpy as jnp
import numpy as np
from jax import lax
from jax.experimental import pallas as pl
from jax.experimental.pallas import tpu as pltpu
from jax.sharding import PartitionSpec as P

LANES = 128
CARDS = 52
step_scale = 0.5
eps_value = 1e-06
MEBI = 1 << 20
CLASSES = (8, 10, 12, 14)
FAR = 5


def padded(count):
    return -(-count // LANES) * LANES


def card_rows(hand_count, wide):
    pairs = [(low, high) for low in range(CARDS) for high in range(low + 1, CARDS)]
    rows = np.full((2, wide), -1, np.int32)
    rows[:, :hand_count] = np.array(pairs[:hand_count], np.int32).T
    return rows


def payoff_kernel(hands, cards_ref, rank_ref, live_ref, out_ref, flat, left, right):
    wide = out_ref.shape[1]
    flat[...] = jnp.zeros(flat.shape, jnp.float32)
    flat[0:1, 0:hands] = rank_ref[...].astype(jnp.float32)
    flat[1:2, 0:hands] = (live_ref[...] > 0).astype(jnp.float32)
    dead = 1.0 - flat[1:2, :]
    feature = lax.broadcasted_iota(jnp.int32, (LANES, wide), 0)
    hit = (feature == cards_ref[0:1, :]) | (feature == cards_ref[1:2, :])
    base = jnp.where(hit, 1.0, 0.0)
    left[...] = jnp.where(feature == CARDS, dead, jnp.where(feature == CARDS + 1, 1.0, base))
    right[...] = jnp.where(
        feature == CARDS, 1.0, jnp.where(feature == CARDS + 1, dead, base)
    ).astype(jnp.bfloat16)
    rank_row = flat[0:1, :]
    for block in range(wide // LANES):
        part = slice(block * LANES, (block + 1) * LANES)
        left_block = left[:, part].T.astype(jnp.bfloat16)
        rank_col = jnp.broadcast_to(flat[0:1, part], (LANES, LANES)).T[:, 0:1]
        hits = jnp.dot(left_block, right[...], preferred_element_type=jnp.float32)
        compat = jnp.where(hits == 0.0, 1.0, 0.0)
        order = jnp.clip(rank_row - rank_col, -1.0, 1.0)
        out_ref[part, :] = (order * compat).astype(jnp.bfloat16)
        out_ref[wide + block * LANES : wide + (block + 1) * LANES, :] = compat.astype(jnp.bfloat16)


def payoff_blocks(hand_rank, live_mask):
    hands = hand_rank.shape[-1]
    wide = padded(hands)
    return pl.pallas_call(
        functools.partial(payoff_kernel, hands),
        out_shape=jax.ShapeDtypeStruct((2 * wide, wide), jnp.bfloat16),
        scratch_shapes=[
            pltpu.VMEM((8, wide), jnp.float32),
            pltpu.VMEM((LANES, wide), jnp.float32),
            pltpu.VMEM((LANES, wide), jnp.bfloat16),
        ],
        compiler_params=pltpu.CompilerParams(vmem_limit_bytes=20 * MEBI),
        cost_estimate=pl.CostEstimate(
            flops=2 * wide * wide * LANES, bytes_accessed=4 * wide * wide, transcendentals=0
        ),
        name="payoff",
    )(jnp.asarray(card_rows(hands, wide)), hand_rank, live_mask)


def row_count(planes, groups):
    return -(-planes * groups // 8) * 8


def plan_of(parent_ref, node_count, groups):
    total = groups * node_count
    first = lax.axis_index("node") * groups
    off = [lax.rem(first - (parent_ref[idx, 0] >> 2) + total, total) for idx in (1, 2, 3)]
    one = off[0]
    two = one + off[1]
    three = two + off[2]
    low = jnp.maximum(one, three - groups)
    high = jnp.minimum(two, groups)
    middle = jnp.minimum(jnp.maximum((one + two + three + 2) >> 2, low), high)
    return middle, middle - one, two - middle, three - middle


def class_of(shift, groups):
    near = jnp.where(shift[3] > groups, 2 * groups - shift[3], shift[3])
    need = jnp.maximum(shift[0] + shift[1], shift[2] + near)
    found = jnp.int32(0)
    for size in CLASSES[:-1]:
        found = found + (need > size).astype(jnp.int32)
    return jnp.where(shift[3] > groups, len(CLASSES) - 1, found)


def fill_messages(
    node, stage, message_refs, size, block_ref, to_left, to_right, skipped=None
):
    _, tiles, planes = stage.shape[:3]
    even = lax.rem(node, 2) == 0
    places = [(tile, plane) for tile in range(tiles) for plane in range(planes)]
    for side, on_left in enumerate((even, jnp.logical_not(even))):
        for near, far in zip(to_left, to_right):
            level = jnp.where(on_left, near[0], far[0])
            start = jnp.where(on_left, near[1], far[1])
            for tile, plane in places:
                block = block_ref[level, tile, plane]
                if skipped is not None:
                    block = ahead(block, jnp.where(level == 3, skipped, 0))
                stage[side, tile, plane, pl.ds(start, 8), :] = block
    for side, message_ref in enumerate(message_refs):
        for tile, plane in places:
            message_ref[tile, plane * size : plane * size + size, :] = stage[
                side, tile, plane, 8 : 8 + size, :
            ]


def prepare_kernel(
    node_count,
    parent_hbm,
    logits_hbm,
    pot_hbm,
    kind_hbm,
    home_ref,
    shift_ref,
    class_ref,
    parent_ref,
    logits_ref,
    pot_ref,
    kind_ref,
    raw,
    flat,
    turned,
    sems,
):
    levels, tiles, planes, groups, _ = home_ref.shape
    slots = 4 * groups
    hands = logits_ref.shape[-1]
    fetches = [
        pltpu.make_async_copy(logits_hbm.at[0, idx], logits_ref.at[idx], sems.at[idx])
        for idx in range(levels)
    ]
    tables = [
        pltpu.make_async_copy(source, target, sems.at[levels + idx])
        for idx, (source, target) in enumerate(
            ((parent_hbm, parent_ref), (pot_hbm, pot_ref), (kind_hbm, kind_ref))
        )
    ]
    for fetch in tables + fetches:
        fetch.start()
    for fetch in tables:
        fetch.wait()
    shift = plan_of(parent_ref, node_count, groups)
    row_id = lax.broadcasted_iota(jnp.int32, shift_ref.shape, 0)
    spread = jnp.zeros(shift_ref.shape, jnp.int32)
    class_ref[...] = jnp.full((1, 1), class_of(shift, groups))
    for idx, value in enumerate(shift):
        spread = jnp.where(row_id == idx, value, spread)
    shift_ref[...] = spread
    pot = pot_ref[...]
    kind = kind_ref[...]
    level = lax.broadcasted_iota(jnp.int32, pot.shape, 0)
    sign = jnp.where(level % 2 == 0, -1.0, 1.0)
    flat[...] = jnp.zeros(flat.shape, jnp.float32)
    flat[0:levels, 0:slots] = jnp.where(kind == 2, pot, 0.0)
    flat[levels : 2 * levels, 0:slots] = jnp.where(kind == 1, pot, 0.0) * sign
    turned[...] = flat[...].T
    lane = lax.broadcasted_iota(jnp.int32, (groups, LANES), 1)
    for idx in range(levels):
        raw[idx, tiles - 1] = jnp.zeros((slots, LANES), jnp.float32)
    for idx in range(levels):
        fetches[idx].wait()
        for tile in range(tiles):
            start = tile * LANES
            stop = min(start + LANES, hands)
            raw[idx, tile, :, 0 : stop - start] = logits_ref[idx, :, start:stop]
            first = raw[idx, tile, pl.ds(0, groups, stride=4), :]
            for plane in range(planes):
                row = raw[idx, tile, pl.ds(plane + 1, groups, stride=4), :] - first
                if tile == tiles - 1 and plane == 0:
                    for slot in range(4):
                        scale = turned[pl.ds(slot, groups, stride=4), :]
                        row = jnp.where(lane == LANES - 8 + slot, scale[:, idx : idx + 1], row)
                        fold = scale[:, levels + idx : levels + idx + 1]
                        row = jnp.where(lane == LANES - 4 + slot, fold, row)
                home_ref[idx, tile, plane] = row


def prepared(logits, pot_size, node_type, parent_slot):
    _, levels, slots, hands = logits.shape
    groups = slots // 4
    tiles = padded(hands) // LANES
    vmem = pl.BlockSpec(memory_space=pltpu.VMEM)
    return pl.pallas_call(
        functools.partial(prepare_kernel, lax.axis_size("node")),
        out_shape=(
            jax.ShapeDtypeStruct((levels, tiles, 3, groups, LANES), jnp.float32),
            jax.ShapeDtypeStruct((8, LANES), jnp.int32),
            jax.ShapeDtypeStruct((1, 1), jnp.int32),
        ),
        in_specs=[pl.BlockSpec(memory_space=pl.ANY)] * 4,
        out_specs=(vmem, vmem, vmem),
        scratch_shapes=[
            pltpu.SMEM(parent_slot.shape, jnp.int32),
            pltpu.VMEM((levels, slots, hands), jnp.float32),
            pltpu.VMEM(pot_size.shape, jnp.float32),
            pltpu.VMEM(node_type.shape, jnp.int32),
            pltpu.VMEM((levels, tiles, slots, LANES), jnp.float32),
            pltpu.VMEM((LANES, LANES), jnp.float32),
            pltpu.VMEM((LANES, LANES), jnp.float32),
            pltpu.SemaphoreType.DMA((levels + 3,)),
        ],
        compiler_params=pltpu.CompilerParams(vmem_limit_bytes=10 * MEBI),
        name="prepare",
    )(parent_slot, logits, pot_size, node_type)


def ahead(rows, count):
    return pltpu.roll(rows, (8 - count) & 7, 0)


def behind(rows, count):
    return pltpu.roll(rows, count & 7, 0)


def shifts_in(shift_ref):
    return [jnp.max(shift_ref[idx : idx + 1, :]) for idx in range(4)]


def pack_kernel(size, far, shift_ref, home_ref, _pot, _kind, _parent, odd_ref, even_ref, *rest):
    far_ref = rest[0] if far else None
    stage = rest[-1]
    _, tiles, planes, groups, _ = home_ref.shape
    shift = shifts_in(shift_ref)
    skipped = jnp.maximum(shift[3] - 8, 0) if far else None
    fill_messages(
        lax.axis_index("node"),
        stage,
        (odd_ref, even_ref),
        size,
        home_ref,
        [(2, 8), (3, 8 + shift[2])],
        [(1, shift[0] + shift[1]), (0, shift[0])],
        skipped,
    )
    if far:
        for tile in range(tiles):
            for plane in range(planes):
                far_ref[tile, plane * FAR : plane * FAR + FAR, :] = home_ref[3, tile, plane, 0:FAR, :]


def message_shapes(planes, wide, size, far):
    tiles = wide // LANES
    message = jax.ShapeDtypeStruct((tiles, row_count(planes, size), LANES), jnp.float32)
    shapes = [message] * 2
    if far:
        shapes.append(jax.ShapeDtypeStruct((tiles, row_count(planes, FAR), LANES), jnp.float32))
    return shapes


def sent_on(odd, even, far, far_steps, order):
    count = lax.axis_size("node")
    edges = [(src, (src + 1) % count) for src in range(count)]
    got = [None, None]
    for side in order:
        pairs = [pair for edge in edges[1 - side :: 2] for pair in (edge, edge[::-1])]
        got[side] = lax.ppermute((odd, even)[side], "node", pairs)
    for message in far:
        pairs = [(src, (src + far_steps) % count) for src in range(count)]
        got.append(lax.ppermute(message, "node", pairs))
    return got


def spread_messages(node, from_left, from_right, odd_ref, even_ref, size):
    tiles, planes = from_left.shape[:2]
    even = lax.rem(node, 2) == 0
    for tile in range(tiles):
        for plane in range(planes):
            place = slice(plane * size, plane * size + size)
            odd_part = odd_ref[tile, place, :]
            even_part = even_ref[tile, place, :]
            from_left[tile, plane, 8 : 8 + size, :] = jnp.where(even, odd_part, even_part)
            from_right[tile, plane, 8 : 8 + size, :] = jnp.where(even, even_part, odd_part)


def inner_sum(inner, rows):
    total = jnp.where(inner[0], rows[0], 0.0)
    for idx in range(1, 4):
        total = total + jnp.where(inner[idx], rows[idx], 0.0)
    return total


def softmax_four(rows):
    top = jnp.maximum(jnp.maximum(rows[0], rows[1]), jnp.maximum(rows[2], 0.0))
    lifted = [jnp.exp(-top)] + [jnp.exp(row - top) for row in rows]
    total = (lifted[0] + lifted[1]) + (lifted[2] + lifted[3])
    return [row / total for row in lifted]


def operator_q(point, show, fold, range_one, range_two, block_ref, cols, put, top_ref=None):
    wide = block_ref.shape[1]
    inner = [
        [(show[idx][slot] == 0.0) & (fold[idx][slot] == 0.0) for slot in range(4)]
        for idx in range(4)
    ]
    strategy = [softmax_four(point[idx]) for idx in range(4)]
    top_one = [range_one * row for row in strategy[0]]
    above_one = inner_sum(inner[0], top_one)
    mid_two = [range_two * row for row in strategy[1]]
    above_two = inner_sum(inner[1], mid_two)
    low_one = [above_one * row for row in strategy[2]]
    last_one = inner_sum(inner[2], low_one)
    end_two = [above_two * row for row in strategy[3]]
    wide_two = jnp.broadcast_to(range_two, above_two.shape)
    units = [
        (0, [wide_two] * 4, 1.0, False),
        (1, mid_two, 1.0, True),
        (2, [above_two] * 4, 1.0, False),
        (3, end_two, 1.0, True),
        (1, [above_one] * 4, -1.0, False),
        (2, low_one, -1.0, True),
        (3, [last_one] * 4, -1.0, False),
    ]
    first_unit = 0 if top_ref is None else 1
    begin = [0] * len(units)
    place = 0
    for unit in range(first_unit, len(units)):
        idx, rows, fold_sign, as_sum = units[unit]
        begin[unit] = place
        for side in range(2):
            lanes = slice(side * wide, side * wide + wide)
            if side == 0:
                scaled = [rows[slot] * show[idx][slot] for slot in range(4)]
            else:
                scaled = [rows[slot] * (fold[idx][slot] * fold_sign) for slot in range(4)]
            if as_sum:
                rounded = [row.astype(jnp.bfloat16).astype(jnp.float32) for row in scaled]
                total = (rounded[0] + rounded[1]) + (rounded[2] + rounded[3])
                high = total.astype(jnp.bfloat16).astype(jnp.float32)
                scaled = [high, total - high]
            for pair in range(0, len(scaled), 2):
                cols[place + pair * 8 : place + pair * 8 + 16, lanes] = jnp.concatenate(
                    scaled[pair : pair + 2], axis=0
                ).astype(jnp.bfloat16)
        place += 16 if as_sum else 32

    def added(rows):
        return (rows[0] + rows[1]) + (rows[2] + rows[3])

    def landed(rows, kept, term):
        return [rows[slot] + jnp.where(kept[slot], term, 0.0) for slot in range(4)]

    total = None
    for start in range(0, wide, 2 * LANES):
        stop = min(start + 2 * LANES, wide)
        pay = jnp.dot(cols[...], block_ref[:, start:stop], preferred_element_type=jnp.float32)

        def paid(unit):
            at = begin[unit]
            return [pay[at + slot * 8 : at + slot * 8 + 8, :] for slot in range(4)]

        def paid_sum(unit):
            at = begin[unit]
            return pay[at : at + 8, :] + pay[at + 8 : at + 16, :]

        def weighed(idx, rows):
            return added([strategy[idx][slot][:, start:stop] * rows[slot] for slot in range(4)])

        value_two_end = paid(6)
        term_two = paid_sum(5) + weighed(3, value_two_end)
        value_two_mid = landed(paid(4), inner[1], term_two)
        value_one_low = landed(paid(2), inner[2], paid_sum(3))
        term_one = paid_sum(1) + weighed(2, value_one_low)
        if top_ref is None:
            value_one_top = landed(paid(0), inner[0], term_one)
        else:
            value_one_top = [
                jnp.where(inner[0][slot], term_one, top_ref[0, slot, :, start:stop])
                for slot in range(4)
            ]
        found = [value_one_top, value_two_mid, value_one_low, value_two_end]
        put(start, stop, found)
        part = squares(found)
        total = part if total is None else total + part
    return total


def squares(found):
    total = None
    for rows in found:
        for row in rows:
            total = row * row if total is None else total + row * row
    return jnp.broadcast_to(jnp.sum(total), (1, LANES))


def scale_columns(rows):
    wide = rows[0][0].shape[1]
    show = [
        [level[0][:, wide - 8 + slot : wide - 7 + slot] for slot in range(4)] for level in rows
    ]
    fold = [
        [level[0][:, wide - 4 + slot : wide - 4 + slot + 1] for slot in range(4)] for level in rows
    ]
    return show, fold


def wide_row(store, place, row_ref):
    hands = row_ref.shape[1]
    store[place : place + 1, 0:hands] = row_ref[...]
    return store[place : place + 1, :]


def first_kernel(size, far, shift_ref, home_ref, odd_ref, even_ref, *rest):
    if far:
        far_ref, rest = rest[0], rest[1:]
    one_ref, two_ref, block_ref, chain_ref, value_ref, square_ref = rest[:6]
    from_left, from_right, window, ranges, cols = rest[6:]
    _, tiles, planes, groups, _ = home_ref.shape
    shift = shifts_in(shift_ref)
    spread_messages(lax.axis_index("node"), from_left, from_right, odd_ref, even_ref, size)
    chain = lax.broadcasted_iota(jnp.int32, (groups, LANES), 0)
    places = [(tile, plane) for tile in range(tiles) for plane in range(planes)]
    if far:
        for tile, plane in places:
            window[tile, plane, 16 : 16 + FAR, :] = far_ref[
                tile, plane * FAR : plane * FAR + FAR, :
            ]
    point = [[[] for _ in range(planes)] for _ in range(4)]
    for tile, plane in places:
        top = jnp.where(
            chain < shift[0],
            from_left[tile, plane, 8:16, :],
            behind(home_ref[0, tile, plane], shift[0]),
        )
        mid = jnp.where(
            chain < shift[1],
            from_left[tile, plane, pl.ds(8 + shift[0], 8), :],
            behind(home_ref[1, tile, plane], shift[1]),
        )
        low = jnp.where(
            chain + shift[2] < 8,
            ahead(home_ref[2, tile, plane], shift[2]),
            from_right[tile, plane, pl.ds(shift[2], 8), :],
        )
        end = jnp.where(
            chain + shift[3] < 8,
            ahead(home_ref[3, tile, plane], shift[3]),
            from_right[tile, plane, pl.ds(shift[2] + jnp.minimum(shift[3], 8), 8), :],
        )
        if far:
            far_part = window[tile, plane, pl.ds(shift[3], 8), :]
            end = jnp.where(chain + shift[3] < 16, end, far_part)
        for idx, row in enumerate((top, mid, low, end)):
            point[idx][plane].append(row)
    point = [[jnp.concatenate(rows, axis=1) for rows in level] for level in point]
    for idx in range(4):
        for plane in range(planes):
            chain_ref[idx, plane] = point[idx][plane]
    show, fold = scale_columns(point)
    ranges[...] = jnp.zeros(ranges.shape, jnp.float32)
    range_one = wide_row(ranges, 0, one_ref)
    range_two = wide_row(ranges, 1, two_ref)

    def put(start, stop, found):
        for idx in range(4):
            for slot in range(4):
                value_ref[idx, slot, :, start:stop] = found[idx][slot]

    square_ref[...] = operator_q(
        point, show, fold, range_one, range_two, block_ref, cols, put
    )


def rate_of(parts_ref, entry_count):
    square_sum = jnp.sum(parts_ref[...], axis=0, keepdims=True)[:, 0:1]
    return step_scale / jnp.sqrt(square_sum / entry_count + eps_value)


def second_kernel(entry_count, size, far, shift_ref, chain_ref, value_ref, *rest):
    parts_ref, one_ref, two_ref, block_ref, own_ref, odd_ref, even_ref = rest[:7]
    rest = rest[7:]
    if far:
        far_ref, rest = rest[0], rest[1:]
    square_ref, stage, ranges, cols = rest
    _, tiles, planes, groups, _ = own_ref.shape
    rate = rate_of(parts_ref, entry_count)
    raw = [[chain_ref[idx, plane] for plane in range(3)] for idx in range(4)]
    show, fold = scale_columns(raw)
    point = [
        [
            raw[idx][plane] + rate * (value_ref[idx, plane + 1] - value_ref[idx, 0])
            for plane in range(3)
        ]
        for idx in range(4)
    ]
    ranges[...] = jnp.zeros(ranges.shape, jnp.float32)
    range_one = wide_row(ranges, 0, one_ref)
    range_two = wide_row(ranges, 1, two_ref)

    def put(start, stop, found):
        for idx in range(4):
            for slot in range(4):
                for lane in range(start, stop, LANES):
                    row = found[idx][slot][:, lane - start : lane - start + LANES]
                    own_ref[idx, lane // LANES, slot] = row

    square_ref[...] = operator_q(
        point, show, fold, range_one, range_two, block_ref, cols, put, value_ref
    )
    shift = shifts_in(shift_ref)
    fill_messages(
        lax.axis_index("node"),
        stage,
        (odd_ref, even_ref),
        size,
        own_ref,
        [(0, 8), (1, 8 + shift[0])],
        [(3, shift[2] + jnp.minimum(shift[3], 8)), (2, shift[2])],
    )
    if far:
        for tile in range(tiles):
            for plane in range(planes):
                part = stage.at[0, tile, plane]
                part[pl.ds(jnp.maximum(shift[3] - 8, 0), 8), :] = own_ref[3, tile, plane]
                far_ref[tile, plane * FAR : plane * FAR + FAR, :] = part[8 : 8 + FAR, :]


def last_kernel(entry_count, size, far, shift_ref, own_ref, even_ref, odd_ref, *rest):
    far_ref, rest = (rest[0], rest[1:]) if far else (None, rest)
    parts_ref, logits_hbm, new_hbm, half_hbm, from_left, from_right, lined = rest[:7]
    logits_ref, new_ref, half_ref, sems = rest[7:]
    levels, tiles, planes, groups, _ = own_ref.shape
    hands = logits_ref.shape[-1]
    fetches = [
        pltpu.make_async_copy(logits_hbm.at[0, idx], logits_ref.at[idx], sems.at[0, idx])
        for idx in range(levels)
    ]
    for fetch in fetches:
        fetch.start()
    shift = shifts_in(shift_ref)
    rate = rate_of(parts_ref, entry_count)
    group = lax.broadcasted_iota(jnp.int32, (groups, LANES), 0)
    spread_messages(lax.axis_index("node"), from_left, from_right, odd_ref, even_ref, size)
    places = [(tile, plane) for tile in range(tiles) for plane in range(planes)]

    def top(tile, plane, own):
        return jnp.where(
            group + shift[0] < 8,
            ahead(own, shift[0]),
            from_right[tile, plane, pl.ds(shift[0], 8), :],
        )

    def mid(tile, plane, own):
        return jnp.where(
            group + shift[1] < 8,
            ahead(own, shift[1]),
            from_right[tile, plane, pl.ds(shift[0] + shift[1], 8), :],
        )

    def low(tile, plane, own):
        return jnp.where(
            group < shift[2], from_left[tile, plane, 8:16, :], behind(own, shift[2])
        )

    def end(tile, plane, own):
        row = jnp.where(
            group < shift[3],
            from_left[tile, plane, pl.ds(8 + shift[2] - jnp.maximum(shift[3] - 8, 0), 8), :],
            behind(own, shift[3]),
        )
        if far:
            far_part = far_ref[tile, plane * FAR : plane * FAR + 8, :]
            row = jnp.where(group < shift[3] - 8, far_part, row)
        return row

    leaving = []

    def leave(source, target, kind, idx):
        leaving.append(pltpu.make_async_copy(source.at[idx], target.at[0, idx], sems.at[kind, idx]))
        leaving[-1].start()

    for idx, found in enumerate((top, mid, low, end)):
        for tile, plane in places:
            row = found(tile, plane, own_ref[idx, tile, plane])
            lined[idx, tile, pl.ds(plane, groups, stride=4), :] = row
        fetches[idx].wait()
        for tile in range(tiles):
            start = tile * LANES
            stop = min(start + LANES, hands)
            value = lined[idx, tile][:, 0 : stop - start]
            half_ref[idx, :, start:stop] = value
            new_ref[idx, :, start:stop] = logits_ref[idx, :, start:stop] + rate * value
        leave(half_ref, half_hbm, 1, idx)
        leave(new_ref, new_hbm, 2, idx)
    for copy in leaving:
        copy.wait()


def shared_parts(part):
    count = lax.axis_size("node") * lax.axis_size("board")
    spread = jnp.broadcast_to(part, (count, LANES))
    return lax.all_to_all(spread, ("node", "board"), 0, 0, tiled=True)


def shared_parts_over_nodes(part):
    nodes = lax.axis_size("node")
    boards = lax.axis_size("board")
    total = part
    for turn in range(1, boards):
        pairs = [(board, (board + turn) % boards) for board in range(boards)]
        total = total + lax.ppermute(part, "board", pairs)
    spread = jnp.broadcast_to(total, (nodes, LANES))
    order = [list(range(nodes))[::-1]]
    return lax.all_to_all(spread, "node", 0, 0, axis_index_groups=order, tiled=True)


def step_of_class(
    size,
    far,
    home,
    shift,
    logits,
    pot_size,
    node_type,
    parent_slot,
    range_one,
    range_two,
    hand_rank,
    live_mask,
):
    _, levels, slots, hands = logits.shape
    wide = padded(hands)
    tiles = wide // LANES
    groups = slots // 4
    entry_count = float(logits.size * lax.axis_size("node") * lax.axis_size("board"))
    vmem = pl.BlockSpec(memory_space=pltpu.VMEM)
    f32 = jnp.float32

    def limit(mebi):
        return pltpu.CompilerParams(vmem_limit_bytes=mebi * MEBI)

    def stage(planes, rows=32):
        return pltpu.VMEM((tiles, planes, rows, LANES), f32)

    def two_stages(planes):
        return pltpu.VMEM((2, tiles, planes, 32, LANES), f32)

    anywhere = pl.BlockSpec(memory_space=pl.ANY)
    sent = pl.pallas_call(
        functools.partial(pack_kernel, size, far),
        out_shape=message_shapes(3, wide, size, far),
        in_specs=[vmem, vmem] + [anywhere] * 3,
        scratch_shapes=[two_stages(3)],
        compiler_params=limit(8),
        name="pack",
    )(shift, home, pot_size, node_type, parent_slot)
    got = sent_on(sent[0], sent[1], sent[2:], -2, (0, 1))
    blocks = payoff_blocks(hand_rank, live_mask)
    rows = 4 * slots + 3 * 16

    def work(count):
        return [
            pltpu.VMEM((8, wide), f32),
            pltpu.VMEM((count, 2 * wide), jnp.bfloat16),
        ]

    def cost(count):
        return pl.CostEstimate(
            flops=4 * count * wide * wide, bytes_accessed=6 * wide * wide, transcendentals=0
        )

    square_shape = jax.ShapeDtypeStruct((1, LANES), f32)
    chain, value, part = pl.pallas_call(
        functools.partial(first_kernel, size, far),
        out_shape=(
            jax.ShapeDtypeStruct((levels, 3, groups, wide), f32),
            jax.ShapeDtypeStruct((levels, 4, groups, wide), f32),
            square_shape,
        ),
        in_specs=[vmem] * (5 + len(got)),
        scratch_shapes=[stage(3), stage(3), stage(3)] + work(rows),
        compiler_params=limit(32),
        cost_estimate=cost(rows),
        name="first",
    )(shift, home, *got, range_one, range_two, blocks)
    parts = shared_parts(part)
    own, *sent, part = pl.pallas_call(
        functools.partial(second_kernel, entry_count, size, far),
        out_shape=[jax.ShapeDtypeStruct((levels, tiles, 4, groups, LANES), f32)]
        + message_shapes(4, wide, size, far)
        + [square_shape],
        in_specs=[vmem] * 7,
        scratch_shapes=[two_stages(4)] + work(rows - slots),
        compiler_params=limit(32),
        cost_estimate=cost(rows - slots),
        name="second",
    )(shift, chain, value, parts, range_one, range_two, blocks)
    got = sent_on(sent[0], sent[1], sent[2:], 2, (1, 0))
    parts = shared_parts_over_nodes(part)
    out_shape = jax.ShapeDtypeStruct(logits.shape, f32)
    level_shape = (levels, slots, hands)
    return pl.pallas_call(
        functools.partial(last_kernel, entry_count, size, far),
        out_shape=(out_shape, out_shape),
        in_specs=[vmem] * (3 + len(got)) + [anywhere],
        out_specs=(anywhere, anywhere),
        scratch_shapes=[
            stage(4),
            stage(4),
            pltpu.VMEM((levels, tiles, slots, LANES), f32),
            pltpu.VMEM(level_shape, f32),
            pltpu.VMEM(level_shape, f32),
            pltpu.VMEM(level_shape, f32),
            pltpu.SemaphoreType.DMA((3, levels)),
        ],
        compiler_params=limit(24),
        name="last",
    )(shift, own, got[1], got[0], *got[2:], parts, logits)


def per_device(
    logits, pot_size, node_type, parent_slot, range_one, range_two, hand_rank, live_mask
):
    branches = [
        functools.partial(step_of_class, size, size == CLASSES[-1]) for size in CLASSES
    ]
    home, shift, found = prepared(logits, pot_size, node_type, parent_slot)
    return lax.switch(
        found[0, 0],
        branches,
        home,
        shift,
        logits,
        pot_size,
        node_type,
        parent_slot,
        range_one,
        range_two,
        hand_rank,
        live_mask,
    )


def solution(mesh):
    return jax.shard_map(
        per_device,
        mesh=mesh,
        in_specs=(
            P("board", None, "node", None),
            P(None, "node"),
            P(None, "node"),
            P(None, "node"),
            P("board", None),
            P("board", None),
            P("board", None),
            P("board", None),
        ),
        out_specs=(P("board", None, "node", None), P("board", None, "node", None)),
        check_vma=False,
    )
```

```python
import functools

import jax
import jax.numpy as jnp
import numpy as np
from jax import lax
from jax.experimental import pallas as pl
from jax.experimental.pallas import tpu as pltpu
from jax.sharding import PartitionSpec as P

LANES = 128
CARDS = 52
step_scale = 0.5
eps_value = 1e-06
MEBI = 1 << 20
CLASSES = (16, 24, 32, 48)
FAR = 5


def padded(count):
    return -(-count // LANES) * LANES


def card_rows(hand_count, wide):
    pairs = [(low, high) for low in range(CARDS) for high in range(low + 1, CARDS)]
    rows = np.full((2, wide), -1, np.int32)
    rows[:, :hand_count] = np.array(pairs[:hand_count], np.int32).T
    return rows


def payoff_kernel(
    hands,
    cards_ref,
    rank_ref,
    live_ref,
    two_ref,
    home_ref,
    head_ref,
    out_ref,
    pay_ref,
    top_ref,
    flat,
    left,
    right,
    cols,
):
    wide = out_ref.shape[1]
    _, tiles, planes, groups, _ = home_ref.shape
    for tile in range(tiles):
        for plane in range(planes):
            place = slice(plane * groups, plane * groups + groups)
            top_ref[tile, place, :] = home_ref[0, tile, plane]
    flat[...] = jnp.zeros(flat.shape, jnp.float32)
    flat[0:1, 0:hands] = rank_ref[...].astype(jnp.float32)
    flat[1:2, 0:hands] = (live_ref[...] > 0).astype(jnp.float32)
    dead = 1.0 - flat[1:2, :]
    feature = lax.broadcasted_iota(jnp.int32, (LANES, wide), 0)
    hit = (feature == cards_ref[0:1, :]) | (feature == cards_ref[1:2, :])
    base = jnp.where(hit, 1.0, 0.0)
    left[...] = jnp.where(feature == CARDS, dead, jnp.where(feature == CARDS + 1, 1.0, base))
    right[...] = jnp.where(
        feature == CARDS, 1.0, jnp.where(feature == CARDS + 1, dead, base)
    ).astype(jnp.bfloat16)
    rank_row = flat[0:1, :]

    @pl.loop(0, wide // LANES)
    def _(block):
        begin = pl.multiple_of(block * LANES, LANES)
        part = pl.ds(begin, LANES)
        left_block = left[:, part].T.astype(jnp.bfloat16)
        rank_col = jnp.broadcast_to(flat[0:1, part], (LANES, LANES)).T[:, 0:1]
        hits = jnp.dot(left_block, right[...], preferred_element_type=jnp.float32)
        compat = jnp.where(hits == 0.0, 1.0, 0.0)
        order = jnp.clip(rank_row - rank_col, -1.0, 1.0)
        out_ref[part, :] = (order * compat).astype(jnp.bfloat16)
        out_ref[pl.ds(begin + wide, LANES), :] = compat.astype(jnp.bfloat16)

    range_two = wide_row(flat, 2, two_ref)
    scale = head_ref[tiles - 1][:, LANES - 8 : LANES]
    for side in range(2):
        rows = [range_two * scale[:, 4 * side + slot : 4 * side + slot + 1] for slot in range(4)]
        cols[:, side * wide : side * wide + wide] = jnp.concatenate(rows, axis=0).astype(
            jnp.bfloat16
        )
    for start in range(0, wide, 2 * LANES):
        stop = min(start + 2 * LANES, wide)
        paid = jnp.dot(cols[...], out_ref[:, start:stop], preferred_element_type=jnp.float32)
        for slot in range(4):
            pay_ref[slot, :, start:stop] = paid[slot * groups : slot * groups + groups, :]


def payoff_blocks(hand_rank, live_mask, range_two, home, head):
    hands = hand_rank.shape[-1]
    wide = padded(hands)
    _, tiles, planes, groups, _ = home.shape
    return pl.pallas_call(
        functools.partial(payoff_kernel, hands),
        out_shape=(
            jax.ShapeDtypeStruct((2 * wide, wide), jnp.bfloat16),
            jax.ShapeDtypeStruct((4, groups, wide), jnp.float32),
            jax.ShapeDtypeStruct((tiles, planes * groups, LANES), jnp.float32),
        ),
        scratch_shapes=[
            pltpu.VMEM((8, wide), jnp.float32),
            pltpu.VMEM((LANES, wide), jnp.float32),
            pltpu.VMEM((LANES, wide), jnp.bfloat16),
            pltpu.VMEM((4 * groups, 2 * wide), jnp.bfloat16),
        ],
        compiler_params=pltpu.CompilerParams(vmem_limit_bytes=20 * MEBI),
        cost_estimate=pl.CostEstimate(
            flops=2 * wide * wide * LANES, bytes_accessed=4 * wide * wide, transcendentals=0
        ),
        name="payoff",
    )(jnp.asarray(card_rows(hands, wide)), hand_rank, live_mask, range_two, home, head)


def row_count(planes, groups):
    return -(-planes * groups // 8) * 8


def rows_out(rows):
    return row_count(1, max(4 * (rows // 3), rows + min(8, rows // 4)))


def plan_of(parent_ref, node_count, groups):
    total = groups * node_count
    first = lax.axis_index("node") * groups
    off = [lax.rem(first - (parent_ref[idx, 0] >> 2) + total, total) for idx in (1, 2, 3)]
    one = off[0]
    two = one + off[1]
    three = two + off[2]
    low = jnp.maximum(one, three - groups)
    high = jnp.minimum(two, groups)
    middle = jnp.minimum(jnp.maximum((3 * (one + two + three) + 5) // 10, low), high)
    return middle, middle - one, two - middle, three - middle


def class_of(shift, groups):
    near = jnp.where(shift[3] > groups, 2 * groups - shift[3], shift[3])
    need = jnp.maximum(shift[0] + 3 * shift[1], 3 * (shift[2] + near))
    found = jnp.int32(0)
    for size in CLASSES[:-1]:
        found = found + (need > size).astype(jnp.int32)
    return jnp.where(shift[3] > groups, len(CLASSES) - 1, found)


def write_messages(node, message_refs, plain, mixed, size, plain_left):
    tiles, planes = plain.shape[:2]
    rows = message_refs[0].shape[1]
    even = lax.rem(node, 2) == 0
    for side, message_ref in enumerate(message_refs):
        is_plain = even if (side == 0) == plain_left else jnp.logical_not(even)
        for tile in range(tiles):
            for plane in range(planes):
                begin = plane * size
                message_ref[tile, begin : begin + size, :] = jnp.where(
                    is_plain,
                    plain[tile, plane, 8 : 8 + size, :],
                    mixed[tile, 8 + begin : 8 + begin + size, :],
                )
            if planes * size < rows:
                message_ref[tile, planes * size : rows, :] = mixed[tile, 8 + planes * size : 8 + rows, :]


def prepare_kernel(
    node_count,
    parent_hbm,
    logits_hbm,
    pot_hbm,
    kind_hbm,
    one_hbm,
    home_ref,
    head_ref,
    shift_ref,
    class_ref,
    parent_ref,
    logits_ref,
    pot_ref,
    kind_ref,
    one_ref,
    ranges,
    raw,
    flat,
    turned,
    sems,
):
    levels, tiles, planes, groups, _ = home_ref.shape
    slots = 4 * groups
    hands = logits_ref.shape[-1]
    fetches = [
        pltpu.make_async_copy(logits_hbm.at[0, idx], logits_ref.at[idx], sems.at[idx])
        for idx in range(levels)
    ]
    tables = [
        pltpu.make_async_copy(source, target, sems.at[levels + idx])
        for idx, (source, target) in enumerate(
            (
                (parent_hbm, parent_ref),
                (pot_hbm, pot_ref),
                (kind_hbm, kind_ref),
                (one_hbm, one_ref),
            )
        )
    ]
    for fetch in tables + fetches:
        fetch.start()
    for fetch in tables:
        fetch.wait()
    shift = plan_of(parent_ref, node_count, groups)
    row_id = lax.broadcasted_iota(jnp.int32, shift_ref.shape, 0)
    spread = jnp.zeros(shift_ref.shape, jnp.int32)
    class_ref[...] = jnp.full((1, 1), class_of(shift, groups))
    for idx, value in enumerate(shift):
        spread = jnp.where(row_id == idx, value, spread)
    shift_ref[...] = spread
    pot = pot_ref[...]
    kind = kind_ref[...]
    level = lax.broadcasted_iota(jnp.int32, pot.shape, 0)
    sign = jnp.where(level % 2 == 0, -1.0, 1.0)
    flat[...] = jnp.zeros(flat.shape, jnp.float32)
    flat[0:levels, 0:slots] = jnp.where(kind == 2, pot, 0.0)
    flat[levels : 2 * levels, 0:slots] = jnp.where(kind == 1, pot, 0.0) * sign
    turned[...] = flat[...].T
    lane = lax.broadcasted_iota(jnp.int32, (groups, LANES), 1)
    ranges[...] = jnp.zeros(ranges.shape, jnp.float32)
    range_one = wide_row(ranges, 0, one_ref)
    scales = [turned[pl.ds(slot, groups, stride=4), :] for slot in range(4)]
    inner = [
        (scale[:, 0:1] == 0.0) & (scale[:, levels : levels + 1] == 0.0) for scale in scales
    ]
    for idx in range(levels):
        raw[idx, tiles - 1] = jnp.zeros((slots, LANES), jnp.float32)
    for idx in range(levels):
        fetches[idx].wait()
        for tile in range(tiles):
            start = tile * LANES
            stop = min(start + LANES, hands)
            raw[idx, tile, :, 0 : stop - start] = logits_ref[idx, :, start:stop]
            first = raw[idx, tile, pl.ds(0, groups, stride=4), :]
            rows = []
            for plane in range(planes):
                row = raw[idx, tile, pl.ds(plane + 1, groups, stride=4), :] - first
                if tile == tiles - 1 and plane == 0:
                    for slot in range(4):
                        show = scales[slot][:, idx : idx + 1]
                        fold = scales[slot][:, levels + idx : levels + idx + 1]
                        row = jnp.where(lane == LANES - 8 + slot, show, row)
                        row = jnp.where(lane == LANES - 4 + slot, fold, row)
                home_ref[idx, tile, plane] = row
                rows.append(row)
            if idx == 0:
                part = range_one[:, start : start + LANES]
                head = inner_sum(inner, [part * row for row in softmax_four(rows)])
                if tile == tiles - 1:
                    head = jnp.where(lane >= LANES - 8, rows[0], head)
                head_ref[tile] = head


def prepared(logits, pot_size, node_type, parent_slot, range_one):
    _, levels, slots, hands = logits.shape
    groups = slots // 4
    tiles = padded(hands) // LANES
    vmem = pl.BlockSpec(memory_space=pltpu.VMEM)
    return pl.pallas_call(
        functools.partial(prepare_kernel, lax.axis_size("node")),
        out_shape=(
            jax.ShapeDtypeStruct((levels, tiles, 3, groups, LANES), jnp.float32),
            jax.ShapeDtypeStruct((tiles, groups, LANES), jnp.float32),
            jax.ShapeDtypeStruct((8, LANES), jnp.int32),
            jax.ShapeDtypeStruct((1, 1), jnp.int32),
        ),
        in_specs=[pl.BlockSpec(memory_space=pl.ANY)] * 5,
        out_specs=(vmem,) * 4,
        scratch_shapes=[
            pltpu.SMEM(parent_slot.shape, jnp.int32),
            pltpu.VMEM((levels, slots, hands), jnp.float32),
            pltpu.VMEM(pot_size.shape, jnp.float32),
            pltpu.VMEM(node_type.shape, jnp.int32),
            pltpu.VMEM(range_one.shape, jnp.float32),
            pltpu.VMEM((8, padded(hands)), jnp.float32),
            pltpu.VMEM((levels, tiles, slots, LANES), jnp.float32),
            pltpu.VMEM((LANES, LANES), jnp.float32),
            pltpu.VMEM((LANES, LANES), jnp.float32),
            pltpu.SemaphoreType.DMA((levels + 4,)),
        ],
        compiler_params=pltpu.CompilerParams(vmem_limit_bytes=10 * MEBI),
        name="prepare",
    )(parent_slot, logits, pot_size, node_type, range_one)


def ahead(rows, count):
    return pltpu.roll(rows, (8 - count) & 7, 0)


def behind(rows, count):
    return pltpu.roll(rows, count & 7, 0)


def shifts_in(shift_ref):
    return [jnp.max(shift_ref[idx : idx + 1, :]) for idx in range(4)]


def pack_kernel(
    size,
    far,
    shift_ref,
    home_ref,
    head_ref,
    _pot,
    _kind,
    _parent,
    odd_ref,
    even_ref,
    *rest,
):
    far_ref = rest[0] if far else None
    plain, mixed = rest[-2:]
    _, tiles, planes, groups, _ = home_ref.shape
    rows = odd_ref.shape[1]
    shift = shifts_in(shift_ref)
    places = [(tile, plane) for tile in range(tiles) for plane in range(planes)]
    for tile, plane in places:
        plain[tile, plane, 8:16, :] = home_ref[2, tile, plane]
    for plane in range(planes - 1, -1, -1):
        start = rows - (planes - 1 - plane) * shift[1]
        for tile in range(tiles):
            mixed[tile, pl.ds(start, 8), :] = home_ref[1, tile, plane]
    for tile, plane in places:
        block = home_ref[3, tile, plane]
        if far:
            block = ahead(block, jnp.maximum(shift[3] - 8, 0))
        plain[tile, plane, pl.ds(8 + shift[2], 8), :] = block
    for tile in range(tiles):
        mixed[tile, pl.ds(shift[0], 8), :] = head_ref[tile]
    write_messages(lax.axis_index("node"), (odd_ref, even_ref), plain, mixed, size, True)
    if far:
        for tile in range(tiles):
            for plane in range(planes):
                far_ref[tile, plane * FAR : plane * FAR + FAR, :] = home_ref[3, tile, plane, 0:FAR, :]


def message_shapes(planes, wide, rows, far):
    tiles = wide // LANES
    message = jax.ShapeDtypeStruct((tiles, rows, LANES), jnp.float32)
    shapes = [message] * 2
    if far:
        shapes.append(jax.ShapeDtypeStruct((tiles, row_count(planes, FAR), LANES), jnp.float32))
    return shapes


def sent_on(odd, even, far, far_steps, order):
    count = lax.axis_size("node")
    edges = [(src, (src + 1) % count) for src in range(count)]
    got = [None, None]
    for side in order:
        pairs = [pair for edge in edges[1 - side :: 2] for pair in (edge, edge[::-1])]
        got[side] = lax.ppermute((odd, even)[side], "node", pairs)
    for message in far:
        pairs = [(src, (src + far_steps) % count) for src in range(count)]
        got.append(lax.ppermute(message, "node", pairs))
    return got


def spread_messages(node, plain, mixed, odd_ref, even_ref, size, mixed_from_left):
    tiles, planes = plain.shape[:2]
    rows = odd_ref.shape[1]
    even = lax.rem(node, 2) == 0
    odd_is_mixed = even if mixed_from_left else jnp.logical_not(even)
    for tile in range(tiles):
        mixed[tile, 8 : 8 + rows, :] = jnp.where(odd_is_mixed, odd_ref[tile], even_ref[tile])
        for plane in range(planes):
            place = slice(plane * size, plane * size + size)
            plain[tile, plane, 8 : 8 + size, :] = jnp.where(
                odd_is_mixed, even_ref[tile, place, :], odd_ref[tile, place, :]
            )


def inner_sum(inner, rows):
    total = jnp.where(inner[0], rows[0], 0.0)
    for idx in range(1, 4):
        total = total + jnp.where(inner[idx], rows[idx], 0.0)
    return total


def softmax_four(rows):
    top = jnp.maximum(jnp.maximum(rows[0], rows[1]), jnp.maximum(rows[2], 0.0))
    lifted = [jnp.exp(-top)] + [jnp.exp(row - top) for row in rows]
    total = (lifted[0] + lifted[1]) + (lifted[2] + lifted[3])
    return [row / total for row in lifted]


def operator_q(point, show, fold, range_one, range_two, block_ref, cols, put, top_ref=None):
    wide = block_ref.shape[1]
    inner = [
        [(show[idx][slot] == 0.0) & (fold[idx][slot] == 0.0) for slot in range(4)]
        for idx in range(4)
    ]
    if isinstance(point[0], list):
        top_one = [range_one * row for row in softmax_four(point[0])]
        above_one = inner_sum(inner[0], top_one)
    else:
        above_one = point[0]
    strategy = [None] + [softmax_four(point[idx]) for idx in range(1, 4)]
    mid_two = [range_two * row for row in strategy[1]]
    above_two = inner_sum(inner[1], mid_two)
    low_one = [above_one * row for row in strategy[2]]
    last_one = inner_sum(inner[2], low_one)
    end_two = [above_two * row for row in strategy[3]]
    wide_two = jnp.broadcast_to(range_two, above_two.shape)
    units = [
        (0, [wide_two] * 4, 1.0, False),
        (1, mid_two, 1.0, True),
        (2, [above_two] * 4, 1.0, False),
        (3, end_two, 1.0, True),
        (1, [above_one] * 4, -1.0, False),
        (2, low_one, -1.0, True),
        (3, [last_one] * 4, -1.0, False),
    ]
    first_unit = 0 if top_ref is None else 1
    begin = [0] * len(units)
    place = 0
    for unit in range(first_unit, len(units)):
        idx, rows, fold_sign, as_sum = units[unit]
        begin[unit] = place
        for side in range(2):
            lanes = slice(side * wide, side * wide + wide)
            if side == 0:
                scaled = [rows[slot] * show[idx][slot] for slot in range(4)]
            else:
                scaled = [rows[slot] * (fold[idx][slot] * fold_sign) for slot in range(4)]
            if as_sum:
                rounded = [row.astype(jnp.bfloat16).astype(jnp.float32) for row in scaled]
                total = (rounded[0] + rounded[1]) + (rounded[2] + rounded[3])
                high = total.astype(jnp.bfloat16).astype(jnp.float32)
                scaled = [high, total - high]
            for pair in range(0, len(scaled), 2):
                cols[place + pair * 8 : place + pair * 8 + 16, lanes] = jnp.concatenate(
                    scaled[pair : pair + 2], axis=0
                ).astype(jnp.bfloat16)
        place += 16 if as_sum else 32

    def added(rows):
        return (rows[0] + rows[1]) + (rows[2] + rows[3])

    def landed(rows, kept, term):
        return [rows[slot] + jnp.where(kept[slot], term, 0.0) for slot in range(4)]

    total = None
    for start in range(0, wide, 2 * LANES):
        stop = min(start + 2 * LANES, wide)
        pay = jnp.dot(cols[...], block_ref[:, start:stop], preferred_element_type=jnp.float32)

        def paid(unit):
            at = begin[unit]
            return [pay[at + slot * 8 : at + slot * 8 + 8, :] for slot in range(4)]

        def paid_sum(unit):
            at = begin[unit]
            return pay[at : at + 8, :] + pay[at + 8 : at + 16, :]

        def weighed(idx, rows):
            return added([strategy[idx][slot][:, start:stop] * rows[slot] for slot in range(4)])

        value_two_end = paid(6)
        term_two = paid_sum(5) + weighed(3, value_two_end)
        value_two_mid = landed(paid(4), inner[1], term_two)
        value_one_low = landed(paid(2), inner[2], paid_sum(3))
        term_one = paid_sum(1) + weighed(2, value_one_low)
        if top_ref is None:
            value_one_top = landed(paid(0), inner[0], term_one)
        else:
            value_one_top = [
                jnp.where(inner[0][slot], term_one, top_ref[0, slot, :, start:stop])
                for slot in range(4)
            ]
        found = [value_one_top, value_two_mid, value_one_low, value_two_end]
        put(start, stop, found, term_one)
        part = squares(found)
        total = part if total is None else total + part
    return total


def squares(found):
    total = None
    for rows in found:
        for row in rows:
            total = row * row if total is None else total + row * row
    return jnp.broadcast_to(jnp.sum(total), (1, LANES))


def scale_columns(rows):
    wide = rows[0].shape[1]
    show = [[row[:, wide - 8 + slot : wide - 7 + slot] for slot in range(4)] for row in rows]
    fold = [[row[:, wide - 4 + slot : wide - 4 + slot + 1] for slot in range(4)] for row in rows]
    return show, fold


def wide_row(store, place, row_ref):
    hands = row_ref.shape[1]
    store[place : place + 1, 0:hands] = row_ref[...]
    return store[place : place + 1, :]


def first_kernel(size, far, shift_ref, home_ref, head_ref, odd_ref, even_ref, *rest):
    if far:
        far_ref, rest = rest[0], rest[1:]
    one_ref, two_ref, block_ref, chain_ref, value_ref, square_ref = rest[:6]
    plain, mixed, window, ranges, cols = rest[6:]
    _, tiles, planes, groups, _ = home_ref.shape
    rows = odd_ref.shape[1]
    shift = shifts_in(shift_ref)
    spread_messages(lax.axis_index("node"), plain, mixed, odd_ref, even_ref, size, True)
    chain = lax.broadcasted_iota(jnp.int32, (groups, LANES), 0)
    places = [(tile, plane) for tile in range(tiles) for plane in range(planes)]
    if far:
        for tile, plane in places:
            window[tile, plane, 16 : 16 + FAR, :] = far_ref[
                tile, plane * FAR : plane * FAR + FAR, :
            ]
    head = [
        jnp.where(chain < shift[0], mixed[tile, 8:16, :], behind(head_ref[tile], shift[0]))
        for tile in range(tiles)
    ]
    point = [[[] for _ in range(planes)] for _ in range(3)]
    for tile, plane in places:
        mid = jnp.where(
            chain < shift[1],
            mixed[tile, pl.ds(8 + rows - (planes - plane) * shift[1], 8), :],
            behind(home_ref[1, tile, plane], shift[1]),
        )
        low = jnp.where(
            chain + shift[2] < 8,
            ahead(home_ref[2, tile, plane], shift[2]),
            plain[tile, plane, pl.ds(shift[2], 8), :],
        )
        end = jnp.where(
            chain + shift[3] < 8,
            ahead(home_ref[3, tile, plane], shift[3]),
            plain[tile, plane, pl.ds(shift[2] + jnp.minimum(shift[3], 8), 8), :],
        )
        if far:
            far_part = window[tile, plane, pl.ds(shift[3], 8), :]
            end = jnp.where(chain + shift[3] < 16, end, far_part)
        for idx, row in enumerate((mid, low, end)):
            point[idx][plane].append(row)
    point = [[jnp.concatenate(rows, axis=1) for rows in level] for level in point]
    head = jnp.concatenate(head, axis=1)
    for idx in range(3):
        for plane in range(planes):
            chain_ref[idx, plane] = point[idx][plane]
    show, fold = scale_columns([head] + [level[0] for level in point])
    ranges[...] = jnp.zeros(ranges.shape, jnp.float32)
    range_one = wide_row(ranges, 0, one_ref)
    range_two = wide_row(ranges, 1, two_ref)

    def put(start, stop, found, term):
        for idx in range(4):
            for slot in range(4):
                value_ref[idx, slot, :, start:stop] = found[idx][slot]

    square_ref[...] = operator_q(
        [head] + point, show, fold, range_one, range_two, block_ref, cols, put
    )


def rate_of(parts_ref, entry_count):
    square_sum = jnp.sum(parts_ref[...], axis=0, keepdims=True)[:, 0:1]
    return step_scale / jnp.sqrt(square_sum / entry_count + eps_value)


def second_kernel(size, far, entry_count, shift_ref, home_ref, top_ref, chain_ref, *rest):
    value_ref, parts_ref, one_ref, two_ref, block_ref, own_ref, term_ref = rest[:7]
    odd_ref, even_ref, rest = rest[7], rest[8], rest[9:]
    if far:
        far_ref, rest = rest[0], rest[1:]
    square_ref, plain, mixed, ranges, cols = rest
    _, tiles, planes, groups, _ = own_ref.shape
    rows = odd_ref.shape[1]
    shift = shifts_in(shift_ref)
    group = lax.broadcasted_iota(jnp.int32, (groups, LANES), 0)
    rate = rate_of(parts_ref, entry_count)
    raw = [[] for _ in range(3)]
    for plane in range(3):
        for tile in range(tiles):
            from_left = top_ref[tile, plane * groups : plane * groups + groups, :]
            row = jnp.where(group + shift[0] >= 8, from_left, home_ref[0, tile, plane])
            raw[plane].append(behind(row, shift[0]))
    raw = [[jnp.concatenate(parts, axis=1) for parts in raw]]
    raw += [[chain_ref[idx, plane] for plane in range(3)] for idx in range(3)]
    show, fold = scale_columns([level[0] for level in raw])
    point = [
        [
            raw[idx][plane] + rate * (value_ref[idx, plane + 1] - value_ref[idx, 0])
            for plane in range(3)
        ]
        for idx in range(4)
    ]
    ranges[...] = jnp.zeros(ranges.shape, jnp.float32)
    range_one = wide_row(ranges, 0, one_ref)
    range_two = wide_row(ranges, 1, two_ref)

    def put(start, stop, found, term):
        for lane in range(start, stop, LANES):
            part = slice(lane - start, lane - start + LANES)
            term_ref[lane // LANES] = term[:, part]
            for idx in range(3):
                for slot in range(4):
                    own_ref[idx, lane // LANES, slot] = found[idx + 1][slot][:, part]

    square_ref[...] = operator_q(
        point, show, fold, range_one, range_two, block_ref, cols, put, value_ref
    )
    places = [(tile, plane) for tile in range(tiles) for plane in range(planes)]
    for tile in range(tiles):
        mixed[tile, 8:16, :] = term_ref[tile]
    for tile, plane in places:
        start = shift[2] + jnp.minimum(shift[3], 8)
        plain[tile, plane, pl.ds(start, 8), :] = own_ref[2, tile, plane]
    for plane in range(planes):
        start = 8 + rows - (planes - plane) * shift[1]
        for tile in range(tiles):
            mixed[tile, pl.ds(start, 8), :] = own_ref[0, tile, plane]
    for tile, plane in places:
        plain[tile, plane, pl.ds(shift[2], 8), :] = own_ref[1, tile, plane]
    write_messages(lax.axis_index("node"), (odd_ref, even_ref), plain, mixed, size, False)
    if far:
        for tile, plane in places:
            part = plain.at[tile, plane]
            part[pl.ds(jnp.maximum(shift[3] - 8, 0), 8), :] = own_ref[2, tile, plane]
            far_ref[tile, plane * FAR : plane * FAR + FAR, :] = part[8 : 8 + FAR, :]


def last_kernel(size, far, entry_count, shift_ref, head_ref, pay_ref, own_ref, term_ref, *rest):
    even_ref, odd_ref, rest = rest[0], rest[1], rest[2:]
    far_ref, rest = (rest[0], rest[1:]) if far else (None, rest)
    parts_ref, logits_hbm, new_hbm, half_hbm, plain, mixed, lined = rest[:7]
    logits_ref, new_ref, half_ref, sems = rest[7:]
    _, tiles, planes, groups, _ = own_ref.shape
    levels, _, hands = logits_ref.shape
    rows = odd_ref.shape[1]
    fetches = [
        pltpu.make_async_copy(logits_hbm.at[0, idx], logits_ref.at[idx], sems.at[0, idx])
        for idx in range(levels)
    ]
    for fetch in fetches:
        fetch.start()
    shift = shifts_in(shift_ref)
    rate = rate_of(parts_ref, entry_count)
    group = lax.broadcasted_iota(jnp.int32, (groups, LANES), 0)
    spread_messages(lax.axis_index("node"), plain, mixed, odd_ref, even_ref, size, False)
    scale = head_ref[tiles - 1][:, LANES - 8 : LANES]
    inner = [
        (scale[:, slot : slot + 1] == 0.0) & (scale[:, slot + 4 : slot + 5] == 0.0)
        for slot in range(4)
    ]

    def top(tile):
        term = jnp.where(
            group + shift[0] < 8,
            ahead(term_ref[tile], shift[0]),
            mixed[tile, pl.ds(shift[0], 8), :],
        )
        lanes = slice(tile * LANES, tile * LANES + LANES)
        return [jnp.where(inner[slot], term, pay_ref[slot, :, lanes]) for slot in range(4)]

    def mid(tile):
        return [
            jnp.where(
                group + shift[1] < 8,
                ahead(own_ref[0, tile, plane], shift[1]),
                mixed[tile, pl.ds(rows - (planes - 1 - plane) * shift[1], 8), :],
            )
            for plane in range(planes)
        ]

    def low(tile):
        return [
            jnp.where(
                group < shift[2],
                plain[tile, plane, 8:16, :],
                behind(own_ref[1, tile, plane], shift[2]),
            )
            for plane in range(planes)
        ]

    def end(tile):
        start = 8 + shift[2] - jnp.maximum(shift[3] - 8, 0)
        found = [
            jnp.where(
                group < shift[3],
                plain[tile, plane, pl.ds(start, 8), :],
                behind(own_ref[2, tile, plane], shift[3]),
            )
            for plane in range(planes)
        ]
        if far:
            found = [
                jnp.where(
                    group < shift[3] - 8, far_ref[tile, plane * FAR : plane * FAR + 8, :], row
                )
                for plane, row in enumerate(found)
            ]
        return found

    leaving = []

    def leave(source, target, kind, idx):
        leaving.append(pltpu.make_async_copy(source.at[idx], target.at[0, idx], sems.at[kind, idx]))
        leaving[-1].start()

    for idx, found in enumerate((top, mid, low, end)):
        for tile in range(tiles):
            for slot, row in enumerate(found(tile)):
                lined[idx, tile, pl.ds(slot, groups, stride=4), :] = row
        fetches[idx].wait()
        for tile in range(tiles):
            start = tile * LANES
            stop = min(start + LANES, hands)
            value = lined[idx, tile][:, 0 : stop - start]
            half_ref[idx, :, start:stop] = value
            new_ref[idx, :, start:stop] = logits_ref[idx, :, start:stop] + rate * value
        leave(half_ref, half_hbm, 1, idx)
        leave(new_ref, new_hbm, 2, idx)
    for copy in leaving:
        copy.wait()


def shared_parts(part):
    count = lax.axis_size("node") * lax.axis_size("board")
    spread = jnp.broadcast_to(part, (count, LANES))
    return lax.all_to_all(spread, ("node", "board"), 0, 0, tiled=True)


def shared_parts_over_nodes(part):
    nodes = lax.axis_size("node")
    boards = lax.axis_size("board")
    total = part
    for turn in range(1, boards):
        pairs = [(board, (board + turn) % boards) for board in range(boards)]
        total = total + lax.ppermute(part, "board", pairs)
    spread = jnp.broadcast_to(total, (nodes, LANES))
    order = [list(range(nodes))[::-1]]
    return lax.all_to_all(spread, "node", 0, 0, axis_index_groups=order, tiled=True)


def step_of_class(
    rows_in,
    far,
    home,
    head,
    shift,
    logits,
    pot_size,
    node_type,
    parent_slot,
    range_one,
    range_two,
    hand_rank,
    live_mask,
):
    _, levels, slots, hands = logits.shape
    wide = padded(hands)
    tiles = wide // LANES
    groups = slots // 4
    entry_count = float(logits.size * lax.axis_size("node") * lax.axis_size("board"))
    vmem = pl.BlockSpec(memory_space=pltpu.VMEM)
    f32 = jnp.float32

    def limit(mebi):
        return pltpu.CompilerParams(vmem_limit_bytes=mebi * MEBI)

    def stage(planes, rows=32):
        return pltpu.VMEM((tiles, planes, rows, LANES), f32)

    def long_stage(rows):
        return pltpu.VMEM((tiles, rows + 24, LANES), f32)

    size = rows_in // 3
    out_rows = rows_out(rows_in)
    out_size = out_rows // 4
    anywhere = pl.BlockSpec(memory_space=pl.ANY)
    sent = pl.pallas_call(
        functools.partial(pack_kernel, size, far),
        out_shape=message_shapes(3, wide, rows_in, far),
        in_specs=[vmem] * 3 + [anywhere] * 3,
        scratch_shapes=[stage(3), long_stage(rows_in)],
        compiler_params=limit(8),
        name="pack",
    )(shift, home, head, pot_size, node_type, parent_slot)
    got = sent_on(sent[0], sent[1], sent[2:], -2, (0, 1))
    blocks, top_pay, top = payoff_blocks(hand_rank, live_mask, range_two, home, head)
    count = lax.axis_size("node")
    top = lax.ppermute(top, "node", [(src, (src + 1) % count) for src in range(count)])
    rows = 4 * slots + 3 * 16

    def work(count):
        return [
            pltpu.VMEM((8, wide), f32),
            pltpu.VMEM((count, 2 * wide), jnp.bfloat16),
        ]

    def cost(count):
        return pl.CostEstimate(
            flops=4 * count * wide * wide, bytes_accessed=6 * wide * wide, transcendentals=0
        )

    square_shape = jax.ShapeDtypeStruct((1, LANES), f32)
    chain, value, part = pl.pallas_call(
        functools.partial(first_kernel, size, far),
        out_shape=(
            jax.ShapeDtypeStruct((levels - 1, 3, groups, wide), f32),
            jax.ShapeDtypeStruct((levels, 4, groups, wide), f32),
            square_shape,
        ),
        in_specs=[vmem] * (6 + len(got)),
        scratch_shapes=[stage(3), long_stage(rows_in), stage(3)] + work(rows),
        compiler_params=limit(32),
        cost_estimate=cost(rows),
        name="first",
    )(shift, home, head, *got, range_one, range_two, blocks)
    parts = shared_parts(part)
    own, term, *sent, part = pl.pallas_call(
        functools.partial(second_kernel, out_size, far, entry_count),
        out_shape=[
            jax.ShapeDtypeStruct((levels - 1, tiles, 4, groups, LANES), f32),
            jax.ShapeDtypeStruct((tiles, groups, LANES), f32),
        ]
        + message_shapes(4, wide, out_rows, far)
        + [square_shape],
        in_specs=[vmem] * 9,
        scratch_shapes=[stage(4), long_stage(out_rows)] + work(rows - slots),
        compiler_params=limit(32),
        cost_estimate=cost(rows - slots),
        name="second",
    )(shift, home, top, chain, value, parts, range_one, range_two, blocks)
    got = sent_on(sent[0], sent[1], sent[2:], 2, (1, 0))
    parts = shared_parts_over_nodes(part)
    out_shape = jax.ShapeDtypeStruct(logits.shape, f32)
    level_shape = (levels, slots, hands)
    return pl.pallas_call(
        functools.partial(last_kernel, out_size, far, entry_count),
        out_shape=(out_shape, out_shape),
        in_specs=[vmem] * (6 + len(got)) + [anywhere],
        out_specs=(anywhere, anywhere),
        scratch_shapes=[
            stage(4),
            long_stage(out_rows),
            pltpu.VMEM((levels, tiles, slots, LANES), f32),
            pltpu.VMEM(level_shape, f32),
            pltpu.VMEM(level_shape, f32),
            pltpu.VMEM(level_shape, f32),
            pltpu.SemaphoreType.DMA((3, levels)),
        ],
        compiler_params=limit(24),
        name="last",
    )(shift, head, top_pay, own, term, got[1], got[0], *got[2:], parts, logits)


def per_device(
    logits, pot_size, node_type, parent_slot, range_one, range_two, hand_rank, live_mask
):
    branches = [
        functools.partial(step_of_class, rows, rows == CLASSES[-1]) for rows in CLASSES
    ]
    home, head, shift, found = prepared(
        logits, pot_size, node_type, parent_slot, range_one
    )
    return lax.switch(
        found[0, 0],
        branches,
        home,
        head,
        shift,
        logits,
        pot_size,
        node_type,
        parent_slot,
        range_one,
        range_two,
        hand_rank,
        live_mask,
    )


def solution(mesh):
    return jax.shard_map(
        per_device,
        mesh=mesh,
        in_specs=(
            P("board", None, "node", None),
            P(None, "node"),
            P(None, "node"),
            P(None, "node"),
            P("board", None),
            P("board", None),
            P("board", None),
            P("board", None),
        ),
        out_specs=(P("board", None, "node", None), P("board", None, "node", None)),
        check_vma=False,
    )
```

```python
import functools

import jax
import jax.numpy as jnp
import numpy as np
from jax import lax
from jax.experimental import pallas as pl
from jax.experimental.pallas import tpu as pltpu
from jax.sharding import PartitionSpec as P

LANES = 128
CARDS = 52
step_scale = 0.5
eps_value = 1e-06
MEBI = 1 << 20
CLASSES = (8, 10, 12, 14)
FAR = 5


def padded(count):
    return -(-count // LANES) * LANES


def card_rows(hand_count, wide):
    pairs = [(low, high) for low in range(CARDS) for high in range(low + 1, CARDS)]
    rows = np.full((2, wide), -1, np.int32)
    rows[:, :hand_count] = np.array(pairs[:hand_count], np.int32).T
    return rows


def payoff_kernel(hands, cards_ref, rank_ref, live_ref, out_ref, flat, left, right):
    wide = out_ref.shape[1]
    flat[...] = jnp.zeros(flat.shape, jnp.float32)
    flat[0:1, 0:hands] = rank_ref[...].astype(jnp.float32)
    flat[1:2, 0:hands] = (live_ref[...] > 0).astype(jnp.float32)
    dead = 1.0 - flat[1:2, :]
    feature = lax.broadcasted_iota(jnp.int32, (LANES, wide), 0)
    hit = (feature == cards_ref[0:1, :]) | (feature == cards_ref[1:2, :])
    base = jnp.where(hit, 1.0, 0.0)
    left[...] = jnp.where(feature == CARDS, dead, jnp.where(feature == CARDS + 1, 1.0, base))
    right[...] = jnp.where(
        feature == CARDS, 1.0, jnp.where(feature == CARDS + 1, dead, base)
    ).astype(jnp.bfloat16)
    rank_row = flat[0:1, :]
    for block in range(wide // LANES):
        part = slice(block * LANES, (block + 1) * LANES)
        left_block = left[:, part].T.astype(jnp.bfloat16)
        rank_col = jnp.broadcast_to(flat[0:1, part], (LANES, LANES)).T[:, 0:1]
        hits = jnp.dot(left_block, right[...], preferred_element_type=jnp.float32)
        compat = jnp.where(hits == 0.0, 1.0, 0.0)
        order = jnp.clip(rank_row - rank_col, -1.0, 1.0)
        out_ref[part, :] = (order * compat).astype(jnp.bfloat16)
        out_ref[wide + block * LANES : wide + (block + 1) * LANES, :] = compat.astype(jnp.bfloat16)


def payoff_blocks(hand_rank, live_mask):
    hands = hand_rank.shape[-1]
    wide = padded(hands)
    return pl.pallas_call(
        functools.partial(payoff_kernel, hands),
        out_shape=jax.ShapeDtypeStruct((2 * wide, wide), jnp.bfloat16),
        scratch_shapes=[
            pltpu.VMEM((8, wide), jnp.float32),
            pltpu.VMEM((LANES, wide), jnp.float32),
            pltpu.VMEM((LANES, wide), jnp.bfloat16),
        ],
        compiler_params=pltpu.CompilerParams(vmem_limit_bytes=20 * MEBI),
        cost_estimate=pl.CostEstimate(
            flops=2 * wide * wide * LANES, bytes_accessed=4 * wide * wide, transcendentals=0
        ),
        name="payoff",
    )(jnp.asarray(card_rows(hands, wide)), hand_rank, live_mask)


def row_count(planes, groups):
    return -(-planes * groups // 8) * 8


def plan_of(parent_ref, node_count, groups):
    total = groups * node_count
    first = lax.axis_index("node") * groups
    off = [lax.rem(first - (parent_ref[idx, 0] >> 2) + total, total) for idx in (1, 2, 3)]
    one = off[0]
    two = one + off[1]
    three = two + off[2]
    low = jnp.maximum(one, three - groups)
    high = jnp.minimum(two, groups)
    middle = jnp.minimum(jnp.maximum((one + two + three + 2) >> 2, low), high)
    return middle, middle - one, two - middle, three - middle


def class_of(shift, groups):
    near = jnp.where(shift[3] > groups, 2 * groups - shift[3], shift[3])
    need = jnp.maximum(shift[0] + shift[1], shift[2] + near)
    found = jnp.int32(0)
    for size in CLASSES[:-1]:
        found = found + (need > size).astype(jnp.int32)
    return jnp.where(shift[3] > groups, len(CLASSES) - 1, found)


def fill_messages(
    node, stage, message_refs, size, block_ref, to_left, to_right, skipped=None
):
    _, tiles, planes = stage.shape[:3]
    even = lax.rem(node, 2) == 0
    places = [(tile, plane) for tile in range(tiles) for plane in range(planes)]
    for side, on_left in enumerate((even, jnp.logical_not(even))):
        for near, far in zip(to_left, to_right):
            level = jnp.where(on_left, near[0], far[0])
            start = jnp.where(on_left, near[1], far[1])
            for tile, plane in places:
                block = block_ref[level, tile, plane]
                if skipped is not None:
                    block = ahead(block, jnp.where(level == 3, skipped, 0))
                stage[side, tile, plane, pl.ds(start, 8), :] = block
    for side, message_ref in enumerate(message_refs):
        for tile, plane in places:
            message_ref[tile, plane * size : plane * size + size, :] = stage[
                side, tile, plane, 8 : 8 + size, :
            ]


def prepare_kernel(
    node_count,
    parent_hbm,
    logits_hbm,
    pot_hbm,
    kind_hbm,
    home_ref,
    shift_ref,
    class_ref,
    parent_ref,
    logits_ref,
    pot_ref,
    kind_ref,
    raw,
    flat,
    turned,
    sems,
):
    levels, tiles, planes, groups, _ = home_ref.shape
    slots = 4 * groups
    hands = logits_ref.shape[-1]
    fetches = [
        pltpu.make_async_copy(logits_hbm.at[0, idx], logits_ref.at[idx], sems.at[idx])
        for idx in range(levels)
    ]
    tables = [
        pltpu.make_async_copy(source, target, sems.at[levels + idx])
        for idx, (source, target) in enumerate(
            ((parent_hbm, parent_ref), (pot_hbm, pot_ref), (kind_hbm, kind_ref))
        )
    ]
    for fetch in tables + fetches:
        fetch.start()
    for fetch in tables[1:]:
        fetch.wait()
    pot = pot_ref[...]
    kind = kind_ref[...]
    level = lax.broadcasted_iota(jnp.int32, pot.shape, 0)
    sign = jnp.where(level % 2 == 0, -1.0, 1.0)
    flat[...] = jnp.zeros(flat.shape, jnp.float32)
    flat[0:levels, 0:slots] = jnp.where(kind == 2, pot, 0.0)
    flat[levels : 2 * levels, 0:slots] = jnp.where(kind == 1, pot, 0.0) * sign
    turned[...] = flat[...].T
    lane = lax.broadcasted_iota(jnp.int32, (groups, LANES), 1)
    for idx in range(levels):
        raw[idx, tiles - 1] = jnp.zeros((slots, LANES), jnp.float32)
    for idx in range(levels):
        fetches[idx].wait()
        for tile in range(tiles):
            start = tile * LANES
            stop = min(start + LANES, hands)
            raw[idx, tile, :, 0 : stop - start] = logits_ref[idx, :, start:stop]
            first = raw[idx, tile, pl.ds(0, groups, stride=4), :]
            for plane in range(planes):
                row = raw[idx, tile, pl.ds(plane + 1, groups, stride=4), :] - first
                if tile == tiles - 1 and plane == 0:
                    for slot in range(4):
                        scale = turned[pl.ds(slot, groups, stride=4), :]
                        row = jnp.where(lane == LANES - 8 + slot, scale[:, idx : idx + 1], row)
                        fold = scale[:, levels + idx : levels + idx + 1]
                        row = jnp.where(lane == LANES - 4 + slot, fold, row)
                home_ref[idx, tile, plane] = row
    tables[0].wait()
    shift = plan_of(parent_ref, node_count, groups)
    row_id = lax.broadcasted_iota(jnp.int32, shift_ref.shape, 0)
    spread = jnp.zeros(shift_ref.shape, jnp.int32)
    class_ref[...] = jnp.full((1, 1), class_of(shift, groups))
    for idx, value in enumerate(shift):
        spread = jnp.where(row_id == idx, value, spread)
    shift_ref[...] = spread


def prepared(logits, pot_size, node_type, parent_slot):
    _, levels, slots, hands = logits.shape
    groups = slots // 4
    tiles = padded(hands) // LANES
    vmem = pl.BlockSpec(memory_space=pltpu.VMEM)
    return pl.pallas_call(
        functools.partial(prepare_kernel, lax.axis_size("node")),
        out_shape=(
            jax.ShapeDtypeStruct((levels, tiles, 3, groups, LANES), jnp.float32),
            jax.ShapeDtypeStruct((8, LANES), jnp.int32),
            jax.ShapeDtypeStruct((1, 1), jnp.int32),
        ),
        in_specs=[pl.BlockSpec(memory_space=pl.ANY)] * 4,
        out_specs=(vmem, vmem, vmem),
        scratch_shapes=[
            pltpu.SMEM(parent_slot.shape, jnp.int32),
            pltpu.VMEM((levels, slots, hands), jnp.float32),
            pltpu.VMEM(pot_size.shape, jnp.float32),
            pltpu.VMEM(node_type.shape, jnp.int32),
            pltpu.VMEM((levels, tiles, slots, LANES), jnp.float32),
            pltpu.VMEM((LANES, LANES), jnp.float32),
            pltpu.VMEM((LANES, LANES), jnp.float32),
            pltpu.SemaphoreType.DMA((levels + 3,)),
        ],
        compiler_params=pltpu.CompilerParams(vmem_limit_bytes=10 * MEBI),
        name="prepare",
    )(parent_slot, logits, pot_size, node_type)


def ahead(rows, count):
    return pltpu.roll(rows, (8 - count) & 7, 0)


def behind(rows, count):
    return pltpu.roll(rows, count & 7, 0)


def shifts_in(shift_ref):
    return [jnp.max(shift_ref[idx : idx + 1, :]) for idx in range(4)]


def pack_kernel(size, far, shift_ref, home_ref, _pot, _kind, _parent, odd_ref, even_ref, *rest):
    far_ref = rest[0] if far else None
    stage = rest[-1]
    _, tiles, planes, groups, _ = home_ref.shape
    shift = shifts_in(shift_ref)
    skipped = jnp.maximum(shift[3] - 8, 0) if far else None
    fill_messages(
        lax.axis_index("node"),
        stage,
        (odd_ref, even_ref),
        size,
        home_ref,
        [(2, 8), (3, 8 + shift[2])],
        [(1, shift[0] + shift[1]), (0, shift[0])],
        skipped,
    )
    if far:
        for tile in range(tiles):
            for plane in range(planes):
                far_ref[tile, plane * FAR : plane * FAR + FAR, :] = home_ref[3, tile, plane, 0:FAR, :]


def message_shapes(planes, wide, size, far):
    tiles = wide // LANES
    message = jax.ShapeDtypeStruct((tiles, row_count(planes, size), LANES), jnp.float32)
    shapes = [message] * 2
    if far:
        shapes.append(jax.ShapeDtypeStruct((tiles, row_count(planes, FAR), LANES), jnp.float32))
    return shapes


def sent_on(odd, even, far, far_steps, order):
    count = lax.axis_size("node")
    edges = [(src, (src + 1) % count) for src in range(count)]
    got = [None, None]
    for side in order:
        pairs = [pair for edge in edges[1 - side :: 2] for pair in (edge, edge[::-1])]
        got[side] = lax.ppermute((odd, even)[side], "node", pairs)
    for message in far:
        pairs = [(src, (src + far_steps) % count) for src in range(count)]
        got.append(lax.ppermute(message, "node", pairs))
    return got


def spread_messages(node, from_left, from_right, odd_ref, even_ref, size):
    tiles, planes = from_left.shape[:2]
    even = lax.rem(node, 2) == 0
    for tile in range(tiles):
        for plane in range(planes):
            place = slice(plane * size, plane * size + size)
            odd_part = odd_ref[tile, place, :]
            even_part = even_ref[tile, place, :]
            from_left[tile, plane, 8 : 8 + size, :] = jnp.where(even, odd_part, even_part)
            from_right[tile, plane, 8 : 8 + size, :] = jnp.where(even, even_part, odd_part)


def inner_sum(inner, rows):
    total = jnp.where(inner[0], rows[0], 0.0)
    for idx in range(1, 4):
        total = total + jnp.where(inner[idx], rows[idx], 0.0)
    return total


def inner_before(inner):
    one = inner[0] | inner[1]
    return [inner[0], one, one | inner[2]]


def softmax_four(rows):
    top = jnp.maximum(jnp.maximum(rows[0], rows[1]), jnp.maximum(rows[2], 0.0))
    lifted = [jnp.exp(-top)] + [jnp.exp(row - top) for row in rows]
    total = (lifted[0] + lifted[1]) + (lifted[2] + lifted[3])
    return [row / total for row in lifted]


def operator_q(point, show, fold, range_one, range_two, block_ref, cols, put, top_ref=None):
    wide = block_ref.shape[1]
    inner = [
        [(show[idx][slot] == 0.0) & (fold[idx][slot] == 0.0) for slot in range(4)]
        for idx in range(4)
    ]
    strategy = [softmax_four(point[idx]) for idx in range(4)]
    top_one = [range_one * row for row in strategy[0]]
    above_one = inner_sum(inner[0], top_one)
    mid_two = [range_two * row for row in strategy[1]]
    above_two = inner_sum(inner[1], mid_two)
    low_one = [above_one * row for row in strategy[2]]
    last_one = inner_sum(inner[2], low_one)
    end_two = [above_two * row for row in strategy[3]]
    wide_two = jnp.broadcast_to(range_two, above_two.shape)
    past = [inner_before(inner[idx]) for idx in range(3)]

    units = [
        (0, [wide_two] * 4, 1.0, False),
        (1, mid_two, 1.0, True),
        (2, [above_two] * 4, 1.0, False),
        (3, end_two, 1.0, True),
        (1, [above_one] * 4, -1.0, False),
        (2, low_one, -1.0, True),
        (3, [last_one] * 4, -1.0, False),
    ]
    first_unit = 0 if top_ref is None else 1
    begin = [0] * len(units)
    for side in range(2):
        blocks = []
        for unit in range(first_unit, len(units)):
            idx, rows, fold_sign, as_sum = units[unit]
            begin[unit] = 8 * len(blocks)
            if side == 0:
                scaled = [rows[slot] * show[idx][slot] for slot in range(4)]
            else:
                scaled = [rows[slot] * (fold[idx][slot] * fold_sign) for slot in range(4)]
            if as_sum:
                rounded = [row.astype(jnp.bfloat16).astype(jnp.float32) for row in scaled]
                total = (rounded[0] + rounded[1]) + (rounded[2] + rounded[3])
                high = total.astype(jnp.bfloat16).astype(jnp.float32)
                scaled = [high, total - high]
            elif idx < 3:
                scaled = [
                    jnp.where(past[idx][slot], scaled[slot + 1], scaled[slot]) for slot in range(3)
                ]
            blocks += scaled
        if len(blocks) % 2:
            blocks.append(jnp.zeros_like(blocks[0]))
        lanes = slice(side * wide, side * wide + wide)
        for pair in range(0, len(blocks), 2):
            cols[pair * 8 : pair * 8 + 16, lanes] = jnp.concatenate(
                blocks[pair : pair + 2], axis=0
            ).astype(jnp.bfloat16)

    def added(rows):
        return (rows[0] + rows[1]) + (rows[2] + rows[3])

    def landed(rows, kept, term):
        return [jnp.where(kept[slot], term, rows[slot]) for slot in range(4)]

    total = None
    for start in range(0, wide, 2 * LANES):
        stop = min(start + 2 * LANES, wide)
        pay = jnp.dot(cols[...], block_ref[:, start:stop], preferred_element_type=jnp.float32)

        def paid(unit):
            at = begin[unit]
            idx = units[unit][0]
            rows = [pay[at + slot * 8 : at + slot * 8 + 8, :] for slot in range(4 if idx == 3 else 3)]
            if idx < 3:
                rows = [
                    rows[0],
                    jnp.where(past[idx][0], rows[0], rows[1]),
                    jnp.where(past[idx][1], rows[1], rows[2]),
                    rows[2],
                ]
            return rows

        def paid_sum(unit):
            at = begin[unit]
            return pay[at : at + 8, :] + pay[at + 8 : at + 16, :]

        def weighed(idx, rows):
            return added([strategy[idx][slot][:, start:stop] * rows[slot] for slot in range(4)])

        value_two_end = paid(6)
        term_two = paid_sum(5) + weighed(3, value_two_end)
        value_two_mid = landed(paid(4), inner[1], term_two)
        value_one_low = landed(paid(2), inner[2], paid_sum(3))
        term_one = paid_sum(1) + weighed(2, value_one_low)
        if top_ref is None:
            value_one_top = landed(paid(0), inner[0], term_one)
        else:
            value_one_top = [
                jnp.where(inner[0][slot], term_one, top_ref[0, slot, :, start:stop])
                for slot in range(4)
            ]
        found = [value_one_top, value_two_mid, value_one_low, value_two_end]
        put(start, stop, found)
        part = squares(found)
        total = part if total is None else total + part
    return total


def squares(found):
    total = None
    for rows in found:
        for row in rows:
            total = row * row if total is None else total + row * row
    return jnp.broadcast_to(jnp.sum(total), (1, LANES))


def scale_columns(rows):
    wide = rows[0][0].shape[1]
    show = [
        [level[0][:, wide - 8 + slot : wide - 7 + slot] for slot in range(4)] for level in rows
    ]
    fold = [
        [level[0][:, wide - 4 + slot : wide - 4 + slot + 1] for slot in range(4)] for level in rows
    ]
    return show, fold


def wide_row(store, place, row_ref):
    hands = row_ref.shape[1]
    store[place : place + 1, 0:hands] = row_ref[...]
    return store[place : place + 1, :]


def first_kernel(size, far, shift_ref, home_ref, odd_ref, even_ref, *rest):
    if far:
        far_ref, rest = rest[0], rest[1:]
    one_ref, two_ref, block_ref, chain_ref, value_ref, square_ref = rest[:6]
    from_left, from_right, window, ranges, cols = rest[6:]
    _, tiles, planes, groups, _ = home_ref.shape
    shift = shifts_in(shift_ref)
    spread_messages(lax.axis_index("node"), from_left, from_right, odd_ref, even_ref, size)
    chain = lax.broadcasted_iota(jnp.int32, (groups, LANES), 0)
    places = [(tile, plane) for tile in range(tiles) for plane in range(planes)]
    if far:
        for tile, plane in places:
            window[tile, plane, 16 : 16 + FAR, :] = far_ref[
                tile, plane * FAR : plane * FAR + FAR, :
            ]
    point = [[[] for _ in range(planes)] for _ in range(4)]
    for tile, plane in places:
        top = jnp.where(
            chain < shift[0],
            from_left[tile, plane, 8:16, :],
            behind(home_ref[0, tile, plane], shift[0]),
        )
        mid = jnp.where(
            chain < shift[1],
            from_left[tile, plane, pl.ds(8 + shift[0], 8), :],
            behind(home_ref[1, tile, plane], shift[1]),
        )
        low = jnp.where(
            chain + shift[2] < 8,
            ahead(home_ref[2, tile, plane], shift[2]),
            from_right[tile, plane, pl.ds(shift[2], 8), :],
        )
        end = jnp.where(
            chain + shift[3] < 8,
            ahead(home_ref[3, tile, plane], shift[3]),
            from_right[tile, plane, pl.ds(shift[2] + jnp.minimum(shift[3], 8), 8), :],
        )
        if far:
            far_part = window[tile, plane, pl.ds(shift[3], 8), :]
            end = jnp.where(chain + shift[3] < 16, end, far_part)
        for idx, row in enumerate((top, mid, low, end)):
            point[idx][plane].append(row)
    point = [[jnp.concatenate(rows, axis=1) for rows in level] for level in point]
    for idx in range(4):
        for plane in range(planes):
            chain_ref[idx, plane] = point[idx][plane]
    show, fold = scale_columns(point)
    ranges[...] = jnp.zeros(ranges.shape, jnp.float32)
    range_one = wide_row(ranges, 0, one_ref)
    range_two = wide_row(ranges, 1, two_ref)

    def put(start, stop, found):
        for idx in range(4):
            for slot in range(4):
                value_ref[idx, slot, :, start:stop] = found[idx][slot]

    square_ref[...] = operator_q(
        point, show, fold, range_one, range_two, block_ref, cols, put
    )


def rate_of(parts_ref, entry_count):
    square_sum = jnp.sum(parts_ref[...], axis=0, keepdims=True)[:, 0:1]
    return step_scale / jnp.sqrt(square_sum / entry_count + eps_value)


def second_kernel(entry_count, size, far, shift_ref, chain_ref, value_ref, *rest):
    parts_ref, one_ref, two_ref, block_ref, own_ref, odd_ref, even_ref = rest[:7]
    rest = rest[7:]
    if far:
        far_ref, rest = rest[0], rest[1:]
    square_ref, stage, ranges, cols = rest
    _, tiles, planes, groups, _ = own_ref.shape
    rate = rate_of(parts_ref, entry_count)
    raw = [[chain_ref[idx, plane] for plane in range(3)] for idx in range(4)]
    show, fold = scale_columns(raw)
    point = [
        [
            raw[idx][plane] + rate * (value_ref[idx, plane + 1] - value_ref[idx, 0])
            for plane in range(3)
        ]
        for idx in range(4)
    ]
    ranges[...] = jnp.zeros(ranges.shape, jnp.float32)
    range_one = wide_row(ranges, 0, one_ref)
    range_two = wide_row(ranges, 1, two_ref)

    def put(start, stop, found):
        for idx in range(4):
            for slot in range(4):
                for lane in range(start, stop, LANES):
                    row = found[idx][slot][:, lane - start : lane - start + LANES]
                    own_ref[idx, lane // LANES, slot] = row

    square_ref[...] = operator_q(
        point, show, fold, range_one, range_two, block_ref, cols, put, value_ref
    )
    shift = shifts_in(shift_ref)
    fill_messages(
        lax.axis_index("node"),
        stage,
        (odd_ref, even_ref),
        size,
        own_ref,
        [(0, 8), (1, 8 + shift[0])],
        [(3, shift[2] + jnp.minimum(shift[3], 8)), (2, shift[2])],
    )
    if far:
        for tile in range(tiles):
            for plane in range(planes):
                part = stage.at[0, tile, plane]
                part[pl.ds(jnp.maximum(shift[3] - 8, 0), 8), :] = own_ref[3, tile, plane]
                far_ref[tile, plane * FAR : plane * FAR + FAR, :] = part[8 : 8 + FAR, :]


def place_kernel(size, far, shift_ref, own_ref, even_ref, odd_ref, *rest):
    far_ref, rest = (rest[0], rest[1:]) if far else (None, rest)
    half_hbm, half_ref, from_left, from_right, lined, sems = rest
    _, tiles, planes, groups, _ = own_ref.shape
    hands = half_ref.shape[-1]
    shift = shifts_in(shift_ref)
    group = lax.broadcasted_iota(jnp.int32, (groups, LANES), 0)
    spread_messages(lax.axis_index("node"), from_left, from_right, odd_ref, even_ref, size)
    places = [(tile, plane) for tile in range(tiles) for plane in range(planes)]

    def top(tile, plane, own):
        return jnp.where(
            group + shift[0] < 8,
            ahead(own, shift[0]),
            from_right[tile, plane, pl.ds(shift[0], 8), :],
        )

    def mid(tile, plane, own):
        return jnp.where(
            group + shift[1] < 8,
            ahead(own, shift[1]),
            from_right[tile, plane, pl.ds(shift[0] + shift[1], 8), :],
        )

    def low(tile, plane, own):
        return jnp.where(
            group < shift[2], from_left[tile, plane, 8:16, :], behind(own, shift[2])
        )

    def end(tile, plane, own):
        row = jnp.where(
            group < shift[3],
            from_left[tile, plane, pl.ds(8 + shift[2] - jnp.maximum(shift[3] - 8, 0), 8), :],
            behind(own, shift[3]),
        )
        if far:
            far_part = far_ref[tile, plane * FAR : plane * FAR + 8, :]
            row = jnp.where(group < shift[3] - 8, far_part, row)
        return row

    leaving = []
    for idx, found in enumerate((top, mid, low, end)):
        for tile, plane in places:
            row = found(tile, plane, own_ref[idx, tile, plane])
            lined[idx, tile, pl.ds(plane, groups, stride=4), :] = row
        for tile in range(tiles):
            start = tile * LANES
            stop = min(start + LANES, hands)
            half_ref[idx, :, start:stop] = lined[idx, tile][:, 0 : stop - start]
        leaving.append(
            pltpu.make_async_copy(half_ref.at[idx], half_hbm.at[0, idx], sems.at[idx])
        )
        leaving[-1].start()
    for copy in leaving:
        copy.wait()


def last_kernel(entry_count, half_ref, parts_ref, logits_ref, new_hbm, new_ref, sems):
    rate = rate_of(parts_ref, entry_count)
    leaving = []
    for idx in range(half_ref.shape[0]):
        new_ref[idx] = logits_ref[0, idx] + rate * half_ref[idx]
        leaving.append(pltpu.make_async_copy(new_ref.at[idx], new_hbm.at[0, idx], sems.at[idx]))
        leaving[-1].start()
    for copy in leaving:
        copy.wait()


def shared_parts(part):
    count = lax.axis_size("node") * lax.axis_size("board")
    spread = jnp.broadcast_to(part, (count, LANES))
    return lax.all_to_all(spread, ("node", "board"), 0, 0, tiled=True)


def shared_parts_over_nodes(part):
    nodes = lax.axis_size("node")
    boards = lax.axis_size("board")
    total = part
    for turn in range(1, boards):
        pairs = [(board, (board + turn) % boards) for board in range(boards)]
        total = total + lax.ppermute(part, "board", pairs)
    spread = jnp.broadcast_to(total, (nodes, LANES))
    order = [list(range(nodes))[::-1]]
    return lax.all_to_all(spread, "node", 0, 0, axis_index_groups=order, tiled=True)


def step_of_class(
    size,
    far,
    home,
    shift,
    logits,
    pot_size,
    node_type,
    parent_slot,
    range_one,
    range_two,
    hand_rank,
    live_mask,
):
    _, levels, slots, hands = logits.shape
    wide = padded(hands)
    tiles = wide // LANES
    groups = slots // 4
    entry_count = float(logits.size * lax.axis_size("node") * lax.axis_size("board"))
    vmem = pl.BlockSpec(memory_space=pltpu.VMEM)
    f32 = jnp.float32

    def limit(mebi):
        return pltpu.CompilerParams(vmem_limit_bytes=mebi * MEBI)

    def stage(planes, rows=32):
        return pltpu.VMEM((tiles, planes, rows, LANES), f32)

    def two_stages(planes):
        return pltpu.VMEM((2, tiles, planes, 32, LANES), f32)

    anywhere = pl.BlockSpec(memory_space=pl.ANY)
    sent = pl.pallas_call(
        functools.partial(pack_kernel, size, far),
        out_shape=message_shapes(3, wide, size, far),
        in_specs=[vmem, vmem] + [anywhere] * 3,
        scratch_shapes=[two_stages(3)],
        compiler_params=limit(8),
        name="pack",
    )(shift, home, pot_size, node_type, parent_slot)
    got = sent_on(sent[0], sent[1], sent[2:], -2, (0, 1))
    blocks = payoff_blocks(hand_rank, live_mask)
    blocks_all = 3 * 3 + 4 + 3 * 2
    rows = 16 * (-(-blocks_all // 2))
    rows_second = 16 * (-(-(blocks_all - 3) // 2))

    def work(count):
        return [
            pltpu.VMEM((8, wide), f32),
            pltpu.VMEM((count, 2 * wide), jnp.bfloat16),
        ]

    def cost(count):
        return pl.CostEstimate(
            flops=4 * count * wide * wide, bytes_accessed=6 * wide * wide, transcendentals=0
        )

    square_shape = jax.ShapeDtypeStruct((1, LANES), f32)
    chain, value, part = pl.pallas_call(
        functools.partial(first_kernel, size, far),
        out_shape=(
            jax.ShapeDtypeStruct((levels, 3, groups, wide), f32),
            jax.ShapeDtypeStruct((levels, 4, groups, wide), f32),
            square_shape,
        ),
        in_specs=[vmem] * (5 + len(got)),
        scratch_shapes=[stage(3), stage(3), stage(3)] + work(rows),
        compiler_params=limit(32),
        cost_estimate=cost(rows),
        name="first",
    )(shift, home, *got, range_one, range_two, blocks)
    parts = shared_parts(part)
    own, *sent, part = pl.pallas_call(
        functools.partial(second_kernel, entry_count, size, far),
        out_shape=[jax.ShapeDtypeStruct((levels, tiles, 4, groups, LANES), f32)]
        + message_shapes(4, wide, size, far)
        + [square_shape],
        in_specs=[vmem] * 7,
        scratch_shapes=[two_stages(4)] + work(rows_second),
        compiler_params=limit(32),
        cost_estimate=cost(rows_second),
        name="second",
    )(shift, chain, value, parts, range_one, range_two, blocks)
    got = sent_on(sent[0], sent[1], sent[2:], 2, (1, 0))
    parts = shared_parts_over_nodes(part)
    out_shape = jax.ShapeDtypeStruct(logits.shape, f32)
    level_shape = (levels, slots, hands)
    half, kept = pl.pallas_call(
        functools.partial(place_kernel, size, far),
        out_shape=(out_shape, jax.ShapeDtypeStruct(level_shape, f32)),
        in_specs=[vmem] * (2 + len(got)),
        out_specs=(anywhere, vmem),
        scratch_shapes=[
            stage(4),
            stage(4),
            pltpu.VMEM((levels, tiles, slots, LANES), f32),
            pltpu.SemaphoreType.DMA((levels,)),
        ],
        compiler_params=limit(12),
        cost_estimate=pl.CostEstimate(
            flops=logits.size, bytes_accessed=16 * logits.size, transcendentals=0
        ),
        name="place",
    )(shift, own, got[1], got[0], *got[2:])
    new = pl.pallas_call(
        functools.partial(last_kernel, entry_count),
        out_shape=out_shape,
        in_specs=[vmem] * 3,
        out_specs=anywhere,
        scratch_shapes=[pltpu.VMEM(level_shape, f32), pltpu.SemaphoreType.DMA((levels,))],
        compiler_params=limit(12),
        name="last",
    )(kept, parts, logits)
    return new, half


def per_device(
    logits, pot_size, node_type, parent_slot, range_one, range_two, hand_rank, live_mask
):
    branches = [
        functools.partial(step_of_class, size, size == CLASSES[-1]) for size in CLASSES
    ]
    home, shift, found = prepared(logits, pot_size, node_type, parent_slot)
    return lax.switch(
        found[0, 0],
        branches,
        home,
        shift,
        logits,
        pot_size,
        node_type,
        parent_slot,
        range_one,
        range_two,
        hand_rank,
        live_mask,
    )


def solution(mesh):
    return jax.shard_map(
        per_device,
        mesh=mesh,
        in_specs=(
            P("board", None, "node", None),
            P(None, "node"),
            P(None, "node"),
            P(None, "node"),
            P("board", None),
            P("board", None),
            P("board", None),
            P("board", None),
        ),
        out_specs=(P("board", None, "node", None), P("board", None, "node", None)),
        check_vma=False,
    )
```

```python
import functools

import jax
import jax.numpy as jnp
import numpy as np
from jax import lax
from jax.experimental import pallas as pl
from jax.experimental.pallas import tpu as pltpu
from jax.sharding import PartitionSpec as P

LANES = 128
CARDS = 52
step_scale = 0.5
eps_value = 1e-06
MEBI = 1 << 20
CLASSES = (8, 10, 12, 14)
FAR = 5


def padded(count):
    return -(-count // LANES) * LANES


def card_rows(hand_count, wide):
    pairs = [(low, high) for low in range(CARDS) for high in range(low + 1, CARDS)]
    rows = np.full((2, wide), -1, np.int32)
    rows[:, :hand_count] = np.array(pairs[:hand_count], np.int32).T
    return rows


def payoff_kernel(hands, cards_ref, rank_ref, live_ref, out_ref, flat, left, right):
    wide = out_ref.shape[1]
    flat[...] = jnp.zeros(flat.shape, jnp.float32)
    flat[0:1, 0:hands] = rank_ref[...].astype(jnp.float32)
    flat[1:2, 0:hands] = (live_ref[...] > 0).astype(jnp.float32)
    dead = 1.0 - flat[1:2, :]
    feature = lax.broadcasted_iota(jnp.int32, (LANES, wide), 0)
    hit = (feature == cards_ref[0:1, :]) | (feature == cards_ref[1:2, :])
    base = jnp.where(hit, 1.0, 0.0)
    left[...] = jnp.where(feature == CARDS, dead, jnp.where(feature == CARDS + 1, 1.0, base))
    right[...] = jnp.where(
        feature == CARDS, 1.0, jnp.where(feature == CARDS + 1, dead, base)
    ).astype(jnp.bfloat16)
    rank_row = flat[0:1, :]
    for block in range(wide // LANES):
        part = slice(block * LANES, (block + 1) * LANES)
        left_block = left[:, part].T.astype(jnp.bfloat16)
        rank_col = jnp.broadcast_to(flat[0:1, part], (LANES, LANES)).T[:, 0:1]
        hits = jnp.dot(left_block, right[...], preferred_element_type=jnp.float32)
        compat = jnp.where(hits == 0.0, 1.0, 0.0)
        order = jnp.clip(rank_row - rank_col, -1.0, 1.0)
        out_ref[part, :] = (order * compat).astype(jnp.bfloat16)
        out_ref[wide + block * LANES : wide + (block + 1) * LANES, :] = compat.astype(jnp.bfloat16)


def payoff_blocks(hand_rank, live_mask):
    hands = hand_rank.shape[-1]
    wide = padded(hands)
    return pl.pallas_call(
        functools.partial(payoff_kernel, hands),
        out_shape=jax.ShapeDtypeStruct((2 * wide, wide), jnp.bfloat16),
        scratch_shapes=[
            pltpu.VMEM((8, wide), jnp.float32),
            pltpu.VMEM((LANES, wide), jnp.float32),
            pltpu.VMEM((LANES, wide), jnp.bfloat16),
        ],
        compiler_params=pltpu.CompilerParams(vmem_limit_bytes=20 * MEBI),
        cost_estimate=pl.CostEstimate(
            flops=2 * wide * wide * LANES, bytes_accessed=4 * wide * wide, transcendentals=0
        ),
        name="payoff",
    )(jnp.asarray(card_rows(hands, wide)), hand_rank, live_mask)


def row_count(planes, groups):
    return -(-planes * groups // 8) * 8


def plan_of(parent_ref, node_count, groups):
    total = groups * node_count
    first = lax.axis_index("node") * groups
    off = [lax.rem(first - (parent_ref[idx, 0] >> 2) + total, total) for idx in (1, 2, 3)]
    one = off[0]
    two = one + off[1]
    three = two + off[2]
    low = jnp.maximum(one, three - groups)
    high = jnp.minimum(two, groups)
    middle = jnp.minimum(jnp.maximum((one + two + three + 2) >> 2, low), high)
    return middle, middle - one, two - middle, three - middle


def class_of(shift, groups):
    near = jnp.where(shift[3] > groups, 2 * groups - shift[3], shift[3])
    need = jnp.maximum(shift[0] + shift[1], shift[2] + near)
    found = jnp.int32(0)
    for size in CLASSES[:-1]:
        found = found + (need > size).astype(jnp.int32)
    return jnp.where(shift[3] > groups, len(CLASSES) - 1, found)


def fill_messages(
    node, stage, message_refs, size, block_ref, to_left, to_right, skipped=None
):
    _, tiles, planes = stage.shape[:3]
    even = lax.rem(node, 2) == 0
    places = [(tile, plane) for tile in range(tiles) for plane in range(planes)]
    for side, on_left in enumerate((even, jnp.logical_not(even))):
        for near, far in zip(to_left, to_right):
            level = jnp.where(on_left, near[0], far[0])
            start = jnp.where(on_left, near[1], far[1])
            for tile, plane in places:
                block = block_ref[level, tile, plane]
                if skipped is not None:
                    block = ahead(block, jnp.where(level == 3, skipped, 0))
                stage[side, tile, plane, pl.ds(start, 8), :] = block
    for side, message_ref in enumerate(message_refs):
        for tile, plane in places:
            message_ref[tile, plane * size : plane * size + size, :] = stage[
                side, tile, plane, 8 : 8 + size, :
            ]


def prepare_kernel(
    node_count,
    parent_hbm,
    logits_hbm,
    pot_hbm,
    kind_hbm,
    home_ref,
    shift_ref,
    class_ref,
    parent_ref,
    logits_ref,
    pot_ref,
    kind_ref,
    raw,
    flat,
    turned,
    sems,
):
    levels, tiles, planes, groups, _ = home_ref.shape
    slots = 4 * groups
    hands = logits_ref.shape[-1]
    fetches = [
        pltpu.make_async_copy(logits_hbm.at[0, idx], logits_ref.at[idx], sems.at[idx])
        for idx in range(levels)
    ]
    tables = [
        pltpu.make_async_copy(source, target, sems.at[levels + idx])
        for idx, (source, target) in enumerate(
            ((parent_hbm, parent_ref), (pot_hbm, pot_ref), (kind_hbm, kind_ref))
        )
    ]
    for fetch in tables + fetches:
        fetch.start()
    for fetch in tables:
        fetch.wait()
    shift = plan_of(parent_ref, node_count, groups)
    row_id = lax.broadcasted_iota(jnp.int32, shift_ref.shape, 0)
    spread = jnp.zeros(shift_ref.shape, jnp.int32)
    class_ref[...] = jnp.full((1, 1), class_of(shift, groups))
    for idx, value in enumerate(shift):
        spread = jnp.where(row_id == idx, value, spread)
    shift_ref[...] = spread
    pot = pot_ref[...]
    kind = kind_ref[...]
    level = lax.broadcasted_iota(jnp.int32, pot.shape, 0)
    sign = jnp.where(level % 2 == 0, -1.0, 1.0)
    flat[...] = jnp.zeros(flat.shape, jnp.float32)
    flat[0:levels, 0:slots] = jnp.where(kind == 2, pot, 0.0)
    flat[levels : 2 * levels, 0:slots] = jnp.where(kind == 1, pot, 0.0) * sign
    turned[...] = flat[...].T
    lane = lax.broadcasted_iota(jnp.int32, (groups, LANES), 1)
    for idx in range(levels):
        raw[idx, tiles - 1] = jnp.zeros((slots, LANES), jnp.float32)
    for idx in range(levels):
        fetches[idx].wait()
        for tile in range(tiles):
            start = tile * LANES
            stop = min(start + LANES, hands)
            raw[idx, tile, :, 0 : stop - start] = logits_ref[idx, :, start:stop]
            first = raw[idx, tile, pl.ds(0, groups, stride=4), :]
            for plane in range(planes):
                row = raw[idx, tile, pl.ds(plane + 1, groups, stride=4), :] - first
                if tile == tiles - 1 and plane == 0:
                    for slot in range(4):
                        scale = turned[pl.ds(slot, groups, stride=4), :]
                        row = jnp.where(lane == LANES - 8 + slot, scale[:, idx : idx + 1], row)
                        fold = scale[:, levels + idx : levels + idx + 1]
                        row = jnp.where(lane == LANES - 4 + slot, fold, row)
                home_ref[idx, tile, plane] = row


def prepared(logits, pot_size, node_type, parent_slot):
    _, levels, slots, hands = logits.shape
    groups = slots // 4
    tiles = padded(hands) // LANES
    vmem = pl.BlockSpec(memory_space=pltpu.VMEM)
    return pl.pallas_call(
        functools.partial(prepare_kernel, lax.axis_size("node")),
        out_shape=(
            jax.ShapeDtypeStruct((levels, tiles, 3, groups, LANES), jnp.float32),
            jax.ShapeDtypeStruct((8, LANES), jnp.int32),
            jax.ShapeDtypeStruct((1, 1), jnp.int32),
        ),
        in_specs=[pl.BlockSpec(memory_space=pl.ANY)] * 4,
        out_specs=(vmem, vmem, vmem),
        scratch_shapes=[
            pltpu.SMEM(parent_slot.shape, jnp.int32),
            pltpu.VMEM((levels, slots, hands), jnp.float32),
            pltpu.VMEM(pot_size.shape, jnp.float32),
            pltpu.VMEM(node_type.shape, jnp.int32),
            pltpu.VMEM((levels, tiles, slots, LANES), jnp.float32),
            pltpu.VMEM((LANES, LANES), jnp.float32),
            pltpu.VMEM((LANES, LANES), jnp.float32),
            pltpu.SemaphoreType.DMA((levels + 3,)),
        ],
        compiler_params=pltpu.CompilerParams(vmem_limit_bytes=10 * MEBI),
        name="prepare",
    )(parent_slot, logits, pot_size, node_type)


def ahead(rows, count):
    return pltpu.roll(rows, (8 - count) & 7, 0)


def behind(rows, count):
    return pltpu.roll(rows, count & 7, 0)


def shifts_in(shift_ref):
    return [jnp.max(shift_ref[idx : idx + 1, :]) for idx in range(4)]


def pack_kernel(size, far, shift_ref, home_ref, _pot, _kind, _parent, odd_ref, even_ref, *rest):
    far_ref = rest[0] if far else None
    stage = rest[-1]
    _, tiles, planes, groups, _ = home_ref.shape
    shift = shifts_in(shift_ref)
    skipped = jnp.maximum(shift[3] - 8, 0) if far else None
    fill_messages(
        lax.axis_index("node"),
        stage,
        (odd_ref, even_ref),
        size,
        home_ref,
        [(2, 8), (3, 8 + shift[2])],
        [(1, shift[0] + shift[1]), (0, shift[0])],
        skipped,
    )
    if far:
        for tile in range(tiles):
            for plane in range(planes):
                far_ref[tile, plane * FAR : plane * FAR + FAR, :] = home_ref[3, tile, plane, 0:FAR, :]


def message_shapes(planes, wide, size, far):
    tiles = wide // LANES
    message = jax.ShapeDtypeStruct((tiles, row_count(planes, size), LANES), jnp.float32)
    shapes = [message] * 2
    if far:
        shapes.append(jax.ShapeDtypeStruct((tiles, row_count(planes, FAR), LANES), jnp.float32))
    return shapes


def sent_on(odd, even, far, far_steps, order):
    count = lax.axis_size("node")
    edges = [(src, (src + 1) % count) for src in range(count)]
    got = [None, None]
    for side in order:
        pairs = [pair for edge in edges[1 - side :: 2] for pair in (edge, edge[::-1])]
        got[side] = lax.ppermute((odd, even)[side], "node", pairs)
    for message in far:
        pairs = [(src, (src + far_steps) % count) for src in range(count)]
        got.append(lax.ppermute(message, "node", pairs))
    return got


def spread_messages(node, from_left, from_right, odd_ref, even_ref, size):
    tiles, planes = from_left.shape[:2]
    even = lax.rem(node, 2) == 0
    for tile in range(tiles):
        for plane in range(planes):
            place = slice(plane * size, plane * size + size)
            odd_part = odd_ref[tile, place, :]
            even_part = even_ref[tile, place, :]
            from_left[tile, plane, 8 : 8 + size, :] = jnp.where(even, odd_part, even_part)
            from_right[tile, plane, 8 : 8 + size, :] = jnp.where(even, even_part, odd_part)


def inner_sum(inner, rows):
    total = jnp.where(inner[0], rows[0], 0.0)
    for idx in range(1, 4):
        total = total + jnp.where(inner[idx], rows[idx], 0.0)
    return total


def inner_before(inner):
    one = inner[0] | inner[1]
    return [inner[0], one, one | inner[2]]


def softmax_four(rows):
    top = jnp.maximum(jnp.maximum(rows[0], rows[1]), jnp.maximum(rows[2], 0.0))
    lifted = [jnp.exp(-top)] + [jnp.exp(row - top) for row in rows]
    total = (lifted[0] + lifted[1]) + (lifted[2] + lifted[3])
    return [row / total for row in lifted]


def operator_q(point, show, fold, range_one, range_two, block_ref, cols, put, top_ref=None):
    wide = block_ref.shape[1]
    inner = [
        [(show[idx][slot] == 0.0) & (fold[idx][slot] == 0.0) for slot in range(4)]
        for idx in range(4)
    ]
    strategy = [softmax_four(point[idx]) for idx in range(4)]
    top_one = [range_one * row for row in strategy[0]]
    above_one = inner_sum(inner[0], top_one)
    mid_two = [range_two * row for row in strategy[1]]
    above_two = inner_sum(inner[1], mid_two)
    low_one = [above_one * row for row in strategy[2]]
    last_one = inner_sum(inner[2], low_one)
    end_two = [above_two * row for row in strategy[3]]
    wide_two = jnp.broadcast_to(range_two, above_two.shape)
    past = [inner_before(inner[idx]) for idx in range(3)]

    units = [
        (0, [wide_two] * 4, 1.0, False),
        (1, mid_two, 1.0, True),
        (2, [above_two] * 4, 1.0, False),
        (3, end_two, 1.0, True),
        (1, [above_one] * 4, -1.0, False),
        (2, low_one, -1.0, True),
        (3, [last_one] * 4, -1.0, False),
    ]
    first_unit = 0 if top_ref is None else 1
    begin = [0] * len(units)
    for side in range(2):
        blocks = []
        for unit in range(first_unit, len(units)):
            idx, rows, fold_sign, as_sum = units[unit]
            begin[unit] = 8 * len(blocks)
            if side == 0:
                scaled = [rows[slot] * show[idx][slot] for slot in range(4)]
            else:
                scaled = [rows[slot] * (fold[idx][slot] * fold_sign) for slot in range(4)]
            if as_sum:
                rounded = [row.astype(jnp.bfloat16).astype(jnp.float32) for row in scaled]
                total = (rounded[0] + rounded[1]) + (rounded[2] + rounded[3])
                high = total.astype(jnp.bfloat16).astype(jnp.float32)
                scaled = [high, total - high]
            elif idx < 3:
                scaled = [
                    jnp.where(past[idx][slot], scaled[slot + 1], scaled[slot]) for slot in range(3)
                ]
            blocks += scaled
        if len(blocks) % 2:
            blocks.append(jnp.zeros_like(blocks[0]))
        lanes = slice(side * wide, side * wide + wide)
        for pair in range(0, len(blocks), 2):
            cols[pair * 8 : pair * 8 + 16, lanes] = jnp.concatenate(
                blocks[pair : pair + 2], axis=0
            ).astype(jnp.bfloat16)

    def added(rows):
        return (rows[0] + rows[1]) + (rows[2] + rows[3])

    def landed(rows, kept, term):
        return [jnp.where(kept[slot], term, rows[slot]) for slot in range(4)]

    total = None
    for start in range(0, wide, 2 * LANES):
        stop = min(start + 2 * LANES, wide)
        pay = jnp.dot(cols[...], block_ref[:, start:stop], preferred_element_type=jnp.float32)

        def paid(unit):
            at = begin[unit]
            idx = units[unit][0]
            rows = [pay[at + slot * 8 : at + slot * 8 + 8, :] for slot in range(4 if idx == 3 else 3)]
            if idx < 3:
                rows = [
                    rows[0],
                    jnp.where(past[idx][0], rows[0], rows[1]),
                    jnp.where(past[idx][1], rows[1], rows[2]),
                    rows[2],
                ]
            return rows

        def paid_sum(unit):
            at = begin[unit]
            return pay[at : at + 8, :] + pay[at + 8 : at + 16, :]

        def weighed(idx, rows):
            return added([strategy[idx][slot][:, start:stop] * rows[slot] for slot in range(4)])

        value_two_end = paid(6)
        term_two = paid_sum(5) + weighed(3, value_two_end)
        value_two_mid = landed(paid(4), inner[1], term_two)
        value_one_low = landed(paid(2), inner[2], paid_sum(3))
        term_one = paid_sum(1) + weighed(2, value_one_low)
        if top_ref is None:
            value_one_top = landed(paid(0), inner[0], term_one)
        else:
            value_one_top = [
                jnp.where(inner[0][slot], term_one, top_ref[0, slot, :, start:stop])
                for slot in range(4)
            ]
        found = [value_one_top, value_two_mid, value_one_low, value_two_end]
        put(start, stop, found)
        part = squares(found)
        total = part if total is None else total + part
    return total


def squares(found):
    total = None
    for rows in found:
        for row in rows:
            total = row * row if total is None else total + row * row
    return jnp.broadcast_to(jnp.sum(total), (1, LANES))


def scale_columns(rows):
    wide = rows[0][0].shape[1]
    show = [
        [level[0][:, wide - 8 + slot : wide - 7 + slot] for slot in range(4)] for level in rows
    ]
    fold = [
        [level[0][:, wide - 4 + slot : wide - 4 + slot + 1] for slot in range(4)] for level in rows
    ]
    return show, fold


def wide_row(store, place, row_ref):
    hands = row_ref.shape[1]
    store[place : place + 1, 0:hands] = row_ref[...]
    return store[place : place + 1, :]


def first_kernel(size, far, shift_ref, home_ref, odd_ref, even_ref, *rest):
    if far:
        far_ref, rest = rest[0], rest[1:]
    one_ref, two_ref, block_ref, chain_ref, value_ref, square_ref = rest[:6]
    from_left, from_right, window, ranges, cols = rest[6:]
    _, tiles, planes, groups, _ = home_ref.shape
    shift = shifts_in(shift_ref)
    spread_messages(lax.axis_index("node"), from_left, from_right, odd_ref, even_ref, size)
    chain = lax.broadcasted_iota(jnp.int32, (groups, LANES), 0)
    places = [(tile, plane) for tile in range(tiles) for plane in range(planes)]
    if far:
        for tile, plane in places:
            window[tile, plane, 16 : 16 + FAR, :] = far_ref[
                tile, plane * FAR : plane * FAR + FAR, :
            ]
    point = [[[] for _ in range(planes)] for _ in range(4)]
    for tile, plane in places:
        top = jnp.where(
            chain < shift[0],
            from_left[tile, plane, 8:16, :],
            behind(home_ref[0, tile, plane], shift[0]),
        )
        mid = jnp.where(
            chain < shift[1],
            from_left[tile, plane, pl.ds(8 + shift[0], 8), :],
            behind(home_ref[1, tile, plane], shift[1]),
        )
        low = jnp.where(
            chain + shift[2] < 8,
            ahead(home_ref[2, tile, plane], shift[2]),
            from_right[tile, plane, pl.ds(shift[2], 8), :],
        )
        end = jnp.where(
            chain + shift[3] < 8,
            ahead(home_ref[3, tile, plane], shift[3]),
            from_right[tile, plane, pl.ds(shift[2] + jnp.minimum(shift[3], 8), 8), :],
        )
        if far:
            far_part = window[tile, plane, pl.ds(shift[3], 8), :]
            end = jnp.where(chain + shift[3] < 16, end, far_part)
        for idx, row in enumerate((top, mid, low, end)):
            point[idx][plane].append(row)
    point = [[jnp.concatenate(rows, axis=1) for rows in level] for level in point]
    for idx in range(4):
        for plane in range(planes):
            chain_ref[idx, plane] = point[idx][plane]
    show, fold = scale_columns(point)
    ranges[...] = jnp.zeros(ranges.shape, jnp.float32)
    range_one = wide_row(ranges, 0, one_ref)
    range_two = wide_row(ranges, 1, two_ref)

    def put(start, stop, found):
        for idx in range(4):
            for slot in range(4):
                value_ref[idx, slot, :, start:stop] = found[idx][slot]

    square_ref[...] = operator_q(
        point, show, fold, range_one, range_two, block_ref, cols, put
    )


def rate_of(parts_ref, entry_count):
    square_sum = jnp.sum(parts_ref[...], axis=0, keepdims=True)[:, 0:1]
    return step_scale / jnp.sqrt(square_sum / entry_count + eps_value)


def second_kernel(entry_count, size, far, shift_ref, chain_ref, value_ref, *rest):
    parts_ref, one_ref, two_ref, block_ref, own_ref, odd_ref, even_ref = rest[:7]
    rest = rest[7:]
    if far:
        far_ref, rest = rest[0], rest[1:]
    square_ref, stage, ranges, cols = rest
    _, tiles, planes, groups, _ = own_ref.shape
    rate = rate_of(parts_ref, entry_count)
    raw = [[chain_ref[idx, plane] for plane in range(3)] for idx in range(4)]
    show, fold = scale_columns(raw)
    point = [
        [
            raw[idx][plane] + rate * (value_ref[idx, plane + 1] - value_ref[idx, 0])
            for plane in range(3)
        ]
        for idx in range(4)
    ]
    ranges[...] = jnp.zeros(ranges.shape, jnp.float32)
    range_one = wide_row(ranges, 0, one_ref)
    range_two = wide_row(ranges, 1, two_ref)

    def put(start, stop, found):
        for idx in range(4):
            for slot in range(4):
                for lane in range(start, stop, LANES):
                    row = found[idx][slot][:, lane - start : lane - start + LANES]
                    own_ref[idx, lane // LANES, slot] = row

    square_ref[...] = operator_q(
        point, show, fold, range_one, range_two, block_ref, cols, put, value_ref
    )
    shift = shifts_in(shift_ref)
    fill_messages(
        lax.axis_index("node"),
        stage,
        (odd_ref, even_ref),
        size,
        own_ref,
        [(0, 8), (1, 8 + shift[0])],
        [(3, shift[2] + jnp.minimum(shift[3], 8)), (2, shift[2])],
    )
    if far:
        for tile in range(tiles):
            for plane in range(planes):
                part = stage.at[0, tile, plane]
                part[pl.ds(jnp.maximum(shift[3] - 8, 0), 8), :] = own_ref[3, tile, plane]
                far_ref[tile, plane * FAR : plane * FAR + FAR, :] = part[8 : 8 + FAR, :]


def last_kernel(entry_count, size, far, shift_ref, own_ref, even_ref, odd_ref, *rest):
    far_ref, rest = (rest[0], rest[1:]) if far else (None, rest)
    parts_ref, logits_ref, new_hbm, half_hbm, from_left, from_right, lined = rest[:7]
    new_ref, half_ref, sems = rest[7:]
    _, tiles, planes, groups, _ = own_ref.shape
    hands = logits_ref.shape[-1]
    shift = shifts_in(shift_ref)
    rate = rate_of(parts_ref, entry_count)
    group = lax.broadcasted_iota(jnp.int32, (groups, LANES), 0)
    spread_messages(lax.axis_index("node"), from_left, from_right, odd_ref, even_ref, size)
    places = [(tile, plane) for tile in range(tiles) for plane in range(planes)]

    def top(tile, plane, own):
        return jnp.where(
            group + shift[0] < 8,
            ahead(own, shift[0]),
            from_right[tile, plane, pl.ds(shift[0], 8), :],
        )

    def mid(tile, plane, own):
        return jnp.where(
            group + shift[1] < 8,
            ahead(own, shift[1]),
            from_right[tile, plane, pl.ds(shift[0] + shift[1], 8), :],
        )

    def low(tile, plane, own):
        return jnp.where(
            group < shift[2], from_left[tile, plane, 8:16, :], behind(own, shift[2])
        )

    def end(tile, plane, own):
        row = jnp.where(
            group < shift[3],
            from_left[tile, plane, pl.ds(8 + shift[2] - jnp.maximum(shift[3] - 8, 0), 8), :],
            behind(own, shift[3]),
        )
        if far:
            far_part = far_ref[tile, plane * FAR : plane * FAR + 8, :]
            row = jnp.where(group < shift[3] - 8, far_part, row)
        return row

    leaving = []

    def leave(source, target, kind, idx):
        leaving.append(pltpu.make_async_copy(source.at[idx], target.at[0, idx], sems.at[kind, idx]))
        leaving[-1].start()

    for idx, found in enumerate((top, mid, low, end)):
        for tile, plane in places:
            row = found(tile, plane, own_ref[idx, tile, plane])
            lined[idx, tile, pl.ds(plane, groups, stride=4), :] = row
        for tile in range(tiles):
            start = tile * LANES
            stop = min(start + LANES, hands)
            value = lined[idx, tile][:, 0 : stop - start]
            half_ref[idx, :, start:stop] = value
            new_ref[idx, :, start:stop] = logits_ref[0, idx, :, start:stop] + rate * value
        leave(half_ref, half_hbm, 0, idx)
        leave(new_ref, new_hbm, 1, idx)
    for copy in leaving:
        copy.wait()


def shared_parts(part):
    count = lax.axis_size("node") * lax.axis_size("board")
    spread = jnp.broadcast_to(part, (count, LANES))
    return lax.all_to_all(spread, ("node", "board"), 0, 0, tiled=True)


def shared_parts_over_nodes(part):
    nodes = lax.axis_size("node")
    boards = lax.axis_size("board")
    total = part
    for turn in range(1, boards):
        pairs = [(board, (board + turn) % boards) for board in range(boards)]
        total = total + lax.ppermute(part, "board", pairs)
    spread = jnp.broadcast_to(total, (nodes, LANES))
    order = [list(range(nodes))[::-1]]
    return lax.all_to_all(spread, "node", 0, 0, axis_index_groups=order, tiled=True)


def step_of_class(
    size,
    far,
    home,
    shift,
    logits,
    pot_size,
    node_type,
    parent_slot,
    range_one,
    range_two,
    hand_rank,
    live_mask,
):
    _, levels, slots, hands = logits.shape
    wide = padded(hands)
    tiles = wide // LANES
    groups = slots // 4
    entry_count = float(logits.size * lax.axis_size("node") * lax.axis_size("board"))
    vmem = pl.BlockSpec(memory_space=pltpu.VMEM)
    f32 = jnp.float32

    def limit(mebi):
        return pltpu.CompilerParams(vmem_limit_bytes=mebi * MEBI)

    def stage(planes, rows=32):
        return pltpu.VMEM((tiles, planes, rows, LANES), f32)

    def two_stages(planes):
        return pltpu.VMEM((2, tiles, planes, 32, LANES), f32)

    anywhere = pl.BlockSpec(memory_space=pl.ANY)
    sent = pl.pallas_call(
        functools.partial(pack_kernel, size, far),
        out_shape=message_shapes(3, wide, size, far),
        in_specs=[vmem, vmem] + [anywhere] * 3,
        scratch_shapes=[two_stages(3)],
        compiler_params=limit(8),
        name="pack",
    )(shift, home, pot_size, node_type, parent_slot)
    got = sent_on(sent[0], sent[1], sent[2:], -2, (0, 1))
    blocks = payoff_blocks(hand_rank, live_mask)
    blocks_all = 3 * 3 + 4 + 3 * 2
    rows = 16 * (-(-blocks_all // 2))
    rows_second = 16 * (-(-(blocks_all - 3) // 2))

    def work(count):
        return [
            pltpu.VMEM((8, wide), f32),
            pltpu.VMEM((count, 2 * wide), jnp.bfloat16),
        ]

    def cost(count):
        return pl.CostEstimate(
            flops=4 * count * wide * wide, bytes_accessed=6 * wide * wide, transcendentals=0
        )

    square_shape = jax.ShapeDtypeStruct((1, LANES), f32)
    chain, value, part = pl.pallas_call(
        functools.partial(first_kernel, size, far),
        out_shape=(
            jax.ShapeDtypeStruct((levels, 3, groups, wide), f32),
            jax.ShapeDtypeStruct((levels, 4, groups, wide), f32),
            square_shape,
        ),
        in_specs=[vmem] * (5 + len(got)),
        scratch_shapes=[stage(3), stage(3), stage(3)] + work(rows),
        compiler_params=limit(32),
        cost_estimate=cost(rows),
        name="first",
    )(shift, home, *got, range_one, range_two, blocks)
    parts = shared_parts(part)
    own, *sent, part = pl.pallas_call(
        functools.partial(second_kernel, entry_count, size, far),
        out_shape=[jax.ShapeDtypeStruct((levels, tiles, 4, groups, LANES), f32)]
        + message_shapes(4, wide, size, far)
        + [square_shape],
        in_specs=[vmem] * 7,
        scratch_shapes=[two_stages(4)] + work(rows_second),
        compiler_params=limit(32),
        cost_estimate=cost(rows_second),
        name="second",
    )(shift, chain, value, parts, range_one, range_two, blocks)
    got = sent_on(sent[0], sent[1], sent[2:], 2, (1, 0))
    parts = shared_parts_over_nodes(part)
    out_shape = jax.ShapeDtypeStruct(logits.shape, f32)
    level_shape = (levels, slots, hands)
    return pl.pallas_call(
        functools.partial(last_kernel, entry_count, size, far),
        out_shape=(out_shape, out_shape),
        in_specs=[vmem] * (4 + len(got)),
        out_specs=(anywhere, anywhere),
        scratch_shapes=[
            stage(4),
            stage(4),
            pltpu.VMEM((levels, tiles, slots, LANES), f32),
            pltpu.VMEM(level_shape, f32),
            pltpu.VMEM(level_shape, f32),
            pltpu.SemaphoreType.DMA((2, levels)),
        ],
        compiler_params=limit(24),
        name="last",
    )(shift, own, got[1], got[0], *got[2:], parts, logits)


def per_device(
    logits, pot_size, node_type, parent_slot, range_one, range_two, hand_rank, live_mask
):
    branches = [
        functools.partial(step_of_class, size, size == CLASSES[-1]) for size in CLASSES
    ]
    home, shift, found = prepared(logits, pot_size, node_type, parent_slot)
    return lax.switch(
        found[0, 0],
        branches,
        home,
        shift,
        logits,
        pot_size,
        node_type,
        parent_slot,
        range_one,
        range_two,
        hand_rank,
        live_mask,
    )


def solution(mesh):
    return jax.shard_map(
        per_device,
        mesh=mesh,
        in_specs=(
            P("board", None, "node", None),
            P(None, "node"),
            P(None, "node"),
            P(None, "node"),
            P("board", None),
            P("board", None),
            P("board", None),
            P("board", None),
        ),
        out_specs=(P("board", None, "node", None), P("board", None, "node", None)),
        check_vma=False,
    )
```

```python
import functools

import jax
import jax.numpy as jnp
import numpy as np
from jax import lax
from jax.experimental import pallas as pl
from jax.experimental.pallas import tpu as pltpu
from jax.sharding import PartitionSpec as P

LANES = 128
CARDS = 52
step_scale = 0.5
eps_value = 1e-06
MEBI = 1 << 20
CLASSES = (8, 10, 12, 14)
FAR = 5


def padded(count):
    return -(-count // LANES) * LANES


def card_rows(hand_count, wide):
    pairs = [(low, high) for low in range(CARDS) for high in range(low + 1, CARDS)]
    rows = np.full((2, wide), -1, np.int32)
    rows[:, :hand_count] = np.array(pairs[:hand_count], np.int32).T
    return rows


def payoff_kernel(hands, cards_ref, rank_ref, live_ref, out_ref, flat, left, right):
    wide = out_ref.shape[1]
    flat[...] = jnp.zeros(flat.shape, jnp.float32)
    flat[0:1, 0:hands] = rank_ref[...].astype(jnp.float32)
    flat[1:2, 0:hands] = (live_ref[...] > 0).astype(jnp.float32)
    dead = 1.0 - flat[1:2, :]
    feature = lax.broadcasted_iota(jnp.int32, (LANES, wide), 0)
    hit = (feature == cards_ref[0:1, :]) | (feature == cards_ref[1:2, :])
    base = jnp.where(hit, 1.0, 0.0)
    left[...] = jnp.where(feature == CARDS, dead, jnp.where(feature == CARDS + 1, 1.0, base))
    right[...] = jnp.where(
        feature == CARDS, 1.0, jnp.where(feature == CARDS + 1, dead, base)
    ).astype(jnp.bfloat16)
    rank_row = flat[0:1, :]
    for block in range(wide // LANES):
        part = slice(block * LANES, (block + 1) * LANES)
        left_block = left[:, part].T.astype(jnp.bfloat16)
        rank_col = jnp.broadcast_to(flat[0:1, part], (LANES, LANES)).T[:, 0:1]
        hits = jnp.dot(left_block, right[...], preferred_element_type=jnp.float32)
        compat = jnp.where(hits == 0.0, 1.0, 0.0)
        order = jnp.clip(rank_row - rank_col, -1.0, 1.0)
        out_ref[part, :] = (order * compat).astype(jnp.bfloat16)
        out_ref[wide + block * LANES : wide + (block + 1) * LANES, :] = compat.astype(jnp.bfloat16)


def payoff_blocks(hand_rank, live_mask):
    hands = hand_rank.shape[-1]
    wide = padded(hands)
    return pl.pallas_call(
        functools.partial(payoff_kernel, hands),
        out_shape=jax.ShapeDtypeStruct((2 * wide, wide), jnp.bfloat16),
        scratch_shapes=[
            pltpu.VMEM((8, wide), jnp.float32),
            pltpu.VMEM((LANES, wide), jnp.float32),
            pltpu.VMEM((LANES, wide), jnp.bfloat16),
        ],
        compiler_params=pltpu.CompilerParams(vmem_limit_bytes=20 * MEBI),
        cost_estimate=pl.CostEstimate(
            flops=2 * wide * wide * LANES, bytes_accessed=4 * wide * wide, transcendentals=0
        ),
        name="payoff",
    )(jnp.asarray(card_rows(hands, wide)), hand_rank, live_mask)


def row_count(planes, groups):
    return -(-planes * groups // 8) * 8


def plan_of(parent_ref, node_count, groups):
    total = groups * node_count
    first = lax.axis_index("node") * groups
    off = [lax.rem(first - (parent_ref[idx, 0] >> 2) + total, total) for idx in (1, 2, 3)]
    one = off[0]
    two = one + off[1]
    three = two + off[2]
    low = jnp.maximum(one, three - groups)
    high = jnp.minimum(two, groups)
    middle = jnp.minimum(jnp.maximum((one + two + three + 2) >> 2, low), high)
    return middle, middle - one, two - middle, three - middle


def class_of(shift, groups):
    near = jnp.where(shift[3] > groups, 2 * groups - shift[3], shift[3])
    need = jnp.maximum(shift[0] + shift[1], shift[2] + near)
    found = jnp.int32(0)
    for size in CLASSES[:-1]:
        found = found + (need > size).astype(jnp.int32)
    return jnp.where(shift[3] > groups, len(CLASSES) - 1, found)


def fill_messages(
    node, stage, message_refs, size, block_ref, to_left, to_right, skipped=None
):
    _, tiles, planes = stage.shape[:3]
    even = lax.rem(node, 2) == 0
    places = [(tile, plane) for tile in range(tiles) for plane in range(planes)]
    for side, on_left in enumerate((even, jnp.logical_not(even))):
        for near, far in zip(to_left, to_right):
            level = jnp.where(on_left, near[0], far[0])
            start = jnp.where(on_left, near[1], far[1])
            for tile, plane in places:
                block = block_ref[level, tile, plane]
                if skipped is not None:
                    block = ahead(block, jnp.where(level == 3, skipped, 0))
                stage[side, tile, plane, pl.ds(start, 8), :] = block
    for side, message_ref in enumerate(message_refs):
        for tile, plane in places:
            message_ref[tile, plane * size : plane * size + size, :] = stage[
                side, tile, plane, 8 : 8 + size, :
            ]


def prepare_kernel(
    node_count,
    parent_hbm,
    logits_hbm,
    pot_hbm,
    kind_hbm,
    home_ref,
    shift_ref,
    class_ref,
    parent_ref,
    logits_ref,
    pot_ref,
    kind_ref,
    raw,
    flat,
    turned,
    sems,
):
    levels, tiles, planes, groups, _ = home_ref.shape
    slots = 4 * groups
    hands = logits_ref.shape[-1]
    fetches = [
        pltpu.make_async_copy(logits_hbm.at[0, idx], logits_ref.at[idx], sems.at[idx])
        for idx in range(levels)
    ]
    tables = [
        pltpu.make_async_copy(source, target, sems.at[levels + idx])
        for idx, (source, target) in enumerate(
            ((parent_hbm, parent_ref), (pot_hbm, pot_ref), (kind_hbm, kind_ref))
        )
    ]
    for fetch in tables + fetches:
        fetch.start()
    for fetch in tables:
        fetch.wait()
    shift = plan_of(parent_ref, node_count, groups)
    row_id = lax.broadcasted_iota(jnp.int32, shift_ref.shape, 0)
    spread = jnp.zeros(shift_ref.shape, jnp.int32)
    class_ref[...] = jnp.full((1, 1), class_of(shift, groups))
    for idx, value in enumerate(shift):
        spread = jnp.where(row_id == idx, value, spread)
    shift_ref[...] = spread
    pot = pot_ref[...]
    kind = kind_ref[...]
    level = lax.broadcasted_iota(jnp.int32, pot.shape, 0)
    sign = jnp.where(level % 2 == 0, -1.0, 1.0)
    flat[...] = jnp.zeros(flat.shape, jnp.float32)
    flat[0:levels, 0:slots] = jnp.where(kind == 2, pot, 0.0)
    flat[levels : 2 * levels, 0:slots] = jnp.where(kind == 1, pot, 0.0) * sign
    turned[...] = flat[...].T
    lane = lax.broadcasted_iota(jnp.int32, (groups, LANES), 1)
    for idx in range(levels):
        raw[idx, tiles - 1] = jnp.zeros((slots, LANES), jnp.float32)
    for idx in range(levels):
        fetches[idx].wait()
        for tile in range(tiles):
            start = tile * LANES
            stop = min(start + LANES, hands)
            raw[idx, tile, :, 0 : stop - start] = logits_ref[idx, :, start:stop]
            first = raw[idx, tile, pl.ds(0, groups, stride=4), :]
            for plane in range(planes):
                row = raw[idx, tile, pl.ds(plane + 1, groups, stride=4), :] - first
                if tile == tiles - 1 and plane == 0:
                    for slot in range(4):
                        scale = turned[pl.ds(slot, groups, stride=4), :]
                        row = jnp.where(lane == LANES - 8 + slot, scale[:, idx : idx + 1], row)
                        fold = scale[:, levels + idx : levels + idx + 1]
                        row = jnp.where(lane == LANES - 4 + slot, fold, row)
                home_ref[idx, tile, plane] = row


def prepared(logits, pot_size, node_type, parent_slot):
    _, levels, slots, hands = logits.shape
    groups = slots // 4
    tiles = padded(hands) // LANES
    vmem = pl.BlockSpec(memory_space=pltpu.VMEM)
    return pl.pallas_call(
        functools.partial(prepare_kernel, lax.axis_size("node")),
        out_shape=(
            jax.ShapeDtypeStruct((levels, tiles, 3, groups, LANES), jnp.float32),
            jax.ShapeDtypeStruct((8, LANES), jnp.int32),
            jax.ShapeDtypeStruct((1, 1), jnp.int32),
        ),
        in_specs=[pl.BlockSpec(memory_space=pl.ANY)] * 4,
        out_specs=(vmem, vmem, vmem),
        scratch_shapes=[
            pltpu.SMEM(parent_slot.shape, jnp.int32),
            pltpu.VMEM((levels, slots, hands), jnp.float32),
            pltpu.VMEM(pot_size.shape, jnp.float32),
            pltpu.VMEM(node_type.shape, jnp.int32),
            pltpu.VMEM((levels, tiles, slots, LANES), jnp.float32),
            pltpu.VMEM((LANES, LANES), jnp.float32),
            pltpu.VMEM((LANES, LANES), jnp.float32),
            pltpu.SemaphoreType.DMA((levels + 3,)),
        ],
        compiler_params=pltpu.CompilerParams(vmem_limit_bytes=10 * MEBI),
        name="prepare",
    )(parent_slot, logits, pot_size, node_type)


def ahead(rows, count):
    return pltpu.roll(rows, (8 - count) & 7, 0)


def behind(rows, count):
    return pltpu.roll(rows, count & 7, 0)


def shifts_in(shift_ref):
    return [jnp.max(shift_ref[idx : idx + 1, :]) for idx in range(4)]


def pack_kernel(size, far, shift_ref, home_ref, _pot, _kind, _parent, odd_ref, even_ref, *rest):
    far_ref = rest[0] if far else None
    stage = rest[-1]
    _, tiles, planes, groups, _ = home_ref.shape
    shift = shifts_in(shift_ref)
    skipped = jnp.maximum(shift[3] - 8, 0) if far else None
    fill_messages(
        lax.axis_index("node"),
        stage,
        (odd_ref, even_ref),
        size,
        home_ref,
        [(2, 8), (3, 8 + shift[2])],
        [(1, shift[0] + shift[1]), (0, shift[0])],
        skipped,
    )
    if far:
        for tile in range(tiles):
            for plane in range(planes):
                far_ref[tile, plane * FAR : plane * FAR + FAR, :] = home_ref[3, tile, plane, 0:FAR, :]


def message_shapes(planes, wide, size, far):
    tiles = wide // LANES
    message = jax.ShapeDtypeStruct((tiles, row_count(planes, size), LANES), jnp.float32)
    shapes = [message] * 2
    if far:
        shapes.append(jax.ShapeDtypeStruct((tiles, row_count(planes, FAR), LANES), jnp.float32))
    return shapes


def sent_on(odd, even, far, far_steps, order):
    count = lax.axis_size("node")
    edges = [(src, (src + 1) % count) for src in range(count)]
    got = [None, None]
    for side in order:
        pairs = [pair for edge in edges[1 - side :: 2] for pair in (edge, edge[::-1])]
        got[side] = lax.ppermute((odd, even)[side], "node", pairs)
    for message in far:
        pairs = [(src, (src + far_steps) % count) for src in range(count)]
        got.append(lax.ppermute(message, "node", pairs))
    return got


def spread_messages(node, from_left, from_right, odd_ref, even_ref, size):
    tiles, planes = from_left.shape[:2]
    even = lax.rem(node, 2) == 0
    for tile in range(tiles):
        for plane in range(planes):
            place = slice(plane * size, plane * size + size)
            odd_part = odd_ref[tile, place, :]
            even_part = even_ref[tile, place, :]
            from_left[tile, plane, 8 : 8 + size, :] = jnp.where(even, odd_part, even_part)
            from_right[tile, plane, 8 : 8 + size, :] = jnp.where(even, even_part, odd_part)


def inner_sum(inner, rows):
    total = jnp.where(inner[0], rows[0], 0.0)
    for idx in range(1, 4):
        total = total + jnp.where(inner[idx], rows[idx], 0.0)
    return total


def inner_before(inner):
    one = inner[0] | inner[1]
    return [inner[0], one, one | inner[2]]


def exponentials(rows):
    top = jnp.maximum(jnp.maximum(rows[0], rows[1]), jnp.maximum(rows[2], 0.0))
    lifted = [jnp.exp(-top)] + [jnp.exp(row - top) for row in rows]
    return lifted, 1.0 / ((lifted[0] + lifted[1]) + (lifted[2] + lifted[3]))


def softmax_four(rows):
    lifted, share = exponentials(rows)
    return [row * share for row in lifted]


def operator_q(point, show, fold, range_one, range_two, block_ref, cols, put, top_ref=None):
    wide = block_ref.shape[1]
    inner = [
        [(show[idx][slot] == 0.0) & (fold[idx][slot] == 0.0) for slot in range(4)]
        for idx in range(4)
    ]
    lifted, share = exponentials(point[0])
    above_one = range_one * (inner_sum(inner[0], lifted) * share)
    strategy = [None] + [softmax_four(point[idx]) for idx in range(1, 4)]
    mid_two = [range_two * row for row in strategy[1]]
    above_two = inner_sum(inner[1], mid_two)
    low_one = [above_one * row for row in strategy[2]]
    last_one = inner_sum(inner[2], low_one)
    end_two = [above_two * row for row in strategy[3]]
    wide_two = jnp.broadcast_to(range_two, above_two.shape)
    past = [inner_before(inner[idx]) for idx in range(3)]

    units = [
        (0, [wide_two] * 4, 1.0, False),
        (1, mid_two, 1.0, True),
        (2, [above_two] * 4, 1.0, False),
        (3, end_two, 1.0, True),
        (1, [above_one] * 4, -1.0, False),
        (2, low_one, -1.0, True),
        (3, [last_one] * 4, -1.0, False),
    ]
    first_unit = 0 if top_ref is None else 1
    begin = [0] * len(units)
    for side in range(2):
        blocks = []
        for unit in range(first_unit, len(units)):
            idx, rows, fold_sign, as_sum = units[unit]
            begin[unit] = 8 * len(blocks)
            if side == 0:
                scaled = [rows[slot] * show[idx][slot] for slot in range(4)]
            else:
                scaled = [rows[slot] * (fold[idx][slot] * fold_sign) for slot in range(4)]
            if as_sum:
                rounded = [row.astype(jnp.bfloat16).astype(jnp.float32) for row in scaled]
                total = (rounded[0] + rounded[1]) + (rounded[2] + rounded[3])
                high = total.astype(jnp.bfloat16).astype(jnp.float32)
                scaled = [high, total - high]
            elif idx < 3:
                scaled = [
                    jnp.where(past[idx][slot], scaled[slot + 1], scaled[slot]) for slot in range(3)
                ]
            blocks += scaled
        if len(blocks) % 2:
            blocks.append(jnp.zeros_like(blocks[0]))
        lanes = slice(side * wide, side * wide + wide)
        for pair in range(0, len(blocks), 2):
            cols[pair * 8 : pair * 8 + 16, lanes] = jnp.concatenate(
                blocks[pair : pair + 2], axis=0
            ).astype(jnp.bfloat16)

    def added(rows):
        return (rows[0] + rows[1]) + (rows[2] + rows[3])

    def landed(rows, kept, term):
        return [jnp.where(kept[slot], term, rows[slot]) for slot in range(4)]

    total = None
    for start in range(0, wide, 2 * LANES):
        stop = min(start + 2 * LANES, wide)
        pay = jnp.dot(cols[...], block_ref[:, start:stop], preferred_element_type=jnp.float32)

        def paid(unit):
            at = begin[unit]
            idx = units[unit][0]
            rows = [pay[at + slot * 8 : at + slot * 8 + 8, :] for slot in range(4 if idx == 3 else 3)]
            if idx < 3:
                rows = [
                    rows[0],
                    jnp.where(past[idx][0], rows[0], rows[1]),
                    jnp.where(past[idx][1], rows[1], rows[2]),
                    rows[2],
                ]
            return rows

        def paid_sum(unit):
            at = begin[unit]
            return pay[at : at + 8, :] + pay[at + 8 : at + 16, :]

        def weighed(idx, rows):
            return added([strategy[idx][slot][:, start:stop] * rows[slot] for slot in range(4)])

        value_two_end = paid(6)
        term_two = paid_sum(5) + weighed(3, value_two_end)
        value_two_mid = landed(paid(4), inner[1], term_two)
        value_one_low = landed(paid(2), inner[2], paid_sum(3))
        term_one = paid_sum(1) + weighed(2, value_one_low)
        if top_ref is None:
            value_one_top = landed(paid(0), inner[0], term_one)
        else:
            value_one_top = [
                jnp.where(inner[0][slot], term_one, top_ref[0, slot, :, start:stop])
                for slot in range(4)
            ]
        found = [value_one_top, value_two_mid, value_one_low, value_two_end]
        put(start, stop, found)
        part = squares(found)
        total = part if total is None else total + part
    return total


def squares(found):
    total = None
    for rows in found:
        for row in rows:
            total = row * row if total is None else total + row * row
    return jnp.broadcast_to(jnp.sum(total), (1, LANES))


def scale_columns(rows):
    wide = rows[0][0].shape[1]
    show = [
        [level[0][:, wide - 8 + slot : wide - 7 + slot] for slot in range(4)] for level in rows
    ]
    fold = [
        [level[0][:, wide - 4 + slot : wide - 4 + slot + 1] for slot in range(4)] for level in rows
    ]
    return show, fold


def wide_row(store, place, row_ref):
    hands = row_ref.shape[1]
    store[place : place + 1, 0:hands] = row_ref[...]
    return store[place : place + 1, :]


def first_kernel(size, far, shift_ref, home_ref, odd_ref, even_ref, *rest):
    if far:
        far_ref, rest = rest[0], rest[1:]
    one_ref, two_ref, block_ref, chain_ref, value_ref, square_ref = rest[:6]
    from_left, from_right, window, ranges, cols = rest[6:]
    _, tiles, planes, groups, _ = home_ref.shape
    shift = shifts_in(shift_ref)
    spread_messages(lax.axis_index("node"), from_left, from_right, odd_ref, even_ref, size)
    chain = lax.broadcasted_iota(jnp.int32, (groups, LANES), 0)
    places = [(tile, plane) for tile in range(tiles) for plane in range(planes)]
    if far:
        for tile, plane in places:
            window[tile, plane, 16 : 16 + FAR, :] = far_ref[
                tile, plane * FAR : plane * FAR + FAR, :
            ]
    point = [[[] for _ in range(planes)] for _ in range(4)]
    for tile, plane in places:
        top = jnp.where(
            chain < shift[0],
            from_left[tile, plane, 8:16, :],
            behind(home_ref[0, tile, plane], shift[0]),
        )
        mid = jnp.where(
            chain < shift[1],
            from_left[tile, plane, pl.ds(8 + shift[0], 8), :],
            behind(home_ref[1, tile, plane], shift[1]),
        )
        low = jnp.where(
            chain + shift[2] < 8,
            ahead(home_ref[2, tile, plane], shift[2]),
            from_right[tile, plane, pl.ds(shift[2], 8), :],
        )
        end = jnp.where(
            chain + shift[3] < 8,
            ahead(home_ref[3, tile, plane], shift[3]),
            from_right[tile, plane, pl.ds(shift[2] + jnp.minimum(shift[3], 8), 8), :],
        )
        if far:
            far_part = window[tile, plane, pl.ds(shift[3], 8), :]
            end = jnp.where(chain + shift[3] < 16, end, far_part)
        for idx, row in enumerate((top, mid, low, end)):
            point[idx][plane].append(row)
    point = [[jnp.concatenate(rows, axis=1) for rows in level] for level in point]
    for idx in range(4):
        for plane in range(planes):
            chain_ref[idx, plane] = point[idx][plane]
    show, fold = scale_columns(point)
    ranges[...] = jnp.zeros(ranges.shape, jnp.float32)
    range_one = wide_row(ranges, 0, one_ref)
    range_two = wide_row(ranges, 1, two_ref)

    def put(start, stop, found):
        for idx in range(4):
            for slot in range(4):
                value_ref[idx, slot, :, start:stop] = found[idx][slot]

    square_ref[...] = operator_q(
        point, show, fold, range_one, range_two, block_ref, cols, put
    )


def rate_of(parts_ref, entry_count):
    square_sum = jnp.sum(parts_ref[...], axis=0, keepdims=True)[:, 0:1]
    return step_scale / jnp.sqrt(square_sum / entry_count + eps_value)


def second_kernel(entry_count, size, far, shift_ref, chain_ref, value_ref, *rest):
    parts_ref, one_ref, two_ref, block_ref, own_ref, odd_ref, even_ref = rest[:7]
    rest = rest[7:]
    if far:
        far_ref, rest = rest[0], rest[1:]
    square_ref, stage, ranges, cols = rest
    _, tiles, planes, groups, _ = own_ref.shape
    rate = rate_of(parts_ref, entry_count)
    raw = [[chain_ref[idx, plane] for plane in range(3)] for idx in range(4)]
    show, fold = scale_columns(raw)
    point = [
        [
            raw[idx][plane] + rate * (value_ref[idx, plane + 1] - value_ref[idx, 0])
            for plane in range(3)
        ]
        for idx in range(4)
    ]
    ranges[...] = jnp.zeros(ranges.shape, jnp.float32)
    range_one = wide_row(ranges, 0, one_ref)
    range_two = wide_row(ranges, 1, two_ref)

    def put(start, stop, found):
        for idx in range(4):
            for slot in range(4):
                for lane in range(start, stop, LANES):
                    row = found[idx][slot][:, lane - start : lane - start + LANES]
                    own_ref[idx, lane // LANES, slot] = row

    square_ref[...] = operator_q(
        point, show, fold, range_one, range_two, block_ref, cols, put, value_ref
    )
    shift = shifts_in(shift_ref)
    fill_messages(
        lax.axis_index("node"),
        stage,
        (odd_ref, even_ref),
        size,
        own_ref,
        [(0, 8), (1, 8 + shift[0])],
        [(3, shift[2] + jnp.minimum(shift[3], 8)), (2, shift[2])],
    )
    if far:
        for tile in range(tiles):
            for plane in range(planes):
                part = stage.at[0, tile, plane]
                part[pl.ds(jnp.maximum(shift[3] - 8, 0), 8), :] = own_ref[3, tile, plane]
                far_ref[tile, plane * FAR : plane * FAR + FAR, :] = part[8 : 8 + FAR, :]


def last_kernel(entry_count, size, far, shift_ref, own_ref, even_ref, odd_ref, *rest):
    far_ref, rest = (rest[0], rest[1:]) if far else (None, rest)
    parts_ref, logits_ref, new_hbm, half_hbm, from_left, from_right, lined = rest[:7]
    new_ref, half_ref, sems = rest[7:]
    _, tiles, planes, groups, _ = own_ref.shape
    hands = logits_ref.shape[-1]
    shift = shifts_in(shift_ref)
    rate = rate_of(parts_ref, entry_count)
    group = lax.broadcasted_iota(jnp.int32, (groups, LANES), 0)
    spread_messages(lax.axis_index("node"), from_left, from_right, odd_ref, even_ref, size)
    places = [(tile, plane) for tile in range(tiles) for plane in range(planes)]

    def top(tile, plane, own):
        return jnp.where(
            group + shift[0] < 8,
            ahead(own, shift[0]),
            from_right[tile, plane, pl.ds(shift[0], 8), :],
        )

    def mid(tile, plane, own):
        return jnp.where(
            group + shift[1] < 8,
            ahead(own, shift[1]),
            from_right[tile, plane, pl.ds(shift[0] + shift[1], 8), :],
        )

    def low(tile, plane, own):
        return jnp.where(
            group < shift[2], from_left[tile, plane, 8:16, :], behind(own, shift[2])
        )

    def end(tile, plane, own):
        row = jnp.where(
            group < shift[3],
            from_left[tile, plane, pl.ds(8 + shift[2] - jnp.maximum(shift[3] - 8, 0), 8), :],
            behind(own, shift[3]),
        )
        if far:
            far_part = far_ref[tile, plane * FAR : plane * FAR + 8, :]
            row = jnp.where(group < shift[3] - 8, far_part, row)
        return row

    leaving = []

    def leave(source, target, kind, idx):
        leaving.append(pltpu.make_async_copy(source.at[idx], target.at[0, idx], sems.at[kind, idx]))
        leaving[-1].start()

    for idx, found in enumerate((top, mid, low, end)):
        for tile, plane in places:
            row = found(tile, plane, own_ref[idx, tile, plane])
            lined[idx, tile, pl.ds(plane, groups, stride=4), :] = row
        for tile in range(tiles):
            start = tile * LANES
            stop = min(start + LANES, hands)
            value = lined[idx, tile][:, 0 : stop - start]
            half_ref[idx, :, start:stop] = value
            new_ref[idx, :, start:stop] = logits_ref[0, idx, :, start:stop] + rate * value
        leave(half_ref, half_hbm, 0, idx)
        leave(new_ref, new_hbm, 1, idx)
    for copy in leaving:
        copy.wait()


def shared_parts(part):
    count = lax.axis_size("node") * lax.axis_size("board")
    spread = jnp.broadcast_to(part, (count, LANES))
    return lax.all_to_all(spread, ("node", "board"), 0, 0, tiled=True)


def shared_parts_over_nodes(part):
    nodes = lax.axis_size("node")
    boards = lax.axis_size("board")
    total = part
    for turn in range(1, boards):
        pairs = [(board, (board + turn) % boards) for board in range(boards)]
        total = total + lax.ppermute(part, "board", pairs)
    spread = jnp.broadcast_to(total, (nodes, LANES))
    order = [list(range(nodes))[::-1]]
    return lax.all_to_all(spread, "node", 0, 0, axis_index_groups=order, tiled=True)


def step_of_class(
    size,
    far,
    home,
    shift,
    logits,
    pot_size,
    node_type,
    parent_slot,
    range_one,
    range_two,
    hand_rank,
    live_mask,
):
    _, levels, slots, hands = logits.shape
    wide = padded(hands)
    tiles = wide // LANES
    groups = slots // 4
    entry_count = float(logits.size * lax.axis_size("node") * lax.axis_size("board"))
    vmem = pl.BlockSpec(memory_space=pltpu.VMEM)
    f32 = jnp.float32

    def limit(mebi):
        return pltpu.CompilerParams(vmem_limit_bytes=mebi * MEBI)

    def stage(planes, rows=32):
        return pltpu.VMEM((tiles, planes, rows, LANES), f32)

    def two_stages(planes):
        return pltpu.VMEM((2, tiles, planes, 32, LANES), f32)

    anywhere = pl.BlockSpec(memory_space=pl.ANY)
    sent = pl.pallas_call(
        functools.partial(pack_kernel, size, far),
        out_shape=message_shapes(3, wide, size, far),
        in_specs=[vmem, vmem] + [anywhere] * 3,
        scratch_shapes=[two_stages(3)],
        compiler_params=limit(8),
        name="pack",
    )(shift, home, pot_size, node_type, parent_slot)
    got = sent_on(sent[0], sent[1], sent[2:], -2, (0, 1))
    blocks = payoff_blocks(hand_rank, live_mask)
    blocks_all = 3 * 3 + 4 + 3 * 2
    rows = 16 * (-(-blocks_all // 2))
    rows_second = 16 * (-(-(blocks_all - 3) // 2))

    def work(count):
        return [
            pltpu.VMEM((8, wide), f32),
            pltpu.VMEM((count, 2 * wide), jnp.bfloat16),
        ]

    def cost(count):
        return pl.CostEstimate(
            flops=4 * count * wide * wide, bytes_accessed=6 * wide * wide, transcendentals=0
        )

    square_shape = jax.ShapeDtypeStruct((1, LANES), f32)
    chain, value, part = pl.pallas_call(
        functools.partial(first_kernel, size, far),
        out_shape=(
            jax.ShapeDtypeStruct((levels, 3, groups, wide), f32),
            jax.ShapeDtypeStruct((levels, 4, groups, wide), f32),
            square_shape,
        ),
        in_specs=[vmem] * (5 + len(got)),
        scratch_shapes=[stage(3), stage(3), stage(3)] + work(rows),
        compiler_params=limit(32),
        cost_estimate=cost(rows),
        name="first",
    )(shift, home, *got, range_one, range_two, blocks)
    parts = shared_parts(part)
    own, *sent, part = pl.pallas_call(
        functools.partial(second_kernel, entry_count, size, far),
        out_shape=[jax.ShapeDtypeStruct((levels, tiles, 4, groups, LANES), f32)]
        + message_shapes(4, wide, size, far)
        + [square_shape],
        in_specs=[vmem] * 7,
        scratch_shapes=[two_stages(4)] + work(rows_second),
        compiler_params=limit(32),
        cost_estimate=cost(rows_second),
        name="second",
    )(shift, chain, value, parts, range_one, range_two, blocks)
    got = sent_on(sent[0], sent[1], sent[2:], 2, (1, 0))
    parts = shared_parts_over_nodes(part)
    out_shape = jax.ShapeDtypeStruct(logits.shape, f32)
    level_shape = (levels, slots, hands)
    return pl.pallas_call(
        functools.partial(last_kernel, entry_count, size, far),
        out_shape=(out_shape, out_shape),
        in_specs=[vmem] * (4 + len(got)),
        out_specs=(anywhere, anywhere),
        scratch_shapes=[
            stage(4),
            stage(4),
            pltpu.VMEM((levels, tiles, slots, LANES), f32),
            pltpu.VMEM(level_shape, f32),
            pltpu.VMEM(level_shape, f32),
            pltpu.SemaphoreType.DMA((2, levels)),
        ],
        compiler_params=limit(24),
        name="last",
    )(shift, own, got[1], got[0], *got[2:], parts, logits)


def per_device(
    logits, pot_size, node_type, parent_slot, range_one, range_two, hand_rank, live_mask
):
    branches = [
        functools.partial(step_of_class, size, size == CLASSES[-1]) for size in CLASSES
    ]
    home, shift, found = prepared(logits, pot_size, node_type, parent_slot)
    return lax.switch(
        found[0, 0],
        branches,
        home,
        shift,
        logits,
        pot_size,
        node_type,
        parent_slot,
        range_one,
        range_two,
        hand_rank,
        live_mask,
    )


def solution(mesh):
    return jax.shard_map(
        per_device,
        mesh=mesh,
        in_specs=(
            P("board", None, "node", None),
            P(None, "node"),
            P(None, "node"),
            P(None, "node"),
            P("board", None),
            P("board", None),
            P("board", None),
            P("board", None),
        ),
        out_specs=(P("board", None, "node", None), P("board", None, "node", None)),
        check_vma=False,
    )
```

```python
import functools

import jax
import jax.numpy as jnp
import numpy as np
from jax import lax
from jax.experimental import pallas as pl
from jax.experimental.pallas import tpu as pltpu
from jax.sharding import PartitionSpec as P

LANES = 128
CARDS = 52
step_scale = 0.5
eps_value = 1e-06
MEBI = 1 << 20
CLASSES = (5, 8, 10, 12, 14)
FAR = 5


def padded(count):
    return -(-count // LANES) * LANES


def card_rows(hand_count, wide):
    pairs = [(low, high) for low in range(CARDS) for high in range(low + 1, CARDS)]
    rows = np.full((2, wide), -1, np.int32)
    rows[:, :hand_count] = np.array(pairs[:hand_count], np.int32).T
    return rows


def payoff_kernel(
    hands, cards_ref, rank_ref, live_ref, out_ref, flat, left, right, left_turned, rank_turned
):
    wide = out_ref.shape[1]
    flat[...] = jnp.zeros(flat.shape, jnp.float32)
    flat[0:1, 0:hands] = rank_ref[...].astype(jnp.float32)
    flat[1:2, 0:hands] = (live_ref[...] > 0).astype(jnp.float32)
    dead = 1.0 - flat[1:2, :]
    feature = lax.broadcasted_iota(jnp.int32, (LANES, wide), 0)
    hit = (feature == cards_ref[0:1, :]) | (feature == cards_ref[1:2, :])
    base = jnp.where(hit, 1.0, 0.0)
    left[...] = jnp.where(feature == CARDS, dead, jnp.where(feature == CARDS + 1, 1.0, base))
    right[...] = jnp.where(
        feature == CARDS, 1.0, jnp.where(feature == CARDS + 1, dead, base)
    ).astype(jnp.bfloat16)
    rank_row = flat[0:1, :]
    for block in range(wide // LANES):
        part = slice(block * LANES, (block + 1) * LANES)
        left_turned[part, :] = left[:, part].T.astype(jnp.bfloat16)
        rank_turned[part, :] = jnp.broadcast_to(flat[0:1, part], (LANES, LANES)).T

    @pl.loop(0, wide // LANES)
    def _(block):
        begin = pl.multiple_of(block * LANES, LANES)
        part = pl.ds(begin, LANES)
        hits = jnp.dot(left_turned[part, :], right[...], preferred_element_type=jnp.float32)
        compat = jnp.where(hits == 0.0, 1.0, 0.0)
        order = jnp.clip(rank_row - rank_turned[part, 0:1], -1.0, 1.0)
        out_ref[part, :] = (order * compat).astype(jnp.bfloat16)
        out_ref[pl.ds(begin + wide, LANES), :] = compat.astype(jnp.bfloat16)


def payoff_blocks(hand_rank, live_mask):
    hands = hand_rank.shape[-1]
    wide = padded(hands)
    return pl.pallas_call(
        functools.partial(payoff_kernel, hands),
        out_shape=jax.ShapeDtypeStruct((2 * wide, wide), jnp.bfloat16),
        scratch_shapes=[
            pltpu.VMEM((8, wide), jnp.float32),
            pltpu.VMEM((LANES, wide), jnp.float32),
            pltpu.VMEM((LANES, wide), jnp.bfloat16),
            pltpu.VMEM((wide, LANES), jnp.bfloat16),
            pltpu.VMEM((wide, LANES), jnp.float32),
        ],
        compiler_params=pltpu.CompilerParams(vmem_limit_bytes=20 * MEBI),
        cost_estimate=pl.CostEstimate(
            flops=2 * wide * wide * LANES, bytes_accessed=4 * wide * wide, transcendentals=0
        ),
        name="payoff",
    )(jnp.asarray(card_rows(hands, wide)), hand_rank, live_mask)


def row_count(planes, groups):
    return -(-planes * groups // 8) * 8


def plan_of(parent_ref, node_count, groups):
    total = groups * node_count
    first = lax.axis_index("node") * groups
    off = [lax.rem(first - (parent_ref[idx, 0] >> 2) + total, total) for idx in (1, 2, 3)]
    one = off[0]
    two = one + off[1]
    three = two + off[2]
    low = jnp.maximum(one, three - groups)
    high = jnp.minimum(two, groups)
    middle = jnp.minimum(jnp.maximum((one + two + three + 2) >> 2, low), high)
    return middle, middle - one, two - middle, three - middle


def class_of(shift, groups):
    near = jnp.where(shift[3] > groups, 2 * groups - shift[3], shift[3])
    need = jnp.maximum(shift[0] + shift[1], shift[2] + near)
    found = jnp.int32(0)
    for size in CLASSES[:-1]:
        found = found + (need > size).astype(jnp.int32)
    return jnp.where(shift[3] > groups, len(CLASSES) - 1, found)


def fill_messages(
    node, stage, message_refs, size, block_ref, to_left, to_right, skipped=None
):
    _, tiles, planes = stage.shape[:3]
    even = lax.rem(node, 2) == 0
    places = [(tile, plane) for tile in range(tiles) for plane in range(planes)]
    for side, on_left in enumerate((even, jnp.logical_not(even))):
        for near, far in zip(to_left, to_right):
            level = jnp.where(on_left, near[0], far[0])
            start = jnp.where(on_left, near[1], far[1])
            for tile, plane in places:
                block = block_ref[level, tile, plane]
                if skipped is not None:
                    block = ahead(block, jnp.where(level == 3, skipped, 0))
                stage[side, tile, plane, pl.ds(start, 8), :] = block
    for side, message_ref in enumerate(message_refs):
        for tile, plane in places:
            message_ref[tile, plane * size : plane * size + size, :] = stage[
                side, tile, plane, 8 : 8 + size, :
            ]


def prepare_kernel(
    node_count,
    parent_hbm,
    logits_hbm,
    pot_hbm,
    kind_hbm,
    home_ref,
    shift_ref,
    class_ref,
    parent_ref,
    logits_ref,
    pot_ref,
    kind_ref,
    raw,
    flat,
    turned,
    sems,
):
    levels, tiles, planes, groups, _ = home_ref.shape
    slots = 4 * groups
    hands = logits_ref.shape[-1]
    fetches = [
        pltpu.make_async_copy(logits_hbm.at[0, idx], logits_ref.at[idx], sems.at[idx])
        for idx in range(levels)
    ]
    tables = [
        pltpu.make_async_copy(source, target, sems.at[levels + idx])
        for idx, (source, target) in enumerate(
            ((parent_hbm, parent_ref), (pot_hbm, pot_ref), (kind_hbm, kind_ref))
        )
    ]
    for fetch in tables + fetches:
        fetch.start()
    for fetch in tables:
        fetch.wait()
    shift = plan_of(parent_ref, node_count, groups)
    row_id = lax.broadcasted_iota(jnp.int32, shift_ref.shape, 0)
    spread = jnp.zeros(shift_ref.shape, jnp.int32)
    class_ref[...] = jnp.full((1, 1), class_of(shift, groups))
    for idx, value in enumerate(shift):
        spread = jnp.where(row_id == idx, value, spread)
    shift_ref[...] = spread
    pot = pot_ref[...]
    kind = kind_ref[...]
    level = lax.broadcasted_iota(jnp.int32, pot.shape, 0)
    sign = jnp.where(level % 2 == 0, -1.0, 1.0)
    flat[...] = jnp.zeros(flat.shape, jnp.float32)
    flat[0:levels, 0:slots] = jnp.where(kind == 2, pot, 0.0)
    flat[levels : 2 * levels, 0:slots] = jnp.where(kind == 1, pot, 0.0) * sign
    turned[...] = flat[...].T
    lane = lax.broadcasted_iota(jnp.int32, (groups, LANES), 1)
    for idx in range(levels):
        raw[idx, tiles - 1] = jnp.zeros((slots, LANES), jnp.float32)
    for idx in range(levels):
        fetches[idx].wait()
        for tile in range(tiles):
            start = tile * LANES
            stop = min(start + LANES, hands)
            raw[idx, tile, :, 0 : stop - start] = logits_ref[idx, :, start:stop]
            first = raw[idx, tile, pl.ds(0, groups, stride=4), :]
            for plane in range(planes):
                row = raw[idx, tile, pl.ds(plane + 1, groups, stride=4), :] - first
                if tile == tiles - 1 and plane == 0:
                    for slot in range(4):
                        scale = turned[pl.ds(slot, groups, stride=4), :]
                        row = jnp.where(lane == LANES - 8 + slot, scale[:, idx : idx + 1], row)
                        fold = scale[:, levels + idx : levels + idx + 1]
                        row = jnp.where(lane == LANES - 4 + slot, fold, row)
                home_ref[idx, tile, plane] = row


def prepared(logits, pot_size, node_type, parent_slot):
    _, levels, slots, hands = logits.shape
    groups = slots // 4
    tiles = padded(hands) // LANES
    vmem = pl.BlockSpec(memory_space=pltpu.VMEM)
    return pl.pallas_call(
        functools.partial(prepare_kernel, lax.axis_size("node")),
        out_shape=(
            jax.ShapeDtypeStruct((levels, tiles, 3, groups, LANES), jnp.float32),
            jax.ShapeDtypeStruct((8, LANES), jnp.int32),
            jax.ShapeDtypeStruct((1, 1), jnp.int32),
        ),
        in_specs=[pl.BlockSpec(memory_space=pl.ANY)] * 4,
        out_specs=(vmem, vmem, vmem),
        scratch_shapes=[
            pltpu.SMEM(parent_slot.shape, jnp.int32),
            pltpu.VMEM((levels, slots, hands), jnp.float32),
            pltpu.VMEM(pot_size.shape, jnp.float32),
            pltpu.VMEM(node_type.shape, jnp.int32),
            pltpu.VMEM((levels, tiles, slots, LANES), jnp.float32),
            pltpu.VMEM((LANES, LANES), jnp.float32),
            pltpu.VMEM((LANES, LANES), jnp.float32),
            pltpu.SemaphoreType.DMA((levels + 3,)),
        ],
        compiler_params=pltpu.CompilerParams(vmem_limit_bytes=10 * MEBI),
        name="prepare",
    )(parent_slot, logits, pot_size, node_type)


def ahead(rows, count):
    return pltpu.roll(rows, (8 - count) & 7, 0)


def behind(rows, count):
    return pltpu.roll(rows, count & 7, 0)


def shifts_in(shift_ref):
    return [jnp.max(shift_ref[idx : idx + 1, :]) for idx in range(4)]


def pack_kernel(size, far, shift_ref, home_ref, _pot, _kind, _parent, odd_ref, even_ref, *rest):
    far_ref = rest[0] if far else None
    stage = rest[-1]
    _, tiles, planes, groups, _ = home_ref.shape
    shift = shifts_in(shift_ref)
    skipped = jnp.maximum(shift[3] - 8, 0) if far else None
    fill_messages(
        lax.axis_index("node"),
        stage,
        (odd_ref, even_ref),
        size,
        home_ref,
        [(2, 8), (3, 8 + shift[2])],
        [(1, shift[0] + shift[1]), (0, shift[0])],
        skipped,
    )
    if far:
        for tile in range(tiles):
            for plane in range(planes):
                far_ref[tile, plane * FAR : plane * FAR + FAR, :] = home_ref[3, tile, plane, 0:FAR, :]


def message_shapes(planes, wide, size, far):
    tiles = wide // LANES
    message = jax.ShapeDtypeStruct((tiles, row_count(planes, size), LANES), jnp.float32)
    shapes = [message] * 2
    if far:
        shapes.append(jax.ShapeDtypeStruct((tiles, row_count(planes, FAR), LANES), jnp.float32))
    return shapes


def sent_on(odd, even, far, far_steps, order):
    count = lax.axis_size("node")
    edges = [(src, (src + 1) % count) for src in range(count)]
    got = [None, None]
    for side in order:
        pairs = [pair for edge in edges[1 - side :: 2] for pair in (edge, edge[::-1])]
        got[side] = lax.ppermute((odd, even)[side], "node", pairs)
    for message in far:
        pairs = [(src, (src + far_steps) % count) for src in range(count)]
        got.append(lax.ppermute(message, "node", pairs))
    return got


def spread_messages(node, from_left, from_right, odd_ref, even_ref, size):
    tiles, planes = from_left.shape[:2]
    even = lax.rem(node, 2) == 0
    for tile in range(tiles):
        for plane in range(planes):
            place = slice(plane * size, plane * size + size)
            odd_part = odd_ref[tile, place, :]
            even_part = even_ref[tile, place, :]
            from_left[tile, plane, 8 : 8 + size, :] = jnp.where(even, odd_part, even_part)
            from_right[tile, plane, 8 : 8 + size, :] = jnp.where(even, even_part, odd_part)


def inner_sum(inner, rows):
    total = jnp.where(inner[0], rows[0], 0.0)
    for idx in range(1, 4):
        total = total + jnp.where(inner[idx], rows[idx], 0.0)
    return total


def inner_before(inner):
    one = inner[0] | inner[1]
    return [inner[0], one, one | inner[2]]


def exponentials(rows):
    top = jnp.maximum(jnp.maximum(rows[0], rows[1]), jnp.maximum(rows[2], 0.0))
    lifted = [jnp.exp(-top)] + [jnp.exp(row - top) for row in rows]
    return lifted, 1.0 / ((lifted[0] + lifted[1]) + (lifted[2] + lifted[3]))


def softmax_four(rows):
    lifted, share = exponentials(rows)
    return [row * share for row in lifted]


def operator_q(point, show, fold, range_one, range_two, block_ref, cols, put, top_ref=None):
    wide = block_ref.shape[1]
    inner = [
        [(show[idx][slot] == 0.0) & (fold[idx][slot] == 0.0) for slot in range(4)]
        for idx in range(4)
    ]
    lifted, share = exponentials(point[0])
    above_one = range_one * (inner_sum(inner[0], lifted) * share)
    strategy = [None] + [softmax_four(point[idx]) for idx in range(1, 4)]
    mid_two = [range_two * row for row in strategy[1]]
    above_two = inner_sum(inner[1], mid_two)
    low_one = [above_one * row for row in strategy[2]]
    last_one = inner_sum(inner[2], low_one)
    end_two = [above_two * row for row in strategy[3]]
    wide_two = jnp.broadcast_to(range_two, above_two.shape)
    past = [inner_before(inner[idx]) for idx in range(3)]

    units = [
        (0, [wide_two] * 4, 1.0, False),
        (1, mid_two, 1.0, True),
        (2, [above_two] * 4, 1.0, False),
        (3, end_two, 1.0, True),
        (1, [above_one] * 4, -1.0, False),
        (2, low_one, -1.0, True),
        (3, [last_one] * 4, -1.0, False),
    ]
    first_unit = 0 if top_ref is None else 1
    begin = [0] * len(units)
    for side in range(2):
        blocks = []
        for unit in range(first_unit, len(units)):
            idx, rows, fold_sign, as_sum = units[unit]
            begin[unit] = 8 * len(blocks)
            if side == 0:
                scaled = [rows[slot] * show[idx][slot] for slot in range(4)]
            else:
                scaled = [rows[slot] * (fold[idx][slot] * fold_sign) for slot in range(4)]
            if as_sum:
                rounded = [row.astype(jnp.bfloat16).astype(jnp.float32) for row in scaled]
                total = (rounded[0] + rounded[1]) + (rounded[2] + rounded[3])
                high = total.astype(jnp.bfloat16).astype(jnp.float32)
                scaled = [high, total - high]
            elif idx < 3:
                scaled = [
                    jnp.where(past[idx][slot], scaled[slot + 1], scaled[slot]) for slot in range(3)
                ]
            blocks += scaled
        if len(blocks) % 2:
            blocks.append(jnp.zeros_like(blocks[0]))
        lanes = slice(side * wide, side * wide + wide)
        for pair in range(0, len(blocks), 2):
            cols[pair * 8 : pair * 8 + 16, lanes] = jnp.concatenate(
                blocks[pair : pair + 2], axis=0
            ).astype(jnp.bfloat16)

    def added(rows):
        return (rows[0] + rows[1]) + (rows[2] + rows[3])

    def landed(rows, kept, term):
        return [jnp.where(kept[slot], term, rows[slot]) for slot in range(4)]

    total = None
    for start in range(0, wide, 2 * LANES):
        stop = min(start + 2 * LANES, wide)
        pay = jnp.dot(cols[...], block_ref[:, start:stop], preferred_element_type=jnp.float32)

        def paid(unit):
            at = begin[unit]
            idx = units[unit][0]
            rows = [pay[at + slot * 8 : at + slot * 8 + 8, :] for slot in range(4 if idx == 3 else 3)]
            if idx < 3:
                rows = [
                    rows[0],
                    jnp.where(past[idx][0], rows[0], rows[1]),
                    jnp.where(past[idx][1], rows[1], rows[2]),
                    rows[2],
                ]
            return rows

        def paid_sum(unit):
            at = begin[unit]
            return pay[at : at + 8, :] + pay[at + 8 : at + 16, :]

        def weighed(idx, rows):
            return added([strategy[idx][slot][:, start:stop] * rows[slot] for slot in range(4)])

        value_two_end = paid(6)
        term_two = paid_sum(5) + weighed(3, value_two_end)
        value_two_mid = landed(paid(4), inner[1], term_two)
        value_one_low = landed(paid(2), inner[2], paid_sum(3))
        term_one = paid_sum(1) + weighed(2, value_one_low)
        if top_ref is None:
            value_one_top = landed(paid(0), inner[0], term_one)
        else:
            value_one_top = [
                jnp.where(inner[0][slot], term_one, top_ref[0, slot, :, start:stop])
                for slot in range(4)
            ]
        found = [value_one_top, value_two_mid, value_one_low, value_two_end]
        put(start, stop, found)
        part = squares(found)
        total = part if total is None else total + part
    return total


def squares(found):
    total = None
    for rows in found:
        for row in rows:
            total = row * row if total is None else total + row * row
    return jnp.broadcast_to(jnp.sum(total), (1, LANES))


def scale_columns(rows):
    wide = rows[0][0].shape[1]
    show = [
        [level[0][:, wide - 8 + slot : wide - 7 + slot] for slot in range(4)] for level in rows
    ]
    fold = [
        [level[0][:, wide - 4 + slot : wide - 4 + slot + 1] for slot in range(4)] for level in rows
    ]
    return show, fold


def wide_row(store, place, row_ref):
    hands = row_ref.shape[1]
    store[place : place + 1, 0:hands] = row_ref[...]
    return store[place : place + 1, :]


def first_kernel(size, far, shift_ref, home_ref, odd_ref, even_ref, *rest):
    if far:
        far_ref, rest = rest[0], rest[1:]
    one_ref, two_ref, block_ref, chain_ref, value_ref, square_ref = rest[:6]
    from_left, from_right, window, ranges, cols = rest[6:]
    _, tiles, planes, groups, _ = home_ref.shape
    shift = shifts_in(shift_ref)
    spread_messages(lax.axis_index("node"), from_left, from_right, odd_ref, even_ref, size)
    chain = lax.broadcasted_iota(jnp.int32, (groups, LANES), 0)
    places = [(tile, plane) for tile in range(tiles) for plane in range(planes)]
    if far:
        for tile, plane in places:
            window[tile, plane, 16 : 16 + FAR, :] = far_ref[
                tile, plane * FAR : plane * FAR + FAR, :
            ]
    point = [[[] for _ in range(planes)] for _ in range(4)]
    for tile, plane in places:
        top = jnp.where(
            chain < shift[0],
            from_left[tile, plane, 8:16, :],
            behind(home_ref[0, tile, plane], shift[0]),
        )
        mid = jnp.where(
            chain < shift[1],
            from_left[tile, plane, pl.ds(8 + shift[0], 8), :],
            behind(home_ref[1, tile, plane], shift[1]),
        )
        low = jnp.where(
            chain + shift[2] < 8,
            ahead(home_ref[2, tile, plane], shift[2]),
            from_right[tile, plane, pl.ds(shift[2], 8), :],
        )
        end = jnp.where(
            chain + shift[3] < 8,
            ahead(home_ref[3, tile, plane], shift[3]),
            from_right[tile, plane, pl.ds(shift[2] + jnp.minimum(shift[3], 8), 8), :],
        )
        if far:
            far_part = window[tile, plane, pl.ds(shift[3], 8), :]
            end = jnp.where(chain + shift[3] < 16, end, far_part)
        for idx, row in enumerate((top, mid, low, end)):
            point[idx][plane].append(row)
    point = [[jnp.concatenate(rows, axis=1) for rows in level] for level in point]
    for idx in range(4):
        for plane in range(planes):
            chain_ref[idx, plane] = point[idx][plane]
    show, fold = scale_columns(point)
    ranges[...] = jnp.zeros(ranges.shape, jnp.float32)
    range_one = wide_row(ranges, 0, one_ref)
    range_two = wide_row(ranges, 1, two_ref)

    def put(start, stop, found):
        for idx in range(4):
            for slot in range(4):
                value_ref[idx, slot, :, start:stop] = found[idx][slot]

    square_ref[...] = operator_q(
        point, show, fold, range_one, range_two, block_ref, cols, put
    )


def rate_of(parts_ref, entry_count):
    square_sum = jnp.sum(parts_ref[...], axis=0, keepdims=True)[:, 0:1]
    return step_scale / jnp.sqrt(square_sum / entry_count + eps_value)


def second_kernel(entry_count, size, far, shift_ref, chain_ref, value_ref, *rest):
    parts_ref, one_ref, two_ref, block_ref, own_ref, odd_ref, even_ref = rest[:7]
    rest = rest[7:]
    if far:
        far_ref, rest = rest[0], rest[1:]
    square_ref, stage, ranges, cols = rest
    _, tiles, planes, groups, _ = own_ref.shape
    rate = rate_of(parts_ref, entry_count)
    raw = [[chain_ref[idx, plane] for plane in range(3)] for idx in range(4)]
    show, fold = scale_columns(raw)
    point = [
        [
            raw[idx][plane] + rate * (value_ref[idx, plane + 1] - value_ref[idx, 0])
            for plane in range(3)
        ]
        for idx in range(4)
    ]
    ranges[...] = jnp.zeros(ranges.shape, jnp.float32)
    range_one = wide_row(ranges, 0, one_ref)
    range_two = wide_row(ranges, 1, two_ref)

    def put(start, stop, found):
        for idx in range(4):
            for slot in range(4):
                for lane in range(start, stop, LANES):
                    row = found[idx][slot][:, lane - start : lane - start + LANES]
                    own_ref[idx, lane // LANES, slot] = row

    square_ref[...] = operator_q(
        point, show, fold, range_one, range_two, block_ref, cols, put, value_ref
    )
    shift = shifts_in(shift_ref)
    fill_messages(
        lax.axis_index("node"),
        stage,
        (odd_ref, even_ref),
        size,
        own_ref,
        [(0, 8), (1, 8 + shift[0])],
        [(3, shift[2] + jnp.minimum(shift[3], 8)), (2, shift[2])],
    )
    if far:
        for tile in range(tiles):
            for plane in range(planes):
                part = stage.at[0, tile, plane]
                part[pl.ds(jnp.maximum(shift[3] - 8, 0), 8), :] = own_ref[3, tile, plane]
                far_ref[tile, plane * FAR : plane * FAR + FAR, :] = part[8 : 8 + FAR, :]


def last_kernel(entry_count, size, far, shift_ref, own_ref, even_ref, odd_ref, *rest):
    far_ref, rest = (rest[0], rest[1:]) if far else (None, rest)
    parts_ref, logits_ref, new_hbm, half_hbm, from_left, from_right, lined = rest[:7]
    new_ref, half_ref, sems = rest[7:]
    _, tiles, planes, groups, _ = own_ref.shape
    hands = logits_ref.shape[-1]
    shift = shifts_in(shift_ref)
    rate = rate_of(parts_ref, entry_count)
    group = lax.broadcasted_iota(jnp.int32, (groups, LANES), 0)
    spread_messages(lax.axis_index("node"), from_left, from_right, odd_ref, even_ref, size)
    places = [(tile, plane) for tile in range(tiles) for plane in range(planes)]

    def top(tile, plane, own):
        return jnp.where(
            group + shift[0] < 8,
            ahead(own, shift[0]),
            from_right[tile, plane, pl.ds(shift[0], 8), :],
        )

    def mid(tile, plane, own):
        return jnp.where(
            group + shift[1] < 8,
            ahead(own, shift[1]),
            from_right[tile, plane, pl.ds(shift[0] + shift[1], 8), :],
        )

    def low(tile, plane, own):
        return jnp.where(
            group < shift[2], from_left[tile, plane, 8:16, :], behind(own, shift[2])
        )

    def end(tile, plane, own):
        row = jnp.where(
            group < shift[3],
            from_left[tile, plane, pl.ds(8 + shift[2] - jnp.maximum(shift[3] - 8, 0), 8), :],
            behind(own, shift[3]),
        )
        if far:
            far_part = far_ref[tile, plane * FAR : plane * FAR + 8, :]
            row = jnp.where(group < shift[3] - 8, far_part, row)
        return row

    leaving = []

    def leave(source, target, kind, idx):
        leaving.append(pltpu.make_async_copy(source.at[idx], target.at[0, idx], sems.at[kind, idx]))
        leaving[-1].start()

    for idx, found in enumerate((top, mid, low, end)):
        for tile, plane in places:
            row = found(tile, plane, own_ref[idx, tile, plane])
            lined[idx, tile, pl.ds(plane, groups, stride=4), :] = row
        for tile in range(tiles):
            start = tile * LANES
            stop = min(start + LANES, hands)
            value = lined[idx, tile][:, 0 : stop - start]
            half_ref[idx, :, start:stop] = value
            new_ref[idx, :, start:stop] = logits_ref[0, idx, :, start:stop] + rate * value
        leave(half_ref, half_hbm, 0, idx)
        leave(new_ref, new_hbm, 1, idx)
    for copy in leaving:
        copy.wait()


def shared_parts(part):
    count = lax.axis_size("node") * lax.axis_size("board")
    spread = jnp.broadcast_to(part, (count, LANES))
    return lax.all_to_all(spread, ("node", "board"), 0, 0, tiled=True)


def shared_parts_over_nodes(part):
    nodes = lax.axis_size("node")
    boards = lax.axis_size("board")
    total = part
    for turn in range(1, boards):
        pairs = [(board, (board + turn) % boards) for board in range(boards)]
        total = total + lax.ppermute(part, "board", pairs)
    spread = jnp.broadcast_to(total, (nodes, LANES))
    order = [list(range(nodes))[::-1]]
    return lax.all_to_all(spread, "node", 0, 0, axis_index_groups=order, tiled=True)


def step_of_class(
    size,
    far,
    home,
    shift,
    logits,
    pot_size,
    node_type,
    parent_slot,
    range_one,
    range_two,
    hand_rank,
    live_mask,
):
    _, levels, slots, hands = logits.shape
    wide = padded(hands)
    tiles = wide // LANES
    groups = slots // 4
    entry_count = float(logits.size * lax.axis_size("node") * lax.axis_size("board"))
    vmem = pl.BlockSpec(memory_space=pltpu.VMEM)
    f32 = jnp.float32

    def limit(mebi):
        return pltpu.CompilerParams(vmem_limit_bytes=mebi * MEBI)

    def stage(planes, rows=32):
        return pltpu.VMEM((tiles, planes, rows, LANES), f32)

    def two_stages(planes):
        return pltpu.VMEM((2, tiles, planes, 32, LANES), f32)

    anywhere = pl.BlockSpec(memory_space=pl.ANY)
    sent = pl.pallas_call(
        functools.partial(pack_kernel, size, far),
        out_shape=message_shapes(3, wide, size, far),
        in_specs=[vmem, vmem] + [anywhere] * 3,
        scratch_shapes=[two_stages(3)],
        compiler_params=limit(8),
        name="pack",
    )(shift, home, pot_size, node_type, parent_slot)
    got = sent_on(sent[0], sent[1], sent[2:], -2, (0, 1))
    blocks = payoff_blocks(hand_rank, live_mask)
    blocks_all = 3 * 3 + 4 + 3 * 2
    rows = 16 * (-(-blocks_all // 2))
    rows_second = 16 * (-(-(blocks_all - 3) // 2))

    def work(count):
        return [
            pltpu.VMEM((8, wide), f32),
            pltpu.VMEM((count, 2 * wide), jnp.bfloat16),
        ]

    def cost(count):
        return pl.CostEstimate(
            flops=4 * count * wide * wide, bytes_accessed=6 * wide * wide, transcendentals=0
        )

    square_shape = jax.ShapeDtypeStruct((1, LANES), f32)
    chain, value, part = pl.pallas_call(
        functools.partial(first_kernel, size, far),
        out_shape=(
            jax.ShapeDtypeStruct((levels, 3, groups, wide), f32),
            jax.ShapeDtypeStruct((levels, 4, groups, wide), f32),
            square_shape,
        ),
        in_specs=[vmem] * (5 + len(got)),
        scratch_shapes=[stage(3), stage(3), stage(3)] + work(rows),
        compiler_params=limit(32),
        cost_estimate=cost(rows),
        name="first",
    )(shift, home, *got, range_one, range_two, blocks)
    parts = shared_parts(part)
    own, *sent, part = pl.pallas_call(
        functools.partial(second_kernel, entry_count, size, far),
        out_shape=[jax.ShapeDtypeStruct((levels, tiles, 4, groups, LANES), f32)]
        + message_shapes(4, wide, size, far)
        + [square_shape],
        in_specs=[vmem] * 7,
        scratch_shapes=[two_stages(4)] + work(rows_second),
        compiler_params=limit(32),
        cost_estimate=cost(rows_second),
        name="second",
    )(shift, chain, value, parts, range_one, range_two, blocks)
    got = sent_on(sent[0], sent[1], sent[2:], 2, (1, 0))
    parts = shared_parts_over_nodes(part)
    out_shape = jax.ShapeDtypeStruct(logits.shape, f32)
    level_shape = (levels, slots, hands)
    return pl.pallas_call(
        functools.partial(last_kernel, entry_count, size, far),
        out_shape=(out_shape, out_shape),
        in_specs=[vmem] * (4 + len(got)),
        out_specs=(anywhere, anywhere),
        scratch_shapes=[
            stage(4),
            stage(4),
            pltpu.VMEM((levels, tiles, slots, LANES), f32),
            pltpu.VMEM(level_shape, f32),
            pltpu.VMEM(level_shape, f32),
            pltpu.SemaphoreType.DMA((2, levels)),
        ],
        compiler_params=limit(24),
        name="last",
    )(shift, own, got[1], got[0], *got[2:], parts, logits)


def per_device(
    logits, pot_size, node_type, parent_slot, range_one, range_two, hand_rank, live_mask
):
    branches = [
        functools.partial(step_of_class, size, size == CLASSES[-1]) for size in CLASSES
    ]
    home, shift, found = prepared(logits, pot_size, node_type, parent_slot)
    return lax.switch(
        found[0, 0],
        branches,
        home,
        shift,
        logits,
        pot_size,
        node_type,
        parent_slot,
        range_one,
        range_two,
        hand_rank,
        live_mask,
    )


def solution(mesh):
    return jax.shard_map(
        per_device,
        mesh=mesh,
        in_specs=(
            P("board", None, "node", None),
            P(None, "node"),
            P(None, "node"),
            P(None, "node"),
            P("board", None),
            P("board", None),
            P("board", None),
            P("board", None),
        ),
        out_specs=(P("board", None, "node", None), P("board", None, "node", None)),
        check_vma=False,
    )
```

```python
import functools

import jax
import jax.numpy as jnp
import numpy as np
from jax import lax
from jax.experimental import pallas as pl
from jax.experimental.pallas import tpu as pltpu
from jax.sharding import PartitionSpec as P

LANES = 128
CARDS = 52
step_scale = 0.5
eps_value = 1e-06
MEBI = 1 << 20
CLASSES = (5, 8, 10, 12, 14)
FAR = 5


def padded(count):
    return -(-count // LANES) * LANES


def card_rows(hand_count, wide):
    pairs = [(low, high) for low in range(CARDS) for high in range(low + 1, CARDS)]
    rows = np.full((2, wide), -1, np.int32)
    rows[:, :hand_count] = np.array(pairs[:hand_count], np.int32).T
    return rows


def payoff_kernel(
    hands, cards_ref, rank_ref, live_ref, out_ref, flat, left, right, left_turned, rank_turned
):
    wide = out_ref.shape[1]
    flat[...] = jnp.zeros(flat.shape, jnp.float32)
    flat[0:1, 0:hands] = rank_ref[...].astype(jnp.float32)
    flat[1:2, 0:hands] = (live_ref[...] > 0).astype(jnp.float32)
    dead = 1.0 - flat[1:2, :]
    feature = lax.broadcasted_iota(jnp.int32, (LANES, wide), 0)
    hit = (feature == cards_ref[0:1, :]) | (feature == cards_ref[1:2, :])
    base = jnp.where(hit, 1.0, 0.0)
    left[...] = jnp.where(feature == CARDS, dead, jnp.where(feature == CARDS + 1, 1.0, base))
    right[...] = jnp.where(
        feature == CARDS, 1.0, jnp.where(feature == CARDS + 1, dead, base)
    ).astype(jnp.bfloat16)
    rank_row = flat[0:1, :]
    for block in range(wide // LANES):
        part = slice(block * LANES, (block + 1) * LANES)
        left_turned[part, :] = left[:, part].T.astype(jnp.bfloat16)
        rank_turned[part, :] = jnp.broadcast_to(flat[0:1, part], (LANES, LANES)).T

    @pl.loop(0, wide // LANES)
    def _(block):
        begin = pl.multiple_of(block * LANES, LANES)
        part = pl.ds(begin, LANES)
        hits = jnp.dot(left_turned[part, :], right[...], preferred_element_type=jnp.float32)
        compat = jnp.where(hits == 0.0, 1.0, 0.0)
        order = jnp.clip(rank_row - rank_turned[part, 0:1], -1.0, 1.0)
        out_ref[part, :] = (order * compat).astype(jnp.bfloat16)
        out_ref[pl.ds(begin + wide, LANES), :] = compat.astype(jnp.bfloat16)


def payoff_blocks(hand_rank, live_mask):
    hands = hand_rank.shape[-1]
    wide = padded(hands)
    return pl.pallas_call(
        functools.partial(payoff_kernel, hands),
        out_shape=jax.ShapeDtypeStruct((2 * wide, wide), jnp.bfloat16),
        scratch_shapes=[
            pltpu.VMEM((8, wide), jnp.float32),
            pltpu.VMEM((LANES, wide), jnp.float32),
            pltpu.VMEM((LANES, wide), jnp.bfloat16),
            pltpu.VMEM((wide, LANES), jnp.bfloat16),
            pltpu.VMEM((wide, LANES), jnp.float32),
        ],
        compiler_params=pltpu.CompilerParams(vmem_limit_bytes=20 * MEBI),
        cost_estimate=pl.CostEstimate(
            flops=2 * wide * wide * LANES, bytes_accessed=4 * wide * wide, transcendentals=0
        ),
        name="payoff",
    )(jnp.asarray(card_rows(hands, wide)), hand_rank, live_mask)


def row_count(planes, groups):
    return -(-planes * groups // 8) * 8


def plan_of(parent_ref, node_count, groups):
    total = groups * node_count
    first = lax.axis_index("node") * groups
    off = [lax.rem(first - (parent_ref[idx, 0] >> 2) + total, total) for idx in (1, 2, 3)]
    off = [jnp.minimum(offset, groups - 1) for offset in off]
    one = off[0]
    two = one + off[1]
    three = two + off[2]
    low = jnp.maximum(one, three - groups)
    high = jnp.minimum(two, groups)
    middle = jnp.minimum(jnp.maximum((one + two + three + 2) >> 2, low), high)
    return middle, middle - one, two - middle, three - middle


def class_of(shift, groups):
    near = jnp.where(shift[3] > groups, 2 * groups - shift[3], shift[3])
    need = jnp.maximum(shift[0] + shift[1], shift[2] + near)
    found = jnp.int32(0)
    for size in CLASSES[:-1]:
        found = found + (need > size).astype(jnp.int32)
    return jnp.where(shift[3] > groups, len(CLASSES) - 1, found)


def fill_messages(
    node, stage, message_refs, size, block_ref, to_left, to_right, skipped=None
):
    _, tiles, planes = stage.shape[:3]
    even = lax.rem(node, 2) == 0
    places = [(tile, plane) for tile in range(tiles) for plane in range(planes)]
    for side, on_left in enumerate((even, jnp.logical_not(even))):
        for near, far in zip(to_left, to_right):
            level = jnp.where(on_left, near[0], far[0])
            start = jnp.where(on_left, near[1], far[1])
            for tile, plane in places:
                block = block_ref[level, tile, plane]
                if skipped is not None:
                    block = ahead(block, jnp.where(level == 3, skipped, 0))
                stage[side, tile, plane, pl.ds(start, 8), :] = block
    for side, message_ref in enumerate(message_refs):
        for tile, plane in places:
            message_ref[tile, plane * size : plane * size + size, :] = stage[
                side, tile, plane, 8 : 8 + size, :
            ]


def prepare_kernel(
    node_count,
    parent_hbm,
    logits_hbm,
    pot_hbm,
    kind_hbm,
    home_ref,
    shift_ref,
    class_ref,
    parent_ref,
    logits_ref,
    pot_ref,
    kind_ref,
    raw,
    flat,
    turned,
    sems,
):
    levels, tiles, planes, groups, _ = home_ref.shape
    slots = 4 * groups
    hands = logits_ref.shape[-1]
    fetches = [
        pltpu.make_async_copy(logits_hbm.at[0, idx], logits_ref.at[idx], sems.at[idx])
        for idx in range(levels)
    ]
    tables = [
        pltpu.make_async_copy(source, target, sems.at[levels + idx])
        for idx, (source, target) in enumerate(
            ((parent_hbm, parent_ref), (pot_hbm, pot_ref), (kind_hbm, kind_ref))
        )
    ]
    for fetch in tables + fetches:
        fetch.start()
    for fetch in tables:
        fetch.wait()
    shift = plan_of(parent_ref, node_count, groups)
    row_id = lax.broadcasted_iota(jnp.int32, shift_ref.shape, 0)
    spread = jnp.zeros(shift_ref.shape, jnp.int32)
    class_ref[...] = jnp.full((1, 1), class_of(shift, groups))
    for idx, value in enumerate(shift):
        spread = jnp.where(row_id == idx, value, spread)
    shift_ref[...] = spread
    pot = pot_ref[...]
    kind = kind_ref[...]
    level = lax.broadcasted_iota(jnp.int32, pot.shape, 0)
    sign = jnp.where(level % 2 == 0, -1.0, 1.0)
    flat[...] = jnp.zeros(flat.shape, jnp.float32)
    flat[0:levels, 0:slots] = jnp.where(kind == 2, pot, 0.0)
    flat[levels : 2 * levels, 0:slots] = jnp.where(kind == 1, pot, 0.0) * sign
    turned[...] = flat[...].T
    lane = lax.broadcasted_iota(jnp.int32, (groups, LANES), 1)
    for idx in range(levels):
        raw[idx, tiles - 1] = jnp.zeros((slots, LANES), jnp.float32)
    for idx in range(levels):
        fetches[idx].wait()
        for tile in range(tiles):
            start = tile * LANES
            stop = min(start + LANES, hands)
            raw[idx, tile, :, 0 : stop - start] = logits_ref[idx, :, start:stop]
            first = raw[idx, tile, pl.ds(0, groups, stride=4), :]
            for plane in range(planes):
                row = raw[idx, tile, pl.ds(plane + 1, groups, stride=4), :] - first
                if tile == tiles - 1 and plane == 0:
                    for slot in range(4):
                        scale = turned[pl.ds(slot, groups, stride=4), :]
                        row = jnp.where(lane == LANES - 8 + slot, scale[:, idx : idx + 1], row)
                        fold = scale[:, levels + idx : levels + idx + 1]
                        row = jnp.where(lane == LANES - 4 + slot, fold, row)
                home_ref[idx, tile, plane] = row


def prepared(logits, pot_size, node_type, parent_slot):
    _, levels, slots, hands = logits.shape
    groups = slots // 4
    tiles = padded(hands) // LANES
    vmem = pl.BlockSpec(memory_space=pltpu.VMEM)
    return pl.pallas_call(
        functools.partial(prepare_kernel, lax.axis_size("node")),
        out_shape=(
            jax.ShapeDtypeStruct((levels, tiles, 3, groups, LANES), jnp.float32),
            jax.ShapeDtypeStruct((8, LANES), jnp.int32),
            jax.ShapeDtypeStruct((1, 1), jnp.int32),
        ),
        in_specs=[pl.BlockSpec(memory_space=pl.ANY)] * 4,
        out_specs=(vmem, vmem, vmem),
        scratch_shapes=[
            pltpu.SMEM(parent_slot.shape, jnp.int32),
            pltpu.VMEM((levels, slots, hands), jnp.float32),
            pltpu.VMEM(pot_size.shape, jnp.float32),
            pltpu.VMEM(node_type.shape, jnp.int32),
            pltpu.VMEM((levels, tiles, slots, LANES), jnp.float32),
            pltpu.VMEM((LANES, LANES), jnp.float32),
            pltpu.VMEM((LANES, LANES), jnp.float32),
            pltpu.SemaphoreType.DMA((levels + 3,)),
        ],
        compiler_params=pltpu.CompilerParams(vmem_limit_bytes=10 * MEBI),
        name="prepare",
    )(parent_slot, logits, pot_size, node_type)


def ahead(rows, count):
    return pltpu.roll(rows, (8 - count) & 7, 0)


def behind(rows, count):
    return pltpu.roll(rows, count & 7, 0)


def shifts_in(shift_ref):
    return [jnp.max(shift_ref[idx : idx + 1, :]) for idx in range(4)]


def pack_kernel(size, far, shift_ref, home_ref, _pot, _kind, _parent, odd_ref, even_ref, *rest):
    far_ref = rest[0] if far else None
    stage = rest[-1]
    _, tiles, planes, groups, _ = home_ref.shape
    shift = shifts_in(shift_ref)
    skipped = jnp.maximum(shift[3] - 8, 0) if far else None
    fill_messages(
        lax.axis_index("node"),
        stage,
        (odd_ref, even_ref),
        size,
        home_ref,
        [(2, 8), (3, 8 + shift[2])],
        [(1, shift[0] + shift[1]), (0, shift[0])],
        skipped,
    )
    if far:
        for tile in range(tiles):
            for plane in range(planes):
                far_ref[tile, plane * FAR : plane * FAR + FAR, :] = home_ref[3, tile, plane, 0:FAR, :]


def message_shapes(planes, wide, size, far):
    tiles = wide // LANES
    message = jax.ShapeDtypeStruct((tiles, row_count(planes, size), LANES), jnp.float32)
    shapes = [message] * 2
    if far:
        shapes.append(jax.ShapeDtypeStruct((tiles, row_count(planes, FAR), LANES), jnp.float32))
    return shapes


def sent_on(odd, even, far, far_steps, order):
    count = lax.axis_size("node")
    edges = [(src, (src + 1) % count) for src in range(count)]
    got = [None, None]
    for side in order:
        pairs = [pair for edge in edges[1 - side :: 2] for pair in (edge, edge[::-1])]
        got[side] = lax.ppermute((odd, even)[side], "node", pairs)
    for message in far:
        pairs = [(src, (src + far_steps) % count) for src in range(count)]
        got.append(lax.ppermute(message, "node", pairs))
    return got


def spread_messages(node, from_left, from_right, odd_ref, even_ref, size):
    tiles, planes = from_left.shape[:2]
    even = lax.rem(node, 2) == 0
    for tile in range(tiles):
        for plane in range(planes):
            place = slice(plane * size, plane * size + size)
            odd_part = odd_ref[tile, place, :]
            even_part = even_ref[tile, place, :]
            from_left[tile, plane, 8 : 8 + size, :] = jnp.where(even, odd_part, even_part)
            from_right[tile, plane, 8 : 8 + size, :] = jnp.where(even, even_part, odd_part)


def inner_sum(inner, rows):
    total = jnp.where(inner[0], rows[0], 0.0)
    for idx in range(1, 4):
        total = total + jnp.where(inner[idx], rows[idx], 0.0)
    return total


def inner_before(inner):
    one = inner[0] | inner[1]
    return [inner[0], one, one | inner[2]]


def exponentials(rows):
    top = jnp.maximum(jnp.maximum(rows[0], rows[1]), jnp.maximum(rows[2], 0.0))
    lifted = [jnp.exp(-top)] + [jnp.exp(row - top) for row in rows]
    return lifted, 1.0 / ((lifted[0] + lifted[1]) + (lifted[2] + lifted[3]))


def softmax_four(rows):
    lifted, share = exponentials(rows)
    return [row * share for row in lifted]


def operator_q(point, show, fold, range_one, range_two, block_ref, cols, put, top_ref=None):
    wide = block_ref.shape[1]
    inner = [
        [(show[idx][slot] == 0.0) & (fold[idx][slot] == 0.0) for slot in range(4)]
        for idx in range(4)
    ]
    lifted, share = exponentials(point[0])
    above_one = range_one * (inner_sum(inner[0], lifted) * share)
    strategy = [None] + [softmax_four(point[idx]) for idx in range(1, 4)]
    mid_two = [range_two * row for row in strategy[1]]
    above_two = inner_sum(inner[1], mid_two)
    low_one = [above_one * row for row in strategy[2]]
    last_one = inner_sum(inner[2], low_one)
    end_two = [above_two * row for row in strategy[3]]
    wide_two = jnp.broadcast_to(range_two, above_two.shape)
    past = [inner_before(inner[idx]) for idx in range(3)]

    units = [
        (0, [wide_two] * 4, 1.0, False),
        (1, mid_two, 1.0, True),
        (2, [above_two] * 4, 1.0, False),
        (3, end_two, 1.0, True),
        (1, [above_one] * 4, -1.0, False),
        (2, low_one, -1.0, True),
        (3, [last_one] * 4, -1.0, False),
    ]
    first_unit = 0 if top_ref is None else 1
    begin = [0] * len(units)
    for side in range(2):
        blocks = []
        for unit in range(first_unit, len(units)):
            idx, rows, fold_sign, as_sum = units[unit]
            begin[unit] = 8 * len(blocks)
            if side == 0:
                scaled = [rows[slot] * show[idx][slot] for slot in range(4)]
            else:
                scaled = [rows[slot] * (fold[idx][slot] * fold_sign) for slot in range(4)]
            if as_sum:
                rounded = [row.astype(jnp.bfloat16).astype(jnp.float32) for row in scaled]
                total = (rounded[0] + rounded[1]) + (rounded[2] + rounded[3])
                high = total.astype(jnp.bfloat16).astype(jnp.float32)
                scaled = [high, total - high]
            elif idx < 3:
                scaled = [
                    jnp.where(past[idx][slot], scaled[slot + 1], scaled[slot]) for slot in range(3)
                ]
            blocks += scaled
        if len(blocks) % 2:
            blocks.append(jnp.zeros_like(blocks[0]))
        lanes = slice(side * wide, side * wide + wide)
        for pair in range(0, len(blocks), 2):
            cols[pair * 8 : pair * 8 + 16, lanes] = jnp.concatenate(
                blocks[pair : pair + 2], axis=0
            ).astype(jnp.bfloat16)

    def added(rows):
        return (rows[0] + rows[1]) + (rows[2] + rows[3])

    def landed(rows, kept, term):
        return [jnp.where(kept[slot], term, rows[slot]) for slot in range(4)]

    total = None
    for start in range(0, wide, 2 * LANES):
        stop = min(start + 2 * LANES, wide)
        pay = jnp.dot(cols[...], block_ref[:, start:stop], preferred_element_type=jnp.float32)

        def paid(unit):
            at = begin[unit]
            idx = units[unit][0]
            rows = [pay[at + slot * 8 : at + slot * 8 + 8, :] for slot in range(4 if idx == 3 else 3)]
            if idx < 3:
                rows = [
                    rows[0],
                    jnp.where(past[idx][0], rows[0], rows[1]),
                    jnp.where(past[idx][1], rows[1], rows[2]),
                    rows[2],
                ]
            return rows

        def paid_sum(unit):
            at = begin[unit]
            return pay[at : at + 8, :] + pay[at + 8 : at + 16, :]

        def weighed(idx, rows):
            return added([strategy[idx][slot][:, start:stop] * rows[slot] for slot in range(4)])

        value_two_end = paid(6)
        term_two = paid_sum(5) + weighed(3, value_two_end)
        value_two_mid = landed(paid(4), inner[1], term_two)
        value_one_low = landed(paid(2), inner[2], paid_sum(3))
        term_one = paid_sum(1) + weighed(2, value_one_low)
        if top_ref is None:
            value_one_top = landed(paid(0), inner[0], term_one)
        else:
            value_one_top = [
                jnp.where(inner[0][slot], term_one, top_ref[0, slot, :, start:stop])
                for slot in range(4)
            ]
        found = [value_one_top, value_two_mid, value_one_low, value_two_end]
        put(start, stop, found)
        part = squares(found)
        total = part if total is None else total + part
    return total


def squares(found):
    total = None
    for rows in found:
        for row in rows:
            total = row * row if total is None else total + row * row
    return jnp.broadcast_to(jnp.sum(total), (1, LANES))


def scale_columns(rows):
    wide = rows[0][0].shape[1]
    show = [
        [level[0][:, wide - 8 + slot : wide - 7 + slot] for slot in range(4)] for level in rows
    ]
    fold = [
        [level[0][:, wide - 4 + slot : wide - 4 + slot + 1] for slot in range(4)] for level in rows
    ]
    return show, fold


def wide_row(store, place, row_ref):
    hands = row_ref.shape[1]
    store[place : place + 1, 0:hands] = row_ref[...]
    return store[place : place + 1, :]


def first_kernel(size, far, shift_ref, home_ref, odd_ref, even_ref, *rest):
    if far:
        far_ref, rest = rest[0], rest[1:]
    one_ref, two_ref, block_ref, chain_ref, value_ref, square_ref = rest[:6]
    from_left, from_right, window, ranges, cols = rest[6:]
    _, tiles, planes, groups, _ = home_ref.shape
    shift = shifts_in(shift_ref)
    spread_messages(lax.axis_index("node"), from_left, from_right, odd_ref, even_ref, size)
    chain = lax.broadcasted_iota(jnp.int32, (groups, LANES), 0)
    places = [(tile, plane) for tile in range(tiles) for plane in range(planes)]
    if far:
        for tile, plane in places:
            window[tile, plane, 16 : 16 + FAR, :] = far_ref[
                tile, plane * FAR : plane * FAR + FAR, :
            ]
    point = [[[] for _ in range(planes)] for _ in range(4)]
    for tile, plane in places:
        top = jnp.where(
            chain < shift[0],
            from_left[tile, plane, 8:16, :],
            behind(home_ref[0, tile, plane], shift[0]),
        )
        mid = jnp.where(
            chain < shift[1],
            from_left[tile, plane, pl.ds(8 + shift[0], 8), :],
            behind(home_ref[1, tile, plane], shift[1]),
        )
        low = jnp.where(
            chain + shift[2] < 8,
            ahead(home_ref[2, tile, plane], shift[2]),
            from_right[tile, plane, pl.ds(shift[2], 8), :],
        )
        end = jnp.where(
            chain + shift[3] < 8,
            ahead(home_ref[3, tile, plane], shift[3]),
            from_right[tile, plane, pl.ds(shift[2] + jnp.minimum(shift[3], 8), 8), :],
        )
        if far:
            far_part = window[tile, plane, pl.ds(shift[3], 8), :]
            end = jnp.where(chain + shift[3] < 16, end, far_part)
        for idx, row in enumerate((top, mid, low, end)):
            point[idx][plane].append(row)
    point = [[jnp.concatenate(rows, axis=1) for rows in level] for level in point]
    for idx in range(4):
        for plane in range(planes):
            chain_ref[idx, plane] = point[idx][plane]
    show, fold = scale_columns(point)
    ranges[...] = jnp.zeros(ranges.shape, jnp.float32)
    range_one = wide_row(ranges, 0, one_ref)
    range_two = wide_row(ranges, 1, two_ref)

    def put(start, stop, found):
        for idx in range(4):
            for slot in range(4):
                value_ref[idx, slot, :, start:stop] = found[idx][slot]

    square_ref[...] = operator_q(
        point, show, fold, range_one, range_two, block_ref, cols, put
    )


def rate_of(parts_ref, entry_count):
    square_sum = jnp.sum(parts_ref[...], axis=0, keepdims=True)[:, 0:1]
    return step_scale / jnp.sqrt(square_sum / entry_count + eps_value)


def second_kernel(entry_count, size, far, shift_ref, chain_ref, value_ref, *rest):
    parts_ref, one_ref, two_ref, block_ref, own_ref, odd_ref, even_ref = rest[:7]
    rest = rest[7:]
    if far:
        far_ref, rest = rest[0], rest[1:]
    square_ref, stage, ranges, cols = rest
    _, tiles, planes, groups, _ = own_ref.shape
    rate = rate_of(parts_ref, entry_count)
    raw = [[chain_ref[idx, plane] for plane in range(3)] for idx in range(4)]
    show, fold = scale_columns(raw)
    point = [
        [
            raw[idx][plane] + rate * (value_ref[idx, plane + 1] - value_ref[idx, 0])
            for plane in range(3)
        ]
        for idx in range(4)
    ]
    ranges[...] = jnp.zeros(ranges.shape, jnp.float32)
    range_one = wide_row(ranges, 0, one_ref)
    range_two = wide_row(ranges, 1, two_ref)

    def put(start, stop, found):
        for idx in range(4):
            for slot in range(4):
                for lane in range(start, stop, LANES):
                    row = found[idx][slot][:, lane - start : lane - start + LANES]
                    own_ref[idx, lane // LANES, slot] = row

    square_ref[...] = operator_q(
        point, show, fold, range_one, range_two, block_ref, cols, put, value_ref
    )
    shift = shifts_in(shift_ref)
    fill_messages(
        lax.axis_index("node"),
        stage,
        (odd_ref, even_ref),
        size,
        own_ref,
        [(0, 8), (1, 8 + shift[0])],
        [(3, shift[2] + jnp.minimum(shift[3], 8)), (2, shift[2])],
    )
    if far:
        for tile in range(tiles):
            for plane in range(planes):
                part = stage.at[0, tile, plane]
                part[pl.ds(jnp.maximum(shift[3] - 8, 0), 8), :] = own_ref[3, tile, plane]
                far_ref[tile, plane * FAR : plane * FAR + FAR, :] = part[8 : 8 + FAR, :]


def last_kernel(entry_count, size, far, shift_ref, own_ref, even_ref, odd_ref, *rest):
    far_ref, rest = (rest[0], rest[1:]) if far else (None, rest)
    parts_ref, logits_ref, new_hbm, half_hbm, from_left, from_right, lined = rest[:7]
    new_ref, half_ref, sems = rest[7:]
    _, tiles, planes, groups, _ = own_ref.shape
    hands = logits_ref.shape[-1]
    shift = shifts_in(shift_ref)
    rate = rate_of(parts_ref, entry_count)
    group = lax.broadcasted_iota(jnp.int32, (groups, LANES), 0)
    spread_messages(lax.axis_index("node"), from_left, from_right, odd_ref, even_ref, size)
    places = [(tile, plane) for tile in range(tiles) for plane in range(planes)]

    def top(tile, plane, own):
        return jnp.where(
            group + shift[0] < 8,
            ahead(own, shift[0]),
            from_right[tile, plane, pl.ds(shift[0], 8), :],
        )

    def mid(tile, plane, own):
        return jnp.where(
            group + shift[1] < 8,
            ahead(own, shift[1]),
            from_right[tile, plane, pl.ds(shift[0] + shift[1], 8), :],
        )

    def low(tile, plane, own):
        return jnp.where(
            group < shift[2], from_left[tile, plane, 8:16, :], behind(own, shift[2])
        )

    def end(tile, plane, own):
        row = jnp.where(
            group < shift[3],
            from_left[tile, plane, pl.ds(8 + shift[2] - jnp.maximum(shift[3] - 8, 0), 8), :],
            behind(own, shift[3]),
        )
        if far:
            far_part = far_ref[tile, plane * FAR : plane * FAR + 8, :]
            row = jnp.where(group < shift[3] - 8, far_part, row)
        return row

    leaving = []

    def leave(source, target, kind, idx):
        leaving.append(pltpu.make_async_copy(source.at[idx], target.at[0, idx], sems.at[kind, idx]))
        leaving[-1].start()

    for idx, found in enumerate((top, mid, low, end)):
        for tile, plane in places:
            row = found(tile, plane, own_ref[idx, tile, plane])
            lined[idx, tile, pl.ds(plane, groups, stride=4), :] = row
        for tile in range(tiles):
            start = tile * LANES
            stop = min(start + LANES, hands)
            value = lined[idx, tile][:, 0 : stop - start]
            half_ref[idx, :, start:stop] = value
            new_ref[idx, :, start:stop] = logits_ref[0, idx, :, start:stop] + rate * value
        leave(half_ref, half_hbm, 0, idx)
        leave(new_ref, new_hbm, 1, idx)
    for copy in leaving:
        copy.wait()


def shared_parts(part):
    count = lax.axis_size("node") * lax.axis_size("board")
    spread = jnp.broadcast_to(part, (count, LANES))
    return lax.all_to_all(spread, ("node", "board"), 0, 0, tiled=True)


def shared_parts_over_nodes(part):
    nodes = lax.axis_size("node")
    boards = lax.axis_size("board")
    total = part
    for turn in range(1, boards):
        pairs = [(board, (board + turn) % boards) for board in range(boards)]
        total = total + lax.ppermute(part, "board", pairs)
    spread = jnp.broadcast_to(total, (nodes, LANES))
    order = [[nodes - 1] + list(range(nodes - 1))]
    return lax.all_to_all(spread, "node", 0, 0, axis_index_groups=order, tiled=True)


def step_of_class(
    size,
    far,
    home,
    shift,
    logits,
    pot_size,
    node_type,
    parent_slot,
    range_one,
    range_two,
    hand_rank,
    live_mask,
):
    _, levels, slots, hands = logits.shape
    wide = padded(hands)
    tiles = wide // LANES
    groups = slots // 4
    entry_count = float(logits.size * lax.axis_size("node") * lax.axis_size("board"))
    vmem = pl.BlockSpec(memory_space=pltpu.VMEM)
    f32 = jnp.float32

    def limit(mebi):
        return pltpu.CompilerParams(vmem_limit_bytes=mebi * MEBI)

    def stage(planes, rows=32):
        return pltpu.VMEM((tiles, planes, rows, LANES), f32)

    def two_stages(planes):
        return pltpu.VMEM((2, tiles, planes, 32, LANES), f32)

    anywhere = pl.BlockSpec(memory_space=pl.ANY)
    sent = pl.pallas_call(
        functools.partial(pack_kernel, size, far),
        out_shape=message_shapes(3, wide, size, far),
        in_specs=[vmem, vmem] + [anywhere] * 3,
        scratch_shapes=[two_stages(3)],
        compiler_params=limit(8),
        name="pack",
    )(shift, home, pot_size, node_type, parent_slot)
    got = sent_on(sent[0], sent[1], sent[2:], -2, (0, 1))
    blocks = payoff_blocks(hand_rank, live_mask)
    blocks_all = 3 * 3 + 4 + 3 * 2
    rows = 16 * (-(-blocks_all // 2))
    rows_second = 16 * (-(-(blocks_all - 3) // 2))

    def work(count):
        return [
            pltpu.VMEM((8, wide), f32),
            pltpu.VMEM((count, 2 * wide), jnp.bfloat16),
        ]

    def cost(count):
        return pl.CostEstimate(
            flops=4 * count * wide * wide, bytes_accessed=6 * wide * wide, transcendentals=0
        )

    square_shape = jax.ShapeDtypeStruct((1, LANES), f32)
    chain, value, part = pl.pallas_call(
        functools.partial(first_kernel, size, far),
        out_shape=(
            jax.ShapeDtypeStruct((levels, 3, groups, wide), f32),
            jax.ShapeDtypeStruct((levels, 4, groups, wide), f32),
            square_shape,
        ),
        in_specs=[vmem] * (5 + len(got)),
        scratch_shapes=[stage(3), stage(3), stage(3)] + work(rows),
        compiler_params=limit(32),
        cost_estimate=cost(rows),
        name="first",
    )(shift, home, *got, range_one, range_two, blocks)
    parts = shared_parts(part)
    own, *sent, part = pl.pallas_call(
        functools.partial(second_kernel, entry_count, size, far),
        out_shape=[jax.ShapeDtypeStruct((levels, tiles, 4, groups, LANES), f32)]
        + message_shapes(4, wide, size, far)
        + [square_shape],
        in_specs=[vmem] * 7,
        scratch_shapes=[two_stages(4)] + work(rows_second),
        compiler_params=limit(32),
        cost_estimate=cost(rows_second),
        name="second",
    )(shift, chain, value, parts, range_one, range_two, blocks)
    got = sent_on(sent[0], sent[1], sent[2:], 2, (1, 0))
    parts = shared_parts_over_nodes(part)
    out_shape = jax.ShapeDtypeStruct(logits.shape, f32)
    level_shape = (levels, slots, hands)
    return pl.pallas_call(
        functools.partial(last_kernel, entry_count, size, far),
        out_shape=(out_shape, out_shape),
        in_specs=[vmem] * (4 + len(got)),
        out_specs=(anywhere, anywhere),
        scratch_shapes=[
            stage(4),
            stage(4),
            pltpu.VMEM((levels, tiles, slots, LANES), f32),
            pltpu.VMEM(level_shape, f32),
            pltpu.VMEM(level_shape, f32),
            pltpu.SemaphoreType.DMA((2, levels)),
        ],
        compiler_params=limit(24),
        name="last",
    )(shift, own, got[1], got[0], *got[2:], parts, logits)


def per_device(
    logits, pot_size, node_type, parent_slot, range_one, range_two, hand_rank, live_mask
):
    branches = [
        functools.partial(step_of_class, size, size == CLASSES[-1]) for size in CLASSES
    ]
    home, shift, found = prepared(logits, pot_size, node_type, parent_slot)
    return lax.switch(
        found[0, 0],
        branches,
        home,
        shift,
        logits,
        pot_size,
        node_type,
        parent_slot,
        range_one,
        range_two,
        hand_rank,
        live_mask,
    )


def solution(mesh):
    return jax.shard_map(
        per_device,
        mesh=mesh,
        in_specs=(
            P("board", None, "node", None),
            P(None, "node"),
            P(None, "node"),
            P(None, "node"),
            P("board", None),
            P("board", None),
            P("board", None),
            P("board", None),
        ),
        out_specs=(P("board", None, "node", None), P("board", None, "node", None)),
        check_vma=False,
    )
```

```python
import functools

import jax
import jax.numpy as jnp
import numpy as np
from jax import lax
from jax.experimental import pallas as pl
from jax.experimental.pallas import tpu as pltpu
from jax.sharding import PartitionSpec as P

LANES = 128
CARDS = 52
step_scale = 0.5
eps_value = 1e-06
MEBI = 1 << 20
CLASSES = (5, 8, 10, 12, 14)
FAR = 5


def padded(count):
    return -(-count // LANES) * LANES


def card_rows(hand_count, wide):
    pairs = [(low, high) for low in range(CARDS) for high in range(low + 1, CARDS)]
    rows = np.full((2, wide), -1, np.int32)
    rows[:, :hand_count] = np.array(pairs[:hand_count], np.int32).T
    return rows


def payoff_kernel(
    hands, cards_ref, rank_ref, live_ref, out_ref, flat, left, right, left_turned, rank_turned
):
    wide = out_ref.shape[1]
    flat[...] = jnp.zeros(flat.shape, jnp.float32)
    flat[0:1, 0:hands] = rank_ref[...].astype(jnp.float32)
    flat[1:2, 0:hands] = (live_ref[...] > 0).astype(jnp.float32)
    dead = 1.0 - flat[1:2, :]
    feature = lax.broadcasted_iota(jnp.int32, (LANES, wide), 0)
    hit = (feature == cards_ref[0:1, :]) | (feature == cards_ref[1:2, :])
    base = jnp.where(hit, 1.0, 0.0)
    left[...] = jnp.where(feature == CARDS, dead, jnp.where(feature == CARDS + 1, 1.0, base))
    right[...] = jnp.where(
        feature == CARDS, 1.0, jnp.where(feature == CARDS + 1, dead, base)
    ).astype(jnp.bfloat16)
    rank_row = flat[0:1, :]
    for block in range(wide // LANES):
        part = slice(block * LANES, (block + 1) * LANES)
        left_turned[part, :] = left[:, part].T.astype(jnp.bfloat16)
        rank_turned[part, :] = jnp.broadcast_to(flat[0:1, part], (LANES, LANES)).T

    def fill(block):
        begin = pl.multiple_of(block * LANES, LANES)
        part = pl.ds(begin, LANES)
        hits = jnp.dot(left_turned[part, :], right[...], preferred_element_type=jnp.float32)
        compat = jnp.where(hits == 0.0, 1.0, 0.0)
        order = jnp.clip(rank_row - rank_turned[part, 0:1], -1.0, 1.0)
        out_ref[part, :] = (order * compat).astype(jnp.bfloat16)
        out_ref[pl.ds(begin + wide, LANES), :] = compat.astype(jnp.bfloat16)

    @pl.loop(0, wide // LANES // 2)
    def _(pair):
        fill(2 * pair)
        fill(2 * pair + 1)

    if wide // LANES % 2:
        fill(jnp.int32(wide // LANES - 1))


def payoff_blocks(hand_rank, live_mask):
    hands = hand_rank.shape[-1]
    wide = padded(hands)
    return pl.pallas_call(
        functools.partial(payoff_kernel, hands),
        out_shape=jax.ShapeDtypeStruct((2 * wide, wide), jnp.bfloat16),
        scratch_shapes=[
            pltpu.VMEM((8, wide), jnp.float32),
            pltpu.VMEM((LANES, wide), jnp.float32),
            pltpu.VMEM((LANES, wide), jnp.bfloat16),
            pltpu.VMEM((wide, LANES), jnp.bfloat16),
            pltpu.VMEM((wide, LANES), jnp.float32),
        ],
        compiler_params=pltpu.CompilerParams(vmem_limit_bytes=20 * MEBI),
        cost_estimate=pl.CostEstimate(
            flops=2 * wide * wide * LANES, bytes_accessed=4 * wide * wide, transcendentals=0
        ),
        name="payoff",
    )(jnp.asarray(card_rows(hands, wide)), hand_rank, live_mask)


def row_count(planes, groups):
    return -(-planes * groups // 8) * 8


def plan_of(parent_ref, node_count, groups):
    total = groups * node_count
    first = lax.axis_index("node") * groups
    off = [lax.rem(first - (parent_ref[idx, 0] >> 2) + total, total) for idx in (1, 2, 3)]
    one = off[0]
    two = one + off[1]
    three = two + off[2]
    low = jnp.maximum(one, three - groups)
    high = jnp.minimum(two, groups)
    middle = jnp.minimum(jnp.maximum((one + two + three + 2) >> 2, low), high)
    return middle, middle - one, two - middle, three - middle


def class_of(shift, groups):
    near = jnp.where(shift[3] > groups, 2 * groups - shift[3], shift[3])
    need = jnp.maximum(shift[0] + shift[1], shift[2] + near)
    found = jnp.int32(0)
    for size in CLASSES[:-1]:
        found = found + (need > size).astype(jnp.int32)
    return jnp.where(shift[3] > groups, len(CLASSES) - 1, found)


def fill_messages(
    node, stage, message_refs, size, block_ref, to_left, to_right, skipped=None
):
    _, tiles, planes = stage.shape[:3]
    even = lax.rem(node, 2) == 0
    places = [(tile, plane) for tile in range(tiles) for plane in range(planes)]
    for side, on_left in enumerate((even, jnp.logical_not(even))):
        for near, far in zip(to_left, to_right):
            level = jnp.where(on_left, near[0], far[0])
            start = jnp.where(on_left, near[1], far[1])
            for tile, plane in places:
                block = block_ref[level, tile, plane]
                if skipped is not None:
                    block = ahead(block, jnp.where(level == 3, skipped, 0))
                stage[side, tile, plane, pl.ds(start, 8), :] = block
    for side, message_ref in enumerate(message_refs):
        for tile, plane in places:
            message_ref[tile, plane * size : plane * size + size, :] = stage[
                side, tile, plane, 8 : 8 + size, :
            ]


def prepare_kernel(
    node_count,
    parent_hbm,
    logits_hbm,
    pot_hbm,
    kind_hbm,
    home_ref,
    shift_ref,
    class_ref,
    parent_ref,
    logits_ref,
    pot_ref,
    kind_ref,
    raw,
    flat,
    turned,
    sems,
):
    levels, tiles, planes, groups, _ = home_ref.shape
    slots = 4 * groups
    hands = logits_ref.shape[-1]
    fetches = [
        pltpu.make_async_copy(logits_hbm.at[0, idx], logits_ref.at[idx], sems.at[idx])
        for idx in range(levels)
    ]
    tables = [
        pltpu.make_async_copy(source, target, sems.at[levels + idx])
        for idx, (source, target) in enumerate(
            ((parent_hbm, parent_ref), (pot_hbm, pot_ref), (kind_hbm, kind_ref))
        )
    ]
    for fetch in tables + fetches:
        fetch.start()
    for fetch in tables:
        fetch.wait()
    shift = plan_of(parent_ref, node_count, groups)
    row_id = lax.broadcasted_iota(jnp.int32, shift_ref.shape, 0)
    spread = jnp.zeros(shift_ref.shape, jnp.int32)
    class_ref[...] = jnp.full((1, 1), class_of(shift, groups))
    for idx, value in enumerate(shift):
        spread = jnp.where(row_id == idx, value, spread)
    shift_ref[...] = spread
    pot = pot_ref[...]
    kind = kind_ref[...]
    level = lax.broadcasted_iota(jnp.int32, pot.shape, 0)
    sign = jnp.where(level % 2 == 0, -1.0, 1.0)
    flat[...] = jnp.zeros(flat.shape, jnp.float32)
    flat[0:levels, 0:slots] = jnp.where(kind == 2, pot, 0.0)
    flat[levels : 2 * levels, 0:slots] = jnp.where(kind == 1, pot, 0.0) * sign
    turned[...] = flat[...].T
    lane = lax.broadcasted_iota(jnp.int32, (groups, LANES), 1)
    for idx in range(levels):
        raw[idx, tiles - 1] = jnp.zeros((slots, LANES), jnp.float32)
    for idx in range(levels):
        fetches[idx].wait()
        for tile in range(tiles):
            start = tile * LANES
            stop = min(start + LANES, hands)
            raw[idx, tile, :, 0 : stop - start] = logits_ref[idx, :, start:stop]
            first = raw[idx, tile, pl.ds(0, groups, stride=4), :]
            for plane in range(planes):
                row = raw[idx, tile, pl.ds(plane + 1, groups, stride=4), :] - first
                if tile == tiles - 1 and plane == 0:
                    for slot in range(4):
                        scale = turned[pl.ds(slot, groups, stride=4), :]
                        row = jnp.where(lane == LANES - 8 + slot, scale[:, idx : idx + 1], row)
                        fold = scale[:, levels + idx : levels + idx + 1]
                        row = jnp.where(lane == LANES - 4 + slot, fold, row)
                home_ref[idx, tile, plane] = row


def prepared(logits, pot_size, node_type, parent_slot):
    _, levels, slots, hands = logits.shape
    groups = slots // 4
    tiles = padded(hands) // LANES
    vmem = pl.BlockSpec(memory_space=pltpu.VMEM)
    return pl.pallas_call(
        functools.partial(prepare_kernel, lax.axis_size("node")),
        out_shape=(
            jax.ShapeDtypeStruct((levels, tiles, 3, groups, LANES), jnp.float32),
            jax.ShapeDtypeStruct((8, LANES), jnp.int32),
            jax.ShapeDtypeStruct((1, 1), jnp.int32),
        ),
        in_specs=[pl.BlockSpec(memory_space=pl.ANY)] * 4,
        out_specs=(vmem, vmem, vmem),
        scratch_shapes=[
            pltpu.SMEM(parent_slot.shape, jnp.int32),
            pltpu.VMEM((levels, slots, hands), jnp.float32),
            pltpu.VMEM(pot_size.shape, jnp.float32),
            pltpu.VMEM(node_type.shape, jnp.int32),
            pltpu.VMEM((levels, tiles, slots, LANES), jnp.float32),
            pltpu.VMEM((LANES, LANES), jnp.float32),
            pltpu.VMEM((LANES, LANES), jnp.float32),
            pltpu.SemaphoreType.DMA((levels + 3,)),
        ],
        compiler_params=pltpu.CompilerParams(vmem_limit_bytes=10 * MEBI),
        name="prepare",
    )(parent_slot, logits, pot_size, node_type)


def ahead(rows, count):
    return pltpu.roll(rows, (8 - count) & 7, 0)


def behind(rows, count):
    return pltpu.roll(rows, count & 7, 0)


def shifts_in(shift_ref):
    return [jnp.max(shift_ref[idx : idx + 1, :]) for idx in range(4)]


def pack_kernel(size, far, shift_ref, home_ref, _pot, _kind, _parent, odd_ref, even_ref, *rest):
    far_ref = rest[0] if far else None
    stage = rest[-1]
    _, tiles, planes, groups, _ = home_ref.shape
    shift = shifts_in(shift_ref)
    skipped = jnp.maximum(shift[3] - 8, 0) if far else None
    fill_messages(
        lax.axis_index("node"),
        stage,
        (odd_ref, even_ref),
        size,
        home_ref,
        [(2, 8), (3, 8 + shift[2])],
        [(1, shift[0] + shift[1]), (0, shift[0])],
        skipped,
    )
    if far:
        for tile in range(tiles):
            for plane in range(planes):
                far_ref[tile, plane * FAR : plane * FAR + FAR, :] = home_ref[3, tile, plane, 0:FAR, :]


def message_shapes(planes, wide, size, far):
    tiles = wide // LANES
    message = jax.ShapeDtypeStruct((tiles, row_count(planes, size), LANES), jnp.float32)
    shapes = [message] * 2
    if far:
        shapes.append(jax.ShapeDtypeStruct((tiles, row_count(planes, FAR), LANES), jnp.float32))
    return shapes


def sent_on(odd, even, far, far_steps, order):
    count = lax.axis_size("node")
    edges = [(src, (src + 1) % count) for src in range(count)]
    got = [None, None]
    for side in order:
        pairs = [pair for edge in edges[1 - side :: 2] for pair in (edge, edge[::-1])]
        got[side] = lax.ppermute((odd, even)[side], "node", pairs)
    for message in far:
        pairs = [(src, (src + far_steps) % count) for src in range(count)]
        got.append(lax.ppermute(message, "node", pairs))
    return got


def spread_messages(node, from_left, from_right, odd_ref, even_ref, size):
    tiles, planes = from_left.shape[:2]
    even = lax.rem(node, 2) == 0
    for tile in range(tiles):
        for plane in range(planes):
            place = slice(plane * size, plane * size + size)
            odd_part = odd_ref[tile, place, :]
            even_part = even_ref[tile, place, :]
            from_left[tile, plane, 8 : 8 + size, :] = jnp.where(even, odd_part, even_part)
            from_right[tile, plane, 8 : 8 + size, :] = jnp.where(even, even_part, odd_part)


def inner_sum(inner, rows):
    total = jnp.where(inner[0], rows[0], 0.0)
    for idx in range(1, 4):
        total = total + jnp.where(inner[idx], rows[idx], 0.0)
    return total


def inner_before(inner):
    one = inner[0] | inner[1]
    return [inner[0], one, one | inner[2]]


def exponentials(rows):
    top = jnp.maximum(jnp.maximum(rows[0], rows[1]), jnp.maximum(rows[2], 0.0))
    lifted = [jnp.exp(-top)] + [jnp.exp(row - top) for row in rows]
    return lifted, 1.0 / ((lifted[0] + lifted[1]) + (lifted[2] + lifted[3]))


def softmax_four(rows):
    lifted, share = exponentials(rows)
    return [row * share for row in lifted]


def operator_q(point, show, fold, range_one, range_two, block_ref, cols, put, top_ref=None):
    wide = block_ref.shape[1]
    inner = [
        [(show[idx][slot] == 0.0) & (fold[idx][slot] == 0.0) for slot in range(4)]
        for idx in range(4)
    ]
    lifted, share = exponentials(point[0])
    above_one = range_one * (inner_sum(inner[0], lifted) * share)
    strategy = [None] + [softmax_four(point[idx]) for idx in range(1, 4)]
    mid_two = [range_two * row for row in strategy[1]]
    above_two = inner_sum(inner[1], mid_two)
    low_one = [above_one * row for row in strategy[2]]
    last_one = inner_sum(inner[2], low_one)
    end_two = [above_two * row for row in strategy[3]]
    wide_two = jnp.broadcast_to(range_two, above_two.shape)
    past = [inner_before(inner[idx]) for idx in range(3)]

    units = [
        (0, [wide_two] * 4, 1.0, False),
        (1, mid_two, 1.0, True),
        (2, [above_two] * 4, 1.0, False),
        (3, end_two, 1.0, True),
        (1, [above_one] * 4, -1.0, False),
        (2, low_one, -1.0, True),
        (3, [last_one] * 4, -1.0, False),
    ]
    first_unit = 0 if top_ref is None else 1
    begin = [0] * len(units)
    for side in range(2):
        blocks = []
        for unit in range(first_unit, len(units)):
            idx, rows, fold_sign, as_sum = units[unit]
            begin[unit] = 8 * len(blocks)
            if side == 0:
                scaled = [rows[slot] * show[idx][slot] for slot in range(4)]
            else:
                scaled = [rows[slot] * (fold[idx][slot] * fold_sign) for slot in range(4)]
            if as_sum:
                rounded = [row.astype(jnp.bfloat16).astype(jnp.float32) for row in scaled]
                total = (rounded[0] + rounded[1]) + (rounded[2] + rounded[3])
                high = total.astype(jnp.bfloat16).astype(jnp.float32)
                scaled = [high, total - high]
            elif idx < 3:
                scaled = [
                    jnp.where(past[idx][slot], scaled[slot + 1], scaled[slot]) for slot in range(3)
                ]
            blocks += scaled
        if len(blocks) % 2:
            blocks.append(jnp.zeros_like(blocks[0]))
        lanes = slice(side * wide, side * wide + wide)
        for pair in range(0, len(blocks), 2):
            cols[pair * 8 : pair * 8 + 16, lanes] = jnp.concatenate(
                blocks[pair : pair + 2], axis=0
            ).astype(jnp.bfloat16)

    def added(rows):
        return (rows[0] + rows[1]) + (rows[2] + rows[3])

    def landed(rows, kept, term):
        return [jnp.where(kept[slot], term, rows[slot]) for slot in range(4)]

    total = None
    for start in range(0, wide, 2 * LANES):
        stop = min(start + 2 * LANES, wide)
        pay = jnp.dot(cols[...], block_ref[:, start:stop], preferred_element_type=jnp.float32)

        def paid(unit):
            at = begin[unit]
            idx = units[unit][0]
            rows = [pay[at + slot * 8 : at + slot * 8 + 8, :] for slot in range(4 if idx == 3 else 3)]
            if idx < 3:
                rows = [
                    rows[0],
                    jnp.where(past[idx][0], rows[0], rows[1]),
                    jnp.where(past[idx][1], rows[1], rows[2]),
                    rows[2],
                ]
            return rows

        def paid_sum(unit):
            at = begin[unit]
            return pay[at : at + 8, :] + pay[at + 8 : at + 16, :]

        def weighed(idx, rows):
            return added([strategy[idx][slot][:, start:stop] * rows[slot] for slot in range(4)])

        value_two_end = paid(6)
        term_two = paid_sum(5) + weighed(3, value_two_end)
        value_two_mid = landed(paid(4), inner[1], term_two)
        value_one_low = landed(paid(2), inner[2], paid_sum(3))
        term_one = paid_sum(1) + weighed(2, value_one_low)
        if top_ref is None:
            value_one_top = landed(paid(0), inner[0], term_one)
        else:
            value_one_top = [
                jnp.where(inner[0][slot], term_one, top_ref[0, slot, :, start:stop])
                for slot in range(4)
            ]
        found = [value_one_top, value_two_mid, value_one_low, value_two_end]
        put(start, stop, found)
        part = squares(found)
        total = part if total is None else total + part
    return total


def squares(found):
    total = None
    for rows in found:
        for row in rows:
            total = row * row if total is None else total + row * row
    return jnp.broadcast_to(jnp.sum(total), (1, LANES))


def scale_columns(rows):
    wide = rows[0][0].shape[1]
    show = [
        [level[0][:, wide - 8 + slot : wide - 7 + slot] for slot in range(4)] for level in rows
    ]
    fold = [
        [level[0][:, wide - 4 + slot : wide - 4 + slot + 1] for slot in range(4)] for level in rows
    ]
    return show, fold


def wide_row(store, place, row_ref):
    hands = row_ref.shape[1]
    store[place : place + 1, 0:hands] = row_ref[...]
    return store[place : place + 1, :]


def first_kernel(size, far, shift_ref, home_ref, odd_ref, even_ref, *rest):
    if far:
        far_ref, rest = rest[0], rest[1:]
    one_ref, two_ref, block_ref, chain_ref, value_ref, square_ref = rest[:6]
    from_left, from_right, window, ranges, cols = rest[6:]
    _, tiles, planes, groups, _ = home_ref.shape
    shift = shifts_in(shift_ref)
    spread_messages(lax.axis_index("node"), from_left, from_right, odd_ref, even_ref, size)
    chain = lax.broadcasted_iota(jnp.int32, (groups, LANES), 0)
    places = [(tile, plane) for tile in range(tiles) for plane in range(planes)]
    if far:
        for tile, plane in places:
            window[tile, plane, 16 : 16 + FAR, :] = far_ref[
                tile, plane * FAR : plane * FAR + FAR, :
            ]
    point = [[[] for _ in range(planes)] for _ in range(4)]
    for tile, plane in places:
        top = jnp.where(
            chain < shift[0],
            from_left[tile, plane, 8:16, :],
            behind(home_ref[0, tile, plane], shift[0]),
        )
        mid = jnp.where(
            chain < shift[1],
            from_left[tile, plane, pl.ds(8 + shift[0], 8), :],
            behind(home_ref[1, tile, plane], shift[1]),
        )
        low = jnp.where(
            chain + shift[2] < 8,
            ahead(home_ref[2, tile, plane], shift[2]),
            from_right[tile, plane, pl.ds(shift[2], 8), :],
        )
        end = jnp.where(
            chain + shift[3] < 8,
            ahead(home_ref[3, tile, plane], shift[3]),
            from_right[tile, plane, pl.ds(shift[2] + jnp.minimum(shift[3], 8), 8), :],
        )
        if far:
            far_part = window[tile, plane, pl.ds(shift[3], 8), :]
            end = jnp.where(chain + shift[3] < 16, end, far_part)
        for idx, row in enumerate((top, mid, low, end)):
            point[idx][plane].append(row)
    point = [[jnp.concatenate(rows, axis=1) for rows in level] for level in point]
    for idx in range(4):
        for plane in range(planes):
            chain_ref[idx, plane] = point[idx][plane]
    show, fold = scale_columns(point)
    ranges[...] = jnp.zeros(ranges.shape, jnp.float32)
    range_one = wide_row(ranges, 0, one_ref)
    range_two = wide_row(ranges, 1, two_ref)

    def put(start, stop, found):
        for idx in range(4):
            for slot in range(4):
                value_ref[idx, slot, :, start:stop] = found[idx][slot]

    square_ref[...] = operator_q(
        point, show, fold, range_one, range_two, block_ref, cols, put
    )


def rate_of(parts_ref, entry_count):
    square_sum = jnp.sum(parts_ref[...], axis=0, keepdims=True)[:, 0:1]
    return step_scale / jnp.sqrt(square_sum / entry_count + eps_value)


def second_kernel(entry_count, size, far, shift_ref, chain_ref, value_ref, *rest):
    parts_ref, one_ref, two_ref, block_ref, own_ref, odd_ref, even_ref = rest[:7]
    rest = rest[7:]
    if far:
        far_ref, rest = rest[0], rest[1:]
    square_ref, stage, ranges, cols = rest
    _, tiles, planes, groups, _ = own_ref.shape
    rate = rate_of(parts_ref, entry_count)
    raw = [[chain_ref[idx, plane] for plane in range(3)] for idx in range(4)]
    show, fold = scale_columns(raw)
    point = [
        [
            raw[idx][plane] + rate * (value_ref[idx, plane + 1] - value_ref[idx, 0])
            for plane in range(3)
        ]
        for idx in range(4)
    ]
    ranges[...] = jnp.zeros(ranges.shape, jnp.float32)
    range_one = wide_row(ranges, 0, one_ref)
    range_two = wide_row(ranges, 1, two_ref)

    def put(start, stop, found):
        for idx in range(4):
            for slot in range(4):
                for lane in range(start, stop, LANES):
                    row = found[idx][slot][:, lane - start : lane - start + LANES]
                    own_ref[idx, lane // LANES, slot] = row

    square_ref[...] = operator_q(
        point, show, fold, range_one, range_two, block_ref, cols, put, value_ref
    )
    shift = shifts_in(shift_ref)
    fill_messages(
        lax.axis_index("node"),
        stage,
        (odd_ref, even_ref),
        size,
        own_ref,
        [(0, 8), (1, 8 + shift[0])],
        [(3, shift[2] + jnp.minimum(shift[3], 8)), (2, shift[2])],
    )
    if far:
        for tile in range(tiles):
            for plane in range(planes):
                part = stage.at[0, tile, plane]
                part[pl.ds(jnp.maximum(shift[3] - 8, 0), 8), :] = own_ref[3, tile, plane]
                far_ref[tile, plane * FAR : plane * FAR + FAR, :] = part[8 : 8 + FAR, :]


def last_kernel(entry_count, size, far, shift_ref, own_ref, even_ref, odd_ref, *rest):
    far_ref, rest = (rest[0], rest[1:]) if far else (None, rest)
    parts_ref, logits_ref, new_hbm, half_hbm, from_left, from_right, lined = rest[:7]
    new_ref, half_ref, sems = rest[7:]
    _, tiles, planes, groups, _ = own_ref.shape
    hands = logits_ref.shape[-1]
    shift = shifts_in(shift_ref)
    rate = rate_of(parts_ref, entry_count)
    group = lax.broadcasted_iota(jnp.int32, (groups, LANES), 0)
    spread_messages(lax.axis_index("node"), from_left, from_right, odd_ref, even_ref, size)
    places = [(tile, plane) for tile in range(tiles) for plane in range(planes)]

    def top(tile, plane, own):
        return jnp.where(
            group + shift[0] < 8,
            ahead(own, shift[0]),
            from_right[tile, plane, pl.ds(shift[0], 8), :],
        )

    def mid(tile, plane, own):
        return jnp.where(
            group + shift[1] < 8,
            ahead(own, shift[1]),
            from_right[tile, plane, pl.ds(shift[0] + shift[1], 8), :],
        )

    def low(tile, plane, own):
        return jnp.where(
            group < shift[2], from_left[tile, plane, 8:16, :], behind(own, shift[2])
        )

    def end(tile, plane, own):
        row = jnp.where(
            group < shift[3],
            from_left[tile, plane, pl.ds(8 + shift[2] - jnp.maximum(shift[3] - 8, 0), 8), :],
            behind(own, shift[3]),
        )
        if far:
            far_part = far_ref[tile, plane * FAR : plane * FAR + 8, :]
            row = jnp.where(group < shift[3] - 8, far_part, row)
        return row

    leaving = []

    def leave(source, target, kind, idx):
        leaving.append(pltpu.make_async_copy(source.at[idx], target.at[0, idx], sems.at[kind, idx]))
        leaving[-1].start()

    for idx, found in enumerate((top, mid, low, end)):
        for tile, plane in places:
            row = found(tile, plane, own_ref[idx, tile, plane])
            lined[idx, tile, pl.ds(plane, groups, stride=4), :] = row
        for tile in range(tiles):
            start = tile * LANES
            stop = min(start + LANES, hands)
            value = lined[idx, tile][:, 0 : stop - start]
            half_ref[idx, :, start:stop] = value
            new_ref[idx, :, start:stop] = logits_ref[0, idx, :, start:stop] + rate * value
        leave(half_ref, half_hbm, 0, idx)
        leave(new_ref, new_hbm, 1, idx)
    for copy in leaving:
        copy.wait()


def shared_parts(part):
    count = lax.axis_size("node") * lax.axis_size("board")
    spread = jnp.broadcast_to(part, (count, LANES))
    return lax.all_to_all(spread, ("node", "board"), 0, 0, tiled=True)


def shared_parts_over_nodes(part):
    nodes = lax.axis_size("node")
    boards = lax.axis_size("board")
    total = part
    for turn in range(1, boards):
        pairs = [(board, (board + turn) % boards) for board in range(boards)]
        total = total + lax.ppermute(part, "board", pairs)
    spread = jnp.broadcast_to(total, (nodes, LANES))
    order = [list(range(nodes))[::-1]]
    return lax.all_to_all(spread, "node", 0, 0, axis_index_groups=order, tiled=True)


def step_of_class(
    size,
    far,
    home,
    shift,
    logits,
    pot_size,
    node_type,
    parent_slot,
    range_one,
    range_two,
    hand_rank,
    live_mask,
):
    _, levels, slots, hands = logits.shape
    wide = padded(hands)
    tiles = wide // LANES
    groups = slots // 4
    entry_count = float(logits.size * lax.axis_size("node") * lax.axis_size("board"))
    vmem = pl.BlockSpec(memory_space=pltpu.VMEM)
    f32 = jnp.float32

    def limit(mebi):
        return pltpu.CompilerParams(vmem_limit_bytes=mebi * MEBI)

    def stage(planes, rows=32):
        return pltpu.VMEM((tiles, planes, rows, LANES), f32)

    def two_stages(planes):
        return pltpu.VMEM((2, tiles, planes, 32, LANES), f32)

    anywhere = pl.BlockSpec(memory_space=pl.ANY)
    sent = pl.pallas_call(
        functools.partial(pack_kernel, size, far),
        out_shape=message_shapes(3, wide, size, far),
        in_specs=[vmem, vmem] + [anywhere] * 3,
        scratch_shapes=[two_stages(3)],
        compiler_params=limit(8),
        name="pack",
    )(shift, home, pot_size, node_type, parent_slot)
    got = sent_on(sent[0], sent[1], sent[2:], -2, (0, 1))
    blocks = payoff_blocks(hand_rank, live_mask)
    blocks_all = 3 * 3 + 4 + 3 * 2
    rows = 16 * (-(-blocks_all // 2))
    rows_second = 16 * (-(-(blocks_all - 3) // 2))

    def work(count):
        return [
            pltpu.VMEM((8, wide), f32),
            pltpu.VMEM((count, 2 * wide), jnp.bfloat16),
        ]

    def cost(count):
        return pl.CostEstimate(
            flops=4 * count * wide * wide, bytes_accessed=6 * wide * wide, transcendentals=0
        )

    square_shape = jax.ShapeDtypeStruct((1, LANES), f32)
    chain, value, part = pl.pallas_call(
        functools.partial(first_kernel, size, far),
        out_shape=(
            jax.ShapeDtypeStruct((levels, 3, groups, wide), f32),
            jax.ShapeDtypeStruct((levels, 4, groups, wide), f32),
            square_shape,
        ),
        in_specs=[vmem] * (5 + len(got)),
        scratch_shapes=[stage(3), stage(3), stage(3)] + work(rows),
        compiler_params=limit(32),
        cost_estimate=cost(rows),
        name="first",
    )(shift, home, *got, range_one, range_two, blocks)
    parts = shared_parts(part)
    own, *sent, part = pl.pallas_call(
        functools.partial(second_kernel, entry_count, size, far),
        out_shape=[jax.ShapeDtypeStruct((levels, tiles, 4, groups, LANES), f32)]
        + message_shapes(4, wide, size, far)
        + [square_shape],
        in_specs=[vmem] * 7,
        scratch_shapes=[two_stages(4)] + work(rows_second),
        compiler_params=limit(32),
        cost_estimate=cost(rows_second),
        name="second",
    )(shift, chain, value, parts, range_one, range_two, blocks)
    got = sent_on(sent[0], sent[1], sent[2:], 2, (1, 0))
    parts = shared_parts_over_nodes(part)
    out_shape = jax.ShapeDtypeStruct(logits.shape, f32)
    level_shape = (levels, slots, hands)
    return pl.pallas_call(
        functools.partial(last_kernel, entry_count, size, far),
        out_shape=(out_shape, out_shape),
        in_specs=[vmem] * (4 + len(got)),
        out_specs=(anywhere, anywhere),
        scratch_shapes=[
            stage(4),
            stage(4),
            pltpu.VMEM((levels, tiles, slots, LANES), f32),
            pltpu.VMEM(level_shape, f32),
            pltpu.VMEM(level_shape, f32),
            pltpu.SemaphoreType.DMA((2, levels)),
        ],
        compiler_params=limit(24),
        name="last",
    )(shift, own, got[1], got[0], *got[2:], parts, logits)


def per_device(
    logits, pot_size, node_type, parent_slot, range_one, range_two, hand_rank, live_mask
):
    branches = [
        functools.partial(step_of_class, size, size == CLASSES[-1]) for size in CLASSES
    ]
    home, shift, found = prepared(logits, pot_size, node_type, parent_slot)
    return lax.switch(
        found[0, 0],
        branches,
        home,
        shift,
        logits,
        pot_size,
        node_type,
        parent_slot,
        range_one,
        range_two,
        hand_rank,
        live_mask,
    )


def solution(mesh):
    return jax.shard_map(
        per_device,
        mesh=mesh,
        in_specs=(
            P("board", None, "node", None),
            P(None, "node"),
            P(None, "node"),
            P(None, "node"),
            P("board", None),
            P("board", None),
            P("board", None),
            P("board", None),
        ),
        out_specs=(P("board", None, "node", None), P("board", None, "node", None)),
        check_vma=False,
    )
```
